32 devices in a mesh: dp: 4 (over y, x), fsdp: 8 (over z, core).
Axes of the slice: x: 2, y: 2, z: 4, core: 2. Of those that a mesh axis runs over, the one named last changes fastest.
Arguments:
- enc_input: bfloat16 [8192, 768], P(('dp', 'fsdp')), may hold values from -6 to 6
- enc_segments: int32 [32, 256], P(('dp', 'fsdp')), may hold values from 0 to 5, never falling along the last dimension, each value on 1 to 49 neighbouring positions
- dec_segments: int32 [32, 1024], P(('dp', 'fsdp')), may hold values from 0 to 3, never falling along the last dimension, each value on 1 to 392 neighbouring positions
- block_order: int32 [4, 64], P('dp', 'fsdp'), may hold values from 0 to 63, each once within a row
- dec_cotangent: bfloat16 [32768, 512], P(('dp', 'fsdp')), may hold values from -6 to 6
- enc_qkv: bfloat16 [768, 2304], P(('dp', 'fsdp')), may hold values from -0.21875 to 0.21875
- enc_proj: bfloat16 [768, 768], P(('dp', 'fsdp')), may hold values from -1.5 to 1.5
- enc_fc1: bfloat16 [768, 3072], P(('dp', 'fsdp')), may hold values from -0.21875 to 0.21875
- enc_fc2: bfloat16 [3072, 768], P(('dp', 'fsdp')), may hold values from -0.109375 to 0.109375
- enc_gains: bfloat16 [3, 768], P(None, ('dp', 'fsdp')), may hold values from 0.5 to 1.5
- enc_biases: bfloat16 [7, 768], P(None, ('dp', 'fsdp')), may hold values from -1.75 to 1.75
- enc_fc1_bias: bfloat16 [3072], P(('dp', 'fsdp')), may hold values from -1.75 to 1.75
- embed: bfloat16 [768, 512], P(('dp', 'fsdp')), may hold values from -0.21875 to 0.21875
- mask_token: bfloat16 [512], P(('dp', 'fsdp')), may hold values from -6 to 6
- dec_qkv: bfloat16 [512, 1536], P(('dp', 'fsdp')), may hold values from -0.25 to 0.25
- dec_proj: bfloat16 [512, 512], P(('dp', 'fsdp')), may hold values from -6 to 6
- dec_fc1: bfloat16 [512, 2048], P(('dp', 'fsdp')), may hold values from -0.25 to 0.25
- dec_fc2: bfloat16 [2048, 512], P(('dp', 'fsdp')), may hold values from -0.125 to 0.125
- dec_gains: bfloat16 [2, 512], P(None, ('dp', 'fsdp')), may hold values from 0.5 to 1.5
- dec_biases: bfloat16 [6, 512], P(None, ('dp', 'fsdp')), may hold values from -1.75 to 1.75
- dec_fc1_bias: bfloat16 [2048], P(('dp', 'fsdp')), may hold values from -1.75 to 1.75
- dec_fc2_bias: bfloat16 [512], P(('dp', 'fsdp')), may hold values from -1.75 to 1.75
Outputs:
- dec_output: bfloat16 [32768, 512], P(('dp', 'fsdp'))
- enc_input_grad: bfloat16 [8192, 768], P(('dp', 'fsdp'))
- enc_qkv_grad: float32 [768, 2304], P(('dp', 'fsdp'))
- enc_proj_grad: float32 [768, 768], P(('dp', 'fsdp'))
- enc_fc1_grad: float32 [768, 3072], P(('dp', 'fsdp'))
- enc_fc2_grad: float32 [3072, 768], P(('dp', 'fsdp'))
- enc_gains_grad: float32 [3, 768], P(None, ('dp', 'fsdp'))
- enc_biases_grad: float32 [7, 768], P(None, ('dp', 'fsdp'))
- enc_fc1_bias_grad: float32 [3072], P(('dp', 'fsdp'))
- embed_grad: float32 [768, 512], P(('dp', 'fsdp'))
- mask_token_grad: float32 [512], P(('dp', 'fsdp'))
- dec_qkv_grad: float32 [512, 1536], P(('dp', 'fsdp'))
- dec_proj_grad: float32 [512, 512], P(('dp', 'fsdp'))
- dec_fc1_grad: float32 [512, 2048], P(('dp', 'fsdp'))
- dec_fc2_grad: float32 [2048, 512], P(('dp', 'fsdp'))
- dec_gains_grad: float32 [2, 512], P(None, ('dp', 'fsdp'))
- dec_biases_grad: float32 [6, 512], P(None, ('dp', 'fsdp'))
- dec_fc1_bias_grad: float32 [2048], P(('dp', 'fsdp'))
- dec_fc2_bias_grad: float32 [512], P(('dp', 'fsdp'))
The draws below stay inside these ranges and needn't reach their ends.
Inputs may be any that keep to these rules, and one draw needn't show every extreme that they name: `enc_segments`: within each row of packed sequence, ids never fall; each image has at most 49 rows. `dec_segments`: within each device's row, ids never fall; each decoder sequence has at most 392 rows. `block_order`: each row is a permutation; values below 16 name an encoder block of the same dp index, the others mark mask blocks.
All inputs are finite; a program needn't handle non-finite values.
Results may differ from the reference program's by a relative error of at most 0.02.
Values may be sent and summed in bfloat16 or wider, within the bound.
No kernel may reach another device: no remote copies, remote signals or barrier semaphores. Data moves between devices by JAX's collectives and lax.ppermute only.
A program may use at most 192 MiB of HBM per device.

```python
import math
import jax
import jax.numpy as jnp
import numpy as np
from jax import lax

D = 768
HEADS = 12
HDIM = 64
FF = 3072
DD = 512
DHEADS = 16
DHDIM = 32
DFF = 2048
ENC_SEQ = 256
IMG_VIS = 49
DEC_SEQ = 392
BLOCK = 128
SEQ_DEV = 1
ENC_DEV = 256
DEC_DEV = 1024
ENC_SEQS = 32
ENC_ROWS = 8192
DEC_ROWS = 32768
EBLK_GROUP = 16
DBLK_GROUP = 64
N_DP = 4
DEVICES = 32


def shard_levels(rng, shape, pieces, smallest, largest):
    gain = 1.0
    for dim, shards_of in pieces:
        steps = jax.random.uniform(jax.random.fold_in(jax.random.fold_in(rng, 6), dim), (shards_of,), jnp.float32, smallest / len(pieces), largest / len(pieces))
        gain = gain * jnp.repeat(jnp.exp(steps), shape[dim] // shards_of).reshape((-1,) + (1,) * (len(shape) - 1 - dim))
    return gain


def length_profile(number_of, total, reach, skew):
    loads = [(1 << 20) // math.isqrt(standing ** skew) + 1 for standing in range(2, number_of + 1)]
    surplus, counts = total - reach - (number_of - 1), [1] * (number_of - 1)
    while surplus > 0:
        free = [i for i in range(number_of - 1) if counts[i] < reach]
        whole, remaining = sum([loads[i] for i in free]), surplus
        for i in free:
            extra = min(reach - counts[i], max(1, remaining * loads[i] // whole), surplus)
            counts[i] = counts[i] + extra
            surplus = surplus - extra
    return np.array([reach] + counts)


def uneven(key, number_of, total, reach, skew):
    if number_of == 2:
        one = jax.random.randint(key, (), max(1, total - reach), min(reach, total - 1) + 1)
        return jnp.stack([one, total - one])
    tallies = jnp.asarray(length_profile(number_of, total, reach, skew), jnp.int32)
    pairs = (number_of - 1) // 2
    source_of, receiver = tallies[1:1 + 2 * pairs:2], tallies[2:2 + 2 * pairs:2]
    slack = jnp.minimum(source_of - 1, reach - receiver)
    moved = jax.random.randint(jax.random.fold_in(key, 1), (pairs,), 0, 1 << 20) % (slack + 1)
    tallies = tallies.at[1:1 + 2 * pairs:2].set(source_of - moved).at[2:2 + 2 * pairs:2].set(receiver + moved)
    return tallies[jax.random.permutation(jax.random.fold_in(key, 2), number_of)]


def gaussian(key, dims, scale, limit, cuts=(), kind=jnp.bfloat16):
    entries = jax.random.normal(key, dims, jnp.float32) * scale
    if len(cuts) > 0:
        entries = shard_levels(key, dims, cuts, -0.22, 0.18) * entries
    return jnp.clip(entries, min=-limit, max=limit).astype(kind)


def setup_inputs(seed: int = 0) -> dict:
    arg_keys = jax.random.split(jax.random.key(seed), 23)
    enc_input = gaussian(arg_keys[0], (ENC_ROWS, D), 1.0, 6.0, ((0, 32),))
    enc_segments = jax.vmap(lambda own: jnp.searchsorted(jnp.cumsum(uneven(own, ENC_SEQ // IMG_VIS + 1, ENC_SEQ, IMG_VIS, 0)), jnp.arange(ENC_SEQ), side="right"))(jax.random.split(arg_keys[1], ENC_SEQS)).reshape((ENC_SEQS, ENC_SEQ)).astype(jnp.int32)
    dec_segments = jax.vmap(lambda own: jnp.searchsorted(jnp.cumsum(uneven(own, DEC_DEV // DEC_SEQ + 2, DEC_DEV, DEC_SEQ, 0)), jnp.arange(DEC_DEV), side="right"))(jax.random.split(arg_keys[2], DEVICES)).reshape((DEVICES, DEC_DEV)).astype(jnp.int32)
    block_order = jax.vmap(lambda own: jax.random.permutation(own, DBLK_GROUP))(jax.random.split(arg_keys[3], N_DP)).reshape((N_DP, DBLK_GROUP)).astype(jnp.int32)
    dec_cotangent = gaussian(arg_keys[4], (DEC_ROWS, DD), 1.0, 6.0, ((0, 32),))
    enc_qkv = gaussian(arg_keys[5], (D, 3 * D), D ** -0.5, 0.21875, ((0, 32),))
    enc_proj = gaussian(arg_keys[6], (D, D), (D // IMG_VIS) ** -0.5, 1.5, ((0, 32),))
    enc_fc1 = gaussian(arg_keys[7], (D, FF), D ** -0.5, 0.21875, ((0, 32),))
    enc_fc2 = gaussian(arg_keys[8], (FF, D), FF ** -0.5, 0.109375, ((0, 32),))
    enc_gains = jnp.clip(1.0 + 0.1 * jax.random.normal(arg_keys[9], (3, D), jnp.float32), 0.5, 1.5).astype(jnp.bfloat16)
    enc_biases = gaussian(arg_keys[10], (7, D), 0.3, 1.75, ((1, 32),))
    enc_fc1_bias = gaussian(arg_keys[11], (FF,), 0.3, 1.75, ((0, 32),))
    embed = gaussian(arg_keys[12], (D, DD), D ** -0.5, 0.21875, ((0, 32),))
    mask_token = gaussian(arg_keys[13], (DD,), 1.0, 6.0, ((0, 32),))
    dec_qkv = gaussian(arg_keys[14], (DD, 3 * DD), DD ** -0.5, 0.25, ((0, 32),))
    dec_proj = gaussian(arg_keys[15], (DD, DD), (max(DD // DEC_SEQ, 1)) ** -0.5, 6.0, ((0, 32),))
    dec_fc1 = gaussian(arg_keys[16], (DD, DFF), DD ** -0.5, 0.25, ((0, 32),))
    dec_fc2 = gaussian(arg_keys[17], (DFF, DD), DFF ** -0.5, 0.125, ((0, 32),))
    dec_gains = jnp.clip(1.0 + 0.1 * jax.random.normal(arg_keys[18], (2, DD), jnp.float32), 0.5, 1.5).astype(jnp.bfloat16)
    dec_biases = gaussian(arg_keys[19], (6, DD), 0.3, 1.75, ((1, 32),))
    dec_fc1_bias = gaussian(arg_keys[20], (DFF,), 0.3, 1.75, ((0, 32),))
    dec_fc2_bias = gaussian(arg_keys[21], (DD,), 0.3, 1.75, ((0, 32),))
    return dict(enc_input=enc_input, enc_segments=enc_segments, dec_segments=dec_segments, block_order=block_order, dec_cotangent=dec_cotangent, enc_qkv=enc_qkv, enc_proj=enc_proj, enc_fc1=enc_fc1, enc_fc2=enc_fc2, enc_gains=enc_gains, enc_biases=enc_biases, enc_fc1_bias=enc_fc1_bias, embed=embed, mask_token=mask_token, dec_qkv=dec_qkv, dec_proj=dec_proj, dec_fc1=dec_fc1, dec_fc2=dec_fc2, dec_gains=dec_gains, dec_biases=dec_biases, dec_fc1_bias=dec_fc1_bias, dec_fc2_bias=dec_fc2_bias)


@jax.custom_vjp
def low(v):
    return lax.optimization_barrier(v.astype(jnp.bfloat16)).astype(jnp.float32)

@jax.custom_vjp
def low_back(v):
    return v

def low_keep(v):
    return (low(v), None)

def low_pass(kept, grad):
    return (grad,)

def back_keep(v):
    return (v, None)

def back_low(kept, grad):
    return (low(grad),)
low.defvjp(low_keep, low_pass)
low_back.defvjp(back_keep, back_low)
EPSILON = 1e-06
NEGATIVE = -1e+30
HIGH = lax.Precision.HIGHEST

def layer_norm(values, gain_vec, shift_vec):
    average = lax.optimization_barrier(jnp.mean(values, axis=-1, keepdims=True))
    centred = values - average
    variance = lax.optimization_barrier(jnp.mean(centred * centred, axis=-1, keepdims=True))
    return centred * lax.rsqrt(variance + EPSILON) * gain_vec + shift_vec

def product(left, right):
    return jnp.dot(left, right, precision=HIGH)

def positions(count, width):
    places = jnp.arange(count, dtype=jnp.float32)[:, None]
    columns = jnp.arange(width)
    rates = jnp.exp((2 * (columns // 2)).astype(jnp.float32) * (-math.log(10000.0) / width))
    angles = places * rates[None, :]
    return jnp.where((columns % 2 == 0)[None, :], jnp.sin(angles), jnp.cos(angles))

def attention(qkv, segments, head_count, head_dim, packs):
    total_rows = qkv.shape[0]
    span = total_rows // packs
    shaped = qkv.reshape(packs, span, 3, head_count, head_dim)
    scores = jnp.einsum('pqhd,pkhd->phqk', shaped[:, :, 0], shaped[:, :, 1], precision=HIGH) * head_dim ** (-0.5)
    scores = low_back(scores)
    groups = segments.reshape(packs, span)
    same_group = (groups[:, :, None] == groups[:, None, :])[:, None]
    probs = low(jax.nn.softmax(jnp.where(same_group, scores, NEGATIVE), axis=-1))
    mixed = jnp.einsum('phqk,pkhd->pqhd', probs, shaped[:, :, 2], precision=HIGH)
    return mixed.reshape(total_rows, head_count * head_dim)

def block(rows_in, segments, weights, head_count, head_dim, packs):
    qkv_w, proj_w, up_w, down_w, gain_rows, shift_rows, up_shift = weights
    normed = layer_norm(rows_in, gain_rows[0], shift_rows[0])
    qkv_shift = jnp.concatenate([shift_rows[1], jnp.zeros_like(shift_rows[1]), shift_rows[2]])
    qkv = low_back(low(product(low(normed), qkv_w) + qkv_shift))
    attended = low_back(low(attention(qkv, segments, head_count, head_dim, packs)))
    middle = rows_in + low_back(product(attended, proj_w) + shift_rows[3])
    normed_two = layer_norm(middle, gain_rows[1], shift_rows[4])
    hidden = low_back(product(low(normed_two), up_w) + up_shift)
    activated = low(jax.nn.gelu(hidden, approximate=False))
    return middle + low_back(product(activated, down_w) + shift_rows[5])

def reference(enc_input, enc_segments, dec_segments, block_order, dec_cotangent, enc_qkv, enc_proj, enc_fc1, enc_fc2, enc_gains, enc_biases, enc_fc1_bias, embed, mask_token, dec_qkv, dec_proj, dec_fc1, dec_fc2, dec_gains, dec_biases, dec_fc1_bias, dec_fc2_bias):

    def to_float(array_in):
        return array_in.astype(jnp.float32)
    enc_params = (to_float(enc_qkv), to_float(enc_proj), to_float(enc_fc1), to_float(enc_fc2), to_float(enc_gains), to_float(enc_biases), to_float(enc_fc1_bias))
    dec_params = (to_float(dec_qkv), to_float(dec_proj), to_float(dec_fc1), to_float(dec_fc2), to_float(dec_gains), to_float(dec_biases), to_float(dec_fc1_bias), to_float(dec_fc2_bias))

    def forward(enc_rows, enc_weights, embed_w, mask_vec, dec_weights):
        qkv_w, proj_w, up_w, down_w, gain_rows, shift_rows, up_shift = enc_weights
        dqkv_w, dproj_w, dup_w, ddown_w, dgain_rows, dshift_rows, dup_shift, ddown_shift = dec_weights
        enc_block = (qkv_w, proj_w, up_w, down_w, gain_rows[:2], shift_rows[:6], up_shift)
        dec_shift_rows = jnp.concatenate([dshift_rows[1:], ddown_shift[None, :]], axis=0)
        dec_block = (dqkv_w, dproj_w, dup_w, ddown_w, dgain_rows, dec_shift_rows, dup_shift)

        def encode_device(carry, inputs):
            rows_in, seg_rows = inputs
            out_rows = block(rows_in, seg_rows, enc_block, HEADS, HDIM, SEQ_DEV)
            final = layer_norm(out_rows, gain_rows[2], shift_rows[6])
            emitted = low_back(low(product(low(final), embed_w) + dshift_rows[0]))
            return (carry, emitted)
        start = jnp.zeros((), jnp.float32)
        _, embedded = lax.scan(jax.checkpoint(encode_device), start, (enc_rows.reshape(DEVICES, ENC_DEV, D), enc_segments.reshape(DEVICES, ENC_DEV)))
        blocks = embedded.reshape(N_DP, EBLK_GROUP, BLOCK, DD)
        chosen = jnp.clip(block_order, 0, EBLK_GROUP - 1).astype(jnp.int32)

        def pick_blocks(group_blocks, group_index):
            return jnp.take(group_blocks, group_index, axis=0)
        taken = jax.vmap(pick_blocks)(blocks, chosen)
        visible = (block_order < EBLK_GROUP)[:, :, None, None]
        dec_in = jnp.where(visible, taken, mask_vec).reshape(DEVICES, DEC_DEV, DD) + positions(DEC_DEV, DD)

        def decode_device(carry, inputs):
            rows_in, seg_rows = inputs
            return (carry, block(rows_in, seg_rows, dec_block, DHEADS, DHDIM, 1))
        _, decoded = lax.scan(jax.checkpoint(decode_device), start, (dec_in, dec_segments))
        return decoded.reshape(DEC_ROWS, DD)
    primal, backward = jax.vjp(forward, to_float(enc_input), enc_params, to_float(embed), to_float(mask_token), dec_params)
    grads = backward(to_float(dec_cotangent))
    enc_grads = grads[1]
    dec_grads = grads[4]
    return (primal.astype(jnp.bfloat16), grads[0].astype(jnp.bfloat16), enc_grads[0], enc_grads[1], enc_grads[2], enc_grads[3], enc_grads[4], enc_grads[5], enc_grads[6], grads[2], grads[3], dec_grads[0], dec_grads[1], dec_grads[2], dec_grads[3], dec_grads[4], dec_grads[5], dec_grads[6], dec_grads[7])
```

```python
import math

import jax
import jax.numpy as jnp
from jax import lax
from jax.sharding import PartitionSpec as P

HDIM = 64
DHDIM = 32
BLOCK = 128


EPSILON = 1e-06
NEGATIVE = -1e30
GROUP_HEADS = 4


def layer_norm(values, gain_vec, shift_vec):
    average = jnp.mean(values, axis=-1, keepdims=True)
    centred = values - average
    variance = jnp.mean(centred * centred, axis=-1, keepdims=True)
    return centred * lax.rsqrt(variance + EPSILON) * gain_vec + shift_vec


def gelu_exact(values):
    return jax.nn.gelu(values, approximate=False)


def product(left, right):
    return jnp.dot(left, right, preferred_element_type=jnp.float32)


def product_tn(left, right):
    return lax.dot_general(
        left, right, (((0,), (0,)), ((), ())), preferred_element_type=jnp.float32
    )


def product_nt(left, right):
    return lax.dot_general(
        left, right, (((1,), (1,)), ((), ())), preferred_element_type=jnp.float32
    )


def column_sum(values):
    return jnp.sum(values, axis=0, dtype=jnp.float32)


def positions(count, width):
    places = jnp.arange(count, dtype=jnp.float32)[:, None]
    columns = jnp.arange(width)
    rates = jnp.exp((2 * (columns // 2)).astype(jnp.float32) * (-math.log(10000.0) / width))
    angles = places * rates[None, :]
    return jnp.where((columns % 2 == 0)[None, :], jnp.sin(angles), jnp.cos(angles))


def block_place(counter, total_rows, query_rows, window, group_count, head_dim):
    block_number = counter // group_count
    group_number = counter % group_count
    query_start = block_number * query_rows
    key_start = jnp.clip(query_start - (window - query_rows) // 2, 0, total_rows - window)
    return (
        query_start,
        key_start,
        group_number * GROUP_HEADS * head_dim,
        group_number * GROUP_HEADS,
    )


def cut_parts(
    queries,
    keys_in,
    values_in,
    segments,
    query_start,
    key_start,
    column,
    query_rows,
    window,
    head_dim,
):
    group_width = GROUP_HEADS * head_dim
    query_part = lax.dynamic_slice(
        queries, (query_start, column), (query_rows, group_width)
    ).reshape(query_rows, GROUP_HEADS, head_dim)
    key_part = lax.dynamic_slice(keys_in, (key_start, column), (window, group_width)).reshape(
        window, GROUP_HEADS, head_dim
    )
    value_part = lax.dynamic_slice(values_in, (key_start, column), (window, group_width)).reshape(
        window, GROUP_HEADS, head_dim
    )
    query_seg = lax.dynamic_slice_in_dim(segments, query_start, query_rows)
    return (query_part, key_part, value_part, query_seg, segments)


def masked_scores(query_part, key_part, query_seg, key_seg, scale):
    scores = (
        jnp.einsum("qhd,khd->hqk", query_part, key_part, preferred_element_type=jnp.float32) * scale
    )
    return jnp.where((query_seg[:, None] == key_seg[None, :])[None], scores, NEGATIVE)


def attend_forward(queries, keys_in, values_in, segments, head_dim, query_rows, window):
    total_rows, width = queries.shape
    group_count = width // (GROUP_HEADS * head_dim)
    steps_total = total_rows // query_rows * group_count
    scale = head_dim ** (-0.5)

    def one_step(counter, carry):
        outputs, log_sums = carry
        query_start, key_start, column, head_start = block_place(
            counter, total_rows, query_rows, window, group_count, head_dim
        )
        query_part, key_part, value_part, query_seg, key_seg = cut_parts(
            queries,
            keys_in,
            values_in,
            segments,
            query_start,
            key_start,
            column,
            query_rows,
            window,
            head_dim,
        )
        scores = masked_scores(query_part, key_part, query_seg, key_seg, scale)
        maxima = jnp.max(scores, axis=-1, keepdims=True)
        unnormed = jnp.exp(scores - maxima)
        totals = jnp.sum(unnormed, axis=-1, keepdims=True)
        probs = (unnormed / totals).astype(jnp.bfloat16)
        mixed = jnp.einsum(
            "hqk,khd->qhd", probs, value_part, preferred_element_type=jnp.float32
        ).reshape(query_rows, GROUP_HEADS * head_dim)
        outputs = lax.dynamic_update_slice(outputs, mixed, (query_start, column))
        log_sums = lax.dynamic_update_slice(
            log_sums, (maxima + jnp.log(totals))[:, :, 0], (head_start, query_start)
        )
        return (outputs, log_sums)

    start = (
        jnp.zeros((total_rows, width), jnp.float32),
        jnp.zeros((width // head_dim, total_rows), jnp.float32),
    )
    return lax.fori_loop(0, steps_total, one_step, start)


def add_into(total, piece, row_start, column):
    current = lax.dynamic_slice(total, (row_start, column), piece.shape)
    return lax.dynamic_update_slice(total, current + piece, (row_start, column))


def attend_backward(
    queries, keys_in, values_in, segments, grad_out, log_sums, head_dim, query_rows, window
):
    total_rows, width = queries.shape
    group_width = GROUP_HEADS * head_dim
    group_count = width // group_width
    steps_total = total_rows // query_rows * group_count
    scale = head_dim ** (-0.5)

    def one_step(counter, carry):
        query_grads, key_grads, value_grads = carry
        query_start, key_start, column, head_start = block_place(
            counter, total_rows, query_rows, window, group_count, head_dim
        )
        query_part, key_part, value_part, query_seg, key_seg = cut_parts(
            queries,
            keys_in,
            values_in,
            segments,
            query_start,
            key_start,
            column,
            query_rows,
            window,
            head_dim,
        )
        scores = masked_scores(query_part, key_part, query_seg, key_seg, scale)
        log_part = lax.dynamic_slice(log_sums, (head_start, query_start), (GROUP_HEADS, query_rows))
        probs = jnp.exp(scores - log_part[:, :, None])
        grad_part = lax.dynamic_slice(
            grad_out, (query_start, column), (query_rows, group_width)
        ).reshape(query_rows, GROUP_HEADS, head_dim)
        grad_probs = jnp.einsum(
            "qhd,khd->hqk", grad_part, value_part, preferred_element_type=jnp.float32
        )
        value_piece = jnp.einsum(
            "hqk,qhd->khd",
            probs.astype(jnp.bfloat16),
            grad_part,
            preferred_element_type=jnp.float32,
        ).reshape(window, group_width)
        inner = jnp.sum(probs * grad_probs, axis=-1, keepdims=True)
        score_grads = (probs * (grad_probs - inner)).astype(jnp.bfloat16)
        query_piece = (
            jnp.einsum(
                "hqk,khd->qhd", score_grads, key_part, preferred_element_type=jnp.float32
            ).reshape(query_rows, group_width)
            * scale
        )
        key_piece = (
            jnp.einsum(
                "hqk,qhd->khd", score_grads, query_part, preferred_element_type=jnp.float32
            ).reshape(window, group_width)
            * scale
        )
        query_grads = lax.dynamic_update_slice(query_grads, query_piece, (query_start, column))
        key_grads = add_into(key_grads, key_piece, key_start, column)
        value_grads = add_into(value_grads, value_piece, key_start, column)
        return (query_grads, key_grads, value_grads)

    empty = jnp.zeros((total_rows, width), jnp.float32)
    return lax.fori_loop(0, steps_total, one_step, (empty, empty, empty))


def block_forward(rows_in, segments, weights, head_dim, query_rows, window):
    qkv_w, proj_w, up_w, down_w, gain_rows, shift_rows, up_shift = weights
    width = rows_in.shape[1]
    normed_low = layer_norm(rows_in, gain_rows[0], shift_rows[0]).astype(jnp.bfloat16)
    qkv_shift = jnp.concatenate([shift_rows[1], jnp.zeros_like(shift_rows[1]), shift_rows[2]])
    qkv = (product(normed_low, qkv_w) + qkv_shift).astype(jnp.bfloat16)
    attended, log_sums = attend_forward(
        qkv[:, :width],
        qkv[:, width : 2 * width],
        qkv[:, 2 * width :],
        segments,
        head_dim,
        query_rows,
        window,
    )
    attended_low = attended.astype(jnp.bfloat16)
    middle = rows_in + product(attended_low, proj_w) + shift_rows[3]
    normed_two_low = layer_norm(middle, gain_rows[1], shift_rows[4]).astype(jnp.bfloat16)
    hidden_pre = product(normed_two_low, up_w) + up_shift
    hidden_low = gelu_exact(hidden_pre).astype(jnp.bfloat16)
    result = middle + product(hidden_low, down_w) + shift_rows[5]
    saved = (
        rows_in,
        middle,
        normed_low,
        qkv,
        attended_low,
        log_sums,
        normed_two_low,
        hidden_pre,
        hidden_low,
    )
    return (result, saved)


def block_backward(grad_out, segments, weights, saved, head_dim, query_rows, window):
    qkv_w, proj_w, up_w, down_w, gain_rows, shift_rows, up_shift = weights
    (
        rows_in,
        middle,
        normed_low,
        qkv,
        attended_low,
        log_sums,
        normed_two_low,
        hidden_pre,
        hidden_low,
    ) = saved
    width = rows_in.shape[1]
    grad_low = grad_out.astype(jnp.bfloat16)
    down_grad = product_tn(hidden_low, grad_low)
    down_shift_grad = column_sum(grad_low)
    hidden_grad = product_nt(grad_low, down_w)
    _, gelu_back = jax.vjp(gelu_exact, hidden_pre)
    pre_low = gelu_back(hidden_grad)[0].astype(jnp.bfloat16)
    up_grad = product_tn(normed_two_low, pre_low)
    up_shift_grad = column_sum(pre_low)
    _, norm_two_back = jax.vjp(layer_norm, middle, gain_rows[1], shift_rows[4])
    middle_part, gain_two_grad, shift_four_grad = norm_two_back(product_nt(pre_low, up_w))
    middle_grad = grad_out + middle_part
    middle_low = middle_grad.astype(jnp.bfloat16)
    proj_grad = product_tn(attended_low, middle_low)
    proj_shift_grad = column_sum(middle_low)
    attended_grad = product_nt(middle_low, proj_w).astype(jnp.bfloat16)
    query_grads, key_grads, value_grads = attend_backward(
        qkv[:, :width],
        qkv[:, width : 2 * width],
        qkv[:, 2 * width :],
        segments,
        attended_grad,
        log_sums,
        head_dim,
        query_rows,
        window,
    )
    qkv_grad_low = jnp.concatenate([query_grads, key_grads, value_grads], axis=1).astype(
        jnp.bfloat16
    )
    qkv_grad = product_tn(normed_low, qkv_grad_low)
    qkv_sums = column_sum(qkv_grad_low)
    _, norm_one_back = jax.vjp(layer_norm, rows_in, gain_rows[0], shift_rows[0])
    input_part, gain_one_grad, shift_zero_grad = norm_one_back(product_nt(qkv_grad_low, qkv_w))
    input_grad = middle_grad + input_part
    gain_grads = jnp.stack([gain_one_grad, gain_two_grad])
    shift_grads = jnp.stack(
        [
            shift_zero_grad,
            qkv_sums[:width],
            qkv_sums[2 * width :],
            proj_shift_grad,
            shift_four_grad,
            down_shift_grad,
        ]
    )
    return (
        input_grad,
        (qkv_grad, proj_grad, up_grad, down_grad, gain_grads, shift_grads, up_shift_grad),
    )


AXES = ("dp", "fsdp")


def pack_vectors(pieces, rows):
    wide = jnp.concatenate([p.reshape(-1, rows) for p in pieces], axis=0)
    wide = jnp.pad(wide, ((0, 128 - wide.shape[0]), (0, 0)))
    return wide.T


def pack_tall(weight, rows):
    parts = weight.shape[0] // rows
    return [weight[i * rows : (i + 1) * rows] for i in range(parts)]


def unpack_tall(columns, devices, width):
    rows = columns.shape[0] // devices
    parts = columns.shape[1] // width
    return (
        columns.reshape(devices, rows, parts, width)
        .transpose(0, 2, 1, 3)
        .reshape(devices * parts * rows, width)
    )


def repack_tall(weight, devices, rows):
    parts = weight.shape[0] // (devices * rows)
    width = weight.shape[1]
    return (
        weight.reshape(devices, parts, rows, width)
        .transpose(0, 2, 1, 3)
        .reshape(devices * rows, parts * width)
    )


def split_columns(array, widths):
    out, at = [], 0
    for w in widths:
        out.append(array[:, at : at + w])
        at += w
    return out


def long_vector(rows_of, devices):
    parts, total = rows_of.shape
    return rows_of.reshape(parts, devices, total // devices).transpose(1, 0, 2).reshape(-1)


def long_rows(vector, devices, rows):
    parts = vector.shape[0] // (devices * rows)
    return vector.reshape(devices, parts, rows).transpose(1, 0, 2).reshape(parts, -1)


def per_device(
    enc_input,
    enc_segments,
    dec_segments,
    block_order,
    dec_cotangent,
    enc_qkv,
    enc_proj,
    enc_fc1,
    enc_fc2,
    enc_gains,
    enc_biases,
    enc_fc1_bias,
    embed,
    mask_token,
    dec_qkv,
    dec_proj,
    dec_fc1,
    dec_fc2,
    dec_gains,
    dec_biases,
    dec_fc1_bias,
    dec_fc2_bias,
):
    devices = lax.axis_size("dp") * lax.axis_size("fsdp")
    seq_rows = enc_segments.shape[1]
    enc_rows, enc_width = enc_input.shape
    dec_rows, dec_width = dec_cotangent.shape
    dec_query = min(512, dec_rows)
    enc_flat = enc_segments.reshape(-1)
    enc_wide = enc_input.astype(jnp.float32)
    erows = enc_qkv.shape[0]
    drows = dec_qkv.shape[0]
    enc_pack = jnp.concatenate(
        [enc_qkv, enc_proj, enc_fc1, embed]
        + pack_tall(enc_fc2, erows)
        + [pack_vectors([enc_gains, enc_biases, enc_fc1_bias], erows)],
        axis=1,
    )
    dec_pack = jnp.concatenate(
        [dec_qkv, dec_proj, dec_fc1]
        + pack_tall(dec_fc2, drows)
        + [
            pack_vectors(
                [dec_gains, dec_biases, dec_fc2_bias[None], mask_token[None], dec_fc1_bias], drows
            )
        ],
        axis=1,
    )
    enc_all = lax.all_gather(enc_pack, AXES, axis=0, tiled=True)
    dec_all = lax.all_gather(dec_pack, AXES, axis=0, tiled=True)
    ff = enc_fc1.shape[1]
    dff = dec_fc1.shape[1]
    qkv_w, proj_w, up_w, embed_full, down_c, vec_c = split_columns(
        enc_all, [3 * enc_width, enc_width, ff, dec_width, ff, 128]
    )
    down_w = unpack_tall(down_c, devices, enc_width)
    vecs = vec_c.T[:14].astype(jnp.float32)
    final_gain = vecs[2]
    final_shift = vecs[9]
    enc_block = (
        qkv_w,
        proj_w,
        up_w,
        down_w,
        vecs[:2],
        vecs[3:9],
        long_vector(vecs[10:14], devices),
    )
    enc_out, enc_saved = block_forward(enc_wide, enc_flat, enc_block, HDIM, seq_rows, seq_rows)
    final_low = layer_norm(enc_out, final_gain, final_shift).astype(jnp.bfloat16)
    dqkv_w, dproj_w, dup_w, ddown_c, dvec_c = split_columns(
        dec_all, [3 * dec_width, dec_width, dff, dff, 128]
    )
    ddown_w = unpack_tall(ddown_c, devices, dec_width)
    dvecs = dvec_c.T[:14].astype(jnp.float32)
    dec_shifts = dvecs[2:8]
    mask_full = dvecs[9]
    dec_shift_rows = dvecs[3:9]
    dec_block = (
        dqkv_w,
        dproj_w,
        dup_w,
        ddown_w,
        dvecs[:2],
        dec_shift_rows,
        long_vector(dvecs[10:14], devices),
    )
    embedded = (product(final_low, embed_full) + dec_shifts[0]).astype(jnp.bfloat16)
    group_blocks = lax.axis_size("fsdp") * enc_rows // BLOCK
    order = block_order[0]
    row_source = (order[:, None] * BLOCK + jnp.arange(BLOCK, dtype=jnp.int32)[None, :]).reshape(-1)
    visible_rows = jnp.broadcast_to(
        (order < group_blocks)[:, None], (order.shape[0], BLOCK)
    ).reshape(-1)
    piece = lax.all_gather(embedded, "fsdp", axis=0, tiled=True)
    local = row_source
    inside = visible_rows & (local >= 0) & (local < piece.shape[0])
    taken = jnp.take(piece, jnp.clip(local, 0, piece.shape[0] - 1), axis=0)
    assembled = jnp.where(inside[:, None], taken, jnp.zeros((dec_rows, dec_width), jnp.bfloat16))
    dec_wide = jnp.where(
        visible_rows[:, None],
        assembled.astype(jnp.float32),
        mask_full[None, :],
    ) + positions(dec_rows, dec_width)
    dec_out, dec_saved = block_forward(
        dec_wide, dec_segments[0], dec_block, DHDIM, dec_query, dec_rows
    )
    dec_in_grad, dg = block_backward(
        dec_cotangent.astype(jnp.float32),
        dec_segments[0],
        dec_block,
        dec_saved,
        DHDIM,
        dec_query,
        dec_rows,
    )
    mask_grad = jnp.sum(jnp.where(visible_rows[:, None], 0.0, dec_in_grad), axis=0)
    local = row_source
    inside = visible_rows & (local >= 0) & (local < lax.axis_size("fsdp") * enc_rows)
    target = jnp.where(inside, local, lax.axis_size("fsdp") * enc_rows)
    embed_row_grad = lax.psum_scatter(
        jnp.zeros((lax.axis_size("fsdp") * enc_rows, dec_width), jnp.float32)
        .at[target]
        .add(dec_in_grad, mode="drop")
        .astype(jnp.bfloat16),
        "fsdp",
        scatter_dimension=0,
        tiled=True,
    )
    embed_grad = product_tn(final_low, embed_row_grad)
    embed_shift_grad = column_sum(embed_row_grad)
    _, final_back = jax.vjp(layer_norm, enc_out, final_gain, final_shift)
    enc_out_grad, final_gain_grad, final_shift_grad = final_back(
        product_nt(embed_row_grad, embed_full)
    )
    low = jnp.bfloat16
    dec_vec_grads = jnp.concatenate(
        [
            dg[4],
            embed_shift_grad[None],
            dg[5],
            mask_grad[None],
            long_rows(dg[6], devices, drows),
            jnp.zeros((114, dec_width), jnp.float32),
        ],
        axis=0,
    ).T
    dec_grad_pack = jnp.concatenate(
        [dg[0].astype(low), dg[1].astype(low), dg[2].astype(low)]
        + [repack_tall(dg[3].astype(low), devices, drows), dec_vec_grads.astype(low)],
        axis=1,
    )
    dec_own = lax.psum_scatter(dec_grad_pack, AXES, scatter_dimension=0, tiled=True)
    enc_in_grad, eg = block_backward(
        enc_out_grad, enc_flat, enc_block, enc_saved, HDIM, seq_rows, seq_rows
    )
    enc_vec_grads = jnp.concatenate(
        [
            eg[4],
            final_gain_grad[None],
            eg[5],
            final_shift_grad[None],
            long_rows(eg[6], devices, erows),
            jnp.zeros((114, enc_width), jnp.float32),
        ],
        axis=0,
    ).T
    enc_grad_pack = jnp.concatenate(
        [
            eg[0].astype(low),
            eg[1].astype(low),
            eg[2].astype(low),
            embed_grad.astype(low),
            repack_tall(eg[3].astype(low), devices, erows),
            enc_vec_grads.astype(low),
        ],
        axis=1,
    )
    enc_own = lax.psum_scatter(enc_grad_pack, AXES, scatter_dimension=0, tiled=True)
    dq, dp, du, dd, dv = split_columns(
        dec_own.astype(jnp.float32), [3 * dec_width, dec_width, dff, dff, 128]
    )
    dv = dv.T
    eq, ep, eu, em, ed, ev = split_columns(
        enc_own.astype(jnp.float32), [3 * enc_width, enc_width, ff, dec_width, ff, 128]
    )
    ev = ev.T
    return (
        dec_out.astype(jnp.bfloat16),
        enc_in_grad.astype(jnp.bfloat16),
        eq,
        ep,
        eu,
        unpack_tall(ed, 1, enc_width),
        ev[:3],
        ev[3:10],
        ev[10:14].reshape(-1),
        em,
        dv[9],
        dq,
        dp,
        du,
        unpack_tall(dd, 1, dec_width),
        dv[:2],
        dv[2:8],
        dv[10:14].reshape(-1),
        dv[8],
    )


def solution(mesh):
    in_specs = (
        P(("dp", "fsdp"), None),
        P(("dp", "fsdp"), None),
        P(("dp", "fsdp"), None),
        P("dp", "fsdp"),
        P(("dp", "fsdp"), None),
        P(("dp", "fsdp"), None),
        P(("dp", "fsdp"), None),
        P(("dp", "fsdp"), None),
        P(("dp", "fsdp"), None),
        P(None, ("dp", "fsdp")),
        P(None, ("dp", "fsdp")),
        P(("dp", "fsdp")),
        P(("dp", "fsdp"), None),
        P(("dp", "fsdp")),
        P(("dp", "fsdp"), None),
        P(("dp", "fsdp"), None),
        P(("dp", "fsdp"), None),
        P(("dp", "fsdp"), None),
        P(None, ("dp", "fsdp")),
        P(None, ("dp", "fsdp")),
        P(("dp", "fsdp")),
        P(("dp", "fsdp")),
    )
    out_specs = (
        P(("dp", "fsdp"), None),
        P(("dp", "fsdp"), None),
        P(("dp", "fsdp"), None),
        P(("dp", "fsdp"), None),
        P(("dp", "fsdp"), None),
        P(("dp", "fsdp"), None),
        P(None, ("dp", "fsdp")),
        P(None, ("dp", "fsdp")),
        P(("dp", "fsdp")),
        P(("dp", "fsdp"), None),
        P(("dp", "fsdp")),
        P(("dp", "fsdp"), None),
        P(("dp", "fsdp"), None),
        P(("dp", "fsdp"), None),
        P(("dp", "fsdp"), None),
        P(None, ("dp", "fsdp")),
        P(None, ("dp", "fsdp")),
        P(("dp", "fsdp")),
        P(("dp", "fsdp")),
    )
    return jax.shard_map(
        per_device, mesh=mesh, in_specs=in_specs, out_specs=out_specs, check_vma=False
    )
```

```python
import functools
import math

import jax
import jax.numpy as jnp
from jax import lax
from jax.experimental import pallas as pl
from jax.experimental.pallas import tpu as pltpu
from jax.sharding import PartitionSpec as P

HDIM = 64
DHDIM = 32
BLOCK = 128
LANES = 128
TILE = 256
EPSILON = 1e-06
NEGATIVE = -1e30
LOG2E = math.log2(math.e)
AXES = ("dp", "fsdp")
F32 = jnp.float32
LOW = jnp.bfloat16
PARAMS = pltpu.CompilerParams(vmem_limit_bytes=56 * 1024 * 1024)


def mm(left, right):
    return jnp.dot(left, right, preferred_element_type=F32)


def mm_tn(left, right):
    return lax.dot_general(left, right, (((0,), (0,)), ((), ())), preferred_element_type=F32)


def mm_nt(left, right):
    return lax.dot_general(left, right, (((1,), (1,)), ((), ())), preferred_element_type=F32)


def col_sum(values):
    return jnp.sum(values, axis=0, keepdims=True)


def norm_parts(values):
    centred = values - jnp.mean(values, axis=-1, keepdims=True)
    variance = jnp.mean(centred * centred, axis=-1, keepdims=True)
    scale = lax.rsqrt(variance + EPSILON)
    return centred * scale, scale


def norm_back(grad, unit, scale, gain):
    inner = grad * gain
    mean_inner = jnp.mean(inner, axis=-1, keepdims=True)
    mean_cross = jnp.mean(inner * unit, axis=-1, keepdims=True)
    return scale * (inner - mean_inner - unit * mean_cross)


def gelu_parts(hidden):
    cdf = 0.5 + 0.5 * lax.erf(hidden * (0.5**0.5))
    density = jnp.exp(hidden * hidden * -0.5) * (1.0 / math.sqrt(2.0 * math.pi))
    return hidden * cdf, cdf + hidden * density


def full(shape):
    return pl.BlockSpec(shape, lambda *_: (0,) * len(shape))


def at_col(rows, cols, index):
    return pl.BlockSpec((rows, cols), lambda *_: (0, index))


def shape(dims, kind):
    return jax.ShapeDtypeStruct(dims, kind)


def lane_mask(head, head_dim, kind):
    lane = lax.broadcasted_iota(jnp.int32, (1, LANES), 1)
    inside = (lane >= head * head_dim) & (lane < (head + 1) * head_dim)
    return inside.astype(F32).astype(kind)


def tile_range(seg_ref, here, tiles):
    first = seg_ref[0, here * TILE]
    last = seg_ref[0, here * TILE + TILE - 1]
    low = jnp.int32(0)
    high = jnp.int32(tiles)
    for other in range(tiles):
        low += (seg_ref[0, other * TILE + TILE - 1] < first).astype(jnp.int32)
        high -= (seg_ref[0, other * TILE] > last).astype(jnp.int32)
    return low, high


def attend_kernel(
    head_dim, tiles, seg_ref, q_ref, k_ref, v_ref, row_ref, col_ref, out_ref, lse_ref, vt, acc, top, tot
):
    heads = LANES // head_dim
    here = pl.program_id(1)
    factor = head_dim ** (-0.5) * LOG2E

    @pl.when(here == 0)
    def _():
        for u in range(tiles):
            vt[u] = v_ref[u * TILE : (u + 1) * TILE, :].astype(F32).T.astype(LOW)

    acc[...] = jnp.zeros_like(acc)
    top[...] = jnp.full_like(top, NEGATIVE)
    tot[...] = jnp.zeros_like(tot)
    query = q_ref[...]
    row = row_ref[...]

    def step(u, carry):
        start = pl.multiple_of(u * TILE, TILE)
        keys = k_ref[pl.ds(start, TILE), :]
        same = col_ref[pl.ds(start, TILE), :] == row
        for h in range(heads):
            scores = mm_nt(keys * lane_mask(h, head_dim, LOW), query) * factor
            scores = jnp.where(same, scores, NEGATIVE)
            old = top[h : h + 1, :]
            new = jnp.maximum(old, jnp.max(scores, axis=0, keepdims=True))
            probs = jnp.exp2(scores - new)
            alpha = jnp.exp2(old - new)
            top[h : h + 1, :] = new
            tot[h : h + 1, :] = tot[h : h + 1, :] * alpha + col_sum(probs)
            span = slice(h * head_dim, (h + 1) * head_dim)
            acc[span, :] = acc[span, :] * alpha + mm(vt[u, span, :], probs.astype(LOW))
        return carry

    low, high = tile_range(seg_ref, here, tiles)
    lax.fori_loop(low, high, step, 0)
    for h in range(heads):
        span = slice(h * head_dim, (h + 1) * head_dim)
        total = tot[h : h + 1, :]
        acc[span, :] = acc[span, :] / total
        lse_ref[0, 0, h : h + 1, :] = top[h : h + 1, :] + jnp.log2(total)
    out_ref[...] = acc[...].T.astype(LOW)


def attend(qkv, segments, seg_col, head_dim):
    rows, width = qkv.shape[0], qkv.shape[1] // 3
    groups, tiles = width // LANES, rows // TILE
    return pl.pallas_call(
        functools.partial(attend_kernel, head_dim, tiles),
        grid_spec=pltpu.PrefetchScalarGridSpec(
            num_scalar_prefetch=1,
            grid=(groups, tiles),
            in_specs=[
                pl.BlockSpec((TILE, LANES), lambda g, t, s: (t, g)),
                pl.BlockSpec((rows, LANES), lambda g, t, s: (0, groups + g)),
                pl.BlockSpec((rows, LANES), lambda g, t, s: (0, 2 * groups + g)),
                pl.BlockSpec((1, TILE), lambda g, t, s: (0, t)),
                pl.BlockSpec((rows, 1), lambda g, t, s: (0, 0)),
            ],
            out_specs=[
                pl.BlockSpec((TILE, LANES), lambda g, t, s: (t, g)),
                pl.BlockSpec((1, 1, 8, TILE), lambda g, t, s: (g, t, 0, 0)),
            ],
            scratch_shapes=[
                pltpu.VMEM((tiles, LANES, TILE), LOW),
                pltpu.VMEM((LANES, TILE), F32),
                pltpu.VMEM((8, TILE), F32),
                pltpu.VMEM((8, TILE), F32),
            ],
        ),
        out_shape=[shape((rows, width), LOW), shape((groups, tiles, 8, TILE), F32)],
        compiler_params=PARAMS,
        name="attend",
    )(segments, qkv, qkv, qkv, segments, seg_col)


def attend_back_kernel(
    head_dim,
    tiles,
    seg_ref,
    q_ref,
    k_ref,
    v_ref,
    o_ref,
    g_ref,
    lse_ref,
    row_ref,
    col_ref,
    dq_ref,
    dk_ref,
    dv_ref,
    dqt,
    delta,
    dk_acc,
    dv_acc,
):
    heads = LANES // head_dim
    here = pl.program_id(1)
    scale = head_dim ** (-0.5)
    factor = scale * LOG2E

    @pl.when(here == 0)
    def _():
        dqt[...] = jnp.zeros_like(dqt)
        for t in range(tiles):
            rows = slice(t * TILE, (t + 1) * TILE)
            both = (g_ref[rows, :].astype(F32) * o_ref[rows, :].astype(F32)).T
            for h in range(heads):
                delta[t, h : h + 1, :] = col_sum(both[h * head_dim : (h + 1) * head_dim, :])

    keys, vals = k_ref[...], v_ref[...]
    keys_t = keys.astype(F32).T.astype(LOW)
    col = col_ref[...]
    dk_acc[...] = jnp.zeros_like(dk_acc)
    dv_acc[...] = jnp.zeros_like(dv_acc)

    def step(t, carry):
        start = pl.multiple_of(t * TILE, TILE)
        query = q_ref[pl.ds(start, TILE), :]
        grads = g_ref[pl.ds(start, TILE), :]
        same = col == row_ref[t]
        for h in range(heads):
            mask = lane_mask(h, head_dim, LOW)
            span = slice(h * head_dim, (h + 1) * head_dim)
            scores = mm_nt(keys * mask, query) * factor
            scores = jnp.where(same, scores, NEGATIVE)
            probs = jnp.exp2(scores - lse_ref[0, t, h : h + 1, :])
            grad_probs = mm_nt(vals * mask, grads)
            grad_scores = (probs * (grad_probs - delta[t, h : h + 1, :])).astype(LOW)
            dv_acc[...] += mm(probs.astype(LOW), grads * mask)
            dk_acc[...] += mm(grad_scores, query * mask)
            dqt[t, span, :] += mm(keys_t[span, :], grad_scores)
        return carry

    low, high = tile_range(seg_ref, here, tiles)
    lax.fori_loop(low, high, step, 0)
    dk_ref[...] = (dk_acc[...] * scale).astype(LOW)
    dv_ref[...] = dv_acc[...].astype(LOW)

    @pl.when(here == tiles - 1)
    def _():
        for t in range(tiles):
            dq_ref[t * TILE : (t + 1) * TILE, :] = (dqt[t] * scale).T.astype(LOW)


def attend_back(qkv, attended, grad, lse, segments, seg_row, seg_col, head_dim):
    rows, width = attended.shape
    groups, tiles = width // LANES, rows // TILE
    whole = pl.BlockSpec((rows, LANES), lambda g, u, s: (0, g))
    piece = pl.BlockSpec((TILE, LANES), lambda g, u, s: (u, g))
    return pl.pallas_call(
        functools.partial(attend_back_kernel, head_dim, tiles),
        grid_spec=pltpu.PrefetchScalarGridSpec(
            num_scalar_prefetch=1,
            grid=(groups, tiles),
            in_specs=[
                whole,
                pl.BlockSpec((TILE, LANES), lambda g, u, s: (u, groups + g)),
                pl.BlockSpec((TILE, LANES), lambda g, u, s: (u, 2 * groups + g)),
                whole,
                whole,
                pl.BlockSpec((1, tiles, 8, TILE), lambda g, u, s: (g, 0, 0, 0)),
                pl.BlockSpec((tiles, 1, TILE), lambda g, u, s: (0, 0, 0)),
                pl.BlockSpec((TILE, 1), lambda g, u, s: (u, 0)),
            ],
            out_specs=[whole, piece, piece],
            scratch_shapes=[
                pltpu.VMEM((tiles, LANES, TILE), F32),
                pltpu.VMEM((tiles, 8, TILE), F32),
                pltpu.VMEM((TILE, LANES), F32),
                pltpu.VMEM((TILE, LANES), F32),
            ],
        ),
        out_shape=[shape((rows, width), LOW)] * 3,
        compiler_params=PARAMS,
        name="attend_back",
    )(segments, qkv, qkv, qkv, attended, grad, lse, seg_row, seg_col)


def enc_qkv_kernel(x_ref, vec_ref, w_ref, out_ref, normed):
    part = pl.program_id(0)

    @pl.when(part == 0)
    def _():
        unit, _ = norm_parts(x_ref[...].astype(F32))
        normed[...] = (unit * vec_ref[0:1, :] + vec_ref[3:4, :]).astype(LOW)

    bias = jnp.where(part == 0, vec_ref[4:5, :], jnp.where(part == 2, vec_ref[5:6, :], 0.0))
    out_ref[...] = (mm(normed[...], w_ref[...]) + bias).astype(LOW)


def enc_qkv_call(rows_in, vecs, weight):
    rows, width = rows_in.shape
    return pl.pallas_call(
        enc_qkv_kernel,
        grid=(3,),
        in_specs=[
            full((rows, width)),
            full(vecs.shape),
            pl.BlockSpec((width, width), lambda i: (0, i)),
        ],
        out_specs=pl.BlockSpec((rows, width), lambda i: (0, i)),
        out_shape=shape((rows, 3 * width), LOW),
        scratch_shapes=[pltpu.VMEM((rows, width), LOW)],
        compiler_params=PARAMS,
        name="enc_qkv",
    )(rows_in, vecs, weight)


def enc_mid_kernel(
    chunks,
    x_ref,
    att_ref,
    vec_ref,
    b1_ref,
    eb_ref,
    wo_ref,
    w1_ref,
    w2_ref,
    we_ref,
    mid_ref,
    out_ref,
    final_ref,
    act_ref,
    slope_ref,
    emb_ref,
    normed,
    acc,
):
    part = pl.program_id(0)

    @pl.when(part == 0)
    def _():
        middle = x_ref[...].astype(F32) + mm(att_ref[...], wo_ref[...]) + vec_ref[6:7, :]
        mid_ref[...] = middle
        unit, _ = norm_parts(middle)
        normed[...] = (unit * vec_ref[1:2, :] + vec_ref[7:8, :]).astype(LOW)
        acc[...] = middle + vec_ref[8:9, :]

    hidden = mm(normed[...], w1_ref[...]) + b1_ref[...]
    value, slope = gelu_parts(hidden)
    value = value.astype(LOW)
    act_ref[...] = value
    slope_ref[...] = slope
    acc[...] += mm(value, w2_ref[...])

    @pl.when(part == chunks - 1)
    def _():
        result = acc[...]
        out_ref[...] = result
        unit, _ = norm_parts(result)
        final = (unit * vec_ref[2:3, :] + vec_ref[9:10, :]).astype(LOW)
        final_ref[...] = final
        emb_ref[...] = (mm(final, we_ref[...]) + eb_ref[...]).astype(LOW)


def enc_mid(rows_in, attended, vecs, up_bias, emb_bias, wide, down_w, proj_at, up_at, emb_at):
    rows, width = rows_in.shape
    hidden = down_w.shape[0]
    emb_width = emb_bias.shape[1]
    chunks = hidden // width
    return pl.pallas_call(
        functools.partial(enc_mid_kernel, chunks),
        grid=(chunks,),
        in_specs=[
            full((rows, width)),
            full((rows, width)),
            full(vecs.shape),
            pl.BlockSpec((1, width), lambda i: (0, i)),
            full((1, emb_width)),
            at_col(width, width, proj_at // width),
            pl.BlockSpec((width, width), lambda i: (0, up_at // width + i)),
            pl.BlockSpec((width, width), lambda i: (i, 0)),
            at_col(width, emb_width, emb_at // emb_width),
        ],
        out_specs=[
            full((rows, width)),
            full((rows, width)),
            full((rows, width)),
            pl.BlockSpec((rows, width), lambda i: (0, i)),
            pl.BlockSpec((rows, width), lambda i: (0, i)),
            full((rows, emb_width)),
        ],
        out_shape=[
            shape((rows, width), F32),
            shape((rows, width), F32),
            shape((rows, width), LOW),
            shape((rows, hidden), LOW),
            shape((rows, hidden), F32),
            shape((rows, emb_width), LOW),
        ],
        scratch_shapes=[pltpu.VMEM((rows, width), LOW), pltpu.VMEM((rows, width), F32)],
        compiler_params=PARAMS,
        name="enc_mid",
    )(rows_in, attended, vecs, up_bias, emb_bias, wide, wide, down_w, wide)


def enc_mid_back_kernel(
    chunks,
    elow_ref,
    final_ref,
    out_ref,
    mid_ref,
    att_ref,
    act_ref,
    slope_ref,
    vec_ref,
    wo_ref,
    w1_ref,
    w2_ref,
    we_ref,
    demb_ref,
    dw2_ref,
    dw1_ref,
    dwo_ref,
    db1_ref,
    esum_ref,
    sum_ref,
    gmid_ref,
    gatt_ref,
    grad,
    grad_low,
    unit_two,
    scale_two,
    normed,
    dnorm,
):
    part = pl.program_id(0)

    @pl.when(part == 0)
    def _():
        elow = elow_ref[...]
        demb_ref[...] = mm_tn(final_ref[...], elow).astype(LOW)
        esum_ref[...] = jnp.zeros_like(esum_ref)
        esum_ref[0:1, :] = col_sum(elow.astype(F32))
        unit, scale = norm_parts(out_ref[...])
        dfinal = mm_nt(elow, we_ref[...])
        sum_ref[...] = jnp.zeros_like(sum_ref)
        sum_ref[0:1, :] = col_sum(dfinal * unit)
        sum_ref[1:2, :] = col_sum(dfinal)
        total = norm_back(dfinal, unit, scale, vec_ref[2:3, :])
        grad[...] = total
        low = total.astype(LOW)
        grad_low[...] = low
        sum_ref[2:3, :] = col_sum(low.astype(F32))
        unit, scale = norm_parts(mid_ref[...])
        unit_two[...] = unit
        scale_two[...] = jnp.broadcast_to(scale, scale_two.shape)
        normed[...] = (unit * vec_ref[1:2, :] + vec_ref[7:8, :]).astype(LOW)
        dnorm[...] = jnp.zeros_like(dnorm)

    low = grad_low[...]
    dw2_ref[...] = mm_tn(act_ref[...], low).astype(LOW)
    dhid = (slope_ref[...] * mm_nt(low, w2_ref[...])).astype(LOW)
    dw1_ref[...] = mm_tn(normed[...], dhid).astype(LOW)
    db1_ref[...] = col_sum(dhid.astype(F32))
    dnorm[...] += mm_nt(dhid, w1_ref[...])

    @pl.when(part == chunks - 1)
    def _():
        dn = dnorm[...]
        unit = unit_two[...]
        sum_ref[3:4, :] = col_sum(dn * unit)
        sum_ref[4:5, :] = col_sum(dn)
        gmid = grad[...] + norm_back(dn, unit, scale_two[:, 0:1], vec_ref[1:2, :])
        gmid_ref[...] = gmid
        mlow = gmid.astype(LOW)
        sum_ref[5:6, :] = col_sum(mlow.astype(F32))
        dwo_ref[...] = mm_tn(att_ref[...], mlow).astype(LOW)
        gatt_ref[...] = mm_nt(mlow, wo_ref[...]).astype(LOW)


def enc_mid_back(
    elow, final, out, mid, attended, act, slope, vecs, wide, down_w, proj_at, up_at, emb_at
):
    rows, width = mid.shape
    hidden = down_w.shape[0]
    emb_width = elow.shape[1]
    chunks = hidden // width
    by_col = pl.BlockSpec((rows, width), lambda i: (0, i))
    return pl.pallas_call(
        functools.partial(enc_mid_back_kernel, chunks),
        grid=(chunks,),
        in_specs=[
            full((rows, emb_width)),
            full((rows, width)),
            full((rows, width)),
            full((rows, width)),
            full((rows, width)),
            by_col,
            by_col,
            full(vecs.shape),
            at_col(width, width, proj_at // width),
            pl.BlockSpec((width, width), lambda i: (0, up_at // width + i)),
            pl.BlockSpec((width, width), lambda i: (i, 0)),
            at_col(width, emb_width, emb_at // emb_width),
        ],
        out_specs=[
            full((width, emb_width)),
            pl.BlockSpec((width, width), lambda i: (i, 0)),
            pl.BlockSpec((width, width), lambda i: (0, i)),
            full((width, width)),
            pl.BlockSpec((1, width), lambda i: (0, i)),
            full((8, emb_width)),
            full((8, width)),
            full((rows, width)),
            full((rows, width)),
        ],
        out_shape=[
            shape((width, emb_width), LOW),
            shape((hidden, width), LOW),
            shape((width, hidden), LOW),
            shape((width, width), LOW),
            shape((1, hidden), F32),
            shape((8, emb_width), F32),
            shape((8, width), F32),
            shape((rows, width), F32),
            shape((rows, width), LOW),
        ],
        scratch_shapes=[
            pltpu.VMEM((rows, width), F32),
            pltpu.VMEM((rows, width), LOW),
            pltpu.VMEM((rows, width), F32),
            pltpu.VMEM((rows, LANES), F32),
            pltpu.VMEM((rows, width), LOW),
            pltpu.VMEM((rows, width), F32),
        ],
        compiler_params=PARAMS,
        name="enc_mid_back",
    )(elow, final, out, mid, attended, act, slope, vecs, wide, wide, down_w, wide)


def enc_qkv_back_kernel(
    x_ref, dq_ref, dk_ref, dv_ref, gmid_ref, vec_ref, w_ref, dw_ref, din_ref, sum_ref, normed, dnorm
):
    part = pl.program_id(0)

    @pl.when(part == 0)
    def _():
        unit, _ = norm_parts(x_ref[...].astype(F32))
        normed[...] = (unit * vec_ref[0:1, :] + vec_ref[3:4, :]).astype(LOW)
        dnorm[...] = jnp.zeros_like(dnorm)
        sum_ref[...] = jnp.zeros_like(sum_ref)
        sum_ref[2:3, :] = col_sum(dq_ref[...].astype(F32))
        sum_ref[3:4, :] = col_sum(dv_ref[...].astype(F32))

    def one(grad):
        dw_ref[...] = mm_tn(normed[...], grad).astype(LOW)
        dnorm[...] += mm_nt(grad, w_ref[...])

    for index, ref in enumerate((dq_ref, dk_ref, dv_ref)):
        pl.when(part == index)(functools.partial(lambda r: one(r[...]), ref))

    @pl.when(part == 2)
    def _():
        unit, scale = norm_parts(x_ref[...].astype(F32))
        dn = dnorm[...]
        sum_ref[0:1, :] = col_sum(dn * unit)
        sum_ref[1:2, :] = col_sum(dn)
        din = gmid_ref[...] + norm_back(dn, unit, scale, vec_ref[0:1, :])
        din_ref[...] = din.astype(LOW)


def enc_qkv_back(rows_in, dq, dk, dv, gmid, vecs, weight):
    rows, width = rows_in.shape
    whole = full((rows, width))
    by_col = pl.BlockSpec((width, width), lambda i: (0, i))
    return pl.pallas_call(
        enc_qkv_back_kernel,
        grid=(3,),
        in_specs=[whole] * 5 + [full(vecs.shape), by_col],
        out_specs=[by_col, whole, full((8, width))],
        out_shape=[
            shape((width, 3 * width), LOW),
            shape((rows, width), LOW),
            shape((8, width), F32),
        ],
        scratch_shapes=[pltpu.VMEM((rows, width), LOW), pltpu.VMEM((rows, width), F32)],
        compiler_params=PARAMS,
        name="enc_qkv_back",
    )(rows_in, dq, dk, dv, gmid, vecs, weight)


def dec_in_kernel(limit, order_ref, one_ref, two_ref, pos_ref, vec_ref, w_ref, in_ref, qkv_ref):
    step = pl.program_id(0)
    width = in_ref.shape[1]
    for half, ref in enumerate((one_ref, two_ref)):
        visible = order_ref[0, 2 * step + half] < limit
        rows = slice(half * BLOCK, (half + 1) * BLOCK)
        in_ref[rows, :] = (
            jnp.where(visible, ref[...].astype(F32), vec_ref[9:10, :]) + pos_ref[rows, :]
        )
    unit, _ = norm_parts(in_ref[...])
    normed = (unit * vec_ref[0:1, :] + vec_ref[3:4, :]).astype(LOW)
    qkv = mm(normed, w_ref[...])
    qkv_ref[:, :width] = (qkv[:, :width] + vec_ref[4:5, :]).astype(LOW)
    qkv_ref[:, width : 2 * width] = qkv[:, width : 2 * width].astype(LOW)
    qkv_ref[:, 2 * width :] = (qkv[:, 2 * width :] + vec_ref[5:6, :]).astype(LOW)


def dec_in_call(order, gathered, pos, vecs, weight):
    rows, width = pos.shape
    limit = gathered.shape[0] // BLOCK

    def chosen(half):
        def index(i, order_ref):
            return (jnp.clip(order_ref[0, 2 * i + half], 0, limit - 1), 0)

        return pl.BlockSpec((BLOCK, width), index)

    return pl.pallas_call(
        functools.partial(dec_in_kernel, limit),
        grid_spec=pltpu.PrefetchScalarGridSpec(
            num_scalar_prefetch=1,
            grid=(rows // TILE,),
            in_specs=[
                chosen(0),
                chosen(1),
                pl.BlockSpec((TILE, width), lambda i, o: (i, 0)),
                full(vecs.shape),
                at_col(width, 3 * width, 0),
            ],
            out_specs=[
                pl.BlockSpec((TILE, width), lambda i, o: (i, 0)),
                pl.BlockSpec((TILE, 3 * width), lambda i, o: (i, 0)),
            ],
        ),
        out_shape=[shape((rows, width), F32), shape((rows, 3 * width), LOW)],
        compiler_params=PARAMS,
        name="dec_in",
    )(order, gathered, gathered, pos, vecs, weight)


def dec_mid_kernel(
    steps,
    chunks,
    x_ref,
    att_ref,
    cot_ref,
    vec_ref,
    b1_ref,
    wo_ref,
    w1_ref,
    w2_ref,
    out_ref,
    gmid_ref,
    gatt_ref,
    dwo_ref,
    dw1_ref,
    dw2_ref,
    db1_ref,
    sum_ref,
    awo,
    aw1,
    aw2,
    acc,
    dnorm,
):
    step = pl.program_id(0)
    width = x_ref.shape[1]

    @pl.when(step == 0)
    def _():
        awo[...] = jnp.zeros_like(awo)
        aw1[...] = jnp.zeros_like(aw1)
        aw2[...] = jnp.zeros_like(aw2)
        db1_ref[...] = jnp.zeros_like(db1_ref)
        sum_ref[...] = jnp.zeros_like(sum_ref)

    att = att_ref[...]
    low = cot_ref[...]
    middle = x_ref[...] + mm(att, wo_ref[...]) + vec_ref[6:7, :]
    unit, scale = norm_parts(middle)
    normed = (unit * vec_ref[1:2, :] + vec_ref[7:8, :]).astype(LOW)
    acc[...] = middle + vec_ref[8:9, :]
    dnorm[...] = jnp.zeros_like(dnorm)

    def chunk(j, carry):
        cols = pl.ds(pl.multiple_of(j * width, width), width)
        up = w1_ref[:, cols]
        down = w2_ref[cols, :]
        value, slope = gelu_parts(mm(normed, up) + b1_ref[j])
        value = value.astype(LOW)
        acc[...] += mm(value, down)
        aw2[cols, :] += mm_tn(value, low)
        dhid = (slope * mm_nt(low, down)).astype(LOW)
        aw1[:, cols] += mm_tn(normed, dhid)
        db1_ref[j] += col_sum(dhid.astype(F32))
        dnorm[...] += mm_nt(dhid, up)
        return carry

    lax.fori_loop(0, chunks, chunk, 0)
    out_ref[...] = acc[...].astype(LOW)
    dn = dnorm[...]
    sum_ref[0:1, :] += col_sum(dn * unit)
    sum_ref[1:2, :] += col_sum(dn)
    gmid = low.astype(F32) + norm_back(dn, unit, scale, vec_ref[1:2, :])
    gmid_ref[...] = gmid
    mlow = gmid.astype(LOW)
    sum_ref[2:3, :] += col_sum(mlow.astype(F32))
    sum_ref[3:4, :] += col_sum(low.astype(F32))
    awo[...] += mm_tn(att, mlow)
    gatt_ref[...] = mm_nt(mlow, wo_ref[...]).astype(LOW)

    @pl.when(step == steps - 1)
    def _():
        dwo_ref[...] = awo[...].astype(LOW)
        dw1_ref[...] = aw1[...].astype(LOW)
        dw2_ref[...] = aw2[...].astype(LOW)


def dec_mid(dec_in, attended, cotangent, vecs, up_bias, wide, down_w, proj_at, up_at):
    rows, width = dec_in.shape
    hidden = down_w.shape[0]
    chunks = hidden // width
    tile = 2 * TILE
    steps = rows // tile
    by_row = pl.BlockSpec((tile, width), lambda i: (i, 0))
    return pl.pallas_call(
        functools.partial(dec_mid_kernel, steps, chunks),
        grid=(steps,),
        in_specs=[
            by_row,
            by_row,
            by_row,
            full(vecs.shape),
            full((chunks, 1, width)),
            at_col(width, width, proj_at // width),
            at_col(width, hidden, up_at // hidden),
            full((hidden, width)),
        ],
        out_specs=[
            by_row,
            by_row,
            by_row,
            full((width, width)),
            full((width, hidden)),
            full((hidden, width)),
            full((chunks, 1, width)),
            full((8, width)),
        ],
        out_shape=[
            shape((rows, width), LOW),
            shape((rows, width), F32),
            shape((rows, width), LOW),
            shape((width, width), LOW),
            shape((width, hidden), LOW),
            shape((hidden, width), LOW),
            shape((chunks, 1, width), F32),
            shape((8, width), F32),
        ],
        scratch_shapes=[
            pltpu.VMEM((width, width), F32),
            pltpu.VMEM((width, hidden), F32),
            pltpu.VMEM((hidden, width), F32),
            pltpu.VMEM((tile, width), F32),
            pltpu.VMEM((tile, width), F32),
        ],
        compiler_params=PARAMS,
        name="dec_mid",
    )(dec_in, attended, cotangent, vecs, up_bias.reshape(chunks, 1, width), wide, wide, down_w)


def dec_back_kernel(
    limit,
    steps,
    order_ref,
    x_ref,
    dq_ref,
    dk_ref,
    dv_ref,
    gmid_ref,
    vec_ref,
    w_ref,
    dw_ref,
    sum_ref,
    send_ref,
    acc,
):
    step = pl.program_id(0)
    width = x_ref.shape[1]

    @pl.when(step == 0)
    def _():
        acc[...] = jnp.zeros_like(acc)
        sum_ref[...] = jnp.zeros_like(sum_ref)
        send_ref[...] = jnp.zeros_like(send_ref)

    unit, scale = norm_parts(x_ref[...])
    normed = (unit * vec_ref[0:1, :] + vec_ref[3:4, :]).astype(LOW)
    grads = (dq_ref[...], dk_ref[...], dv_ref[...])
    dn = None
    for i, grad in enumerate(grads):
        cols = slice(i * width, (i + 1) * width)
        acc[:, cols] += mm_tn(normed, grad)
        piece = mm_nt(grad, w_ref[:, cols])
        dn = piece if dn is None else dn + piece
    sum_ref[0:1, :] += col_sum(dn * unit)
    sum_ref[1:2, :] += col_sum(dn)
    sum_ref[2:3, :] += col_sum(grads[0].astype(F32))
    sum_ref[3:4, :] += col_sum(grads[2].astype(F32))
    din = gmid_ref[...] + norm_back(dn, unit, scale, vec_ref[0:1, :])
    per = x_ref.shape[0] // BLOCK
    for b in range(per):
        place = order_ref[0, per * step + b]
        rows = din[b * BLOCK : (b + 1) * BLOCK, :]

        @pl.when(place < limit)
        def _():
            send_ref[pl.ds(pl.multiple_of(place * BLOCK, BLOCK), BLOCK), :] = rows.astype(LOW)

        @pl.when(place >= limit)
        def _():
            sum_ref[4:5, :] += col_sum(rows)

    @pl.when(step == steps - 1)
    def _():
        dw_ref[...] = acc[...].astype(LOW)


def dec_back(order, dec_in, dq, dk, dv, gmid, vecs, weight, limit):
    rows, width = dec_in.shape
    tile = 2 * TILE
    steps = rows // tile
    by_row = pl.BlockSpec((tile, width), lambda i, o: (i, 0))
    return pl.pallas_call(
        functools.partial(dec_back_kernel, limit, steps),
        grid_spec=pltpu.PrefetchScalarGridSpec(
            num_scalar_prefetch=1,
            grid=(steps,),
            in_specs=[by_row] * 5 + [full(vecs.shape), at_col(width, 3 * width, 0)],
            out_specs=[
                full((width, 3 * width)),
                full((8, width)),
                full((limit * BLOCK, width)),
            ],
            scratch_shapes=[pltpu.VMEM((width, 3 * width), F32)],
        ),
        out_shape=[
            shape((width, 3 * width), LOW),
            shape((8, width), F32),
            shape((limit * BLOCK, width), LOW),
        ],
        compiler_params=PARAMS,
        name="dec_back",
    )(order, dec_in, dq, dk, dv, gmid, vecs, weight)


def positions(count, width):
    places = jnp.arange(count, dtype=jnp.float32)[:, None]
    columns = jnp.arange(width)
    rates = jnp.exp((2 * (columns // 2)).astype(jnp.float32) * (-math.log(10000.0) / width))
    angles = places * rates[None, :]
    return jnp.where((columns % 2 == 0)[None, :], jnp.sin(angles), jnp.cos(angles))


def pack_vectors(pieces, rows):
    wide = jnp.concatenate([p.reshape(-1, rows) for p in pieces], axis=0)
    wide = jnp.pad(wide, ((0, LANES - wide.shape[0]), (0, 0)))
    return wide.T


def pack_tall(weight, rows):
    parts = weight.shape[0] // rows
    return [weight[i * rows : (i + 1) * rows] for i in range(parts)]


def unpack_tall(columns, devices, width):
    rows = columns.shape[0] // devices
    parts = columns.shape[1] // width
    return (
        columns.reshape(devices, rows, parts, width)
        .transpose(0, 2, 1, 3)
        .reshape(devices * parts * rows, width)
    )


def repack_tall(weight, devices, rows):
    parts = weight.shape[0] // (devices * rows)
    width = weight.shape[1]
    return (
        weight.reshape(devices, parts, rows, width)
        .transpose(0, 2, 1, 3)
        .reshape(devices * rows, parts * width)
    )


def split_columns(array, widths):
    out, at = [], 0
    for w in widths:
        out.append(array[:, at : at + w])
        at += w
    return out


def long_vector(rows_of, devices):
    parts, total = rows_of.shape
    return rows_of.reshape(parts, devices, total // devices).transpose(1, 0, 2).reshape(1, -1)


def long_rows(vector, devices, rows):
    parts = vector.shape[0] // (devices * rows)
    return vector.reshape(devices, parts, rows).transpose(1, 0, 2).reshape(parts, -1)


def per_device(
    enc_input,
    enc_segments,
    dec_segments,
    block_order,
    dec_cotangent,
    enc_qkv,
    enc_proj,
    enc_fc1,
    enc_fc2,
    enc_gains,
    enc_biases,
    enc_fc1_bias,
    embed,
    mask_token,
    dec_qkv,
    dec_proj,
    dec_fc1,
    dec_fc2,
    dec_gains,
    dec_biases,
    dec_fc1_bias,
    dec_fc2_bias,
):
    devices = lax.axis_size("dp") * lax.axis_size("fsdp")
    enc_rows, width = enc_input.shape
    dec_rows, dwidth = dec_cotangent.shape
    erows = enc_qkv.shape[0]
    drows = dec_qkv.shape[0]
    ff = enc_fc1.shape[1]
    dff = dec_fc1.shape[1]
    enc_pack = jnp.concatenate(
        [enc_qkv, enc_proj, enc_fc1]
        + pack_tall(enc_fc2, erows)
        + [embed, pack_vectors([enc_gains, enc_biases, enc_fc1_bias], erows)],
        axis=1,
    )
    dec_pack = jnp.concatenate(
        [dec_qkv, dec_proj, dec_fc1]
        + pack_tall(dec_fc2, drows)
        + [
            pack_vectors(
                [dec_gains, dec_biases, dec_fc2_bias[None], mask_token[None], dec_fc1_bias], drows
            )
        ],
        axis=1,
    )
    enc_all = lax.all_gather(enc_pack, AXES, axis=0, tiled=True)
    dec_all = lax.all_gather(dec_pack, AXES, axis=0, tiled=True)
    proj_at, up_at, down_at, emb_at = 3 * width, 4 * width, 4 * width + ff, 4 * width + 2 * ff
    vec_at = emb_at + dwidth
    dproj_at, dup_at, ddown_at = 3 * dwidth, 4 * dwidth, 4 * dwidth + dff
    dvec_at = ddown_at + dff
    down_w = unpack_tall(enc_all[:, down_at:emb_at], devices, width)
    ddown_w = unpack_tall(dec_all[:, ddown_at:dvec_at], devices, dwidth)
    evecs = enc_all[:, vec_at:].T[:16].astype(F32)
    dvecs = dec_all[:, dvec_at:].T[:16].astype(F32)
    up_bias = long_vector(evecs[10:14], devices)
    dup_bias = long_vector(dvecs[10:14], devices)

    qkv = enc_qkv_call(enc_input, evecs, enc_all)
    enc_col = enc_segments.reshape(-1, 1)
    enc_row = enc_segments.reshape(-1, 1, TILE)
    attended, lse = attend(qkv, enc_segments, enc_col, HDIM)
    mid, enc_out, final, act, slope, embedded = enc_mid(
        enc_input,
        attended,
        evecs,
        up_bias,
        dvecs[2:3],
        enc_all,
        down_w,
        proj_at,
        up_at,
        emb_at,
    )
    gathered = lax.all_gather(embedded, "fsdp", axis=0, tiled=True)
    limit = gathered.shape[0] // BLOCK
    dec_in, dqkv = dec_in_call(block_order, gathered, positions(dec_rows, dwidth), dvecs, dec_all)
    dec_col = dec_segments.reshape(-1, 1)
    dec_row = dec_segments.reshape(-1, 1, TILE)
    dattended, dlse = attend(dqkv, dec_segments, dec_col, DHDIM)
    dec_out, dgmid, dgatt, dwo, dw1, dw2, db1, dsum_mid = dec_mid(
        dec_in,
        dattended,
        dec_cotangent,
        dvecs,
        dup_bias,
        dec_all,
        ddown_w,
        dproj_at,
        dup_at,
    )
    ddq, ddk, ddv = attend_back(
        dqkv, dattended, dgatt, dlse, dec_segments, dec_row, dec_col, DHDIM
    )
    dwqkv, dsum, send = dec_back(
        block_order, dec_in, ddq, ddk, ddv, dgmid, dvecs, dec_all, limit
    )
    elow = lax.psum_scatter(send, "fsdp", scatter_dimension=0, tiled=True)
    demb, ew2, ew1, ewo, eb1, esum_emb, esum_mid, gmid, gatt = enc_mid_back(
        elow,
        final,
        enc_out,
        mid,
        attended,
        act,
        slope,
        evecs,
        enc_all,
        down_w,
        proj_at,
        up_at,
        emb_at,
    )
    dec_vec_grads = jnp.concatenate(
        [
            dsum[0:1],
            dsum_mid[0:1],
            esum_emb[0:1],
            dsum[1:4],
            dsum_mid[2:3],
            dsum_mid[1:2],
            dsum_mid[3:4],
            dsum[4:5],
            long_rows(db1.reshape(-1), devices, drows),
            jnp.zeros((LANES - 14, dwidth), F32),
        ],
        axis=0,
    ).T
    dec_grad_pack = jnp.concatenate(
        [dwqkv, dwo, dw1, repack_tall(dw2, devices, drows), dec_vec_grads.astype(LOW)], axis=1
    )
    dec_own = lax.psum_scatter(dec_grad_pack, AXES, scatter_dimension=0, tiled=True)
    dq, dk, dv = attend_back(qkv, attended, gatt, lse, enc_segments, enc_row, enc_col, HDIM)
    ewqkv, enc_in_grad, esum = enc_qkv_back(enc_input, dq, dk, dv, gmid, evecs, enc_all)
    enc_vec_grads = jnp.concatenate(
        [
            esum[0:1],
            esum_mid[3:4],
            esum_mid[0:1],
            esum[1:4],
            esum_mid[5:6],
            esum_mid[4:5],
            esum_mid[2:3],
            esum_mid[1:2],
            long_rows(eb1.reshape(-1), devices, erows),
            jnp.zeros((LANES - 14, width), F32),
        ],
        axis=0,
    ).T
    enc_grad_pack = jnp.concatenate(
        [ewqkv, ewo, ew1, repack_tall(ew2, devices, erows), demb, enc_vec_grads.astype(LOW)],
        axis=1,
    )
    enc_own = lax.psum_scatter(enc_grad_pack, AXES, scatter_dimension=0, tiled=True)
    rq, rp, ru, rd, rv = split_columns(
        dec_own.astype(F32), [3 * dwidth, dwidth, dff, dff, LANES]
    )
    rv = rv.T
    eq, ep, eu, ed, em, ev = split_columns(
        enc_own.astype(F32), [3 * width, width, ff, ff, dwidth, LANES]
    )
    ev = ev.T
    return (
        dec_out,
        enc_in_grad,
        eq,
        ep,
        eu,
        unpack_tall(ed, 1, width),
        ev[:3],
        ev[3:10],
        ev[10:14].reshape(-1),
        em,
        rv[9],
        rq,
        rp,
        ru,
        unpack_tall(rd, 1, dwidth),
        rv[:2],
        rv[2:8],
        rv[10:14].reshape(-1),
        rv[8],
    )


def solution(mesh):
    in_specs = (
        P(("dp", "fsdp"), None),
        P(("dp", "fsdp"), None),
        P(("dp", "fsdp"), None),
        P("dp", "fsdp"),
        P(("dp", "fsdp"), None),
        P(("dp", "fsdp"), None),
        P(("dp", "fsdp"), None),
        P(("dp", "fsdp"), None),
        P(("dp", "fsdp"), None),
        P(None, ("dp", "fsdp")),
        P(None, ("dp", "fsdp")),
        P(("dp", "fsdp")),
        P(("dp", "fsdp"), None),
        P(("dp", "fsdp")),
        P(("dp", "fsdp"), None),
        P(("dp", "fsdp"), None),
        P(("dp", "fsdp"), None),
        P(("dp", "fsdp"), None),
        P(None, ("dp", "fsdp")),
        P(None, ("dp", "fsdp")),
        P(("dp", "fsdp")),
        P(("dp", "fsdp")),
    )
    out_specs = (
        P(("dp", "fsdp"), None),
        P(("dp", "fsdp"), None),
        P(("dp", "fsdp"), None),
        P(("dp", "fsdp"), None),
        P(("dp", "fsdp"), None),
        P(("dp", "fsdp"), None),
        P(None, ("dp", "fsdp")),
        P(None, ("dp", "fsdp")),
        P(("dp", "fsdp")),
        P(("dp", "fsdp"), None),
        P(("dp", "fsdp")),
        P(("dp", "fsdp"), None),
        P(("dp", "fsdp"), None),
        P(("dp", "fsdp"), None),
        P(("dp", "fsdp"), None),
        P(None, ("dp", "fsdp")),
        P(None, ("dp", "fsdp")),
        P(("dp", "fsdp")),
        P(("dp", "fsdp")),
    )
    return jax.shard_map(
        per_device, mesh=mesh, in_specs=in_specs, out_specs=out_specs, check_vma=False
    )
```

```python
import functools
import math

import jax
import jax.numpy as jnp
from jax import lax
from jax.experimental import pallas as pl
from jax.experimental.pallas import tpu as pltpu
from jax.sharding import PartitionSpec as P

HDIM = 64
DHDIM = 32
BLOCK = 128
LANES = 128
TILE = 256
EPSILON = 1e-06
NEGATIVE = -1e30
LOG2E = math.log2(math.e)
AXES = ("dp", "fsdp")
F32 = jnp.float32
LOW = jnp.bfloat16
PARAMS = pltpu.CompilerParams(vmem_limit_bytes=56 * 1024 * 1024)


def mm(left, right):
    return jnp.dot(left, right, preferred_element_type=F32)


def mm_tn(left, right):
    return lax.dot_general(left, right, (((0,), (0,)), ((), ())), preferred_element_type=F32)


def mm_nt(left, right):
    return lax.dot_general(left, right, (((1,), (1,)), ((), ())), preferred_element_type=F32)


def col_sum(values):
    return jnp.sum(values, axis=0, keepdims=True)


def norm_parts(values):
    centred = values - jnp.mean(values, axis=-1, keepdims=True)
    variance = jnp.mean(centred * centred, axis=-1, keepdims=True)
    scale = lax.rsqrt(variance + EPSILON)
    return centred * scale, scale


def norm_back(grad, unit, scale, gain):
    inner = grad * gain
    mean_inner = jnp.mean(inner, axis=-1, keepdims=True)
    mean_cross = jnp.mean(inner * unit, axis=-1, keepdims=True)
    return scale * (inner - mean_inner - unit * mean_cross)


def gelu_parts(hidden):
    cdf = 0.5 + 0.5 * lax.erf(hidden * (0.5**0.5))
    density = jnp.exp(hidden * hidden * -0.5) * (1.0 / math.sqrt(2.0 * math.pi))
    return hidden * cdf, cdf + hidden * density


def full(shape):
    return pl.BlockSpec(shape, lambda *_: (0,) * len(shape))


def at_col(rows, cols, index):
    return pl.BlockSpec((rows, cols), lambda *_: (0, index))


def shape(dims, kind):
    return jax.ShapeDtypeStruct(dims, kind)


def lane_mask(head, head_dim, kind):
    lane = lax.broadcasted_iota(jnp.int32, (1, LANES), 1)
    inside = (lane >= head * head_dim) & (lane < (head + 1) * head_dim)
    return inside.astype(F32).astype(kind)


def tile_range(seg_ref, here, tiles):
    first = seg_ref[0, here * TILE]
    last = seg_ref[0, here * TILE + TILE - 1]
    low = jnp.int32(0)
    high = jnp.int32(tiles)
    for other in range(tiles):
        low += (seg_ref[0, other * TILE + TILE - 1] < first).astype(jnp.int32)
        high -= (seg_ref[0, other * TILE] > last).astype(jnp.int32)
    return low, high


def attend_kernel(
    head_dim, tiles, seg_ref, q_ref, k_ref, v_ref, row_ref, col_ref, out_ref, lse_ref, vt, acc, top, tot
):
    heads = LANES // head_dim
    here = pl.program_id(1)
    factor = head_dim ** (-0.5) * LOG2E

    @pl.when(here == 0)
    def _():
        for u in range(tiles):
            vt[u] = v_ref[u * TILE : (u + 1) * TILE, :].astype(F32).T.astype(LOW)

    acc[...] = jnp.zeros_like(acc)
    top[...] = jnp.full_like(top, NEGATIVE)
    tot[...] = jnp.zeros_like(tot)
    query = q_ref[...]
    row = row_ref[...]

    def step(u, carry):
        start = pl.multiple_of(u * TILE, TILE)
        keys = k_ref[pl.ds(start, TILE), :]
        same = col_ref[pl.ds(start, TILE), :] == row
        for h in range(heads):
            scores = mm_nt(keys * lane_mask(h, head_dim, LOW), query) * factor
            scores = jnp.where(same, scores, NEGATIVE)
            old = top[h : h + 1, :]
            new = jnp.maximum(old, jnp.max(scores, axis=0, keepdims=True))
            probs = jnp.exp2(scores - new)
            alpha = jnp.exp2(old - new)
            top[h : h + 1, :] = new
            tot[h : h + 1, :] = tot[h : h + 1, :] * alpha + col_sum(probs)
            span = slice(h * head_dim, (h + 1) * head_dim)
            acc[span, :] = acc[span, :] * alpha + mm(vt[u, span, :], probs.astype(LOW))
        return carry

    low, high = tile_range(seg_ref, here, tiles)
    lax.fori_loop(low, high, step, 0)
    for h in range(heads):
        span = slice(h * head_dim, (h + 1) * head_dim)
        total = tot[h : h + 1, :]
        acc[span, :] = acc[span, :] / total
        lse_ref[0, 0, h : h + 1, :] = top[h : h + 1, :] + jnp.log2(total)
    out_ref[...] = acc[...].T.astype(LOW)


def attend(qkv, segments, seg_col, head_dim):
    rows, width = qkv.shape[0], qkv.shape[1] // 3
    groups, tiles = width // LANES, rows // TILE
    return pl.pallas_call(
        functools.partial(attend_kernel, head_dim, tiles),
        grid_spec=pltpu.PrefetchScalarGridSpec(
            num_scalar_prefetch=1,
            grid=(groups, tiles),
            in_specs=[
                pl.BlockSpec((TILE, LANES), lambda g, t, s: (t, g)),
                pl.BlockSpec((rows, LANES), lambda g, t, s: (0, groups + g)),
                pl.BlockSpec((rows, LANES), lambda g, t, s: (0, 2 * groups + g)),
                pl.BlockSpec((1, TILE), lambda g, t, s: (0, t)),
                pl.BlockSpec((rows, 1), lambda g, t, s: (0, 0)),
            ],
            out_specs=[
                pl.BlockSpec((TILE, LANES), lambda g, t, s: (t, g)),
                pl.BlockSpec((1, 1, 8, TILE), lambda g, t, s: (g, t, 0, 0)),
            ],
            scratch_shapes=[
                pltpu.VMEM((tiles, LANES, TILE), LOW),
                pltpu.VMEM((LANES, TILE), F32),
                pltpu.VMEM((8, TILE), F32),
                pltpu.VMEM((8, TILE), F32),
            ],
        ),
        out_shape=[shape((rows, width), LOW), shape((groups, tiles, 8, TILE), F32)],
        compiler_params=PARAMS,
        name="attend",
    )(segments, qkv, qkv, qkv, segments, seg_col)


def attend_back_kernel(
    head_dim,
    tiles,
    seg_ref,
    q_ref,
    k_ref,
    v_ref,
    o_ref,
    g_ref,
    lse_ref,
    row_ref,
    col_ref,
    dq_ref,
    dk_ref,
    dv_ref,
    dqt,
    delta,
    dk_acc,
    dv_acc,
):
    heads = LANES // head_dim
    here = pl.program_id(1)
    scale = head_dim ** (-0.5)
    factor = scale * LOG2E

    @pl.when(here == 0)
    def _():
        dqt[...] = jnp.zeros_like(dqt)
        for t in range(tiles):
            rows = slice(t * TILE, (t + 1) * TILE)
            both = (g_ref[rows, :].astype(F32) * o_ref[rows, :].astype(F32)).T
            for h in range(heads):
                delta[t, h : h + 1, :] = col_sum(both[h * head_dim : (h + 1) * head_dim, :])

    keys, vals = k_ref[...], v_ref[...]
    keys_t = keys.astype(F32).T.astype(LOW)
    col = col_ref[...]
    dk_acc[...] = jnp.zeros_like(dk_acc)
    dv_acc[...] = jnp.zeros_like(dv_acc)

    def step(t, carry):
        start = pl.multiple_of(t * TILE, TILE)
        query = q_ref[pl.ds(start, TILE), :]
        grads = g_ref[pl.ds(start, TILE), :]
        same = col == row_ref[t]
        for h in range(heads):
            mask = lane_mask(h, head_dim, LOW)
            span = slice(h * head_dim, (h + 1) * head_dim)
            scores = mm_nt(keys * mask, query) * factor
            scores = jnp.where(same, scores, NEGATIVE)
            probs = jnp.exp2(scores - lse_ref[0, t, h : h + 1, :])
            grad_probs = mm_nt(vals * mask, grads)
            grad_scores = (probs * (grad_probs - delta[t, h : h + 1, :])).astype(LOW)
            dv_acc[...] += mm(probs.astype(LOW), grads * mask)
            dk_acc[...] += mm(grad_scores, query * mask)
            dqt[t, span, :] += mm(keys_t[span, :], grad_scores)
        return carry

    low, high = tile_range(seg_ref, here, tiles)
    lax.fori_loop(low, high, step, 0)
    dk_ref[...] = (dk_acc[...] * scale).astype(LOW)
    dv_ref[...] = dv_acc[...].astype(LOW)

    @pl.when(here == tiles - 1)
    def _():
        for t in range(tiles):
            dq_ref[t * TILE : (t + 1) * TILE, :] = (dqt[t] * scale).T.astype(LOW)


def attend_back(qkv, attended, grad, lse, segments, seg_row, seg_col, head_dim):
    rows, width = attended.shape
    groups, tiles = width // LANES, rows // TILE
    whole = pl.BlockSpec((rows, LANES), lambda g, u, s: (0, g))
    piece = pl.BlockSpec((TILE, LANES), lambda g, u, s: (u, g))
    return pl.pallas_call(
        functools.partial(attend_back_kernel, head_dim, tiles),
        grid_spec=pltpu.PrefetchScalarGridSpec(
            num_scalar_prefetch=1,
            grid=(groups, tiles),
            in_specs=[
                whole,
                pl.BlockSpec((TILE, LANES), lambda g, u, s: (u, groups + g)),
                pl.BlockSpec((TILE, LANES), lambda g, u, s: (u, 2 * groups + g)),
                whole,
                whole,
                pl.BlockSpec((1, tiles, 8, TILE), lambda g, u, s: (g, 0, 0, 0)),
                pl.BlockSpec((tiles, 1, TILE), lambda g, u, s: (0, 0, 0)),
                pl.BlockSpec((TILE, 1), lambda g, u, s: (u, 0)),
            ],
            out_specs=[whole, piece, piece],
            scratch_shapes=[
                pltpu.VMEM((tiles, LANES, TILE), F32),
                pltpu.VMEM((tiles, 8, TILE), F32),
                pltpu.VMEM((TILE, LANES), F32),
                pltpu.VMEM((TILE, LANES), F32),
            ],
        ),
        out_shape=[shape((rows, width), LOW)] * 3,
        compiler_params=PARAMS,
        name="attend_back",
    )(segments, qkv, qkv, qkv, attended, grad, lse, seg_row, seg_col)


def enc_qkv_kernel(x_ref, vec_ref, w_ref, out_ref, normed):
    part = pl.program_id(0)

    @pl.when(part == 0)
    def _():
        unit, _ = norm_parts(x_ref[...].astype(F32))
        normed[...] = (unit * vec_ref[0:1, :] + vec_ref[3:4, :]).astype(LOW)

    bias = jnp.where(part == 0, vec_ref[4:5, :], jnp.where(part == 2, vec_ref[5:6, :], 0.0))
    out_ref[...] = (mm(normed[...], w_ref[...]) + bias).astype(LOW)


def enc_qkv_call(rows_in, vecs, weight):
    rows, width = rows_in.shape
    return pl.pallas_call(
        enc_qkv_kernel,
        grid=(3,),
        in_specs=[
            full((rows, width)),
            full(vecs.shape),
            pl.BlockSpec((width, width), lambda i: (0, i)),
        ],
        out_specs=pl.BlockSpec((rows, width), lambda i: (0, i)),
        out_shape=shape((rows, 3 * width), LOW),
        scratch_shapes=[pltpu.VMEM((rows, width), LOW)],
        compiler_params=PARAMS,
        name="enc_qkv",
    )(rows_in, vecs, weight)


def enc_mid_kernel(
    chunks,
    x_ref,
    att_ref,
    vec_ref,
    b1_ref,
    eb_ref,
    wo_ref,
    w1_ref,
    w2_ref,
    we_ref,
    mid_ref,
    out_ref,
    final_ref,
    act_ref,
    slope_ref,
    emb_ref,
    normed,
    acc,
):
    part = pl.program_id(0)

    @pl.when(part == 0)
    def _():
        middle = x_ref[...].astype(F32) + mm(att_ref[...], wo_ref[...]) + vec_ref[6:7, :]
        mid_ref[...] = middle
        unit, _ = norm_parts(middle)
        normed[...] = (unit * vec_ref[1:2, :] + vec_ref[7:8, :]).astype(LOW)
        acc[...] = middle + vec_ref[8:9, :]

    hidden = mm(normed[...], w1_ref[...]) + b1_ref[...]
    value, slope = gelu_parts(hidden)
    value = value.astype(LOW)
    act_ref[...] = value
    slope_ref[...] = slope
    acc[...] += mm(value, w2_ref[...])

    @pl.when(part == chunks - 1)
    def _():
        result = acc[...]
        out_ref[...] = result
        unit, _ = norm_parts(result)
        final = (unit * vec_ref[2:3, :] + vec_ref[9:10, :]).astype(LOW)
        final_ref[...] = final
        emb_ref[...] = (mm(final, we_ref[...]) + eb_ref[...]).astype(LOW)


def enc_mid(rows_in, attended, vecs, up_bias, emb_bias, wide, up_w, down_w, proj_at, emb_at):
    rows, width = rows_in.shape
    hidden = down_w.shape[0]
    emb_width = emb_bias.shape[1]
    chunks = hidden // width
    return pl.pallas_call(
        functools.partial(enc_mid_kernel, chunks),
        grid=(chunks,),
        in_specs=[
            full((rows, width)),
            full((rows, width)),
            full(vecs.shape),
            pl.BlockSpec((1, width), lambda i: (0, i)),
            full((1, emb_width)),
            at_col(width, width, proj_at // width),
            pl.BlockSpec((width, width), lambda i: (0, i)),
            pl.BlockSpec((width, width), lambda i: (i, 0)),
            at_col(width, emb_width, emb_at // emb_width),
        ],
        out_specs=[
            full((rows, width)),
            full((rows, width)),
            full((rows, width)),
            pl.BlockSpec((rows, width), lambda i: (0, i)),
            pl.BlockSpec((rows, width), lambda i: (0, i)),
            full((rows, emb_width)),
        ],
        out_shape=[
            shape((rows, width), F32),
            shape((rows, width), F32),
            shape((rows, width), LOW),
            shape((rows, hidden), LOW),
            shape((rows, hidden), F32),
            shape((rows, emb_width), LOW),
        ],
        scratch_shapes=[pltpu.VMEM((rows, width), LOW), pltpu.VMEM((rows, width), F32)],
        compiler_params=PARAMS,
        name="enc_mid",
    )(rows_in, attended, vecs, up_bias, emb_bias, wide, up_w, down_w, wide)


def enc_mid_back_kernel(
    chunks,
    elow_ref,
    final_ref,
    out_ref,
    mid_ref,
    att_ref,
    act_ref,
    slope_ref,
    vec_ref,
    wo_ref,
    w1_ref,
    w2_ref,
    we_ref,
    demb_ref,
    dw2_ref,
    dw1_ref,
    dwo_ref,
    db1_ref,
    esum_ref,
    sum_ref,
    gmid_ref,
    gatt_ref,
    grad,
    grad_low,
    unit_two,
    scale_two,
    normed,
    dnorm,
):
    part = pl.program_id(0)

    @pl.when(part == 0)
    def _():
        elow = elow_ref[...]
        demb_ref[...] = mm_tn(final_ref[...], elow).astype(LOW)
        esum_ref[...] = jnp.zeros_like(esum_ref)
        esum_ref[0:1, :] = col_sum(elow.astype(F32))
        unit, scale = norm_parts(out_ref[...])
        dfinal = mm_nt(elow, we_ref[...])
        sum_ref[...] = jnp.zeros_like(sum_ref)
        sum_ref[0:1, :] = col_sum(dfinal * unit)
        sum_ref[1:2, :] = col_sum(dfinal)
        total = norm_back(dfinal, unit, scale, vec_ref[2:3, :])
        grad[...] = total
        low = total.astype(LOW)
        grad_low[...] = low
        sum_ref[2:3, :] = col_sum(low.astype(F32))
        unit, scale = norm_parts(mid_ref[...])
        unit_two[...] = unit
        scale_two[...] = jnp.broadcast_to(scale, scale_two.shape)
        normed[...] = (unit * vec_ref[1:2, :] + vec_ref[7:8, :]).astype(LOW)
        dnorm[...] = jnp.zeros_like(dnorm)

    low = grad_low[...]
    dw2_ref[...] = mm_tn(act_ref[...], low).astype(LOW)
    dhid = (slope_ref[...] * mm_nt(low, w2_ref[...])).astype(LOW)
    dw1_ref[...] = mm_tn(normed[...], dhid).astype(LOW)
    db1_ref[...] = col_sum(dhid.astype(F32))
    dnorm[...] += mm_nt(dhid, w1_ref[...])

    @pl.when(part == chunks - 1)
    def _():
        dn = dnorm[...]
        unit = unit_two[...]
        sum_ref[3:4, :] = col_sum(dn * unit)
        sum_ref[4:5, :] = col_sum(dn)
        gmid = grad[...] + norm_back(dn, unit, scale_two[:, 0:1], vec_ref[1:2, :])
        gmid_ref[...] = gmid
        mlow = gmid.astype(LOW)
        sum_ref[5:6, :] = col_sum(mlow.astype(F32))
        dwo_ref[...] = mm_tn(att_ref[...], mlow).astype(LOW)
        gatt_ref[...] = mm_nt(mlow, wo_ref[...]).astype(LOW)


def enc_mid_back(
    elow, final, out, mid, attended, act, slope, vecs, wide, up_w, down_w, proj_at, emb_at
):
    rows, width = mid.shape
    hidden = down_w.shape[0]
    emb_width = elow.shape[1]
    chunks = hidden // width
    by_col = pl.BlockSpec((rows, width), lambda i: (0, i))
    return pl.pallas_call(
        functools.partial(enc_mid_back_kernel, chunks),
        grid=(chunks,),
        in_specs=[
            full((rows, emb_width)),
            full((rows, width)),
            full((rows, width)),
            full((rows, width)),
            full((rows, width)),
            by_col,
            by_col,
            full(vecs.shape),
            at_col(width, width, proj_at // width),
            pl.BlockSpec((width, width), lambda i: (0, i)),
            pl.BlockSpec((width, width), lambda i: (i, 0)),
            at_col(width, emb_width, emb_at // emb_width),
        ],
        out_specs=[
            full((width, emb_width)),
            pl.BlockSpec((width, width), lambda i: (i, 0)),
            pl.BlockSpec((width, width), lambda i: (0, i)),
            full((width, width)),
            pl.BlockSpec((1, width), lambda i: (0, i)),
            full((8, emb_width)),
            full((8, width)),
            full((rows, width)),
            full((rows, width)),
        ],
        out_shape=[
            shape((width, emb_width), LOW),
            shape((hidden, width), LOW),
            shape((width, hidden), LOW),
            shape((width, width), LOW),
            shape((1, hidden), F32),
            shape((8, emb_width), F32),
            shape((8, width), F32),
            shape((rows, width), F32),
            shape((rows, width), LOW),
        ],
        scratch_shapes=[
            pltpu.VMEM((rows, width), F32),
            pltpu.VMEM((rows, width), LOW),
            pltpu.VMEM((rows, width), F32),
            pltpu.VMEM((rows, LANES), F32),
            pltpu.VMEM((rows, width), LOW),
            pltpu.VMEM((rows, width), F32),
        ],
        compiler_params=PARAMS,
        name="enc_mid_back",
    )(elow, final, out, mid, attended, act, slope, vecs, wide, up_w, down_w, wide)


def enc_qkv_back_kernel(
    x_ref, dq_ref, dk_ref, dv_ref, gmid_ref, vec_ref, w_ref, dw_ref, din_ref, sum_ref, normed, dnorm
):
    part = pl.program_id(0)

    @pl.when(part == 0)
    def _():
        unit, _ = norm_parts(x_ref[...].astype(F32))
        normed[...] = (unit * vec_ref[0:1, :] + vec_ref[3:4, :]).astype(LOW)
        dnorm[...] = jnp.zeros_like(dnorm)
        sum_ref[...] = jnp.zeros_like(sum_ref)
        sum_ref[2:3, :] = col_sum(dq_ref[...].astype(F32))
        sum_ref[3:4, :] = col_sum(dv_ref[...].astype(F32))

    def one(grad):
        dw_ref[...] = mm_tn(normed[...], grad).astype(LOW)
        dnorm[...] += mm_nt(grad, w_ref[...])

    for index, ref in enumerate((dq_ref, dk_ref, dv_ref)):
        pl.when(part == index)(functools.partial(lambda r: one(r[...]), ref))

    @pl.when(part == 2)
    def _():
        unit, scale = norm_parts(x_ref[...].astype(F32))
        dn = dnorm[...]
        sum_ref[0:1, :] = col_sum(dn * unit)
        sum_ref[1:2, :] = col_sum(dn)
        din = gmid_ref[...] + norm_back(dn, unit, scale, vec_ref[0:1, :])
        din_ref[...] = din.astype(LOW)


def enc_qkv_back(rows_in, dq, dk, dv, gmid, vecs, weight):
    rows, width = rows_in.shape
    whole = full((rows, width))
    by_col = pl.BlockSpec((width, width), lambda i: (0, i))
    return pl.pallas_call(
        enc_qkv_back_kernel,
        grid=(3,),
        in_specs=[whole] * 5 + [full(vecs.shape), by_col],
        out_specs=[by_col, whole, full((8, width))],
        out_shape=[
            shape((width, 3 * width), LOW),
            shape((rows, width), LOW),
            shape((8, width), F32),
        ],
        scratch_shapes=[pltpu.VMEM((rows, width), LOW), pltpu.VMEM((rows, width), F32)],
        compiler_params=PARAMS,
        name="enc_qkv_back",
    )(rows_in, dq, dk, dv, gmid, vecs, weight)


def dec_in_kernel(limit, order_ref, one_ref, two_ref, pos_ref, vec_ref, w_ref, in_ref, qkv_ref):
    step = pl.program_id(0)
    width = in_ref.shape[1]
    for half, ref in enumerate((one_ref, two_ref)):
        visible = order_ref[0, 2 * step + half] < limit
        rows = slice(half * BLOCK, (half + 1) * BLOCK)
        in_ref[rows, :] = (
            jnp.where(visible, ref[...].astype(F32), vec_ref[9:10, :]) + pos_ref[rows, :]
        )
    unit, _ = norm_parts(in_ref[...])
    normed = (unit * vec_ref[0:1, :] + vec_ref[3:4, :]).astype(LOW)
    qkv = mm(normed, w_ref[...])
    qkv_ref[:, :width] = (qkv[:, :width] + vec_ref[4:5, :]).astype(LOW)
    qkv_ref[:, width : 2 * width] = qkv[:, width : 2 * width].astype(LOW)
    qkv_ref[:, 2 * width :] = (qkv[:, 2 * width :] + vec_ref[5:6, :]).astype(LOW)


def dec_in_call(order, gathered, pos, vecs, weight):
    rows, width = pos.shape
    limit = gathered.shape[0] // BLOCK

    def chosen(half):
        def index(i, order_ref):
            return (jnp.clip(order_ref[0, 2 * i + half], 0, limit - 1), 0)

        return pl.BlockSpec((BLOCK, width), index)

    return pl.pallas_call(
        functools.partial(dec_in_kernel, limit),
        grid_spec=pltpu.PrefetchScalarGridSpec(
            num_scalar_prefetch=1,
            grid=(rows // TILE,),
            in_specs=[
                chosen(0),
                chosen(1),
                pl.BlockSpec((TILE, width), lambda i, o: (i, 0)),
                full(vecs.shape),
                at_col(width, 3 * width, 0),
            ],
            out_specs=[
                pl.BlockSpec((TILE, width), lambda i, o: (i, 0)),
                pl.BlockSpec((TILE, 3 * width), lambda i, o: (i, 0)),
            ],
        ),
        out_shape=[shape((rows, width), F32), shape((rows, 3 * width), LOW)],
        compiler_params=PARAMS,
        name="dec_in",
    )(order, gathered, gathered, pos, vecs, weight)


def dec_mid_kernel(
    steps,
    chunks,
    x_ref,
    att_ref,
    cot_ref,
    vec_ref,
    b1_ref,
    wo_ref,
    w1_ref,
    w2_ref,
    out_ref,
    gmid_ref,
    gatt_ref,
    dwo_ref,
    dw1_ref,
    dw2_ref,
    db1_ref,
    sum_ref,
    awo,
    aw1,
    aw2,
    acc,
    dnorm,
):
    step = pl.program_id(0)
    width = x_ref.shape[1]

    @pl.when(step == 0)
    def _():
        awo[...] = jnp.zeros_like(awo)
        aw1[...] = jnp.zeros_like(aw1)
        aw2[...] = jnp.zeros_like(aw2)
        db1_ref[...] = jnp.zeros_like(db1_ref)
        sum_ref[...] = jnp.zeros_like(sum_ref)

    att = att_ref[...]
    low = cot_ref[...]
    middle = x_ref[...] + mm(att, wo_ref[...]) + vec_ref[6:7, :]
    unit, scale = norm_parts(middle)
    normed = (unit * vec_ref[1:2, :] + vec_ref[7:8, :]).astype(LOW)
    acc[...] = middle + vec_ref[8:9, :]
    dnorm[...] = jnp.zeros_like(dnorm)

    def chunk(j, carry):
        cols = pl.ds(pl.multiple_of(j * width, width), width)
        up = w1_ref[:, cols]
        down = w2_ref[cols, :]
        value, slope = gelu_parts(mm(normed, up) + b1_ref[j])
        value = value.astype(LOW)
        acc[...] += mm(value, down)
        aw2[cols, :] += mm_tn(value, low)
        dhid = (slope * mm_nt(low, down)).astype(LOW)
        aw1[:, cols] += mm_tn(normed, dhid)
        db1_ref[j] += col_sum(dhid.astype(F32))
        dnorm[...] += mm_nt(dhid, up)
        return carry

    lax.fori_loop(0, chunks, chunk, 0)
    out_ref[...] = acc[...].astype(LOW)
    dn = dnorm[...]
    sum_ref[0:1, :] += col_sum(dn * unit)
    sum_ref[1:2, :] += col_sum(dn)
    gmid = low.astype(F32) + norm_back(dn, unit, scale, vec_ref[1:2, :])
    gmid_ref[...] = gmid
    mlow = gmid.astype(LOW)
    sum_ref[2:3, :] += col_sum(mlow.astype(F32))
    sum_ref[3:4, :] += col_sum(low.astype(F32))
    awo[...] += mm_tn(att, mlow)
    gatt_ref[...] = mm_nt(mlow, wo_ref[...]).astype(LOW)

    @pl.when(step == steps - 1)
    def _():
        dwo_ref[...] = awo[...].astype(LOW)
        dw1_ref[...] = aw1[...].astype(LOW)
        dw2_ref[...] = aw2[...].astype(LOW)


def dec_mid(dec_in, attended, cotangent, vecs, up_bias, wide, up_w, down_w, proj_at):
    rows, width = dec_in.shape
    hidden = down_w.shape[0]
    chunks = hidden // width
    tile = 2 * TILE
    steps = rows // tile
    by_row = pl.BlockSpec((tile, width), lambda i: (i, 0))
    return pl.pallas_call(
        functools.partial(dec_mid_kernel, steps, chunks),
        grid=(steps,),
        in_specs=[
            by_row,
            by_row,
            by_row,
            full(vecs.shape),
            full((chunks, 1, width)),
            at_col(width, width, proj_at // width),
            full((width, hidden)),
            full((hidden, width)),
        ],
        out_specs=[
            by_row,
            by_row,
            by_row,
            full((width, width)),
            full((width, hidden)),
            full((hidden, width)),
            full((chunks, 1, width)),
            full((8, width)),
        ],
        out_shape=[
            shape((rows, width), LOW),
            shape((rows, width), F32),
            shape((rows, width), LOW),
            shape((width, width), LOW),
            shape((width, hidden), LOW),
            shape((hidden, width), LOW),
            shape((chunks, 1, width), F32),
            shape((8, width), F32),
        ],
        scratch_shapes=[
            pltpu.VMEM((width, width), F32),
            pltpu.VMEM((width, hidden), F32),
            pltpu.VMEM((hidden, width), F32),
            pltpu.VMEM((tile, width), F32),
            pltpu.VMEM((tile, width), F32),
        ],
        compiler_params=PARAMS,
        name="dec_mid",
    )(dec_in, attended, cotangent, vecs, up_bias.reshape(chunks, 1, width), wide, up_w, down_w)


def dec_back_kernel(
    limit,
    steps,
    order_ref,
    x_ref,
    dq_ref,
    dk_ref,
    dv_ref,
    gmid_ref,
    vec_ref,
    w_ref,
    dw_ref,
    sum_ref,
    send_ref,
    acc,
):
    step = pl.program_id(0)
    width = x_ref.shape[1]

    @pl.when(step == 0)
    def _():
        acc[...] = jnp.zeros_like(acc)
        sum_ref[...] = jnp.zeros_like(sum_ref)
        send_ref[...] = jnp.zeros_like(send_ref)

    unit, scale = norm_parts(x_ref[...])
    normed = (unit * vec_ref[0:1, :] + vec_ref[3:4, :]).astype(LOW)
    grads = (dq_ref[...], dk_ref[...], dv_ref[...])
    dn = None
    for i, grad in enumerate(grads):
        cols = slice(i * width, (i + 1) * width)
        acc[:, cols] += mm_tn(normed, grad)
        piece = mm_nt(grad, w_ref[:, cols])
        dn = piece if dn is None else dn + piece
    sum_ref[0:1, :] += col_sum(dn * unit)
    sum_ref[1:2, :] += col_sum(dn)
    sum_ref[2:3, :] += col_sum(grads[0].astype(F32))
    sum_ref[3:4, :] += col_sum(grads[2].astype(F32))
    din = gmid_ref[...] + norm_back(dn, unit, scale, vec_ref[0:1, :])
    per = x_ref.shape[0] // BLOCK
    for b in range(per):
        place = order_ref[0, per * step + b]
        rows = din[b * BLOCK : (b + 1) * BLOCK, :]

        @pl.when(place < limit)
        def _():
            send_ref[pl.ds(pl.multiple_of(place * BLOCK, BLOCK), BLOCK), :] = rows.astype(LOW)

        @pl.when(place >= limit)
        def _():
            sum_ref[4:5, :] += col_sum(rows)

    @pl.when(step == steps - 1)
    def _():
        dw_ref[...] = acc[...].astype(LOW)


def dec_back(order, dec_in, dq, dk, dv, gmid, vecs, weight, limit):
    rows, width = dec_in.shape
    tile = 2 * TILE
    steps = rows // tile
    by_row = pl.BlockSpec((tile, width), lambda i, o: (i, 0))
    return pl.pallas_call(
        functools.partial(dec_back_kernel, limit, steps),
        grid_spec=pltpu.PrefetchScalarGridSpec(
            num_scalar_prefetch=1,
            grid=(steps,),
            in_specs=[by_row] * 5 + [full(vecs.shape), at_col(width, 3 * width, 0)],
            out_specs=[
                full((width, 3 * width)),
                full((8, width)),
                full((limit * BLOCK, width)),
            ],
            scratch_shapes=[pltpu.VMEM((width, 3 * width), F32)],
        ),
        out_shape=[
            shape((width, 3 * width), LOW),
            shape((8, width), F32),
            shape((limit * BLOCK, width), LOW),
        ],
        compiler_params=PARAMS,
        name="dec_back",
    )(order, dec_in, dq, dk, dv, gmid, vecs, weight)


def positions(count, width):
    places = jnp.arange(count, dtype=jnp.float32)[:, None]
    columns = jnp.arange(width)
    rates = jnp.exp((2 * (columns // 2)).astype(jnp.float32) * (-math.log(10000.0) / width))
    angles = places * rates[None, :]
    return jnp.where((columns % 2 == 0)[None, :], jnp.sin(angles), jnp.cos(angles))


def stages():
    dp, fsdp = lax.axis_size("dp"), lax.axis_size("fsdp")
    return {
        "outer": ("dp", 2, dp // 2),
        "inner": ("dp", 1, 2),
        "z": ("fsdp", 2, fsdp // 2),
        "core": ("fsdp", 1, 2),
    }


def place_of(name):
    axis, stride, size = stages()[name]
    return lax.axis_index(axis) // stride % size


def shift(value, name, by):
    axis, stride, size = stages()[name]
    pairs = []
    for source in range(lax.axis_size(axis)):
        at = source // stride % size
        pairs.append((source, source + ((at + by) % size - at) * stride))
    return lax.ppermute(value, axis, pairs)


def spread(value, name, dim):
    size = stages()[name][2]
    here = place_of(name)
    got = [value] + [shift(value, name, by) for by in range(1, size)]
    ordered = []
    for slot in range(size):
        one = got[0]
        for by in range(1, size):
            one = jnp.where((here - slot) % size == by, got[by], one)
        ordered.append(one)
    return jnp.stack(ordered, axis=dim)


def line_up(pieces):
    lined = []
    for piece in pieces:
        if lined:
            piece, lined[-1] = lax.optimization_barrier((piece, lined[-1]))
        lined.append(spread(piece, "z", 0))
    return lined


def gather_rest(lined, cut):
    one = spread(spread(lined[:, :, :cut], "inner", 0), "outer", 0)
    two = spread(spread(lined[:, :, cut:], "outer", 0), "inner", 1)
    one = spread(one, "core", 3)
    two = spread(two, "core", 3)
    both = jnp.concatenate([one, two], axis=-1)
    return both.reshape(-1, both.shape[-1])


def take(value, dim, index):
    return lax.dynamic_index_in_dim(value, index, dim, keepdims=False)


def fold(value, name, dim, kind):
    size = stages()[name][2]
    here = place_of(name)
    total = take(value, dim, here).astype(F32)
    for by in range(1, size):
        sent = take(value, dim, (here + by) % size)
        total = total + shift(sent, name, by).astype(F32)
    return total.astype(kind)


def reduce_chunk(grads, cut):
    dims = [stages()[n][2] for n in ("outer", "inner", "z", "core")]
    rows = grads.shape[0] // math.prod(dims)
    split = grads.reshape(*dims, rows, grads.shape[1])
    half = fold(split, "core", 3, LOW)
    one = fold(fold(half[..., :cut], "inner", 1, LOW), "outer", 0, LOW)
    two = fold(fold(half[..., cut:], "outer", 0, LOW), "inner", 0, LOW)
    return jnp.concatenate([fold(one, "z", 0, F32), fold(two, "z", 0, F32)], axis=-1)


def pack_vectors(pieces, rows):
    wide = jnp.concatenate([p.reshape(-1, rows) for p in pieces], axis=0)
    wide = jnp.pad(wide, ((0, LANES - wide.shape[0]), (0, 0)))
    return wide.T


def split_columns(array, widths):
    out, at = [], 0
    for w in widths:
        out.append(array[:, at : at + w])
        at += w
    return out


def long_vector(rows_of, devices):
    parts, total = rows_of.shape
    return rows_of.reshape(parts, devices, total // devices).transpose(1, 0, 2).reshape(1, -1)


def long_rows(vector, devices, rows):
    parts = vector.shape[0] // (devices * rows)
    return vector.reshape(devices, parts, rows).transpose(1, 0, 2).reshape(parts, -1)


def per_device(
    enc_input,
    enc_segments,
    dec_segments,
    block_order,
    dec_cotangent,
    enc_qkv,
    enc_proj,
    enc_fc1,
    enc_fc2,
    enc_gains,
    enc_biases,
    enc_fc1_bias,
    embed,
    mask_token,
    dec_qkv,
    dec_proj,
    dec_fc1,
    dec_fc2,
    dec_gains,
    dec_biases,
    dec_fc1_bias,
    dec_fc2_bias,
):
    devices = lax.axis_size("dp") * lax.axis_size("fsdp")
    enc_rows, width = enc_input.shape
    dec_rows, dwidth = dec_cotangent.shape
    erows = enc_qkv.shape[0]
    drows = dec_qkv.shape[0]
    ff = enc_fc1.shape[1]
    dff = dec_fc1.shape[1]
    enc_first = jnp.concatenate(
        [enc_qkv, enc_proj, embed, pack_vectors([enc_gains, enc_biases, enc_fc1_bias], erows)],
        axis=1,
    )
    dec_first = jnp.concatenate(
        [
            dec_qkv,
            dec_proj,
            pack_vectors(
                [dec_gains, dec_biases, dec_fc2_bias[None], mask_token[None], dec_fc1_bias], drows
            ),
        ],
        axis=1,
    )
    ecut = (4 * width + dwidth) // 2 // LANES * LANES
    dcut = 2 * dwidth
    lined = line_up([enc_first, enc_fc1, enc_fc2, dec_first, dec_fc1, dec_fc2])
    enc_all = gather_rest(lined[0], ecut)
    up_w = gather_rest(lined[1], ff // 2)
    down_w = gather_rest(lined[2], width // 2)
    dec_all = gather_rest(lined[3], dcut)
    dup_w = gather_rest(lined[4], dff // 2)
    ddown_w = gather_rest(lined[5], dwidth // 2)
    proj_at, emb_at = 3 * width, 4 * width
    vec_at = emb_at + dwidth
    dproj_at = 3 * dwidth
    dvec_at = 4 * dwidth
    evecs = enc_all[:, vec_at:].T[:16].astype(F32)
    dvecs = dec_all[:, dvec_at:].T[:16].astype(F32)
    up_bias = long_vector(evecs[10:14], devices)
    dup_bias = long_vector(dvecs[10:14], devices)

    qkv = enc_qkv_call(enc_input, evecs, enc_all)
    enc_col = enc_segments.reshape(-1, 1)
    enc_row = enc_segments.reshape(-1, 1, TILE)
    attended, lse = attend(qkv, enc_segments, enc_col, HDIM)
    mid, enc_out, final, act, slope, embedded = enc_mid(
        enc_input,
        attended,
        evecs,
        up_bias,
        dvecs[2:3],
        enc_all,
        up_w,
        down_w,
        proj_at,
        emb_at,
    )
    gathered = lax.all_gather(embedded, "fsdp", axis=0, tiled=True)
    limit = gathered.shape[0] // BLOCK
    dec_in, dqkv = dec_in_call(block_order, gathered, positions(dec_rows, dwidth), dvecs, dec_all)
    dec_col = dec_segments.reshape(-1, 1)
    dec_row = dec_segments.reshape(-1, 1, TILE)
    dattended, dlse = attend(dqkv, dec_segments, dec_col, DHDIM)
    dec_out, dgmid, dgatt, dwo, dw1, dw2, db1, dsum_mid = dec_mid(
        dec_in,
        dattended,
        dec_cotangent,
        dvecs,
        dup_bias,
        dec_all,
        dup_w,
        ddown_w,
        dproj_at,
    )
    ddq, ddk, ddv = attend_back(
        dqkv, dattended, dgatt, dlse, dec_segments, dec_row, dec_col, DHDIM
    )
    dwqkv, dsum, send = dec_back(
        block_order, dec_in, ddq, ddk, ddv, dgmid, dvecs, dec_all, limit
    )
    elow = lax.psum_scatter(send, "fsdp", scatter_dimension=0, tiled=True)
    demb, ew2, ew1, ewo, eb1, esum_emb, esum_mid, gmid, gatt = enc_mid_back(
        elow,
        final,
        enc_out,
        mid,
        attended,
        act,
        slope,
        evecs,
        enc_all,
        up_w,
        down_w,
        proj_at,
        emb_at,
    )
    dec_vec_grads = jnp.concatenate(
        [
            dsum[0:1],
            dsum_mid[0:1],
            esum_emb[0:1],
            dsum[1:4],
            dsum_mid[2:3],
            dsum_mid[1:2],
            dsum_mid[3:4],
            dsum[4:5],
            long_rows(db1.reshape(-1), devices, drows),
            jnp.zeros((LANES - 14, dwidth), F32),
        ],
        axis=0,
    ).T
    dec_grads = jnp.concatenate([dwqkv, dwo, dec_vec_grads.astype(LOW)], axis=1)
    rd = reduce_chunk(dw2, dwidth // 2)
    ru = reduce_chunk(dw1, dff // 2)
    rq, rp, rv = split_columns(reduce_chunk(dec_grads, dcut), [3 * dwidth, dwidth, LANES])
    dq, dk, dv = attend_back(qkv, attended, gatt, lse, enc_segments, enc_row, enc_col, HDIM)
    ewqkv, enc_in_grad, esum = enc_qkv_back(enc_input, dq, dk, dv, gmid, evecs, enc_all)
    enc_vec_grads = jnp.concatenate(
        [
            esum[0:1],
            esum_mid[3:4],
            esum_mid[0:1],
            esum[1:4],
            esum_mid[5:6],
            esum_mid[4:5],
            esum_mid[2:3],
            esum_mid[1:2],
            long_rows(eb1.reshape(-1), devices, erows),
            jnp.zeros((LANES - 14, width), F32),
        ],
        axis=0,
    ).T
    enc_grads = jnp.concatenate([ewqkv, ewo, demb, enc_vec_grads.astype(LOW)], axis=1)
    ed = reduce_chunk(ew2, width // 2)
    eu = reduce_chunk(ew1, ff // 2)
    eq, ep, em, ev = split_columns(
        reduce_chunk(enc_grads, ecut), [3 * width, width, dwidth, LANES]
    )
    rv = rv.T
    ev = ev.T
    return (
        dec_out,
        enc_in_grad,
        eq,
        ep,
        eu,
        ed,
        ev[:3],
        ev[3:10],
        ev[10:14].reshape(-1),
        em,
        rv[9],
        rq,
        rp,
        ru,
        rd,
        rv[:2],
        rv[2:8],
        rv[10:14].reshape(-1),
        rv[8],
    )


def solution(mesh):
    in_specs = (
        P(("dp", "fsdp"), None),
        P(("dp", "fsdp"), None),
        P(("dp", "fsdp"), None),
        P("dp", "fsdp"),
        P(("dp", "fsdp"), None),
        P(("dp", "fsdp"), None),
        P(("dp", "fsdp"), None),
        P(("dp", "fsdp"), None),
        P(("dp", "fsdp"), None),
        P(None, ("dp", "fsdp")),
        P(None, ("dp", "fsdp")),
        P(("dp", "fsdp")),
        P(("dp", "fsdp"), None),
        P(("dp", "fsdp")),
        P(("dp", "fsdp"), None),
        P(("dp", "fsdp"), None),
        P(("dp", "fsdp"), None),
        P(("dp", "fsdp"), None),
        P(None, ("dp", "fsdp")),
        P(None, ("dp", "fsdp")),
        P(("dp", "fsdp")),
        P(("dp", "fsdp")),
    )
    out_specs = (
        P(("dp", "fsdp"), None),
        P(("dp", "fsdp"), None),
        P(("dp", "fsdp"), None),
        P(("dp", "fsdp"), None),
        P(("dp", "fsdp"), None),
        P(("dp", "fsdp"), None),
        P(None, ("dp", "fsdp")),
        P(None, ("dp", "fsdp")),
        P(("dp", "fsdp")),
        P(("dp", "fsdp"), None),
        P(("dp", "fsdp")),
        P(("dp", "fsdp"), None),
        P(("dp", "fsdp"), None),
        P(("dp", "fsdp"), None),
        P(("dp", "fsdp"), None),
        P(None, ("dp", "fsdp")),
        P(None, ("dp", "fsdp")),
        P(("dp", "fsdp")),
        P(("dp", "fsdp")),
    )
    return jax.shard_map(
        per_device, mesh=mesh, in_specs=in_specs, out_specs=out_specs, check_vma=False
    )
```

```python
import functools
import math

import jax
import jax.numpy as jnp
from jax import lax
from jax.experimental import pallas as pl
from jax.experimental.pallas import tpu as pltpu
from jax.sharding import PartitionSpec as P

HDIM = 64
DHDIM = 32
BLOCK = 128
LANES = 128
TILE = 256
EPSILON = 1e-06
NEGATIVE = -1e30
LOG2E = math.log2(math.e)
AXES = ("dp", "fsdp")
F32 = jnp.float32
LOW = jnp.bfloat16
PARAMS = pltpu.CompilerParams(vmem_limit_bytes=56 * 1024 * 1024)


def mm(left, right):
    return jnp.dot(left, right, preferred_element_type=F32)


def mm_tn(left, right):
    return lax.dot_general(left, right, (((0,), (0,)), ((), ())), preferred_element_type=F32)


def mm_nt(left, right):
    return lax.dot_general(left, right, (((1,), (1,)), ((), ())), preferred_element_type=F32)


def col_sum(values):
    return jnp.sum(values, axis=0, keepdims=True)


def norm_parts(values):
    centred = values - jnp.mean(values, axis=-1, keepdims=True)
    variance = jnp.mean(centred * centred, axis=-1, keepdims=True)
    scale = lax.rsqrt(variance + EPSILON)
    return centred * scale, scale


def norm_back(grad, unit, scale, gain):
    inner = grad * gain
    mean_inner = jnp.mean(inner, axis=-1, keepdims=True)
    mean_cross = jnp.mean(inner * unit, axis=-1, keepdims=True)
    return scale * (inner - mean_inner - unit * mean_cross)


def gelu_parts(hidden):
    cdf = 0.5 + 0.5 * lax.erf(hidden * (0.5**0.5))
    density = jnp.exp(hidden * hidden * -0.5) * (1.0 / math.sqrt(2.0 * math.pi))
    return hidden * cdf, cdf + hidden * density


def cost(micros):
    return pl.CostEstimate(
        flops=int(micros * 1.1e9), bytes_accessed=int(micros * 3.5e6), transcendentals=0
    )


def full(shape):
    return pl.BlockSpec(shape, lambda *_: (0,) * len(shape))


def at_col(rows, cols, index):
    return pl.BlockSpec((rows, cols), lambda *_: (0, index))


def shape(dims, kind):
    return jax.ShapeDtypeStruct(dims, kind)


def lane_mask(head, head_dim, kind):
    lane = lax.broadcasted_iota(jnp.int32, (1, LANES), 1)
    inside = (lane >= head * head_dim) & (lane < (head + 1) * head_dim)
    return inside.astype(F32).astype(kind)


def tile_range(seg_ref, here, tiles):
    first = seg_ref[0, here * TILE]
    last = seg_ref[0, here * TILE + TILE - 1]
    low = jnp.int32(0)
    high = jnp.int32(tiles)
    for other in range(tiles):
        low += (seg_ref[0, other * TILE + TILE - 1] < first).astype(jnp.int32)
        high -= (seg_ref[0, other * TILE] > last).astype(jnp.int32)
    return low, high


def attend_kernel(
    head_dim,
    tiles,
    seg_ref,
    q_ref,
    k_ref,
    v_ref,
    row_ref,
    col_ref,
    out_ref,
    lse_ref,
    vt,
    held,
    acc,
    top,
    tot,
):
    heads = LANES // head_dim
    here = pl.program_id(1)
    factor = head_dim ** (-0.5) * LOG2E

    @pl.when(here == 0)
    def _():
        for u in range(tiles):
            vt[u] = v_ref[u * TILE : (u + 1) * TILE, :].astype(F32).T.astype(LOW)

    acc[...] = jnp.zeros_like(acc)
    top[...] = jnp.full_like(top, NEGATIVE)
    tot[...] = jnp.zeros_like(tot)
    query = q_ref[...]
    row = row_ref[...]

    def score(u, carry):
        start = pl.multiple_of(u * TILE, TILE)
        keys = k_ref[pl.ds(start, TILE), :]
        same = col_ref[pl.ds(start, TILE), :] == row
        for h in range(heads):
            scores = mm_nt(keys * lane_mask(h, head_dim, LOW), query)
            scores = jnp.where(same, scores, NEGATIVE)
            held[u, h] = scores
            top[h : h + 1, :] = jnp.maximum(
                top[h : h + 1, :], jnp.max(scores, axis=0, keepdims=True)
            )
        return carry

    def mix(u, carry):
        for h in range(heads):
            probs = jnp.exp2((held[u, h] - top[h : h + 1, :]) * factor)
            tot[h : h + 1, :] += col_sum(probs)
            span = slice(h * head_dim, (h + 1) * head_dim)
            acc[span, :] += mm(vt[u, span, :], probs.astype(LOW))
        return carry

    low, high = tile_range(seg_ref, here, tiles)
    lax.fori_loop(low, high, score, 0)
    lax.fori_loop(low, high, mix, 0)
    for h in range(heads):
        span = slice(h * head_dim, (h + 1) * head_dim)
        total = tot[h : h + 1, :]
        acc[span, :] = acc[span, :] / total
        lse_ref[0, 0, h : h + 1, :] = top[h : h + 1, :] * factor + jnp.log2(total)
    out_ref[...] = acc[...].T.astype(LOW)


def attend(qkv, segments, seg_col, head_dim):
    rows, width = qkv.shape[0], qkv.shape[1] // 3
    groups, tiles = width // LANES, rows // TILE
    return pl.pallas_call(
        functools.partial(attend_kernel, head_dim, tiles),
        grid_spec=pltpu.PrefetchScalarGridSpec(
            num_scalar_prefetch=1,
            grid=(groups, tiles),
            in_specs=[
                pl.BlockSpec((TILE, LANES), lambda g, t, s: (t, g)),
                pl.BlockSpec((rows, LANES), lambda g, t, s: (0, groups + g)),
                pl.BlockSpec((rows, LANES), lambda g, t, s: (0, 2 * groups + g)),
                pl.BlockSpec((1, TILE), lambda g, t, s: (0, t)),
                pl.BlockSpec((rows, 1), lambda g, t, s: (0, 0)),
            ],
            out_specs=[
                pl.BlockSpec((TILE, LANES), lambda g, t, s: (t, g)),
                pl.BlockSpec((1, 1, 8, TILE), lambda g, t, s: (g, t, 0, 0)),
            ],
            scratch_shapes=[
                pltpu.VMEM((tiles, LANES, TILE), LOW),
                pltpu.VMEM((tiles, LANES // head_dim, TILE, TILE), F32),
                pltpu.VMEM((LANES, TILE), F32),
                pltpu.VMEM((8, TILE), F32),
                pltpu.VMEM((8, TILE), F32),
            ],
        ),
        out_shape=[shape((rows, width), LOW), shape((groups, tiles, 8, TILE), F32)],
        compiler_params=PARAMS,
        cost_estimate=cost(9 if tiles == 1 else 40),
        name="attend",
    )(segments, qkv, qkv, qkv, segments, seg_col)


def attend_back_kernel(
    head_dim,
    tiles,
    seg_ref,
    q_ref,
    k_ref,
    v_ref,
    o_ref,
    g_ref,
    lse_ref,
    row_ref,
    col_ref,
    dq_ref,
    dk_ref,
    dv_ref,
    qt,
    gt,
    dqt,
    delta,
    dkt,
    dvt,
):
    heads = LANES // head_dim
    here = pl.program_id(1)
    scale = head_dim ** (-0.5)
    factor = scale * LOG2E

    @pl.when(here == 0)
    def _():
        dqt[...] = jnp.zeros_like(dqt)
        for t in range(tiles):
            rows = slice(t * TILE, (t + 1) * TILE)
            grad_t = g_ref[rows, :].astype(F32).T
            both = grad_t * o_ref[rows, :].astype(F32).T
            qt[t] = q_ref[rows, :].astype(F32).T.astype(LOW)
            gt[t] = grad_t.astype(LOW)
            for h in range(heads):
                delta[t, h : h + 1, :] = col_sum(both[h * head_dim : (h + 1) * head_dim, :])

    keys, vals = k_ref[...], v_ref[...]
    keys_t = keys.astype(F32).T.astype(LOW)
    col = col_ref[...]
    dkt[...] = jnp.zeros_like(dkt)
    dvt[...] = jnp.zeros_like(dvt)

    def step(t, carry):
        start = pl.multiple_of(t * TILE, TILE)
        query = q_ref[pl.ds(start, TILE), :]
        grads = g_ref[pl.ds(start, TILE), :]
        same = col == row_ref[t]
        for h in range(heads):
            mask = lane_mask(h, head_dim, LOW)
            span = slice(h * head_dim, (h + 1) * head_dim)
            scores = mm_nt(keys * mask, query) * factor
            scores = jnp.where(same, scores, NEGATIVE)
            probs = jnp.exp2(scores - lse_ref[0, t, h : h + 1, :])
            grad_probs = mm_nt(vals * mask, grads)
            grad_scores = (probs * (grad_probs - delta[t, h : h + 1, :])).astype(LOW)
            dvt[span, :] += mm_nt(gt[t, span, :], probs.astype(LOW))
            dkt[span, :] += mm_nt(qt[t, span, :], grad_scores)
            dqt[t, span, :] += mm(keys_t[span, :], grad_scores)
        return carry

    low, high = tile_range(seg_ref, here, tiles)
    lax.fori_loop(low, high, step, 0)
    dk_ref[...] = (dkt[...] * scale).T.astype(LOW)
    dv_ref[...] = dvt[...].T.astype(LOW)

    @pl.when(here == tiles - 1)
    def _():
        for t in range(tiles):
            dq_ref[t * TILE : (t + 1) * TILE, :] = (dqt[t] * scale).T.astype(LOW)


def attend_back(qkv, attended, grad, lse, segments, seg_row, seg_col, head_dim):
    rows, width = attended.shape
    groups, tiles = width // LANES, rows // TILE
    whole = pl.BlockSpec((rows, LANES), lambda g, u, s: (0, g))
    piece = pl.BlockSpec((TILE, LANES), lambda g, u, s: (u, g))
    return pl.pallas_call(
        functools.partial(attend_back_kernel, head_dim, tiles),
        grid_spec=pltpu.PrefetchScalarGridSpec(
            num_scalar_prefetch=1,
            grid=(groups, tiles),
            in_specs=[
                whole,
                pl.BlockSpec((TILE, LANES), lambda g, u, s: (u, groups + g)),
                pl.BlockSpec((TILE, LANES), lambda g, u, s: (u, 2 * groups + g)),
                whole,
                whole,
                pl.BlockSpec((1, tiles, 8, TILE), lambda g, u, s: (g, 0, 0, 0)),
                pl.BlockSpec((tiles, 1, TILE), lambda g, u, s: (0, 0, 0)),
                pl.BlockSpec((TILE, 1), lambda g, u, s: (u, 0)),
            ],
            out_specs=[whole, piece, piece],
            scratch_shapes=[
                pltpu.VMEM((tiles, LANES, TILE), LOW),
                pltpu.VMEM((tiles, LANES, TILE), LOW),
                pltpu.VMEM((tiles, LANES, TILE), F32),
                pltpu.VMEM((tiles, 8, TILE), F32),
                pltpu.VMEM((LANES, TILE), F32),
                pltpu.VMEM((LANES, TILE), F32),
            ],
        ),
        out_shape=[shape((rows, width), LOW)] * 3,
        compiler_params=PARAMS,
        cost_estimate=cost(9 if tiles == 1 else 50),
        name="attend_back",
    )(segments, qkv, qkv, qkv, attended, grad, lse, seg_row, seg_col)


def enc_qkv_kernel(x_ref, vec_ref, w_ref, out_ref, normed):
    part = pl.program_id(0)

    @pl.when(part == 0)
    def _():
        unit, _ = norm_parts(x_ref[...].astype(F32))
        normed[...] = (unit * vec_ref[0:1, :] + vec_ref[3:4, :]).astype(LOW)

    bias = jnp.where(part == 0, vec_ref[4:5, :], jnp.where(part == 2, vec_ref[5:6, :], 0.0))
    out_ref[...] = (mm(normed[...], w_ref[...]) + bias).astype(LOW)


def enc_qkv_call(rows_in, vecs, weight):
    rows, width = rows_in.shape
    return pl.pallas_call(
        enc_qkv_kernel,
        grid=(3,),
        in_specs=[
            full((rows, width)),
            full(vecs.shape),
            pl.BlockSpec((width, width), lambda i: (0, i)),
        ],
        out_specs=pl.BlockSpec((rows, width), lambda i: (0, i)),
        out_shape=shape((rows, 3 * width), LOW),
        scratch_shapes=[pltpu.VMEM((rows, width), LOW)],
        compiler_params=PARAMS,
        cost_estimate=cost(5),
        name="enc_qkv",
    )(rows_in, vecs, weight)


def enc_mid_kernel(
    chunks,
    x_ref,
    att_ref,
    vec_ref,
    b1_ref,
    eb_ref,
    wo_ref,
    w1_ref,
    w2_ref,
    we_ref,
    mid_ref,
    out_ref,
    final_ref,
    act_ref,
    slope_ref,
    emb_ref,
    normed,
    acc,
):
    part = pl.program_id(0)

    @pl.when(part == 0)
    def _():
        middle = x_ref[...].astype(F32) + mm(att_ref[...], wo_ref[...]) + vec_ref[6:7, :]
        mid_ref[...] = middle
        unit, _ = norm_parts(middle)
        normed[...] = (unit * vec_ref[1:2, :] + vec_ref[7:8, :]).astype(LOW)
        acc[...] = middle + vec_ref[8:9, :]

    hidden = mm(normed[...], w1_ref[...]) + b1_ref[...]
    value, slope = gelu_parts(hidden)
    value = value.astype(LOW)
    act_ref[...] = value
    slope_ref[...] = slope
    acc[...] += mm(value, w2_ref[...])

    @pl.when(part == chunks - 1)
    def _():
        result = acc[...]
        out_ref[...] = result
        unit, _ = norm_parts(result)
        final = (unit * vec_ref[2:3, :] + vec_ref[9:10, :]).astype(LOW)
        final_ref[...] = final
        emb_ref[...] = (mm(final, we_ref[...]) + eb_ref[...]).astype(LOW)


def enc_mid(rows_in, attended, vecs, up_bias, emb_bias, wide, up_w, down_w, proj_at, emb_at):
    rows, width = rows_in.shape
    hidden = down_w.shape[0]
    emb_width = emb_bias.shape[1]
    chunks = hidden // width
    return pl.pallas_call(
        functools.partial(enc_mid_kernel, chunks),
        grid=(chunks,),
        in_specs=[
            full((rows, width)),
            full((rows, width)),
            full(vecs.shape),
            pl.BlockSpec((1, width), lambda i: (0, i)),
            full((1, emb_width)),
            at_col(width, width, proj_at // width),
            pl.BlockSpec((width, width), lambda i: (0, i)),
            pl.BlockSpec((width, width), lambda i: (i, 0)),
            at_col(width, emb_width, emb_at // emb_width),
        ],
        out_specs=[
            full((rows, width)),
            full((rows, width)),
            full((rows, width)),
            pl.BlockSpec((rows, width), lambda i: (0, i)),
            pl.BlockSpec((rows, width), lambda i: (0, i)),
            full((rows, emb_width)),
        ],
        out_shape=[
            shape((rows, width), F32),
            shape((rows, width), F32),
            shape((rows, width), LOW),
            shape((rows, hidden), LOW),
            shape((rows, hidden), F32),
            shape((rows, emb_width), LOW),
        ],
        scratch_shapes=[pltpu.VMEM((rows, width), LOW), pltpu.VMEM((rows, width), F32)],
        compiler_params=PARAMS,
        cost_estimate=cost(11),
        name="enc_mid",
    )(rows_in, attended, vecs, up_bias, emb_bias, wide, up_w, down_w, wide)


def enc_mid_back_kernel(
    chunks,
    elow_ref,
    final_ref,
    out_ref,
    mid_ref,
    att_ref,
    act_ref,
    slope_ref,
    vec_ref,
    wo_ref,
    w1_ref,
    w2_ref,
    we_ref,
    demb_ref,
    dw2_ref,
    dw1_ref,
    dwo_ref,
    db1_ref,
    esum_ref,
    sum_ref,
    gmid_ref,
    gatt_ref,
    grad,
    grad_low,
    unit_two,
    scale_two,
    normed,
    dnorm,
):
    part = pl.program_id(0)

    @pl.when(part == 0)
    def _():
        elow = elow_ref[...]
        demb_ref[...] = mm_tn(final_ref[...], elow).astype(LOW)
        esum_ref[...] = jnp.zeros_like(esum_ref)
        esum_ref[0:1, :] = col_sum(elow.astype(F32))
        unit, scale = norm_parts(out_ref[...])
        dfinal = mm_nt(elow, we_ref[...])
        sum_ref[...] = jnp.zeros_like(sum_ref)
        sum_ref[0:1, :] = col_sum(dfinal * unit)
        sum_ref[1:2, :] = col_sum(dfinal)
        total = norm_back(dfinal, unit, scale, vec_ref[2:3, :])
        grad[...] = total
        low = total.astype(LOW)
        grad_low[...] = low
        sum_ref[2:3, :] = col_sum(low.astype(F32))
        unit, scale = norm_parts(mid_ref[...])
        unit_two[...] = unit
        scale_two[...] = jnp.broadcast_to(scale, scale_two.shape)
        normed[...] = (unit * vec_ref[1:2, :] + vec_ref[7:8, :]).astype(LOW)
        dnorm[...] = jnp.zeros_like(dnorm)

    low = grad_low[...]
    dw2_ref[...] = mm_tn(act_ref[...], low).astype(LOW)
    dhid = (slope_ref[...] * mm_nt(low, w2_ref[...])).astype(LOW)
    dw1_ref[...] = mm_tn(normed[...], dhid).astype(LOW)
    db1_ref[...] = col_sum(dhid.astype(F32))
    dnorm[...] += mm_nt(dhid, w1_ref[...])

    @pl.when(part == chunks - 1)
    def _():
        dn = dnorm[...]
        unit = unit_two[...]
        sum_ref[3:4, :] = col_sum(dn * unit)
        sum_ref[4:5, :] = col_sum(dn)
        gmid = grad[...] + norm_back(dn, unit, scale_two[:, 0:1], vec_ref[1:2, :])
        gmid_ref[...] = gmid
        mlow = gmid.astype(LOW)
        sum_ref[5:6, :] = col_sum(mlow.astype(F32))
        dwo_ref[...] = mm_tn(att_ref[...], mlow).astype(LOW)
        gatt_ref[...] = mm_nt(mlow, wo_ref[...]).astype(LOW)


def enc_mid_back(
    elow, final, out, mid, attended, act, slope, vecs, wide, up_w, down_w, proj_at, emb_at
):
    rows, width = mid.shape
    hidden = down_w.shape[0]
    emb_width = elow.shape[1]
    chunks = hidden // width
    by_col = pl.BlockSpec((rows, width), lambda i: (0, i))
    return pl.pallas_call(
        functools.partial(enc_mid_back_kernel, chunks),
        grid=(chunks,),
        in_specs=[
            full((rows, emb_width)),
            full((rows, width)),
            full((rows, width)),
            full((rows, width)),
            full((rows, width)),
            by_col,
            by_col,
            full(vecs.shape),
            at_col(width, width, proj_at // width),
            pl.BlockSpec((width, width), lambda i: (0, i)),
            pl.BlockSpec((width, width), lambda i: (i, 0)),
            at_col(width, emb_width, emb_at // emb_width),
        ],
        out_specs=[
            full((width, emb_width)),
            pl.BlockSpec((width, width), lambda i: (i, 0)),
            pl.BlockSpec((width, width), lambda i: (0, i)),
            full((width, width)),
            pl.BlockSpec((1, width), lambda i: (0, i)),
            full((8, emb_width)),
            full((8, width)),
            full((rows, width)),
            full((rows, width)),
        ],
        out_shape=[
            shape((width, emb_width), LOW),
            shape((hidden, width), LOW),
            shape((width, hidden), LOW),
            shape((width, width), LOW),
            shape((1, hidden), F32),
            shape((8, emb_width), F32),
            shape((8, width), F32),
            shape((rows, width), F32),
            shape((rows, width), LOW),
        ],
        scratch_shapes=[
            pltpu.VMEM((rows, width), F32),
            pltpu.VMEM((rows, width), LOW),
            pltpu.VMEM((rows, width), F32),
            pltpu.VMEM((rows, LANES), F32),
            pltpu.VMEM((rows, width), LOW),
            pltpu.VMEM((rows, width), F32),
        ],
        compiler_params=PARAMS,
        cost_estimate=cost(17),
        name="enc_mid_back",
    )(elow, final, out, mid, attended, act, slope, vecs, wide, up_w, down_w, wide)


def enc_qkv_back_kernel(
    x_ref, dq_ref, dk_ref, dv_ref, gmid_ref, vec_ref, w_ref, dw_ref, din_ref, sum_ref, normed, dnorm
):
    part = pl.program_id(0)

    @pl.when(part == 0)
    def _():
        unit, _ = norm_parts(x_ref[...].astype(F32))
        normed[...] = (unit * vec_ref[0:1, :] + vec_ref[3:4, :]).astype(LOW)
        dnorm[...] = jnp.zeros_like(dnorm)
        sum_ref[...] = jnp.zeros_like(sum_ref)
        sum_ref[2:3, :] = col_sum(dq_ref[...].astype(F32))
        sum_ref[3:4, :] = col_sum(dv_ref[...].astype(F32))

    def one(grad):
        dw_ref[...] = mm_tn(normed[...], grad).astype(LOW)
        dnorm[...] += mm_nt(grad, w_ref[...])

    for index, ref in enumerate((dq_ref, dk_ref, dv_ref)):
        pl.when(part == index)(functools.partial(lambda r: one(r[...]), ref))

    @pl.when(part == 2)
    def _():
        unit, scale = norm_parts(x_ref[...].astype(F32))
        dn = dnorm[...]
        sum_ref[0:1, :] = col_sum(dn * unit)
        sum_ref[1:2, :] = col_sum(dn)
        din = gmid_ref[...] + norm_back(dn, unit, scale, vec_ref[0:1, :])
        din_ref[...] = din.astype(LOW)


def enc_qkv_back(rows_in, dq, dk, dv, gmid, vecs, weight):
    rows, width = rows_in.shape
    whole = full((rows, width))
    by_col = pl.BlockSpec((width, width), lambda i: (0, i))
    return pl.pallas_call(
        enc_qkv_back_kernel,
        grid=(3,),
        in_specs=[whole] * 5 + [full(vecs.shape), by_col],
        out_specs=[by_col, whole, full((8, width))],
        out_shape=[
            shape((width, 3 * width), LOW),
            shape((rows, width), LOW),
            shape((8, width), F32),
        ],
        scratch_shapes=[pltpu.VMEM((rows, width), LOW), pltpu.VMEM((rows, width), F32)],
        compiler_params=PARAMS,
        cost_estimate=cost(7),
        name="enc_qkv_back",
    )(rows_in, dq, dk, dv, gmid, vecs, weight)


def dec_in_kernel(limit, order_ref, one_ref, two_ref, pos_ref, vec_ref, w_ref, in_ref, qkv_ref):
    step = pl.program_id(0)
    width = in_ref.shape[1]
    for half, ref in enumerate((one_ref, two_ref)):
        visible = order_ref[0, 2 * step + half] < limit
        rows = slice(half * BLOCK, (half + 1) * BLOCK)
        in_ref[rows, :] = (
            jnp.where(visible, ref[...].astype(F32), vec_ref[9:10, :]) + pos_ref[rows, :]
        )
    unit, _ = norm_parts(in_ref[...])
    normed = (unit * vec_ref[0:1, :] + vec_ref[3:4, :]).astype(LOW)
    qkv = mm(normed, w_ref[...])
    qkv_ref[:, :width] = (qkv[:, :width] + vec_ref[4:5, :]).astype(LOW)
    qkv_ref[:, width : 2 * width] = qkv[:, width : 2 * width].astype(LOW)
    qkv_ref[:, 2 * width :] = (qkv[:, 2 * width :] + vec_ref[5:6, :]).astype(LOW)


def dec_in_call(order, gathered, pos, vecs, weight):
    rows, width = pos.shape
    limit = gathered.shape[0] // BLOCK

    def chosen(half):
        def index(i, order_ref):
            return (jnp.clip(order_ref[0, 2 * i + half], 0, limit - 1), 0)

        return pl.BlockSpec((BLOCK, width), index)

    return pl.pallas_call(
        functools.partial(dec_in_kernel, limit),
        grid_spec=pltpu.PrefetchScalarGridSpec(
            num_scalar_prefetch=1,
            grid=(rows // TILE,),
            in_specs=[
                chosen(0),
                chosen(1),
                pl.BlockSpec((TILE, width), lambda i, o: (i, 0)),
                full(vecs.shape),
                at_col(width, 3 * width, 0),
            ],
            out_specs=[
                pl.BlockSpec((TILE, width), lambda i, o: (i, 0)),
                pl.BlockSpec((TILE, 3 * width), lambda i, o: (i, 0)),
            ],
        ),
        out_shape=[shape((rows, width), F32), shape((rows, 3 * width), LOW)],
        compiler_params=PARAMS,
        cost_estimate=cost(7),
        name="dec_in",
    )(order, gathered, gathered, pos, vecs, weight)


def dec_mid_kernel(
    steps,
    chunks,
    x_ref,
    att_ref,
    cot_ref,
    vec_ref,
    b1_ref,
    wo_ref,
    w1_ref,
    w2_ref,
    out_ref,
    gmid_ref,
    gatt_ref,
    dwo_ref,
    dw1_ref,
    dw2_ref,
    db1_ref,
    sum_ref,
    awo,
    aw1,
    aw2,
    acc,
    dnorm,
):
    step = pl.program_id(0)
    width = x_ref.shape[1]

    @pl.when(step == 0)
    def _():
        awo[...] = jnp.zeros_like(awo)
        aw1[...] = jnp.zeros_like(aw1)
        aw2[...] = jnp.zeros_like(aw2)
        db1_ref[...] = jnp.zeros_like(db1_ref)
        sum_ref[...] = jnp.zeros_like(sum_ref)

    att = att_ref[...]
    low = cot_ref[...]
    middle = x_ref[...] + mm(att, wo_ref[...]) + vec_ref[6:7, :]
    unit, scale = norm_parts(middle)
    normed = (unit * vec_ref[1:2, :] + vec_ref[7:8, :]).astype(LOW)
    acc[...] = middle + vec_ref[8:9, :]
    dnorm[...] = jnp.zeros_like(dnorm)

    def chunk(j, carry):
        cols = pl.ds(pl.multiple_of(j * width, width), width)
        up = w1_ref[:, cols]
        down = w2_ref[cols, :]
        value, slope = gelu_parts(mm(normed, up) + b1_ref[j])
        value = value.astype(LOW)
        acc[...] += mm(value, down)
        aw2[cols, :] += mm_tn(value, low)
        dhid = (slope * mm_nt(low, down)).astype(LOW)
        aw1[:, cols] += mm_tn(normed, dhid)
        db1_ref[j] += col_sum(dhid.astype(F32))
        dnorm[...] += mm_nt(dhid, up)
        return carry

    lax.fori_loop(0, chunks, chunk, 0)
    out_ref[...] = acc[...].astype(LOW)
    dn = dnorm[...]
    sum_ref[0:1, :] += col_sum(dn * unit)
    sum_ref[1:2, :] += col_sum(dn)
    gmid = low.astype(F32) + norm_back(dn, unit, scale, vec_ref[1:2, :])
    gmid_ref[...] = gmid
    mlow = gmid.astype(LOW)
    sum_ref[2:3, :] += col_sum(mlow.astype(F32))
    sum_ref[3:4, :] += col_sum(low.astype(F32))
    awo[...] += mm_tn(att, mlow)
    gatt_ref[...] = mm_nt(mlow, wo_ref[...]).astype(LOW)

    @pl.when(step == steps - 1)
    def _():
        dwo_ref[...] = awo[...].astype(LOW)
        dw1_ref[...] = aw1[...].astype(LOW)
        dw2_ref[...] = aw2[...].astype(LOW)


def dec_mid(dec_in, attended, cotangent, vecs, up_bias, wide, up_w, down_w, proj_at):
    rows, width = dec_in.shape
    hidden = down_w.shape[0]
    chunks = hidden // width
    tile = 2 * TILE
    steps = rows // tile
    by_row = pl.BlockSpec((tile, width), lambda i: (i, 0))
    return pl.pallas_call(
        functools.partial(dec_mid_kernel, steps, chunks),
        grid=(steps,),
        in_specs=[
            by_row,
            by_row,
            by_row,
            full(vecs.shape),
            full((chunks, 1, width)),
            at_col(width, width, proj_at // width),
            full((width, hidden)),
            full((hidden, width)),
        ],
        out_specs=[
            by_row,
            by_row,
            by_row,
            full((width, width)),
            full((width, hidden)),
            full((hidden, width)),
            full((chunks, 1, width)),
            full((8, width)),
        ],
        out_shape=[
            shape((rows, width), LOW),
            shape((rows, width), F32),
            shape((rows, width), LOW),
            shape((width, width), LOW),
            shape((width, hidden), LOW),
            shape((hidden, width), LOW),
            shape((chunks, 1, width), F32),
            shape((8, width), F32),
        ],
        scratch_shapes=[
            pltpu.VMEM((width, width), F32),
            pltpu.VMEM((width, hidden), F32),
            pltpu.VMEM((hidden, width), F32),
            pltpu.VMEM((tile, width), F32),
            pltpu.VMEM((tile, width), F32),
        ],
        compiler_params=PARAMS,
        cost_estimate=cost(28),
        name="dec_mid",
    )(dec_in, attended, cotangent, vecs, up_bias.reshape(chunks, 1, width), wide, up_w, down_w)


def dec_back_kernel(
    limit,
    steps,
    order_ref,
    x_ref,
    dq_ref,
    dk_ref,
    dv_ref,
    gmid_ref,
    vec_ref,
    w_ref,
    dw_ref,
    sum_ref,
    send_ref,
    acc,
):
    step = pl.program_id(0)
    width = x_ref.shape[1]

    @pl.when(step == 0)
    def _():
        acc[...] = jnp.zeros_like(acc)
        sum_ref[...] = jnp.zeros_like(sum_ref)
        send_ref[...] = jnp.zeros_like(send_ref)

    unit, scale = norm_parts(x_ref[...])
    normed = (unit * vec_ref[0:1, :] + vec_ref[3:4, :]).astype(LOW)
    grads = (dq_ref[...], dk_ref[...], dv_ref[...])
    dn = None
    for i, grad in enumerate(grads):
        cols = slice(i * width, (i + 1) * width)
        acc[:, cols] += mm_tn(normed, grad)
        piece = mm_nt(grad, w_ref[:, cols])
        dn = piece if dn is None else dn + piece
    sum_ref[0:1, :] += col_sum(dn * unit)
    sum_ref[1:2, :] += col_sum(dn)
    sum_ref[2:3, :] += col_sum(grads[0].astype(F32))
    sum_ref[3:4, :] += col_sum(grads[2].astype(F32))
    din = gmid_ref[...] + norm_back(dn, unit, scale, vec_ref[0:1, :])
    per = x_ref.shape[0] // BLOCK
    for b in range(per):
        place = order_ref[0, per * step + b]
        rows = din[b * BLOCK : (b + 1) * BLOCK, :]

        @pl.when(place < limit)
        def _():
            send_ref[pl.ds(pl.multiple_of(place * BLOCK, BLOCK), BLOCK), :] = rows.astype(LOW)

        @pl.when(place >= limit)
        def _():
            sum_ref[4:5, :] += col_sum(rows)

    @pl.when(step == steps - 1)
    def _():
        dw_ref[...] = acc[...].astype(LOW)


def dec_back(order, dec_in, dq, dk, dv, gmid, vecs, weight, limit):
    rows, width = dec_in.shape
    tile = 2 * TILE
    steps = rows // tile
    by_row = pl.BlockSpec((tile, width), lambda i, o: (i, 0))
    return pl.pallas_call(
        functools.partial(dec_back_kernel, limit, steps),
        grid_spec=pltpu.PrefetchScalarGridSpec(
            num_scalar_prefetch=1,
            grid=(steps,),
            in_specs=[by_row] * 5 + [full(vecs.shape), at_col(width, 3 * width, 0)],
            out_specs=[
                full((width, 3 * width)),
                full((8, width)),
                full((limit * BLOCK, width)),
            ],
            scratch_shapes=[pltpu.VMEM((width, 3 * width), F32)],
        ),
        out_shape=[
            shape((width, 3 * width), LOW),
            shape((8, width), F32),
            shape((limit * BLOCK, width), LOW),
        ],
        compiler_params=PARAMS,
        cost_estimate=cost(12),
        name="dec_back",
    )(order, dec_in, dq, dk, dv, gmid, vecs, weight)


def positions(count, width):
    places = jnp.arange(count, dtype=jnp.float32)[:, None]
    columns = jnp.arange(width)
    rates = jnp.exp((2 * (columns // 2)).astype(jnp.float32) * (-math.log(10000.0) / width))
    angles = places * rates[None, :]
    return jnp.where((columns % 2 == 0)[None, :], jnp.sin(angles), jnp.cos(angles))


def bits_of(axis):
    size, out = lax.axis_size(axis), []
    while size > 1:
        size //= 2
        out.append((axis, size))
    return out


def all_bits():
    return bits_of("dp") + bits_of("fsdp")


def bit_here(bit):
    axis, stride = bit
    return lax.axis_index(axis) // stride % 2


def swap(value, bit):
    axis, stride = bit
    return lax.ppermute(value, axis, [(i, i ^ stride) for i in range(lax.axis_size(axis))])


def join_kernel(parts, here_ref, own_ref, got_ref, out_ref, sems):
    here = here_ref[0]
    lead = own_ref.shape[0] // parts
    copies = []
    for p in range(parts):
        rows = pl.ds(p * lead, lead)
        copies.append(
            pltpu.make_async_copy(own_ref.at[rows], out_ref.at[rows, here], sems.at[0, p])
        )
        copies.append(
            pltpu.make_async_copy(got_ref.at[rows], out_ref.at[rows, 1 - here], sems.at[1, p])
        )
    for copy in copies:
        copy.start()
    for copy in copies:
        copy.wait()


def join(own, got, here, dim):
    dims = own.shape
    left = math.prod(dims[:dim])
    flat = (left,) + dims[dim:]
    parts = math.gcd(left, 4)
    out = pl.pallas_call(
        functools.partial(join_kernel, parts),
        in_specs=[
            pl.BlockSpec(memory_space=pltpu.SMEM),
            pl.BlockSpec(memory_space=pl.ANY),
            pl.BlockSpec(memory_space=pl.ANY),
        ],
        out_specs=pl.BlockSpec(memory_space=pl.ANY),
        out_shape=shape((left, 2) + dims[dim:], own.dtype),
        scratch_shapes=[pltpu.SemaphoreType.DMA((2, parts))],
        name="join",
    )(here.reshape(1), own.reshape(flat), got.reshape(flat))
    return out.reshape(dims[:dim] + (2,) + dims[dim:])


def gather(piece, order, held=()):
    held, canon = list(held), all_bits()
    for bit in order:
        got = swap(piece, bit)
        dim = sum(canon.index(b) < canon.index(bit) for b in held)
        piece = join(piece, got, bit_here(bit), dim)
        held.append(bit)
    return piece


def flat_rows(value):
    return value.reshape(-1, value.shape[-1])


def term_sum(terms, kind):
    total = terms[0].astype(F32)
    for term in terms[1:]:
        total = total + term.astype(F32)
    return total.astype(kind)


class Fold:
    def __init__(self, terms, order, held=None):
        self.terms, self.order = list(terms), list(order)
        self.left = list(all_bits() if held is None else held)

    def cut(self):
        bit = self.order[0]
        dim = self.left.index(bit)
        here = bit_here(bit)

        def half(index):
            return [lax.dynamic_index_in_dim(t, index, dim, keepdims=False) for t in self.terms]

        self.send, self.terms = term_sum(half(1 - here), LOW), half(here)

    def pass_on(self):
        bit = self.order.pop(0)
        self.left.remove(bit)
        self.terms.append(swap(self.send, bit))

    def rest(self, kind):
        while self.order:
            self.cut()
            self.pass_on()
        return term_sum(self.terms, kind)


def start_beside(folds, inputs):
    for fold in folds:
        fold.cut()
    sends, inputs = lax.optimization_barrier(([f.send for f in folds], inputs))
    for fold, send in zip(folds, sends):
        fold.send = send
        fold.pass_on()
    return inputs


def end_beside(folds, outputs):
    last, outputs = lax.optimization_barrier(([f.terms[-1] for f in folds], outputs))
    for fold, got in zip(folds, last):
        fold.terms[-1] = got
    return outputs


def by_bits(grads):
    bits = len(all_bits())
    rows = grads.shape[0] >> bits
    return grads.reshape((2,) * bits + (rows, grads.shape[1]))


def orders():
    dp, fsdp = bits_of("dp"), bits_of("fsdp")
    line, core = fsdp[:-1], fsdp[-1:]
    return line + dp[::-1] + core, line + dp + core, dp[::-1] + line + core


def pack_vectors(pieces, rows):
    wide = jnp.concatenate([p.reshape(-1, rows) for p in pieces], axis=0)
    wide = jnp.pad(wide, ((0, LANES - wide.shape[0]), (0, 0)))
    return wide.T


def split_columns(array, widths):
    out, at = [], 0
    for w in widths:
        out.append(array[:, at : at + w])
        at += w
    return out


def long_vector(rows_of, devices):
    parts, total = rows_of.shape
    return rows_of.reshape(parts, devices, total // devices).transpose(1, 0, 2).reshape(1, -1)


def long_rows(vector, devices, rows):
    parts = vector.shape[0] // (devices * rows)
    return vector.reshape(devices, parts, rows).transpose(1, 0, 2).reshape(parts, -1)


def per_device(
    enc_input,
    enc_segments,
    dec_segments,
    block_order,
    dec_cotangent,
    enc_qkv,
    enc_proj,
    enc_fc1,
    enc_fc2,
    enc_gains,
    enc_biases,
    enc_fc1_bias,
    embed,
    mask_token,
    dec_qkv,
    dec_proj,
    dec_fc1,
    dec_fc2,
    dec_gains,
    dec_biases,
    dec_fc1_bias,
    dec_fc2_bias,
):
    devices = lax.axis_size("dp") * lax.axis_size("fsdp")
    enc_rows, width = enc_input.shape
    dec_rows, dwidth = dec_cotangent.shape
    erows = enc_qkv.shape[0]
    drows = dec_qkv.shape[0]
    ff = enc_fc1.shape[1]
    dff = dec_fc1.shape[1]
    enc_first = jnp.concatenate(
        [enc_qkv, enc_proj, embed, pack_vectors([enc_gains, enc_biases, enc_fc1_bias], erows)],
        axis=1,
    )
    dec_first = jnp.concatenate(
        [
            dec_qkv,
            dec_proj,
            pack_vectors(
                [dec_gains, dec_biases, dec_fc2_bias[None], mask_token[None], dec_fc1_bias], drows
            ),
        ],
        axis=1,
    )
    ecut = (4 * width + dwidth) // 2 // LANES * LANES
    zxy, zyx, xyz = orders()
    core = zxy[-1:]
    first_one = gather(enc_first[:, :ecut], zxy[:-1])
    first_two = gather(enc_first[:, ecut:], zyx[:-1])
    up_w = flat_rows(gather(enc_fc1, xyz))
    down_w = flat_rows(gather(enc_fc2, zyx))
    dec_first, dec_fc1, dec_fc2, first_one, first_two = lax.optimization_barrier(
        (dec_first, dec_fc1, dec_fc2, first_one, first_two)
    )
    first = jnp.concatenate([first_one, first_two], axis=-1)
    enc_all = flat_rows(gather(first, core, zxy[:-1]))
    dec_all = flat_rows(gather(dec_first, zxy))
    dup_w = flat_rows(gather(dec_fc1, xyz))
    ddown_w = flat_rows(gather(dec_fc2, zyx))
    proj_at, emb_at = 3 * width, 4 * width
    vec_at = emb_at + dwidth
    dproj_at = 3 * dwidth
    dvec_at = 4 * dwidth
    evecs = enc_all[:, vec_at:].T[:16].astype(F32)
    dvecs = dec_all[:, dvec_at:].T[:16].astype(F32)
    up_bias = long_vector(evecs[10:14], devices)
    dup_bias = long_vector(dvecs[10:14], devices)

    qkv = enc_qkv_call(enc_input, evecs, enc_all)
    enc_col = enc_segments.reshape(-1, 1)
    enc_row = enc_segments.reshape(-1, 1, TILE)
    attended, lse = attend(qkv, enc_segments, enc_col, HDIM)
    mid, enc_out, final, act, slope, embedded = enc_mid(
        enc_input,
        attended,
        evecs,
        up_bias,
        dvecs[2:3],
        enc_all,
        up_w,
        down_w,
        proj_at,
        emb_at,
    )
    gathered = lax.all_gather(embedded, "fsdp", axis=0, tiled=True)
    limit = gathered.shape[0] // BLOCK
    dec_in, dqkv = dec_in_call(block_order, gathered, positions(dec_rows, dwidth), dvecs, dec_all)
    dec_col = dec_segments.reshape(-1, 1)
    dec_row = dec_segments.reshape(-1, 1, TILE)
    dattended, dlse = attend(dqkv, dec_segments, dec_col, DHDIM)
    dec_out, dgmid, dgatt, dwo, dw1, dw2, db1, dsum_mid = dec_mid(
        dec_in,
        dattended,
        dec_cotangent,
        dvecs,
        dup_bias,
        dec_all,
        dup_w,
        ddown_w,
        dproj_at,
    )
    down_fold = Fold([by_bits(dw2)], zyx[::-1])
    up_fold = Fold([by_bits(dw1)], xyz[::-1])
    dgatt = start_beside([down_fold, up_fold], dgatt)
    ddq, ddk, ddv = attend_back(
        dqkv, dattended, dgatt, dlse, dec_segments, dec_row, dec_col, DHDIM
    )
    ddq, ddk, ddv = end_beside([down_fold, up_fold], (ddq, ddk, ddv))
    ddq, ddk, ddv = start_beside([down_fold, up_fold], (ddq, ddk, ddv))
    dwqkv, dsum, send = dec_back(
        block_order, dec_in, ddq, ddk, ddv, dgmid, dvecs, dec_all, limit
    )
    ring = bits_of("fsdp")
    emb_fold = Fold([send.reshape((2,) * len(ring) + (enc_rows, dwidth))], ring[::-1], ring)
    elow = emb_fold.rest(LOW)
    elow = start_beside([down_fold, up_fold], elow)
    demb, ew2, ew1, ewo, eb1, esum_emb, esum_mid, gmid, gatt = enc_mid_back(
        elow,
        final,
        enc_out,
        mid,
        attended,
        act,
        slope,
        evecs,
        enc_all,
        up_w,
        down_w,
        proj_at,
        emb_at,
    )
    dec_vec_grads = jnp.concatenate(
        [
            dsum[0:1],
            dsum_mid[0:1],
            esum_emb[0:1],
            dsum[1:4],
            dsum_mid[2:3],
            dsum_mid[1:2],
            dsum_mid[3:4],
            dsum[4:5],
            long_rows(db1.reshape(-1), devices, drows),
            jnp.zeros((LANES - 14, dwidth), F32),
        ],
        axis=0,
    ).T
    dec_grads = jnp.concatenate([dwqkv, dwo, dec_vec_grads.astype(LOW)], axis=1)
    edown_fold = Fold([by_bits(ew2)], zyx[::-1])
    eup_fold = Fold([by_bits(ew1)], xyz[::-1])
    dfirst_fold = Fold([by_bits(dec_grads)], zxy[::-1])
    early = [edown_fold, eup_fold, dfirst_fold, down_fold, up_fold]
    gatt = start_beside(early, gatt)
    dq, dk, dv = attend_back(qkv, attended, gatt, lse, enc_segments, enc_row, enc_col, HDIM)
    dq, dk, dv = end_beside(early, (dq, dk, dv))
    dq, dk, dv = start_beside(early, (dq, dk, dv))
    ewqkv, enc_in_grad, esum = enc_qkv_back(enc_input, dq, dk, dv, gmid, evecs, enc_all)
    enc_vec_grads = jnp.concatenate(
        [
            esum[0:1],
            esum_mid[3:4],
            esum_mid[0:1],
            esum[1:4],
            esum_mid[5:6],
            esum_mid[4:5],
            esum_mid[2:3],
            esum_mid[1:2],
            long_rows(eb1.reshape(-1), devices, erows),
            jnp.zeros((LANES - 14, width), F32),
        ],
        axis=0,
    ).T
    enc_grads = jnp.concatenate([ewqkv, ewo, demb, enc_vec_grads.astype(LOW)], axis=1)
    chip = Fold([by_bits(enc_grads)], core)
    chip.cut()
    chip.pass_on()
    one = Fold([t[..., :ecut] for t in chip.terms], zxy[-2::-1], all_bits()[:-1])
    two = Fold([t[..., ecut:] for t in chip.terms], zyx[-2::-1], all_bits()[:-1])
    rd, ru, rfirst = down_fold.rest(F32), up_fold.rest(F32), dfirst_fold.rest(F32)
    rq, rp, rv = split_columns(rfirst, [3 * dwidth, dwidth, LANES])
    ed, eu = edown_fold.rest(F32), eup_fold.rest(F32)
    efirst = jnp.concatenate([one.rest(F32), two.rest(F32)], axis=-1)
    eq, ep, em, ev = split_columns(efirst, [3 * width, width, dwidth, LANES])
    rv = rv.T
    ev = ev.T
    return (
        dec_out,
        enc_in_grad,
        eq,
        ep,
        eu,
        ed,
        ev[:3],
        ev[3:10],
        ev[10:14].reshape(-1),
        em,
        rv[9],
        rq,
        rp,
        ru,
        rd,
        rv[:2],
        rv[2:8],
        rv[10:14].reshape(-1),
        rv[8],
    )


def solution(mesh):
    in_specs = (
        P(("dp", "fsdp"), None),
        P(("dp", "fsdp"), None),
        P(("dp", "fsdp"), None),
        P("dp", "fsdp"),
        P(("dp", "fsdp"), None),
        P(("dp", "fsdp"), None),
        P(("dp", "fsdp"), None),
        P(("dp", "fsdp"), None),
        P(("dp", "fsdp"), None),
        P(None, ("dp", "fsdp")),
        P(None, ("dp", "fsdp")),
        P(("dp", "fsdp")),
        P(("dp", "fsdp"), None),
        P(("dp", "fsdp")),
        P(("dp", "fsdp"), None),
        P(("dp", "fsdp"), None),
        P(("dp", "fsdp"), None),
        P(("dp", "fsdp"), None),
        P(None, ("dp", "fsdp")),
        P(None, ("dp", "fsdp")),
        P(("dp", "fsdp")),
        P(("dp", "fsdp")),
    )
    out_specs = (
        P(("dp", "fsdp"), None),
        P(("dp", "fsdp"), None),
        P(("dp", "fsdp"), None),
        P(("dp", "fsdp"), None),
        P(("dp", "fsdp"), None),
        P(("dp", "fsdp"), None),
        P(None, ("dp", "fsdp")),
        P(None, ("dp", "fsdp")),
        P(("dp", "fsdp")),
        P(("dp", "fsdp"), None),
        P(("dp", "fsdp")),
        P(("dp", "fsdp"), None),
        P(("dp", "fsdp"), None),
        P(("dp", "fsdp"), None),
        P(("dp", "fsdp"), None),
        P(None, ("dp", "fsdp")),
        P(None, ("dp", "fsdp")),
        P(("dp", "fsdp")),
        P(("dp", "fsdp")),
    )
    return jax.shard_map(
        per_device, mesh=mesh, in_specs=in_specs, out_specs=out_specs, check_vma=False
    )
```

```python
import functools
import math

import jax
import jax.numpy as jnp
from jax import lax
from jax.experimental import pallas as pl
from jax.experimental.pallas import tpu as pltpu
from jax.sharding import PartitionSpec as P

HDIM = 64
DHDIM = 32
BLOCK = 128
LANES = 128
TILE = 256
EPSILON = 1e-06
NEGATIVE = -1e30
LOG2E = math.log2(math.e)
AXES = ("dp", "fsdp")
F32 = jnp.float32
LOW = jnp.bfloat16
PARAMS = pltpu.CompilerParams(vmem_limit_bytes=56 * 1024 * 1024)


def mm(left, right):
    return jnp.dot(left, right, preferred_element_type=F32)


def mm_tn(left, right):
    return lax.dot_general(left, right, (((0,), (0,)), ((), ())), preferred_element_type=F32)


def mm_nt(left, right):
    return lax.dot_general(left, right, (((1,), (1,)), ((), ())), preferred_element_type=F32)


def col_sum(values):
    return jnp.sum(values, axis=0, keepdims=True)


def norm_parts(values):
    centred = values - jnp.mean(values, axis=-1, keepdims=True)
    variance = jnp.mean(centred * centred, axis=-1, keepdims=True)
    scale = lax.rsqrt(variance + EPSILON)
    return centred * scale, scale


def norm_back(grad, unit, scale, gain):
    inner = grad * gain
    mean_inner = jnp.mean(inner, axis=-1, keepdims=True)
    mean_cross = jnp.mean(inner * unit, axis=-1, keepdims=True)
    return scale * (inner - mean_inner - unit * mean_cross)


def gelu_parts(hidden):
    cdf = 0.5 + 0.5 * lax.erf(hidden * (0.5**0.5))
    density = jnp.exp(hidden * hidden * -0.5) * (1.0 / math.sqrt(2.0 * math.pi))
    return hidden * cdf, cdf + hidden * density


CHEAP = pl.CostEstimate(flops=1 << 20, bytes_accessed=1 << 16, transcendentals=0)


def full(shape):
    return pl.BlockSpec(shape, lambda *_: (0,) * len(shape))


def at_col(rows, cols, index):
    return pl.BlockSpec((rows, cols), lambda *_: (0, index))


def shape(dims, kind):
    return jax.ShapeDtypeStruct(dims, kind)


def lane_mask(head, head_dim, kind):
    lane = lax.broadcasted_iota(jnp.int32, (1, LANES), 1)
    inside = (lane >= head * head_dim) & (lane < (head + 1) * head_dim)
    return inside.astype(F32).astype(kind)


def tile_range(seg_ref, here, tiles):
    first = seg_ref[0, here * TILE]
    last = seg_ref[0, here * TILE + TILE - 1]
    low = jnp.int32(0)
    high = jnp.int32(tiles)
    for other in range(tiles):
        low += (seg_ref[0, other * TILE + TILE - 1] < first).astype(jnp.int32)
        high -= (seg_ref[0, other * TILE] > last).astype(jnp.int32)
    return low, high


def attend_kernel(
    head_dim,
    tiles,
    seg_ref,
    q_ref,
    k_ref,
    v_ref,
    row_ref,
    col_ref,
    out_ref,
    lse_ref,
    vt,
    held,
    acc,
    top,
    tot,
):
    heads = LANES // head_dim
    here = pl.program_id(1)
    factor = head_dim ** (-0.5) * LOG2E

    @pl.when(here == 0)
    def _():
        for u in range(tiles):
            vt[u] = v_ref[u * TILE : (u + 1) * TILE, :].astype(F32).T.astype(LOW)

    acc[...] = jnp.zeros_like(acc)
    top[...] = jnp.full_like(top, NEGATIVE)
    tot[...] = jnp.zeros_like(tot)
    query = q_ref[...]
    row = row_ref[...]

    def score(u, carry):
        start = pl.multiple_of(u * TILE, TILE)
        keys = k_ref[pl.ds(start, TILE), :]
        same = col_ref[pl.ds(start, TILE), :] == row
        for h in range(heads):
            scores = mm_nt(keys * lane_mask(h, head_dim, LOW), query)
            scores = jnp.where(same, scores, NEGATIVE)
            held[u, h] = scores
            top[h : h + 1, :] = jnp.maximum(
                top[h : h + 1, :], jnp.max(scores, axis=0, keepdims=True)
            )
        return carry

    def mix(u, carry):
        for h in range(heads):
            probs = jnp.exp2((held[u, h] - top[h : h + 1, :]) * factor)
            tot[h : h + 1, :] += col_sum(probs)
            span = slice(h * head_dim, (h + 1) * head_dim)
            acc[span, :] += mm(vt[u, span, :], probs.astype(LOW))
        return carry

    low, high = tile_range(seg_ref, here, tiles)
    lax.fori_loop(low, high, score, 0)
    lax.fori_loop(low, high, mix, 0)
    for h in range(heads):
        span = slice(h * head_dim, (h + 1) * head_dim)
        total = tot[h : h + 1, :]
        acc[span, :] = acc[span, :] / total
        lse_ref[0, 0, h : h + 1, :] = top[h : h + 1, :] * factor + jnp.log2(total)
    out_ref[...] = acc[...].T.astype(LOW)


def attend(qkv, segments, seg_col, head_dim):
    rows, width = qkv.shape[0], qkv.shape[1] // 3
    groups, tiles = width // LANES, rows // TILE
    return pl.pallas_call(
        functools.partial(attend_kernel, head_dim, tiles),
        grid_spec=pltpu.PrefetchScalarGridSpec(
            num_scalar_prefetch=1,
            grid=(groups, tiles),
            in_specs=[
                pl.BlockSpec((TILE, LANES), lambda g, t, s: (t, g)),
                pl.BlockSpec((rows, LANES), lambda g, t, s: (0, groups + g)),
                pl.BlockSpec((rows, LANES), lambda g, t, s: (0, 2 * groups + g)),
                pl.BlockSpec((1, TILE), lambda g, t, s: (0, t)),
                pl.BlockSpec((rows, 1), lambda g, t, s: (0, 0)),
            ],
            out_specs=[
                pl.BlockSpec((TILE, LANES), lambda g, t, s: (t, g)),
                pl.BlockSpec((1, 1, 8, TILE), lambda g, t, s: (g, t, 0, 0)),
            ],
            scratch_shapes=[
                pltpu.VMEM((tiles, LANES, TILE), LOW),
                pltpu.VMEM((tiles, LANES // head_dim, TILE, TILE), F32),
                pltpu.VMEM((LANES, TILE), F32),
                pltpu.VMEM((8, TILE), F32),
                pltpu.VMEM((8, TILE), F32),
            ],
        ),
        out_shape=[shape((rows, width), LOW), shape((groups, tiles, 8, TILE), F32)],
        compiler_params=PARAMS,
        cost_estimate=CHEAP,
        name="attend",
    )(segments, qkv, qkv, qkv, segments, seg_col)


def attend_back_kernel(
    head_dim,
    tiles,
    seg_ref,
    q_ref,
    k_ref,
    v_ref,
    o_ref,
    g_ref,
    lse_ref,
    row_ref,
    col_ref,
    dq_ref,
    dk_ref,
    dv_ref,
    dqt,
    delta,
    dk_acc,
    dv_acc,
):
    heads = LANES // head_dim
    here = pl.program_id(1)
    scale = head_dim ** (-0.5)
    factor = scale * LOG2E

    @pl.when(here == 0)
    def _():
        dqt[...] = jnp.zeros_like(dqt)
        for t in range(tiles):
            rows = slice(t * TILE, (t + 1) * TILE)
            both = (g_ref[rows, :].astype(F32) * o_ref[rows, :].astype(F32)).T
            for h in range(heads):
                delta[t, h : h + 1, :] = col_sum(both[h * head_dim : (h + 1) * head_dim, :])

    keys, vals = k_ref[...], v_ref[...]
    keys_t = keys.astype(F32).T.astype(LOW)
    col = col_ref[...]
    dk_acc[...] = jnp.zeros_like(dk_acc)
    dv_acc[...] = jnp.zeros_like(dv_acc)

    def step(t, carry):
        start = pl.multiple_of(t * TILE, TILE)
        query = q_ref[pl.ds(start, TILE), :]
        grads = g_ref[pl.ds(start, TILE), :]
        same = col == row_ref[t]
        for h in range(heads):
            mask = lane_mask(h, head_dim, LOW)
            span = slice(h * head_dim, (h + 1) * head_dim)
            scores = mm_nt(keys * mask, query) * factor
            scores = jnp.where(same, scores, NEGATIVE)
            probs = jnp.exp2(scores - lse_ref[0, t, h : h + 1, :])
            grad_probs = mm_nt(vals * mask, grads)
            grad_scores = (probs * (grad_probs - delta[t, h : h + 1, :])).astype(LOW)
            dv_acc[...] += mm(probs.astype(LOW), grads * mask)
            dk_acc[...] += mm(grad_scores, query * mask)
            dqt[t, span, :] += mm(keys_t[span, :], grad_scores)
        return carry

    low, high = tile_range(seg_ref, here, tiles)
    lax.fori_loop(low, high, step, 0)
    dk_ref[...] = (dk_acc[...] * scale).astype(LOW)
    dv_ref[...] = dv_acc[...].astype(LOW)

    @pl.when(here == tiles - 1)
    def _():
        for t in range(tiles):
            dq_ref[t * TILE : (t + 1) * TILE, :] = (dqt[t] * scale).T.astype(LOW)


def attend_back(qkv, attended, grad, lse, segments, seg_row, seg_col, head_dim):
    rows, width = attended.shape
    groups, tiles = width // LANES, rows // TILE
    whole = pl.BlockSpec((rows, LANES), lambda g, u, s: (0, g))
    piece = pl.BlockSpec((TILE, LANES), lambda g, u, s: (u, g))
    return pl.pallas_call(
        functools.partial(attend_back_kernel, head_dim, tiles),
        grid_spec=pltpu.PrefetchScalarGridSpec(
            num_scalar_prefetch=1,
            grid=(groups, tiles),
            in_specs=[
                whole,
                pl.BlockSpec((TILE, LANES), lambda g, u, s: (u, groups + g)),
                pl.BlockSpec((TILE, LANES), lambda g, u, s: (u, 2 * groups + g)),
                whole,
                whole,
                pl.BlockSpec((1, tiles, 8, TILE), lambda g, u, s: (g, 0, 0, 0)),
                pl.BlockSpec((tiles, 1, TILE), lambda g, u, s: (0, 0, 0)),
                pl.BlockSpec((TILE, 1), lambda g, u, s: (u, 0)),
            ],
            out_specs=[whole, piece, piece],
            scratch_shapes=[
                pltpu.VMEM((tiles, LANES, TILE), F32),
                pltpu.VMEM((tiles, 8, TILE), F32),
                pltpu.VMEM((TILE, LANES), F32),
                pltpu.VMEM((TILE, LANES), F32),
            ],
        ),
        out_shape=[shape((rows, width), LOW)] * 3,
        compiler_params=PARAMS,
        cost_estimate=CHEAP,
        name="attend_back",
    )(segments, qkv, qkv, qkv, attended, grad, lse, seg_row, seg_col)


def enc_qkv_kernel(x_ref, vec_ref, w_ref, out_ref, normed):
    part = pl.program_id(0)

    @pl.when(part == 0)
    def _():
        unit, _ = norm_parts(x_ref[...].astype(F32))
        normed[...] = (unit * vec_ref[0:1, :] + vec_ref[3:4, :]).astype(LOW)

    bias = jnp.where(part == 0, vec_ref[4:5, :], jnp.where(part == 2, vec_ref[5:6, :], 0.0))
    out_ref[...] = (mm(normed[...], w_ref[...]) + bias).astype(LOW)


def enc_qkv_call(rows_in, vecs, weight):
    rows, width = rows_in.shape
    return pl.pallas_call(
        enc_qkv_kernel,
        grid=(3,),
        in_specs=[
            full((rows, width)),
            full(vecs.shape),
            pl.BlockSpec((width, width), lambda i: (0, i)),
        ],
        out_specs=pl.BlockSpec((rows, width), lambda i: (0, i)),
        out_shape=shape((rows, 3 * width), LOW),
        scratch_shapes=[pltpu.VMEM((rows, width), LOW)],
        compiler_params=PARAMS,
        cost_estimate=CHEAP,
        name="enc_qkv",
    )(rows_in, vecs, weight)


def natural_rows(block, group):
    if group is None:
        return block
    width = block.shape[1] // 4
    wide = block.astype(F32)
    pieces = []
    for at in range(0, block.shape[0], group):
        for part in range(4):
            pieces.append(wide[at : at + group, part * width : (part + 1) * width])
    return jnp.concatenate(pieces, axis=0).astype(LOW)


def enc_mid_kernel(
    chunks,
    group,
    x_ref,
    att_ref,
    vec_ref,
    b1_ref,
    eb_ref,
    wo_ref,
    w1_ref,
    w2_ref,
    we_ref,
    mid_ref,
    out_ref,
    final_ref,
    act_ref,
    slope_ref,
    emb_ref,
    natural_ref,
    normed,
    acc,
):
    part = pl.program_id(0)

    @pl.when(part == 0)
    def _():
        middle = x_ref[...].astype(F32) + mm(att_ref[...], wo_ref[...]) + vec_ref[6:7, :]
        mid_ref[...] = middle
        unit, _ = norm_parts(middle)
        normed[...] = (unit * vec_ref[1:2, :] + vec_ref[7:8, :]).astype(LOW)
        acc[...] = middle + vec_ref[8:9, :]

    hidden = mm(normed[...], w1_ref[...]) + b1_ref[...]
    value, slope = gelu_parts(hidden)
    value = value.astype(LOW)
    act_ref[...] = value
    slope_ref[...] = slope
    down = natural_rows(w2_ref[...], group)
    natural_ref[...] = down
    acc[...] += mm(value, down)

    @pl.when(part == chunks - 1)
    def _():
        result = acc[...]
        out_ref[...] = result
        unit, _ = norm_parts(result)
        final = (unit * vec_ref[2:3, :] + vec_ref[9:10, :]).astype(LOW)
        final_ref[...] = final
        emb_ref[...] = (mm(final, we_ref[...]) + eb_ref[...]).astype(LOW)


def enc_mid(rows_in, attended, vecs, up_bias, emb_bias, wide, rest, down_w, proj_at, emb_at):
    rows, width = rows_in.shape
    hidden = up_bias.shape[1]
    emb_width = emb_bias.shape[1]
    chunks = hidden // width
    devices = lax.axis_size("dp") * lax.axis_size("fsdp")
    if down_w is None:
        group = width // devices
        down_spec = pl.BlockSpec((width // 4, hidden), lambda i: (i, 1))
        down_w = rest
    else:
        group = None
        down_spec = pl.BlockSpec((width, width), lambda i: (i, 0))
    return pl.pallas_call(
        functools.partial(enc_mid_kernel, chunks, group),
        grid=(chunks,),
        in_specs=[
            full((rows, width)),
            full((rows, width)),
            full(vecs.shape),
            pl.BlockSpec((1, width), lambda i: (0, i)),
            full((1, emb_width)),
            at_col(width, width, proj_at // width),
            pl.BlockSpec((width, width), lambda i: (0, i)),
            down_spec,
            at_col(width, emb_width, emb_at // emb_width),
        ],
        out_specs=[
            full((rows, width)),
            full((rows, width)),
            full((rows, width)),
            pl.BlockSpec((rows, width), lambda i: (0, i)),
            pl.BlockSpec((rows, width), lambda i: (0, i)),
            full((rows, emb_width)),
            pl.BlockSpec((width, width), lambda i: (i, 0)),
        ],
        out_shape=[
            shape((rows, width), F32),
            shape((rows, width), F32),
            shape((rows, width), LOW),
            shape((rows, hidden), LOW),
            shape((rows, hidden), F32),
            shape((rows, emb_width), LOW),
            shape((hidden, width), LOW),
        ],
        scratch_shapes=[pltpu.VMEM((rows, width), LOW), pltpu.VMEM((rows, width), F32)],
        compiler_params=PARAMS,
        cost_estimate=CHEAP,
        name="enc_mid",
    )(rows_in, attended, vecs, up_bias, emb_bias, wide, rest, down_w, wide)


def enc_mid_back_kernel(
    chunks,
    elow_ref,
    final_ref,
    out_ref,
    mid_ref,
    att_ref,
    act_ref,
    slope_ref,
    vec_ref,
    wo_ref,
    w1_ref,
    w2_ref,
    we_ref,
    demb_ref,
    dw2_ref,
    dw1_ref,
    dwo_ref,
    db1_ref,
    esum_ref,
    sum_ref,
    gmid_ref,
    gatt_ref,
    grad,
    grad_low,
    unit_two,
    scale_two,
    normed,
    dnorm,
):
    part = pl.program_id(0)

    @pl.when(part == 0)
    def _():
        elow = elow_ref[...]
        demb_ref[...] = mm_tn(final_ref[...], elow).astype(LOW)
        esum_ref[...] = jnp.zeros_like(esum_ref)
        esum_ref[0:1, :] = col_sum(elow.astype(F32))
        unit, scale = norm_parts(out_ref[...])
        dfinal = mm_nt(elow, we_ref[...])
        sum_ref[...] = jnp.zeros_like(sum_ref)
        sum_ref[0:1, :] = col_sum(dfinal * unit)
        sum_ref[1:2, :] = col_sum(dfinal)
        total = norm_back(dfinal, unit, scale, vec_ref[2:3, :])
        grad[...] = total
        low = total.astype(LOW)
        grad_low[...] = low
        sum_ref[2:3, :] = col_sum(low.astype(F32))
        unit, scale = norm_parts(mid_ref[...])
        unit_two[...] = unit
        scale_two[...] = jnp.broadcast_to(scale, scale_two.shape)
        normed[...] = (unit * vec_ref[1:2, :] + vec_ref[7:8, :]).astype(LOW)
        dnorm[...] = jnp.zeros_like(dnorm)

    low = grad_low[...]
    dw2_ref[...] = mm_tn(act_ref[...], low).astype(LOW)
    dhid = (slope_ref[...] * mm_nt(low, w2_ref[...])).astype(LOW)
    dw1_ref[...] = mm_tn(normed[...], dhid).astype(LOW)
    db1_ref[...] = col_sum(dhid.astype(F32))
    dnorm[...] += mm_nt(dhid, w1_ref[...])

    @pl.when(part == chunks - 1)
    def _():
        dn = dnorm[...]
        unit = unit_two[...]
        sum_ref[3:4, :] = col_sum(dn * unit)
        sum_ref[4:5, :] = col_sum(dn)
        gmid = grad[...] + norm_back(dn, unit, scale_two[:, 0:1], vec_ref[1:2, :])
        gmid_ref[...] = gmid
        mlow = gmid.astype(LOW)
        sum_ref[5:6, :] = col_sum(mlow.astype(F32))
        dwo_ref[...] = mm_tn(att_ref[...], mlow).astype(LOW)
        gatt_ref[...] = mm_nt(mlow, wo_ref[...]).astype(LOW)


def enc_mid_back(
    elow, final, out, mid, attended, act, slope, vecs, wide, up_w, down_w, proj_at, emb_at
):
    rows, width = mid.shape
    hidden = down_w.shape[0]
    emb_width = elow.shape[1]
    chunks = hidden // width
    by_col = pl.BlockSpec((rows, width), lambda i: (0, i))
    return pl.pallas_call(
        functools.partial(enc_mid_back_kernel, chunks),
        grid=(chunks,),
        in_specs=[
            full((rows, emb_width)),
            full((rows, width)),
            full((rows, width)),
            full((rows, width)),
            full((rows, width)),
            by_col,
            by_col,
            full(vecs.shape),
            at_col(width, width, proj_at // width),
            pl.BlockSpec((width, width), lambda i: (0, i)),
            pl.BlockSpec((width, width), lambda i: (i, 0)),
            at_col(width, emb_width, emb_at // emb_width),
        ],
        out_specs=[
            full((width, emb_width)),
            pl.BlockSpec((width, width), lambda i: (i, 0)),
            pl.BlockSpec((width, width), lambda i: (0, i)),
            full((width, width)),
            pl.BlockSpec((1, width), lambda i: (0, i)),
            full((8, emb_width)),
            full((8, width)),
            full((rows, width)),
            full((rows, width)),
        ],
        out_shape=[
            shape((width, emb_width), LOW),
            shape((hidden, width), LOW),
            shape((width, hidden), LOW),
            shape((width, width), LOW),
            shape((1, hidden), F32),
            shape((8, emb_width), F32),
            shape((8, width), F32),
            shape((rows, width), F32),
            shape((rows, width), LOW),
        ],
        scratch_shapes=[
            pltpu.VMEM((rows, width), F32),
            pltpu.VMEM((rows, width), LOW),
            pltpu.VMEM((rows, width), F32),
            pltpu.VMEM((rows, LANES), F32),
            pltpu.VMEM((rows, width), LOW),
            pltpu.VMEM((rows, width), F32),
        ],
        compiler_params=PARAMS,
        cost_estimate=CHEAP,
        name="enc_mid_back",
    )(elow, final, out, mid, attended, act, slope, vecs, wide, up_w, down_w, wide)


def enc_qkv_back_kernel(
    x_ref, dq_ref, dk_ref, dv_ref, gmid_ref, vec_ref, w_ref, dw_ref, din_ref, sum_ref, normed, dnorm
):
    part = pl.program_id(0)

    @pl.when(part == 0)
    def _():
        unit, _ = norm_parts(x_ref[...].astype(F32))
        normed[...] = (unit * vec_ref[0:1, :] + vec_ref[3:4, :]).astype(LOW)
        dnorm[...] = jnp.zeros_like(dnorm)
        sum_ref[...] = jnp.zeros_like(sum_ref)
        sum_ref[2:3, :] = col_sum(dq_ref[...].astype(F32))
        sum_ref[3:4, :] = col_sum(dv_ref[...].astype(F32))

    def one(grad):
        dw_ref[...] = mm_tn(normed[...], grad).astype(LOW)
        dnorm[...] += mm_nt(grad, w_ref[...])

    for index, ref in enumerate((dq_ref, dk_ref, dv_ref)):
        pl.when(part == index)(functools.partial(lambda r: one(r[...]), ref))

    @pl.when(part == 2)
    def _():
        unit, scale = norm_parts(x_ref[...].astype(F32))
        dn = dnorm[...]
        sum_ref[0:1, :] = col_sum(dn * unit)
        sum_ref[1:2, :] = col_sum(dn)
        din = gmid_ref[...] + norm_back(dn, unit, scale, vec_ref[0:1, :])
        din_ref[...] = din.astype(LOW)


def enc_qkv_back(rows_in, dq, dk, dv, gmid, vecs, weight):
    rows, width = rows_in.shape
    whole = full((rows, width))
    by_col = pl.BlockSpec((width, width), lambda i: (0, i))
    return pl.pallas_call(
        enc_qkv_back_kernel,
        grid=(3,),
        in_specs=[whole] * 5 + [full(vecs.shape), by_col],
        out_specs=[by_col, whole, full((8, width))],
        out_shape=[
            shape((width, 3 * width), LOW),
            shape((rows, width), LOW),
            shape((8, width), F32),
        ],
        scratch_shapes=[pltpu.VMEM((rows, width), LOW), pltpu.VMEM((rows, width), F32)],
        compiler_params=PARAMS,
        cost_estimate=CHEAP,
        name="enc_qkv_back",
    )(rows_in, dq, dk, dv, gmid, vecs, weight)


def dec_in_kernel(limit, order_ref, one_ref, two_ref, pos_ref, vec_ref, w_ref, in_ref, qkv_ref):
    step = pl.program_id(0)
    width = in_ref.shape[1]
    for half, ref in enumerate((one_ref, two_ref)):
        visible = order_ref[0, 2 * step + half] < limit
        rows = slice(half * BLOCK, (half + 1) * BLOCK)
        in_ref[rows, :] = (
            jnp.where(visible, ref[...].astype(F32), vec_ref[9:10, :]) + pos_ref[rows, :]
        )
    unit, _ = norm_parts(in_ref[...])
    normed = (unit * vec_ref[0:1, :] + vec_ref[3:4, :]).astype(LOW)
    qkv = mm(normed, w_ref[...])
    qkv_ref[:, :width] = (qkv[:, :width] + vec_ref[4:5, :]).astype(LOW)
    qkv_ref[:, width : 2 * width] = qkv[:, width : 2 * width].astype(LOW)
    qkv_ref[:, 2 * width :] = (qkv[:, 2 * width :] + vec_ref[5:6, :]).astype(LOW)


def dec_in_call(order, gathered, pos, vecs, weight):
    rows, width = pos.shape
    limit = gathered.shape[0] // BLOCK

    def chosen(half):
        def index(i, order_ref):
            return (jnp.clip(order_ref[0, 2 * i + half], 0, limit - 1), 0)

        return pl.BlockSpec((BLOCK, width), index)

    return pl.pallas_call(
        functools.partial(dec_in_kernel, limit),
        grid_spec=pltpu.PrefetchScalarGridSpec(
            num_scalar_prefetch=1,
            grid=(rows // TILE,),
            in_specs=[
                chosen(0),
                chosen(1),
                pl.BlockSpec((TILE, width), lambda i, o: (i, 0)),
                full(vecs.shape),
                at_col(width, 3 * width, 0),
            ],
            out_specs=[
                pl.BlockSpec((TILE, width), lambda i, o: (i, 0)),
                pl.BlockSpec((TILE, 3 * width), lambda i, o: (i, 0)),
            ],
        ),
        out_shape=[shape((rows, width), F32), shape((rows, 3 * width), LOW)],
        compiler_params=PARAMS,
        cost_estimate=CHEAP,
        name="dec_in",
    )(order, gathered, gathered, pos, vecs, weight)


def packed_places(rows, group, width):
    return [
        ((4 * (row // group) + part) * group, row, part * width)
        for row in range(0, rows, group)
        for part in range(4)
    ]


def dec_mid_kernel(
    steps,
    chunks,
    group,
    outer,
    x_ref,
    att_ref,
    cot_ref,
    vec_ref,
    b1_ref,
    wo_ref,
    w1_ref,
    w2_ref,
    out_ref,
    gmid_ref,
    gatt_ref,
    dw_ref,
    db1_ref,
    sum_ref,
    awo,
    aw1,
    aw2,
    acc,
    dnorm,
    natural,
):
    step = pl.program_id(0)
    width = x_ref.shape[1]

    @pl.when(step == 0)
    def _():
        awo[...] = jnp.zeros_like(awo)
        aw1[...] = jnp.zeros_like(aw1)
        aw2[...] = jnp.zeros_like(aw2)
        db1_ref[...] = jnp.zeros_like(db1_ref)
        sum_ref[...] = jnp.zeros_like(sum_ref)
        if group is None:
            natural[...] = w2_ref[...]
        else:
            for at, row, col in packed_places(width, group, width):
                natural[at : at + group, :] = w2_ref[row : row + group, col : col + width]

    att = att_ref[...]
    low = cot_ref[...]
    middle = x_ref[...] + mm(att, wo_ref[...]) + vec_ref[6:7, :]
    unit, scale = norm_parts(middle)
    normed = (unit * vec_ref[1:2, :] + vec_ref[7:8, :]).astype(LOW)
    acc[...] = middle + vec_ref[8:9, :]
    dnorm[...] = jnp.zeros_like(dnorm)

    def chunk(j, carry):
        cols = pl.ds(pl.multiple_of(j * width, width), width)
        up = w1_ref[:, cols]
        down = natural[cols, :]
        value, slope = gelu_parts(mm(normed, up) + b1_ref[j])
        value = value.astype(LOW)
        acc[...] += mm(value, down)
        aw2[cols, :] += mm_tn(value, low)
        dhid = (slope * mm_nt(low, down)).astype(LOW)
        aw1[:, cols] += mm_tn(normed, dhid)
        db1_ref[j] += col_sum(dhid.astype(F32))
        dnorm[...] += mm_nt(dhid, up)
        return carry

    lax.fori_loop(0, chunks, chunk, 0)
    out_ref[...] = acc[...].astype(LOW)
    dn = dnorm[...]
    sum_ref[0:1, :] += col_sum(dn * unit)
    sum_ref[1:2, :] += col_sum(dn)
    gmid = low.astype(F32) + norm_back(dn, unit, scale, vec_ref[1:2, :])
    gmid_ref[...] = gmid
    mlow = gmid.astype(LOW)
    sum_ref[2:3, :] += col_sum(mlow.astype(F32))
    sum_ref[3:4, :] += col_sum(low.astype(F32))
    awo[...] += mm_tn(att, mlow)
    gatt_ref[...] = mm_nt(mlow, wo_ref[...]).astype(LOW)

    @pl.when(step == steps - 1)
    def _():
        hidden = chunks * width
        if group is None:
            dw_ref[:, :hidden] = aw1[...].astype(LOW)
            dw_ref[:, 2 * hidden :] = awo[...].astype(LOW)
            for c in range(chunks):
                dw_ref[:, hidden + c * width : hidden + (c + 1) * width] = aw2[
                    c * width : (c + 1) * width, :
                ].astype(LOW)
        else:
            inner = width // group // outer
            for row in range(0, width, group):
                device = row // group
                to = (device % inner * outer + device // inner) * group
                dw_ref[to : to + group, :hidden] = aw1[row : row + group, :].astype(LOW)
                dw_ref[to : to + group, 2 * hidden :] = awo[row : row + group, :].astype(LOW)
                for part in range(4):
                    at, col = (4 * device + part) * group, hidden + part * width
                    dw_ref[to : to + group, col : col + width] = aw2[at : at + group, :].astype(LOW)


def dec_mid(dec_in, attended, cotangent, vecs, up_bias, wide, rest, down_w, proj_at):
    rows, width = dec_in.shape
    hidden = up_bias.shape[1]
    chunks = hidden // width
    if down_w is None:
        group = width // (lax.axis_size("dp") * lax.axis_size("fsdp"))
        down_spec = at_col(width, hidden, 1)
        down_w = rest
    else:
        group = None
        down_spec = full((hidden, width))
    tile = 2 * TILE
    steps = rows // tile
    by_row = pl.BlockSpec((tile, width), lambda i: (i, 0))
    return pl.pallas_call(
        functools.partial(dec_mid_kernel, steps, chunks, group, lax.axis_size("dp")),
        grid=(steps,),
        in_specs=[
            by_row,
            by_row,
            by_row,
            full(vecs.shape),
            full((chunks, 1, width)),
            at_col(width, width, proj_at // width),
            at_col(width, hidden, 0),
            down_spec,
        ],
        out_specs=[
            by_row,
            by_row,
            by_row,
            full((width, 2 * hidden + width)),
            full((chunks, 1, width)),
            full((8, width)),
        ],
        out_shape=[
            shape((rows, width), LOW),
            shape((rows, width), F32),
            shape((rows, width), LOW),
            shape((width, 2 * hidden + width), LOW),
            shape((chunks, 1, width), F32),
            shape((8, width), F32),
        ],
        scratch_shapes=[
            pltpu.VMEM((width, width), F32),
            pltpu.VMEM((width, hidden), F32),
            pltpu.VMEM((hidden, width), F32),
            pltpu.VMEM((tile, width), F32),
            pltpu.VMEM((tile, width), F32),
            pltpu.VMEM((hidden, width), LOW),
        ],
        compiler_params=PARAMS,
        cost_estimate=CHEAP,
        name="dec_mid",
    )(dec_in, attended, cotangent, vecs, up_bias.reshape(chunks, 1, width), wide, rest, down_w)


def dec_back_kernel(
    limit,
    steps,
    order_ref,
    x_ref,
    dq_ref,
    dk_ref,
    dv_ref,
    gmid_ref,
    vec_ref,
    w_ref,
    dw_ref,
    sum_ref,
    send_ref,
    acc,
):
    step = pl.program_id(0)
    width = x_ref.shape[1]

    @pl.when(step == 0)
    def _():
        acc[...] = jnp.zeros_like(acc)
        sum_ref[...] = jnp.zeros_like(sum_ref)
        send_ref[...] = jnp.zeros_like(send_ref)

    unit, scale = norm_parts(x_ref[...])
    normed = (unit * vec_ref[0:1, :] + vec_ref[3:4, :]).astype(LOW)
    grads = (dq_ref[...], dk_ref[...], dv_ref[...])
    dn = None
    for i, grad in enumerate(grads):
        cols = slice(i * width, (i + 1) * width)
        acc[:, cols] += mm_tn(normed, grad)
        piece = mm_nt(grad, w_ref[:, cols])
        dn = piece if dn is None else dn + piece
    sum_ref[0:1, :] += col_sum(dn * unit)
    sum_ref[1:2, :] += col_sum(dn)
    sum_ref[2:3, :] += col_sum(grads[0].astype(F32))
    sum_ref[3:4, :] += col_sum(grads[2].astype(F32))
    din = gmid_ref[...] + norm_back(dn, unit, scale, vec_ref[0:1, :])
    per = x_ref.shape[0] // BLOCK
    for b in range(per):
        place = order_ref[0, per * step + b]
        rows = din[b * BLOCK : (b + 1) * BLOCK, :]

        @pl.when(place < limit)
        def _():
            send_ref[pl.ds(pl.multiple_of(place * BLOCK, BLOCK), BLOCK), :] = rows.astype(LOW)

        @pl.when(place >= limit)
        def _():
            sum_ref[4:5, :] += col_sum(rows)

    @pl.when(step == steps - 1)
    def _():
        dw_ref[...] = acc[...].astype(LOW)


def dec_back(order, dec_in, dq, dk, dv, gmid, vecs, weight, limit):
    rows, width = dec_in.shape
    tile = 2 * TILE
    steps = rows // tile
    by_row = pl.BlockSpec((tile, width), lambda i, o: (i, 0))
    return pl.pallas_call(
        functools.partial(dec_back_kernel, limit, steps),
        grid_spec=pltpu.PrefetchScalarGridSpec(
            num_scalar_prefetch=1,
            grid=(steps,),
            in_specs=[by_row] * 5 + [full(vecs.shape), at_col(width, 3 * width, 0)],
            out_specs=[
                full((width, 3 * width)),
                full((8, width)),
                full((limit * BLOCK, width)),
            ],
            scratch_shapes=[pltpu.VMEM((width, 3 * width), F32)],
        ),
        out_shape=[
            shape((width, 3 * width), LOW),
            shape((8, width), F32),
            shape((limit * BLOCK, width), LOW),
        ],
        compiler_params=PARAMS,
        cost_estimate=CHEAP,
        name="dec_back",
    )(order, dec_in, dq, dk, dv, gmid, vecs, weight)


def positions(count, width):
    places = jnp.arange(count, dtype=jnp.float32)[:, None]
    columns = jnp.arange(width)
    rates = jnp.exp((2 * (columns // 2)).astype(jnp.float32) * (-math.log(10000.0) / width))
    angles = places * rates[None, :]
    return jnp.where((columns % 2 == 0)[None, :], jnp.sin(angles), jnp.cos(angles))


def bits_of(axis):
    size, out = lax.axis_size(axis), []
    while size > 1:
        size //= 2
        out.append((axis, size))
    return out


def all_bits():
    return bits_of("dp") + bits_of("fsdp")


def bit_here(bit):
    axis, stride = bit
    return lax.axis_index(axis) // stride % 2


def swap(value, bit):
    axis, stride = bit
    return lax.ppermute(value, axis, [(i, i ^ stride) for i in range(lax.axis_size(axis))])


def pair(own, got, here, dim):
    dims = tuple(2 if d == dim else 1 for d in range(own.ndim + 1))
    mine = lax.broadcasted_iota(jnp.int32, dims, dim) == here
    return jnp.where(mine, jnp.expand_dims(own, dim), jnp.expand_dims(got, dim))


class Gather:
    def __init__(self, piece, order, held=()):
        self.piece, self.order, self.held = piece, list(order), list(held)

    def step(self):
        canon, bit = all_bits(), self.order.pop(0)
        got = swap(self.piece, bit)
        dim = sum(canon.index(b) < canon.index(bit) for b in self.held)
        self.piece = pair(self.piece, got, bit_here(bit), dim)
        self.held.append(bit)

    def rest(self):
        while self.order:
            self.step()
        return self.piece

    def tie(self, other):
        self.piece, other = lax.optimization_barrier((self.piece, other))
        return other


def gather(piece, order, held=()):
    return Gather(piece, order, held).rest()


def join(pieces, bit):
    both = [pair(own, swap(own, bit), bit_here(bit), own.ndim - 2) for own in pieces]
    both = both[0] if len(both) == 1 else jnp.concatenate(both, axis=-1)
    return both.reshape(-1, both.shape[-1])


def term_sum(terms, kind):
    total = terms[0].astype(F32)
    for term in terms[1:]:
        total = total + term.astype(F32)
    return total.astype(kind)


class Fold:
    def __init__(self, terms, order, held=None):
        self.terms, self.order = list(terms), list(order)
        self.left = list(all_bits() if held is None else held)

    def cut(self):
        bit = self.order[0]
        dim = self.left.index(bit)
        here = bit_here(bit)

        def half(index):
            return [lax.dynamic_index_in_dim(t, index, dim, keepdims=False) for t in self.terms]

        self.send, self.terms = term_sum(half(1 - here), LOW), half(here)

    def pass_on(self):
        bit = self.order.pop(0)
        self.left.remove(bit)
        self.terms.append(swap(self.send, bit))


def start_beside(folds, inputs):
    for fold in folds:
        fold.cut()
    sends, inputs = lax.optimization_barrier(([f.send for f in folds], inputs))
    for fold, send in zip(folds, sends):
        fold.send = send
        fold.pass_on()
    return inputs


def end_beside(folds, outputs):
    last, outputs = lax.optimization_barrier(([f.terms[-1] for f in folds], outputs))
    for fold, got in zip(folds, last):
        fold.terms[-1] = got
    return outputs


def one_round(folds):
    start_beside(folds, ())
    end_beside(folds, ())


def by_bits(grads):
    bits = len(all_bits())
    rows = grads.shape[0] >> bits
    return grads.reshape((2,) * bits + (rows, grads.shape[1]))


def pack_vectors(pieces, rows):
    wide = jnp.concatenate([p.reshape(-1, rows) for p in pieces], axis=0)
    wide = jnp.pad(wide, ((0, LANES - wide.shape[0]), (0, 0)))
    return wide.T


def pack_tall(weight, rows):
    parts = weight.shape[0] // rows
    return [weight[i * rows : (i + 1) * rows] for i in range(parts)]


def unpack_tall(columns, devices, width):
    rows = columns.shape[0] // devices
    parts = columns.shape[1] // width
    return (
        columns.reshape(devices, rows, parts, width)
        .transpose(0, 2, 1, 3)
        .reshape(devices * parts * rows, width)
    )


def repack_tall(weight, devices, rows):
    parts = weight.shape[0] // (devices * rows)
    width = weight.shape[1]
    return (
        weight.reshape(devices, parts, rows, width)
        .transpose(0, 2, 1, 3)
        .reshape(devices * rows, parts * width)
    )


def split_columns(array, widths):
    out, at = [], 0
    for w in widths:
        out.append(array[:, at : at + w])
        at += w
    return out


def long_vector(rows_of, devices):
    parts, total = rows_of.shape
    return rows_of.reshape(parts, devices, total // devices).transpose(1, 0, 2).reshape(1, -1)


def long_rows(vector, devices, rows):
    parts = vector.shape[0] // (devices * rows)
    return vector.reshape(devices, parts, rows).transpose(1, 0, 2).reshape(parts, -1)


def per_device(
    enc_input,
    enc_segments,
    dec_segments,
    block_order,
    dec_cotangent,
    enc_qkv,
    enc_proj,
    enc_fc1,
    enc_fc2,
    enc_gains,
    enc_biases,
    enc_fc1_bias,
    embed,
    mask_token,
    dec_qkv,
    dec_proj,
    dec_fc1,
    dec_fc2,
    dec_gains,
    dec_biases,
    dec_fc1_bias,
    dec_fc2_bias,
):
    devices = lax.axis_size("dp") * lax.axis_size("fsdp")
    enc_rows, width = enc_input.shape
    dec_rows, dwidth = dec_cotangent.shape
    erows = enc_qkv.shape[0]
    drows = dec_qkv.shape[0]
    ff = enc_fc1.shape[1]
    dff = dec_fc1.shape[1]
    enc_first = jnp.concatenate(
        [enc_qkv, enc_proj, embed, pack_vectors([enc_gains, enc_biases, enc_fc1_bias], erows)],
        axis=1,
    )
    dec_first = jnp.concatenate(
        [
            dec_qkv,
            dec_proj,
            pack_vectors(
                [dec_gains, dec_biases, dec_fc2_bias[None], mask_token[None], dec_fc1_bias], drows
            ),
        ],
        axis=1,
    )
    ecut = (4 * width + dwidth) // 2 // LANES * LANES
    dp, fsdp = bits_of("dp"), bits_of("fsdp")
    line, core = fsdp[:-1], fsdp[-1]
    enc_rest = jnp.concatenate([enc_fc1] + pack_tall(enc_fc2, erows), axis=1)
    dec_rest = jnp.concatenate([dec_fc1] + pack_tall(dec_fc2, drows), axis=1)
    enc_rest = lax.all_gather(enc_rest, AXES, axis=0, tiled=True)
    lined = gather(enc_first, line)
    one = gather(lined[..., :ecut], dp[::-1], line)
    two = gather(lined[..., ecut:], dp, line)
    enc_all = join([one, two], core)
    dec_rest = lax.all_gather(dec_rest, AXES, axis=0, tiled=True)
    down_w = None if erows % 8 == 0 else unpack_tall(enc_rest[:, ff:], devices, width)
    ddown_w = None if drows % 16 == 0 else unpack_tall(dec_rest[:, dff:], devices, dwidth)
    proj_at, emb_at = 3 * width, 4 * width
    vec_at = emb_at + dwidth
    dproj_at = 3 * dwidth
    dvec_at = 4 * dwidth
    evecs = enc_all[:, vec_at:].T[:16].astype(F32)
    up_bias = long_vector(evecs[10:14], devices)
    dec_gather = Gather(dec_first, line + dp)
    enc_all = dec_gather.tie(enc_all)
    dec_gather.step()
    qkv = enc_qkv_call(enc_input, evecs, enc_all)
    enc_col = enc_segments.reshape(-1, 1)
    enc_row = enc_segments.reshape(-1, 1, TILE)
    qkv = dec_gather.tie(qkv)
    dec_gather.step()
    attended, lse = attend(qkv, enc_segments, enc_col, HDIM)
    attended = dec_gather.tie(attended)
    dec_all = join([dec_gather.rest()], core)
    dvecs = dec_all[:, dvec_at:].T[:16].astype(F32)
    dup_bias = long_vector(dvecs[10:14], devices)
    mid, enc_out, final, act, slope, embedded, natural_w = enc_mid(
        enc_input,
        attended,
        evecs,
        up_bias,
        dvecs[2:3],
        enc_all,
        enc_rest,
        down_w,
        proj_at,
        emb_at,
    )
    gathered = gather(embedded, fsdp).reshape(-1, dwidth)
    limit = gathered.shape[0] // BLOCK
    dec_in, dqkv = dec_in_call(block_order, gathered, positions(dec_rows, dwidth), dvecs, dec_all)
    dec_col = dec_segments.reshape(-1, 1)
    dec_row = dec_segments.reshape(-1, 1, TILE)
    dattended, dlse = attend(dqkv, dec_segments, dec_col, DHDIM)
    dec_out, dgmid, dgatt, dw_rest, db1, dsum_mid = dec_mid(
        dec_in,
        dattended,
        dec_cotangent,
        dvecs,
        dup_bias,
        dec_all,
        dec_rest,
        ddown_w,
        dproj_at,
    )
    if ddown_w is not None:
        chunks = dff // dwidth
        tall = dw_rest[:, dff : 2 * dff].reshape(dwidth, chunks, dwidth).transpose(1, 0, 2)
        tall = repack_tall(tall.reshape(dff, dwidth), devices, drows)
        dw_rest = jnp.concatenate([dw_rest[:, :dff], tall, dw_rest[:, 2 * dff :]], axis=1)
        dw_rest = dw_rest.reshape(lax.axis_size("dp"), -1, drows, dw_rest.shape[1])
        dw_rest = dw_rest.transpose(1, 0, 2, 3).reshape(dwidth, -1)
    dec_own = lax.psum_scatter(dw_rest, "fsdp", scatter_dimension=0, tiled=True)
    ddq, ddk, ddv = attend_back(
        dqkv, dattended, dgatt, dlse, dec_segments, dec_row, dec_col, DHDIM
    )
    dwqkv, dsum, send = dec_back(
        block_order, dec_in, ddq, ddk, ddv, dgmid, dvecs, dec_all, limit
    )
    dwqkv, dsum, send, dec_own = lax.optimization_barrier((dwqkv, dsum, send, dec_own))
    dec_own = lax.psum_scatter(dec_own, "dp", scatter_dimension=0, tiled=True)
    dec_vec_grads = jnp.concatenate(
        [
            dsum[0:1],
            dsum_mid[0:1],
            dsum[1:4],
            dsum_mid[2:3],
            dsum_mid[1:2],
            dsum_mid[3:4],
            dsum[4:5],
            long_rows(db1.reshape(-1), devices, drows),
            jnp.zeros((LANES - 13, dwidth), F32),
        ],
        axis=0,
    ).T
    dec_grads = jnp.concatenate([dwqkv, dec_vec_grads.astype(LOW)], axis=1)
    emb_fold = Fold([send.reshape((2,) * len(fsdp) + (enc_rows, dwidth))], fsdp[::-1], fsdp)
    dfirst = Fold([by_bits(dec_grads)], [core] + dp + line[::-1])
    emb_fold.cut()
    emb_fold.pass_on()
    for _ in line:
        one_round([emb_fold, dfirst])
    elow = start_beside([dfirst], term_sum(emb_fold.terms, LOW))
    demb, ew2, ew1, ewo, eb1, esum_emb, esum_mid, gmid, gatt = enc_mid_back(
        elow,
        final,
        enc_out,
        mid,
        attended,
        act,
        slope,
        evecs,
        enc_all,
        enc_rest,
        natural_w,
        proj_at,
        emb_at,
    )
    gatt, dec_own = end_beside([dfirst], (gatt, dec_own))
    eup = Fold([by_bits(ew1)], [core] + dp[:1] + line[::-1] + dp[1:])
    edown = Fold([by_bits(ew2)], [core] + dp[::-1][:1] + line[::-1][:1] + dp[::-1][1:] + line[::-1][1:])
    gatt = start_beside([dfirst, eup, edown], gatt)
    dq, dk, dv = attend_back(qkv, attended, gatt, lse, enc_segments, enc_row, enc_col, HDIM)
    dq, dk, dv = end_beside([dfirst, eup, edown], (dq, dk, dv))
    dq, dk, dv = start_beside([dfirst, eup, edown], (dq, dk, dv))
    ewqkv, enc_in_grad, esum = enc_qkv_back(enc_input, dq, dk, dv, gmid, evecs, enc_all)
    emb_bias = jnp.pad(esum_emb[0].reshape(devices, drows), ((0, 0), (0, erows - drows)))
    enc_vec_grads = jnp.concatenate(
        [
            esum[0:1],
            esum_mid[3:4],
            esum_mid[0:1],
            esum[1:4],
            esum_mid[5:6],
            esum_mid[4:5],
            esum_mid[2:3],
            esum_mid[1:2],
            long_rows(eb1.reshape(-1), devices, erows),
            emb_bias.reshape(1, -1),
            jnp.zeros((LANES - 15, width), F32),
        ],
        axis=0,
    ).T
    enc_grads = jnp.concatenate([ewqkv, ewo, demb, enc_vec_grads.astype(LOW)], axis=1)
    chip = Fold([by_bits(enc_grads)], [core])
    chip.cut()
    chip.pass_on()
    end_beside([chip, dfirst, eup, edown], ())
    one = Fold([t[..., :ecut] for t in chip.terms], dp + line[::-1], all_bits()[:-1])
    two = Fold([t[..., ecut:] for t in chip.terms], dp[::-1] + line[::-1], all_bits()[:-1])
    one_round([one, two, eup])
    while one.order:
        one_round([f for f in (one, two, eup, edown, dfirst) if f.order])
    while any(f.order for f in (eup, edown, dfirst)):
        one_round([f for f in (eup, edown, dfirst) if f.order])
    rfirst, eu, ed = (term_sum(f.terms, F32) for f in (dfirst, eup, edown))
    efirst = jnp.concatenate([term_sum(one.terms, F32), term_sum(two.terms, F32)], axis=-1)
    rq, rv = split_columns(rfirst, [3 * dwidth, LANES])
    ru, rd, rp = split_columns(dec_own.astype(F32), [dff, dff, dwidth])
    rd = unpack_tall(rd, 1, dwidth)
    eq, ep, em, ev = split_columns(efirst, [3 * width, width, dwidth, LANES])
    rv = rv.T
    ev = ev.T
    return (
        dec_out,
        enc_in_grad,
        eq,
        ep,
        eu,
        ed,
        ev[:3],
        ev[3:10],
        ev[10:14].reshape(-1),
        em,
        rv[8],
        rq,
        rp,
        ru,
        rd,
        rv[:2],
        jnp.concatenate([ev[14:15, :drows], rv[2:7]], axis=0),
        rv[9:13].reshape(-1),
        rv[7],
    )


def solution(mesh):
    in_specs = (
        P(("dp", "fsdp"), None),
        P(("dp", "fsdp"), None),
        P(("dp", "fsdp"), None),
        P("dp", "fsdp"),
        P(("dp", "fsdp"), None),
        P(("dp", "fsdp"), None),
        P(("dp", "fsdp"), None),
        P(("dp", "fsdp"), None),
        P(("dp", "fsdp"), None),
        P(None, ("dp", "fsdp")),
        P(None, ("dp", "fsdp")),
        P(("dp", "fsdp")),
        P(("dp", "fsdp"), None),
        P(("dp", "fsdp")),
        P(("dp", "fsdp"), None),
        P(("dp", "fsdp"), None),
        P(("dp", "fsdp"), None),
        P(("dp", "fsdp"), None),
        P(None, ("dp", "fsdp")),
        P(None, ("dp", "fsdp")),
        P(("dp", "fsdp")),
        P(("dp", "fsdp")),
    )
    out_specs = (
        P(("dp", "fsdp"), None),
        P(("dp", "fsdp"), None),
        P(("dp", "fsdp"), None),
        P(("dp", "fsdp"), None),
        P(("dp", "fsdp"), None),
        P(("dp", "fsdp"), None),
        P(None, ("dp", "fsdp")),
        P(None, ("dp", "fsdp")),
        P(("dp", "fsdp")),
        P(("dp", "fsdp"), None),
        P(("dp", "fsdp")),
        P(("dp", "fsdp"), None),
        P(("dp", "fsdp"), None),
        P(("dp", "fsdp"), None),
        P(("dp", "fsdp"), None),
        P(None, ("dp", "fsdp")),
        P(None, ("dp", "fsdp")),
        P(("dp", "fsdp")),
        P(("dp", "fsdp")),
    )
    return jax.shard_map(
        per_device, mesh=mesh, in_specs=in_specs, out_specs=out_specs, check_vma=False
    )
```

```python
import functools
import math

import jax
import jax.numpy as jnp
from jax import lax
from jax.experimental import pallas as pl
from jax.experimental.pallas import tpu as pltpu
from jax.sharding import PartitionSpec as P

HDIM = 64
DHDIM = 32
BLOCK = 128
LANES = 128
TILE = 256
EPSILON = 1e-06
NEGATIVE = -1e30
LOG2E = math.log2(math.e)
AXES = ("dp", "fsdp")
F32 = jnp.float32
LOW = jnp.bfloat16
PARAMS = pltpu.CompilerParams(vmem_limit_bytes=56 * 1024 * 1024)


def mm(left, right):
    return jnp.dot(left, right, preferred_element_type=F32)


def mm_tn(left, right):
    return lax.dot_general(left, right, (((0,), (0,)), ((), ())), preferred_element_type=F32)


def mm_nt(left, right):
    return lax.dot_general(left, right, (((1,), (1,)), ((), ())), preferred_element_type=F32)


def col_sum(values):
    return jnp.sum(values, axis=0, keepdims=True)


def norm_parts(values):
    centred = values - jnp.mean(values, axis=-1, keepdims=True)
    variance = jnp.mean(centred * centred, axis=-1, keepdims=True)
    scale = lax.rsqrt(variance + EPSILON)
    return centred * scale, scale


def norm_back(grad, unit, scale, gain):
    inner = grad * gain
    mean_inner = jnp.mean(inner, axis=-1, keepdims=True)
    mean_cross = jnp.mean(inner * unit, axis=-1, keepdims=True)
    return scale * (inner - mean_inner - unit * mean_cross)


def gelu_parts(hidden):
    cdf = 0.5 + 0.5 * lax.erf(hidden * (0.5**0.5))
    density = jnp.exp(hidden * hidden * -0.5) * (1.0 / math.sqrt(2.0 * math.pi))
    return hidden * cdf, cdf + hidden * density


CHEAP = pl.CostEstimate(flops=1 << 20, bytes_accessed=1 << 16, transcendentals=0)


def full(shape):
    return pl.BlockSpec(shape, lambda *_: (0,) * len(shape))


def at_col(rows, cols, index):
    return pl.BlockSpec((rows, cols), lambda *_: (0, index))


def shape(dims, kind):
    return jax.ShapeDtypeStruct(dims, kind)


def lane_mask(head, head_dim, kind):
    lane = lax.broadcasted_iota(jnp.int32, (1, LANES), 1)
    inside = (lane >= head * head_dim) & (lane < (head + 1) * head_dim)
    return inside.astype(F32).astype(kind)


def tile_range(seg_ref, here, tiles):
    first = seg_ref[0, here * TILE]
    last = seg_ref[0, here * TILE + TILE - 1]
    low = jnp.int32(0)
    high = jnp.int32(tiles)
    for other in range(tiles):
        low += (seg_ref[0, other * TILE + TILE - 1] < first).astype(jnp.int32)
        high -= (seg_ref[0, other * TILE] > last).astype(jnp.int32)
    return low, high


def attend_kernel(
    head_dim,
    tiles,
    seg_ref,
    q_ref,
    k_ref,
    v_ref,
    row_ref,
    col_ref,
    out_ref,
    inv_ref,
    exp_ref,
    vt,
    held,
    acc,
    top,
    tot,
):
    heads = LANES // head_dim
    here = pl.program_id(1)
    factor = head_dim ** (-0.5) * LOG2E

    @pl.when(here == 0)
    def _():
        for u in range(tiles):
            vt[u] = v_ref[u * TILE : (u + 1) * TILE, :].astype(F32).T.astype(LOW)

    acc[...] = jnp.zeros_like(acc)
    top[...] = jnp.full_like(top, NEGATIVE)
    tot[...] = jnp.zeros_like(tot)
    query = q_ref[...]
    row = row_ref[...]

    def score(u, carry):
        start = pl.multiple_of(u * TILE, TILE)
        keys = k_ref[pl.ds(start, TILE), :]
        same = col_ref[pl.ds(start, TILE), :] == row
        for h in range(heads):
            scores = mm_nt(keys * lane_mask(h, head_dim, LOW), query)
            scores = jnp.where(same, scores, NEGATIVE)
            held[u, h] = scores
            top[h : h + 1, :] = jnp.maximum(
                top[h : h + 1, :], jnp.max(scores, axis=0, keepdims=True)
            )
        return carry

    def mix(u, carry):
        for h in range(heads):
            weights = jnp.exp2((held[u, h] - top[h : h + 1, :]) * factor)
            tot[h : h + 1, :] += col_sum(weights)
            span = slice(h * head_dim, (h + 1) * head_dim)
            weights = weights.astype(LOW)
            exp_ref[0, 0, u, h] = weights
            acc[span, :] += mm(vt[u, span, :], weights)
        return carry

    low, high = tile_range(seg_ref, here, tiles)
    lax.fori_loop(low, high, score, 0)
    lax.fori_loop(low, high, mix, 0)
    for h in range(heads):
        span = slice(h * head_dim, (h + 1) * head_dim)
        inverse = jnp.broadcast_to(1.0 / tot[h : h + 1, :], (head_dim, TILE))
        acc[span, :] = acc[span, :] * inverse
        held[0, 0, span, :] = inverse
    out_ref[...] = acc[...].T.astype(LOW)
    inv_ref[...] = held[0, 0, :LANES, :].T


def attend(qkv, segments, seg_col, head_dim):
    rows, width = qkv.shape[0], qkv.shape[1] // 3
    groups, tiles, heads = width // LANES, rows // TILE, LANES // head_dim
    return pl.pallas_call(
        functools.partial(attend_kernel, head_dim, tiles),
        grid_spec=pltpu.PrefetchScalarGridSpec(
            num_scalar_prefetch=1,
            grid=(groups, tiles),
            in_specs=[
                pl.BlockSpec((TILE, LANES), lambda g, t, s: (t, g)),
                pl.BlockSpec((rows, LANES), lambda g, t, s: (0, groups + g)),
                pl.BlockSpec((rows, LANES), lambda g, t, s: (0, 2 * groups + g)),
                pl.BlockSpec((1, TILE), lambda g, t, s: (0, t)),
                pl.BlockSpec((rows, 1), lambda g, t, s: (0, 0)),
            ],
            out_specs=[
                pl.BlockSpec((TILE, LANES), lambda g, t, s: (t, g)),
                pl.BlockSpec((TILE, LANES), lambda g, t, s: (t, g)),
                pl.BlockSpec((1, 1, tiles, heads, TILE, TILE), lambda g, t, s: (g, t, 0, 0, 0, 0)),
            ],
            scratch_shapes=[
                pltpu.VMEM((tiles, LANES, TILE), LOW),
                pltpu.VMEM((tiles, heads, TILE, TILE), F32),
                pltpu.VMEM((LANES, TILE), F32),
                pltpu.VMEM((8, TILE), F32),
                pltpu.VMEM((8, TILE), F32),
            ],
        ),
        out_shape=[
            shape((rows, width), LOW),
            shape((rows, width), F32),
            shape((groups, tiles, tiles, heads, TILE, TILE), LOW),
        ],
        compiler_params=PARAMS,
        cost_estimate=CHEAP,
        name="attend",
    )(segments, qkv, qkv, qkv, segments, seg_col)


def attend_back_kernel(
    head_dim,
    tiles,
    seg_ref,
    q_ref,
    k_ref,
    v_ref,
    o_ref,
    g_ref,
    exp_ref,
    dq_ref,
    dk_ref,
    dv_ref,
    dqt,
    delta,
    dk_acc,
    dv_acc,
):
    heads = LANES // head_dim
    here = pl.program_id(1)
    scale = head_dim ** (-0.5)

    @pl.when(here == 0)
    def _():
        dqt[...] = jnp.zeros_like(dqt)
        for t in range(tiles):
            rows = slice(t * TILE, (t + 1) * TILE)
            both = (g_ref[rows, :].astype(F32) * o_ref[rows, :].astype(F32)).T
            for h in range(heads):
                delta[t, h : h + 1, :] = col_sum(both[h * head_dim : (h + 1) * head_dim, :])

    keys, vals = k_ref[...], v_ref[...]
    keys_t = keys.astype(F32).T.astype(LOW)
    dk_acc[...] = jnp.zeros_like(dk_acc)
    dv_acc[...] = jnp.zeros_like(dv_acc)

    def step(t, carry):
        start = pl.multiple_of(t * TILE, TILE)
        query = q_ref[pl.ds(start, TILE), :]
        grads = g_ref[pl.ds(start, TILE), :]
        for h in range(heads):
            mask = lane_mask(h, head_dim, LOW)
            span = slice(h * head_dim, (h + 1) * head_dim)
            weights = exp_ref[0, t, 0, h]
            grad_probs = mm_nt(vals * mask, grads) - delta[t, h : h + 1, :]
            grad_scores = (weights.astype(F32) * grad_probs).astype(LOW)
            dv_acc[...] += mm(weights, grads * mask)
            dk_acc[...] += mm(grad_scores, query * mask)
            dqt[t, span, :] += mm(keys_t[span, :], grad_scores)
        return carry

    low, high = tile_range(seg_ref, here, tiles)
    lax.fori_loop(low, high, step, 0)
    dk_ref[...] = (dk_acc[...] * scale).astype(LOW)
    dv_ref[...] = dv_acc[...].astype(LOW)

    @pl.when(here == tiles - 1)
    def _():
        for t in range(tiles):
            dq_ref[t * TILE : (t + 1) * TILE, :] = (dqt[t] * scale).T.astype(LOW)


def attend_back(qkv, attended, grad, weights, segments, head_dim):
    rows, width = attended.shape
    groups, tiles, heads = width // LANES, rows // TILE, LANES // head_dim
    whole = pl.BlockSpec((rows, LANES), lambda g, u, s: (0, g))
    piece = pl.BlockSpec((TILE, LANES), lambda g, u, s: (u, g))
    return pl.pallas_call(
        functools.partial(attend_back_kernel, head_dim, tiles),
        grid_spec=pltpu.PrefetchScalarGridSpec(
            num_scalar_prefetch=1,
            grid=(groups, tiles),
            in_specs=[
                whole,
                pl.BlockSpec((TILE, LANES), lambda g, u, s: (u, groups + g)),
                pl.BlockSpec((TILE, LANES), lambda g, u, s: (u, 2 * groups + g)),
                whole,
                whole,
                pl.BlockSpec((1, tiles, 1, heads, TILE, TILE), lambda g, u, s: (g, 0, u, 0, 0, 0)),
            ],
            out_specs=[whole, piece, piece],
            scratch_shapes=[
                pltpu.VMEM((tiles, LANES, TILE), F32),
                pltpu.VMEM((tiles, 8, TILE), F32),
                pltpu.VMEM((TILE, LANES), F32),
                pltpu.VMEM((TILE, LANES), F32),
            ],
        ),
        out_shape=[shape((rows, width), LOW)] * 3,
        compiler_params=PARAMS,
        cost_estimate=CHEAP,
        name="attend_back",
    )(segments, qkv, qkv, qkv, attended, grad, weights)


def pack_groups(weights):
    return jnp.concatenate(
        [w[at : at + 8] for w in weights for at in range(0, w.shape[0], 8)], axis=1
    )


def natural_rows(pieces):
    cols = pieces[0].shape[1]
    stacked = jnp.stack([p.astype(F32).reshape(-1, 8, cols) for p in pieces], axis=1)
    return stacked.reshape(-1, cols).astype(LOW)


def column_pieces(block, count):
    width = block.shape[1] // count
    return [block[:, i * width : (i + 1) * width] for i in range(count)]


def enc_qkv_kernel(x_ref, vec_ref, w_ref, out_ref, normed):
    part = pl.program_id(0)

    @pl.when(part == 0)
    def _():
        unit, _ = norm_parts(x_ref[...].astype(F32))
        normed[...] = (unit * vec_ref[0:1, :] + vec_ref[3:4, :]).astype(LOW)

    bias = jnp.where(part == 0, vec_ref[4:5, :], jnp.where(part == 2, vec_ref[5:6, :], 0.0))
    out_ref[...] = (mm(normed[...], w_ref[...]) + bias).astype(LOW)


def enc_qkv_call(rows_in, vecs, weight):
    rows, width = rows_in.shape
    return pl.pallas_call(
        enc_qkv_kernel,
        grid=(3,),
        in_specs=[
            full((rows, width)),
            full(vecs.shape),
            pl.BlockSpec((width, width), lambda i: (0, i)),
        ],
        out_specs=pl.BlockSpec((rows, width), lambda i: (0, i)),
        out_shape=shape((rows, 3 * width), LOW),
        scratch_shapes=[pltpu.VMEM((rows, width), LOW)],
        compiler_params=PARAMS,
        cost_estimate=CHEAP,
        name="enc_qkv",
    )(rows_in, vecs, weight)


def enc_mid_kernel(
    chunks,
    packed,
    x_ref,
    att_ref,
    vec_ref,
    b1_ref,
    eb_ref,
    wo_ref,
    we_ref,
    *refs,
):
    ups, (down_ref, *refs) = refs[: packed or 1], refs[packed or 1 :]
    mid_ref, out_ref, final_ref, act_ref, slope_ref, emb_ref, *refs = refs
    naturals, (normed, acc) = refs[:-2], refs[-2:]
    part = pl.program_id(0)

    @pl.when(part == 0)
    def _():
        middle = x_ref[...].astype(F32) + mm(att_ref[...], wo_ref[...]) + vec_ref[6:7, :]
        mid_ref[...] = middle
        unit, _ = norm_parts(middle)
        normed[...] = (unit * vec_ref[1:2, :] + vec_ref[7:8, :]).astype(LOW)
        acc[...] = middle + vec_ref[8:9, :]

    if packed:
        up, down = naturals
        up[...] = natural_rows([ref[...] for ref in ups])
        down[...] = natural_rows(column_pieces(down_ref[...], 4 * packed))
    else:
        up, down = ups[0], down_ref
    hidden = mm(normed[...], up[...]) + b1_ref[...]
    value, slope = gelu_parts(hidden)
    value = value.astype(LOW)
    act_ref[...] = value
    slope_ref[...] = slope
    acc[...] += mm(value, down[...])

    @pl.when(part == chunks - 1)
    def _():
        result = acc[...]
        out_ref[...] = result
        unit, _ = norm_parts(result)
        final = (unit * vec_ref[2:3, :] + vec_ref[9:10, :]).astype(LOW)
        final_ref[...] = final
        emb_ref[...] = (mm(final, we_ref[...]) + eb_ref[...]).astype(LOW)


def enc_mid(rows_in, attended, vecs, up_bias, emb_bias, wide, weights, proj_at, emb_at):
    rows, width = rows_in.shape
    hidden = up_bias.shape[1]
    emb_width = emb_bias.shape[1]
    chunks = hidden // width
    by_col = pl.BlockSpec((width, width), lambda i: (0, i))
    by_row = pl.BlockSpec((width, width), lambda i: (i, 0))
    if len(weights) == 1:
        lead = weights[0].shape[0]
        packed = width // lead
        specs = [
            pl.BlockSpec((lead, width), lambda i, a=a: (0, chunks * a + i)) for a in range(packed)
        ] + [pl.BlockSpec((lead // chunks, chunks * packed * width), lambda i: (i, 1))]
        operands = [weights[0]] * (packed + 1)
        natural_specs = [by_col, by_row]
        natural_shapes = [shape((width, hidden), LOW), shape((hidden, width), LOW)]
    else:
        packed = 0
        specs, operands, natural_specs, natural_shapes = [by_col, by_row], list(weights), [], []
    outs = pl.pallas_call(
        functools.partial(enc_mid_kernel, chunks, packed),
        grid=(chunks,),
        in_specs=[
            full((rows, width)),
            full((rows, width)),
            full(vecs.shape),
            pl.BlockSpec((1, width), lambda i: (0, i)),
            full((1, emb_width)),
            at_col(width, width, proj_at // width),
            at_col(width, emb_width, emb_at // emb_width),
        ]
        + specs,
        out_specs=[
            full((rows, width)),
            full((rows, width)),
            full((rows, width)),
            pl.BlockSpec((rows, width), lambda i: (0, i)),
            pl.BlockSpec((rows, width), lambda i: (0, i)),
            full((rows, emb_width)),
        ]
        + natural_specs,
        out_shape=[
            shape((rows, width), F32),
            shape((rows, width), F32),
            shape((rows, width), LOW),
            shape((rows, hidden), LOW),
            shape((rows, hidden), F32),
            shape((rows, emb_width), LOW),
        ]
        + natural_shapes,
        scratch_shapes=[pltpu.VMEM((rows, width), LOW), pltpu.VMEM((rows, width), F32)],
        compiler_params=PARAMS,
        cost_estimate=CHEAP,
        name="enc_mid",
    )(rows_in, attended, vecs, up_bias, emb_bias, wide, wide, *operands)
    return outs if packed else list(outs) + list(weights)


def enc_mid_back_kernel(
    chunks,
    elow_ref,
    final_ref,
    out_ref,
    mid_ref,
    att_ref,
    act_ref,
    slope_ref,
    vec_ref,
    wo_ref,
    w1_ref,
    w2_ref,
    we_ref,
    inv_ref,
    dpe_ref,
    dw2_ref,
    dw1_ref,
    db1_ref,
    esum_ref,
    sum_ref,
    gmid_ref,
    gatt_ref,
    grad,
    grad_low,
    unit_two,
    scale_two,
    normed,
    dnorm,
):
    part = pl.program_id(0)

    @pl.when(part == 0)
    def _():
        elow = elow_ref[...]
        width = final_ref.shape[1]
        dpe_ref[:, width:] = mm_tn(final_ref[...], elow).astype(LOW)
        esum_ref[...] = jnp.zeros_like(esum_ref)
        esum_ref[0:1, :] = col_sum(elow.astype(F32))
        unit, scale = norm_parts(out_ref[...])
        dfinal = mm_nt(elow, we_ref[...])
        sum_ref[...] = jnp.zeros_like(sum_ref)
        sum_ref[0:1, :] = col_sum(dfinal * unit)
        sum_ref[1:2, :] = col_sum(dfinal)
        total = norm_back(dfinal, unit, scale, vec_ref[2:3, :])
        grad[...] = total
        low = total.astype(LOW)
        grad_low[...] = low
        sum_ref[2:3, :] = col_sum(low.astype(F32))
        unit, scale = norm_parts(mid_ref[...])
        unit_two[...] = unit
        scale_two[...] = jnp.broadcast_to(scale, scale_two.shape)
        normed[...] = (unit * vec_ref[1:2, :] + vec_ref[7:8, :]).astype(LOW)
        dnorm[...] = jnp.zeros_like(dnorm)

    low = grad_low[...]
    dw2_ref[...] = mm_tn(act_ref[...], low).astype(LOW)
    dhid = (slope_ref[...] * mm_nt(low, w2_ref[...])).astype(LOW)
    dw1_ref[...] = mm_tn(normed[...], dhid).astype(LOW)
    db1_ref[...] = col_sum(dhid.astype(F32))
    dnorm[...] += mm_nt(dhid, w1_ref[...])

    @pl.when(part == chunks - 1)
    def _():
        dn = dnorm[...]
        unit = unit_two[...]
        sum_ref[3:4, :] = col_sum(dn * unit)
        sum_ref[4:5, :] = col_sum(dn)
        gmid = grad[...] + norm_back(dn, unit, scale_two[:, 0:1], vec_ref[1:2, :])
        gmid_ref[...] = gmid
        mlow = gmid.astype(LOW)
        sum_ref[5:6, :] = col_sum(mlow.astype(F32))
        dpe_ref[:, : mlow.shape[1]] = mm_tn(att_ref[...], mlow).astype(LOW)
        gatt_ref[...] = (mm_nt(mlow, wo_ref[...]) * inv_ref[...]).astype(LOW)


def enc_mid_back(
    elow, final, out, mid, attended, act, slope, inverse, vecs, wide, up_w, down_w, proj_at, emb_at
):
    rows, width = mid.shape
    hidden = down_w.shape[0]
    emb_width = elow.shape[1]
    chunks = hidden // width
    by_col = pl.BlockSpec((rows, width), lambda i: (0, i))
    return pl.pallas_call(
        functools.partial(enc_mid_back_kernel, chunks),
        grid=(chunks,),
        in_specs=[
            full((rows, emb_width)),
            full((rows, width)),
            full((rows, width)),
            full((rows, width)),
            full((rows, width)),
            by_col,
            by_col,
            full(vecs.shape),
            at_col(width, width, proj_at // width),
            pl.BlockSpec((width, width), lambda i: (0, i)),
            pl.BlockSpec((width, width), lambda i: (i, 0)),
            at_col(width, emb_width, emb_at // emb_width),
            full((rows, width)),
        ],
        out_specs=[
            full((width, width + emb_width)),
            pl.BlockSpec((width, width), lambda i: (i, 0)),
            pl.BlockSpec((width, width), lambda i: (0, i)),
            pl.BlockSpec((1, width), lambda i: (0, i)),
            full((8, emb_width)),
            full((8, width)),
            full((rows, width)),
            full((rows, width)),
        ],
        out_shape=[
            shape((width, width + emb_width), LOW),
            shape((hidden, width), LOW),
            shape((width, hidden), LOW),
            shape((1, hidden), F32),
            shape((8, emb_width), F32),
            shape((8, width), F32),
            shape((rows, width), F32),
            shape((rows, width), LOW),
        ],
        scratch_shapes=[
            pltpu.VMEM((rows, width), F32),
            pltpu.VMEM((rows, width), LOW),
            pltpu.VMEM((rows, width), F32),
            pltpu.VMEM((rows, LANES), F32),
            pltpu.VMEM((rows, width), LOW),
            pltpu.VMEM((rows, width), F32),
        ],
        compiler_params=PARAMS,
        cost_estimate=CHEAP,
        name="enc_mid_back",
    )(elow, final, out, mid, attended, act, slope, vecs, wide, up_w, down_w, wide, inverse)


def enc_qkv_back_kernel(
    x_ref, dq_ref, dk_ref, dv_ref, gmid_ref, vec_ref, more_ref, w_ref, dw_ref, din_ref, sums
):
    width = x_ref.shape[1]
    unit, scale = norm_parts(x_ref[...].astype(F32))
    normed = (unit * vec_ref[0:1, :] + vec_ref[3:4, :]).astype(LOW)
    dn = None
    for i, ref in enumerate((dq_ref, dk_ref, dv_ref)):
        cols = slice(i * width, (i + 1) * width)
        grad = ref[...]
        dw_ref[:, cols] = mm_tn(normed, grad).astype(LOW)
        piece = mm_nt(grad, w_ref[:, cols])
        dn = piece if dn is None else dn + piece
    sums[...] = jnp.zeros_like(sums)
    sums[0:16, :] = more_ref[...]
    sums[0:1, :] = col_sum(dn * unit)
    sums[3:4, :] = col_sum(dn)
    sums[4:5, :] = col_sum(dq_ref[...].astype(F32))
    sums[5:6, :] = col_sum(dv_ref[...].astype(F32))
    dw_ref[:, 3 * width :] = sums[...].T.astype(LOW)
    din = gmid_ref[...] + norm_back(dn, unit, scale, vec_ref[0:1, :])
    din_ref[...] = din.astype(LOW)


def enc_qkv_back(rows_in, dq, dk, dv, gmid, vecs, more, weight):
    rows, width = rows_in.shape
    whole = full((rows, width))
    packed = (width, 3 * width + LANES)
    return pl.pallas_call(
        enc_qkv_back_kernel,
        grid=(1,),
        in_specs=[whole] * 5 + [full(vecs.shape), full((16, width)), at_col(width, 3 * width, 0)],
        out_specs=[full(packed), whole],
        out_shape=[shape(packed, LOW), shape((rows, width), LOW)],
        scratch_shapes=[pltpu.VMEM((LANES, width), F32)],
        compiler_params=PARAMS,
        cost_estimate=CHEAP,
        name="enc_qkv_back",
    )(rows_in, dq, dk, dv, gmid, vecs, more, weight)


def dec_in_kernel(limit, order_ref, one_ref, two_ref, pos_ref, vec_ref, w_ref, in_ref, qkv_ref):
    step = pl.program_id(0)
    width = in_ref.shape[1]
    for half, ref in enumerate((one_ref, two_ref)):
        visible = order_ref[0, 2 * step + half] < limit
        rows = slice(half * BLOCK, (half + 1) * BLOCK)
        in_ref[rows, :] = (
            jnp.where(visible, ref[...].astype(F32), vec_ref[9:10, :]) + pos_ref[rows, :]
        )
    unit, _ = norm_parts(in_ref[...])
    normed = (unit * vec_ref[0:1, :] + vec_ref[3:4, :]).astype(LOW)
    qkv = mm(normed, w_ref[...])
    qkv_ref[:, :width] = (qkv[:, :width] + vec_ref[4:5, :]).astype(LOW)
    qkv_ref[:, width : 2 * width] = qkv[:, width : 2 * width].astype(LOW)
    qkv_ref[:, 2 * width :] = (qkv[:, 2 * width :] + vec_ref[5:6, :]).astype(LOW)


def dec_in_call(order, gathered, pos, vecs, weight):
    rows, width = pos.shape
    limit = gathered.shape[0] // BLOCK

    def chosen(half):
        def index(i, order_ref):
            return (jnp.clip(order_ref[0, 2 * i + half], 0, limit - 1), 0)

        return pl.BlockSpec((BLOCK, width), index)

    return pl.pallas_call(
        functools.partial(dec_in_kernel, limit),
        grid_spec=pltpu.PrefetchScalarGridSpec(
            num_scalar_prefetch=1,
            grid=(rows // TILE,),
            in_specs=[
                chosen(0),
                chosen(1),
                pl.BlockSpec((TILE, width), lambda i, o: (i, 0)),
                full(vecs.shape),
                at_col(width, 3 * width, 0),
            ],
            out_specs=[
                pl.BlockSpec((TILE, width), lambda i, o: (i, 0)),
                pl.BlockSpec((TILE, 3 * width), lambda i, o: (i, 0)),
            ],
        ),
        out_shape=[shape((rows, width), F32), shape((rows, 3 * width), LOW)],
        compiler_params=PARAMS,
        cost_estimate=CHEAP,
        name="dec_in",
    )(order, gathered, gathered, pos, vecs, weight)


def dec_mid_kernel(
    steps,
    chunks,
    packed,
    outer,
    x_ref,
    att_ref,
    cot_ref,
    inv_ref,
    vec_ref,
    b1_ref,
    wo_ref,
    *refs,
):
    ups, refs = refs[: packed or 1], refs[packed or 1 :]
    downs, refs = refs[: packed or 1], refs[packed or 1 :]
    out_ref, gmid_ref, gatt_ref, dw_ref, db1_ref, sum_ref, *refs = refs
    aw1, aw2, acc, dnorm, *naturals = refs
    step = pl.program_id(0)
    width = x_ref.shape[1]
    hidden = chunks * width
    up_w, down_w = naturals if packed else (ups[0], downs[0])

    @pl.when(step == 0)
    def _():
        aw1[...] = jnp.zeros_like(aw1)
        aw2[...] = jnp.zeros_like(aw2)
        db1_ref[...] = jnp.zeros_like(db1_ref)
        sum_ref[...] = jnp.zeros_like(sum_ref)
        if packed:

            def unpack(i, carry):
                rows = pl.ds(pl.multiple_of(i * 16, 16), 16)
                to = pl.ds(pl.multiple_of(i * 16 * packed, 16 * packed), 16 * packed)
                up_w[to, :] = natural_rows([ref[rows, :] for ref in ups])
                to = pl.ds(pl.multiple_of(i * 64 * packed, 64 * packed), 64 * packed)
                parts = [p for ref in downs for p in column_pieces(ref[rows, :], chunks)]
                down_w[to, :] = natural_rows(parts)
                return carry

            lax.fori_loop(0, ups[0].shape[0] // 16, unpack, 0)

    att = att_ref[...]
    low = cot_ref[...]
    middle = x_ref[...] + mm(att, wo_ref[...]) + vec_ref[6:7, :]
    unit, scale = norm_parts(middle)
    normed = (unit * vec_ref[1:2, :] + vec_ref[7:8, :]).astype(LOW)
    acc[...] = middle + vec_ref[8:9, :]
    dnorm[...] = jnp.zeros_like(dnorm)

    def chunk(j, carry):
        cols = pl.ds(pl.multiple_of(j * width, width), width)
        up = up_w[:, cols]
        down = down_w[cols, :]
        value, slope = gelu_parts(mm(normed, up) + b1_ref[j])
        value = value.astype(LOW)
        acc[...] += mm(value, down)
        aw2[cols, :] += mm_tn(value, low)
        dhid = (slope * mm_nt(low, down)).astype(LOW)
        aw1[:, cols] += mm_tn(normed, dhid)
        db1_ref[j] += col_sum(dhid.astype(F32))
        dnorm[...] += mm_nt(dhid, up)
        return carry

    lax.fori_loop(0, chunks, chunk, 0)
    out_ref[...] = acc[...].astype(LOW)
    dn = dnorm[...]
    sum_ref[0:1, :] += col_sum(dn * unit)
    sum_ref[1:2, :] += col_sum(dn)
    gmid = low.astype(F32) + norm_back(dn, unit, scale, vec_ref[1:2, :])
    gmid_ref[...] = gmid
    mlow = gmid.astype(LOW)
    sum_ref[2:3, :] += col_sum(mlow.astype(F32))
    sum_ref[3:4, :] += col_sum(low.astype(F32))
    aw1[:, hidden:] += mm_tn(att, mlow)
    gatt_ref[...] = (mm_nt(mlow, wo_ref[...]) * inv_ref[...]).astype(LOW)

    @pl.when(step == steps - 1)
    def _():
        if packed:
            group = 8 * packed
            inner = width // group // outer

            def pack(device, carry):
                to = device % inner * outer + device // inner
                to = pl.ds(pl.multiple_of(to * group, group), group)
                rows = pl.ds(pl.multiple_of(device * group, group), group)
                dw_ref[to, : hidden + width] = aw1[rows, :].astype(LOW)
                for part in range(4):
                    rows = pl.ds(pl.multiple_of((4 * device + part) * group, group), group)
                    col = hidden + (1 + part) * width
                    dw_ref[to, col : col + width] = aw2[rows, :].astype(LOW)
                return carry

            lax.fori_loop(0, width // group, pack, 0)
        else:
            dw_ref[:, : hidden + width] = aw1[...].astype(LOW)
            for c in range(chunks):
                col = hidden + (1 + c) * width
                dw_ref[:, col : col + width] = aw2[c * width : (c + 1) * width, :].astype(LOW)


def dec_mid(dec_in, attended, cotangent, inverse, vecs, up_bias, wide, weights, proj_at):
    rows, width = dec_in.shape
    hidden = up_bias.shape[1]
    chunks = hidden // width
    tile = 2 * TILE
    steps = rows // tile
    by_row = pl.BlockSpec((tile, width), lambda i: (i, 0))
    naturals = []
    if len(weights) == 1:
        lead = weights[0].shape[0]
        packed = width // lead
        end = weights[0].shape[1] // hidden
        specs = [at_col(lead, hidden, end - 2 * packed + a) for a in range(2 * packed)]
        operands = [weights[0]] * (2 * packed)
        naturals = [pltpu.VMEM((width, hidden), LOW), pltpu.VMEM((hidden, width), LOW)]
    else:
        packed = 0
        specs, operands = [full((width, hidden)), full((hidden, width))], list(weights)
    return pl.pallas_call(
        functools.partial(dec_mid_kernel, steps, chunks, packed, lax.axis_size("dp")),
        grid=(steps,),
        in_specs=[
            by_row,
            by_row,
            by_row,
            by_row,
            full(vecs.shape),
            full((chunks, 1, width)),
            at_col(width, width, proj_at // width),
        ]
        + specs,
        out_specs=[
            by_row,
            by_row,
            by_row,
            full((width, 2 * hidden + width)),
            full((chunks, 1, width)),
            full((8, width)),
        ],
        out_shape=[
            shape((rows, width), LOW),
            shape((rows, width), F32),
            shape((rows, width), LOW),
            shape((width, 2 * hidden + width), LOW),
            shape((chunks, 1, width), F32),
            shape((8, width), F32),
        ],
        scratch_shapes=[
            pltpu.VMEM((width, hidden + width), F32),
            pltpu.VMEM((hidden, width), F32),
            pltpu.VMEM((tile, width), F32),
            pltpu.VMEM((tile, width), F32),
        ]
        + naturals,
        compiler_params=PARAMS,
        cost_estimate=CHEAP,
        name="dec_mid",
    )(
        dec_in,
        attended,
        cotangent,
        inverse,
        vecs,
        up_bias.reshape(chunks, 1, width),
        wide,
        *operands,
    )


def dec_back_kernel(
    limit,
    steps,
    order_ref,
    x_ref,
    dq_ref,
    dk_ref,
    dv_ref,
    gmid_ref,
    vec_ref,
    more_ref,
    w_ref,
    dw_ref,
    send_ref,
    acc,
    sums,
):
    step = pl.program_id(0)
    width = x_ref.shape[1]

    @pl.when(step == 0)
    def _():
        acc[...] = jnp.zeros_like(acc)
        sums[...] = jnp.zeros_like(sums)
        sums[0:16, :] = more_ref[...]
        send_ref[...] = jnp.zeros_like(send_ref)

    unit, scale = norm_parts(x_ref[...])
    normed = (unit * vec_ref[0:1, :] + vec_ref[3:4, :]).astype(LOW)
    grads = (dq_ref[...], dk_ref[...], dv_ref[...])
    dn = None
    for i, grad in enumerate(grads):
        cols = slice(i * width, (i + 1) * width)
        acc[:, cols] += mm_tn(normed, grad)
        piece = mm_nt(grad, w_ref[:, cols])
        dn = piece if dn is None else dn + piece
    sums[0:1, :] += col_sum(dn * unit)
    sums[2:3, :] += col_sum(dn)
    sums[3:4, :] += col_sum(grads[0].astype(F32))
    sums[4:5, :] += col_sum(grads[2].astype(F32))
    din = gmid_ref[...] + norm_back(dn, unit, scale, vec_ref[0:1, :])
    per = x_ref.shape[0] // BLOCK
    for b in range(per):
        place = order_ref[0, per * step + b]
        rows = din[b * BLOCK : (b + 1) * BLOCK, :]

        @pl.when(place < limit)
        def _():
            send_ref[pl.ds(pl.multiple_of(place * BLOCK, BLOCK), BLOCK), :] = rows.astype(LOW)

        @pl.when(place >= limit)
        def _():
            sums[8:9, :] += col_sum(rows)

    @pl.when(step == steps - 1)
    def _():
        dw_ref[:, : 3 * width] = acc[...].astype(LOW)
        dw_ref[:, 3 * width :] = sums[...].T.astype(LOW)


def dec_back(order, dec_in, dq, dk, dv, gmid, vecs, more, weight, limit):
    rows, width = dec_in.shape
    tile = 2 * TILE
    steps = rows // tile
    by_row = pl.BlockSpec((tile, width), lambda i, o: (i, 0))
    packed = (width, 3 * width + LANES)
    return pl.pallas_call(
        functools.partial(dec_back_kernel, limit, steps),
        grid_spec=pltpu.PrefetchScalarGridSpec(
            num_scalar_prefetch=1,
            grid=(steps,),
            in_specs=[by_row] * 5
            + [full(vecs.shape), full((16, width)), at_col(width, 3 * width, 0)],
            out_specs=[full(packed), full((limit * BLOCK, width))],
            scratch_shapes=[
                pltpu.VMEM((width, 3 * width), F32),
                pltpu.VMEM((LANES, width), F32),
            ],
        ),
        out_shape=[shape(packed, LOW), shape((limit * BLOCK, width), LOW)],
        compiler_params=PARAMS,
        cost_estimate=CHEAP,
        name="dec_back",
    )(order, dec_in, dq, dk, dv, gmid, vecs, more, weight)


def positions(count, width):
    places = jnp.arange(count, dtype=jnp.float32)[:, None]
    columns = jnp.arange(width)
    rates = jnp.exp((2 * (columns // 2)).astype(jnp.float32) * (-math.log(10000.0) / width))
    angles = places * rates[None, :]
    return jnp.where((columns % 2 == 0)[None, :], jnp.sin(angles), jnp.cos(angles))


def bits_of(axis):
    size, out = lax.axis_size(axis), []
    while size > 1:
        size //= 2
        out.append((axis, size))
    return out


def all_bits():
    return bits_of("dp") + bits_of("fsdp")


def bit_here(bit):
    axis, stride = bit
    return lax.axis_index(axis) // stride % 2


def swap(value, bit):
    axis, stride = bit
    return lax.ppermute(value, axis, [(i, i ^ stride) for i in range(lax.axis_size(axis))])


def pair(own, got, here, dim):
    dims = tuple(2 if d == dim else 1 for d in range(own.ndim + 1))
    mine = lax.broadcasted_iota(jnp.int32, dims, dim) == here
    return jnp.where(mine, jnp.expand_dims(own, dim), jnp.expand_dims(got, dim))


class Gather:
    def __init__(self, piece, order, held=()):
        self.piece, self.order, self.held = piece, list(order), list(held)

    def step(self):
        canon, bit = all_bits(), self.order.pop(0)
        got = swap(self.piece, bit)
        dim = sum(canon.index(b) < canon.index(bit) for b in self.held)
        self.piece = pair(self.piece, got, bit_here(bit), dim)
        self.held.append(bit)

    def rest(self):
        while self.order:
            self.step()
        return self.piece

    def tie(self, other):
        self.piece, other = lax.optimization_barrier((self.piece, other))
        return other


def gather(piece, order, held=()):
    return Gather(piece, order, held).rest()


def join(pieces, bit):
    both = [pair(own, swap(own, bit), bit_here(bit), own.ndim - 2) for own in pieces]
    both = both[0] if len(both) == 1 else jnp.concatenate(both, axis=-1)
    return both.reshape(-1, both.shape[-1])


def term_sum(terms, kind):
    total = terms[0].astype(F32)
    for term in terms[1:]:
        total = total + term.astype(F32)
    return total.astype(kind)


class Fold:
    def __init__(self, terms, order, held=None):
        self.terms, self.order = list(terms), list(order)
        self.left = list(all_bits() if held is None else held)

    def cut(self):
        bit = self.order[0]
        dim = self.left.index(bit)
        here = bit_here(bit)

        def half(index):
            return [lax.dynamic_index_in_dim(t, index, dim, keepdims=False) for t in self.terms]

        self.send, self.terms = term_sum(half(1 - here), LOW), half(here)

    def pass_on(self):
        bit = self.order.pop(0)
        self.left.remove(bit)
        self.terms.append(swap(self.send, bit))


def start_beside(folds, inputs):
    for fold in folds:
        fold.cut()
    sends, inputs = lax.optimization_barrier(([f.send for f in folds], inputs))
    for fold, send in zip(folds, sends):
        fold.send = send
        fold.pass_on()
    return inputs


def end_beside(folds, outputs):
    last, outputs = lax.optimization_barrier(([f.terms[-1] for f in folds], outputs))
    for fold, got in zip(folds, last):
        fold.terms[-1] = got
    return outputs


def one_round(folds):
    start_beside(folds, ())
    end_beside(folds, ())


def by_bits(grads):
    bits = len(all_bits())
    rows = grads.shape[0] >> bits
    return grads.reshape((2,) * bits + (rows, grads.shape[1]))


def pack_vectors(pieces, rows):
    wide = jnp.concatenate([p.reshape(-1, rows) for p in pieces], axis=0)
    wide = jnp.pad(wide, ((0, LANES - wide.shape[0]), (0, 0)))
    return wide.T


def pack_tall(weight, rows):
    parts = weight.shape[0] // rows
    return [weight[i * rows : (i + 1) * rows] for i in range(parts)]


def unpack_tall(columns, devices, width):
    rows = columns.shape[0] // devices
    parts = columns.shape[1] // width
    return (
        columns.reshape(devices, rows, parts, width)
        .transpose(0, 2, 1, 3)
        .reshape(devices * parts * rows, width)
    )


def repack_tall(weight, devices, rows):
    parts = weight.shape[0] // (devices * rows)
    width = weight.shape[1]
    return (
        weight.reshape(devices, parts, rows, width)
        .transpose(0, 2, 1, 3)
        .reshape(devices * rows, parts * width)
    )


def split_columns(array, widths):
    out, at = [], 0
    for w in widths:
        out.append(array[:, at : at + w])
        at += w
    return out


def long_vector(rows_of, devices):
    parts, total = rows_of.shape
    return rows_of.reshape(parts, devices, total // devices).transpose(1, 0, 2).reshape(1, -1)


def long_rows(vector, devices, rows):
    parts = vector.shape[0] // (devices * rows)
    return vector.reshape(devices, parts, rows).transpose(1, 0, 2).reshape(parts, -1)


def per_device(
    enc_input,
    enc_segments,
    dec_segments,
    block_order,
    dec_cotangent,
    enc_qkv,
    enc_proj,
    enc_fc1,
    enc_fc2,
    enc_gains,
    enc_biases,
    enc_fc1_bias,
    embed,
    mask_token,
    dec_qkv,
    dec_proj,
    dec_fc1,
    dec_fc2,
    dec_gains,
    dec_biases,
    dec_fc1_bias,
    dec_fc2_bias,
):
    devices = lax.axis_size("dp") * lax.axis_size("fsdp")
    enc_rows, width = enc_input.shape
    dec_rows, dwidth = dec_cotangent.shape
    erows = enc_qkv.shape[0]
    drows = dec_qkv.shape[0]
    ff = enc_fc1.shape[1]
    dff = dec_fc1.shape[1]
    emb_row = jnp.pad(dec_biases[0], (0, erows - drows))
    enc_first = jnp.concatenate(
        [
            enc_qkv,
            enc_proj,
            embed,
            pack_vectors([enc_gains, enc_biases, enc_fc1_bias, emb_row], erows),
        ],
        axis=1,
    )
    dec_first = jnp.concatenate(
        [
            dec_qkv,
            dec_proj,
            pack_vectors(
                [dec_gains, dec_biases, dec_fc2_bias[None], mask_token[None], dec_fc1_bias], drows
            ),
        ],
        axis=1,
    )
    proj_at, emb_at = 3 * width, 4 * width
    vec_at = emb_at + dwidth
    dproj_at, dvec_at = 3 * dwidth, 4 * dwidth
    ecut = vec_at // 2 // LANES * LANES
    dp, fsdp = bits_of("dp"), bits_of("fsdp")
    line, core = fsdp[:-1], fsdp[-1]
    packed = erows % 8 == 0 and drows % 8 == 0
    tall = [enc_fc1, enc_fc2, dec_fc1, dec_fc2]
    if packed:
        rest = lax.all_gather(pack_groups(tall), AXES, axis=0, tiled=True)
        enc_rest = dec_rest = (rest,)
    else:
        tall = [lax.all_gather(w, AXES, axis=0, tiled=True) for w in tall]
        enc_rest, dec_rest = tall[:2], tall[2:]
    lined = gather(enc_first, line)
    one = gather(lined[..., :ecut], dp[::-1], line)
    two = gather(lined[..., ecut:], dp, line)
    enc_all = join([one, two], core)
    evecs = enc_all[:, vec_at:].T[:16].astype(F32)
    up_bias = long_vector(evecs[10:14], devices)
    emb_bias = evecs[14].reshape(devices, erows)[:, :drows].reshape(1, -1)

    dec_gather = Gather(dec_first, line + dp)
    enc_all, evecs = dec_gather.tie((enc_all, evecs))
    dec_gather.step()
    pos = positions(dec_rows, dwidth)
    qkv = enc_qkv_call(enc_input, evecs, enc_all)
    enc_col = enc_segments.reshape(-1, 1)
    qkv, pos = dec_gather.tie((qkv, pos))
    dec_gather.step()
    attended, inverse, weights = attend(qkv, enc_segments, enc_col, HDIM)
    attended = dec_gather.tie(attended)
    while len(dec_gather.order) > 1:
        dec_gather.step()
    attended = dec_gather.tie(attended)
    dec_gather.step()
    mid, enc_out, final, act, slope, embedded, up_w, down_w = enc_mid(
        enc_input,
        attended,
        evecs,
        up_bias,
        emb_bias,
        enc_all,
        enc_rest,
        proj_at,
        emb_at,
    )
    emb_gather = Gather(embedded, fsdp)
    emb_gather.step()
    dec_all = join([dec_gather.piece], core)
    dvecs = dec_all[:, dvec_at:].T[:16].astype(F32)
    dup_bias = long_vector(dvecs[10:14], devices)
    gathered = emb_gather.rest().reshape(-1, dwidth)
    limit = gathered.shape[0] // BLOCK
    dec_in, dqkv = dec_in_call(block_order, gathered, pos, dvecs, dec_all)
    dec_col = dec_segments.reshape(-1, 1)
    dattended, dinverse, dweights = attend(dqkv, dec_segments, dec_col, DHDIM)
    dec_out, dgmid, dgatt, dw_rest, db1, dsum_mid = dec_mid(
        dec_in,
        dattended,
        dec_cotangent,
        dinverse,
        dvecs,
        dup_bias,
        dec_all,
        dec_rest,
        dproj_at,
    )
    if not packed:
        chunks = dff // dwidth
        tall = dw_rest[:, dff + dwidth :].reshape(dwidth, chunks, dwidth).transpose(1, 0, 2)
        tall = repack_tall(tall.reshape(dff, dwidth), devices, drows)
        dw_rest = jnp.concatenate([dw_rest[:, : dff + dwidth], tall], axis=1)
        dw_rest = dw_rest.reshape(lax.axis_size("dp"), -1, drows, dw_rest.shape[1])
        dw_rest = dw_rest.transpose(1, 0, 2, 3).reshape(dwidth, -1)
    dec_own = lax.psum_scatter(dw_rest, "fsdp", scatter_dimension=0, tiled=True)
    dec_more = jnp.concatenate(
        [
            jnp.zeros((1, dwidth), F32),
            dsum_mid[0:1],
            jnp.zeros((3, dwidth), F32),
            dsum_mid[2:3],
            dsum_mid[1:2],
            dsum_mid[3:4],
            jnp.zeros((1, dwidth), F32),
            long_rows(db1.reshape(-1), devices, drows),
            jnp.zeros((3, dwidth), F32),
        ],
        axis=0,
    )
    dgatt, dec_more = lax.optimization_barrier((dgatt, dec_more))
    ddq, ddk, ddv = attend_back(dqkv, dattended, dgatt, dweights, dec_segments, DHDIM)
    dec_grads, send = dec_back(
        block_order, dec_in, ddq, ddk, ddv, dgmid, dvecs, dec_more, dec_all, limit
    )
    dec_grads, send, dec_own = lax.optimization_barrier((dec_grads, send, dec_own))
    dec_own = lax.psum_scatter(dec_own, "dp", scatter_dimension=0, tiled=True)
    emb_fold = Fold([send.reshape((2,) * len(fsdp) + (enc_rows, dwidth))], fsdp[::-1], fsdp)
    dfirst = Fold([by_bits(dec_grads)], [core] + dp + line[::-1])
    emb_fold.cut()
    emb_fold.pass_on()
    for _ in line:
        one_round([emb_fold, dfirst])
    elow = start_beside([dfirst], term_sum(emb_fold.terms, LOW))
    dpe, ew2, ew1, eb1, esum_emb, esum_mid, gmid, gatt = enc_mid_back(
        elow,
        final,
        enc_out,
        mid,
        attended,
        act,
        slope,
        inverse,
        evecs,
        enc_all,
        up_w,
        down_w,
        proj_at,
        emb_at,
    )
    gatt, dec_own = end_beside([dfirst], (gatt, dec_own))
    eup = Fold([by_bits(ew1)], [core] + dp[:1] + line[::-1] + dp[1:])
    edown = Fold(
        [by_bits(ew2)],
        [core] + dp[::-1][:1] + line[::-1][:1] + dp[::-1][1:] + line[::-1][1:],
    )
    early = Fold([by_bits(dpe)], [core] + line[::-1] + dp)
    side = [eup, edown, early, dfirst]
    gatt = start_beside(side, gatt)
    emb_sum = jnp.pad(esum_emb[0].reshape(devices, drows), ((0, 0), (0, erows - drows)))
    enc_more = jnp.concatenate(
        [
            jnp.zeros((1, width), F32),
            esum_mid[3:4],
            esum_mid[0:1],
            jnp.zeros((3, width), F32),
            esum_mid[5:6],
            esum_mid[4:5],
            esum_mid[2:3],
            esum_mid[1:2],
            long_rows(eb1.reshape(-1), devices, erows),
            emb_sum.reshape(1, -1),
            jnp.zeros((1, width), F32),
        ],
        axis=0,
    )
    gatt, enc_more = lax.optimization_barrier((gatt, enc_more))
    dq, dk, dv = attend_back(qkv, attended, gatt, weights, enc_segments, HDIM)
    dq, dk, dv = end_beside(side, (dq, dk, dv))
    dq, dk, dv = start_beside(side, (dq, dk, dv))
    enc_grads, enc_in_grad = enc_qkv_back(
        enc_input, dq, dk, dv, gmid, evecs, enc_more, enc_all
    )
    chip = Fold([by_bits(enc_grads)], [core])
    chip.cut()
    chip.pass_on()
    gcut = 10 * LANES * width // 768
    one = Fold([t[..., :gcut] for t in chip.terms], dp + line[::-1], all_bits()[:-1])
    two = Fold([t[..., gcut:] for t in chip.terms], dp[::-1] + line[::-1], all_bits()[:-1])
    end_beside(side, ())
    while one.order:
        more = [f for f in side if f.order]
        start_beside([one, two], ())
        start_beside(more, ())
        end_beside([one, two], ())
        end_beside(more, ())
    while any(f.order for f in side):
        one_round([f for f in side if f.order])
    rfirst, eu, ed, epe = (term_sum(f.terms, F32) for f in (dfirst, eup, edown, early))
    efirst = jnp.concatenate([term_sum(one.terms, F32), term_sum(two.terms, F32)], axis=-1)
    rq, rv = split_columns(rfirst, [3 * dwidth, LANES])
    ru, rp, rd = split_columns(dec_own.astype(F32), [dff, dwidth, dff])
    rd = unpack_tall(rd, 1, dwidth)
    ep, em = split_columns(epe, [width, dwidth])
    eq, ev = split_columns(efirst, [3 * width, LANES])
    rv = rv.T
    ev = ev.T
    return (
        dec_out,
        enc_in_grad,
        eq,
        ep,
        eu,
        ed,
        ev[:3],
        ev[3:10],
        ev[10:14].reshape(-1),
        em,
        rv[8],
        rq,
        rp,
        ru,
        rd,
        rv[:2],
        jnp.concatenate([ev[14:15, :drows], rv[2:7]], axis=0),
        rv[9:13].reshape(-1),
        rv[7],
    )


def solution(mesh):
    in_specs = (
        P(("dp", "fsdp"), None),
        P(("dp", "fsdp"), None),
        P(("dp", "fsdp"), None),
        P("dp", "fsdp"),
        P(("dp", "fsdp"), None),
        P(("dp", "fsdp"), None),
        P(("dp", "fsdp"), None),
        P(("dp", "fsdp"), None),
        P(("dp", "fsdp"), None),
        P(None, ("dp", "fsdp")),
        P(None, ("dp", "fsdp")),
        P(("dp", "fsdp")),
        P(("dp", "fsdp"), None),
        P(("dp", "fsdp")),
        P(("dp", "fsdp"), None),
        P(("dp", "fsdp"), None),
        P(("dp", "fsdp"), None),
        P(("dp", "fsdp"), None),
        P(None, ("dp", "fsdp")),
        P(None, ("dp", "fsdp")),
        P(("dp", "fsdp")),
        P(("dp", "fsdp")),
    )
    out_specs = (
        P(("dp", "fsdp"), None),
        P(("dp", "fsdp"), None),
        P(("dp", "fsdp"), None),
        P(("dp", "fsdp"), None),
        P(("dp", "fsdp"), None),
        P(("dp", "fsdp"), None),
        P(None, ("dp", "fsdp")),
        P(None, ("dp", "fsdp")),
        P(("dp", "fsdp")),
        P(("dp", "fsdp"), None),
        P(("dp", "fsdp")),
        P(("dp", "fsdp"), None),
        P(("dp", "fsdp"), None),
        P(("dp", "fsdp"), None),
        P(("dp", "fsdp"), None),
        P(None, ("dp", "fsdp")),
        P(None, ("dp", "fsdp")),
        P(("dp", "fsdp")),
        P(("dp", "fsdp")),
    )
    return jax.shard_map(
        per_device, mesh=mesh, in_specs=in_specs, out_specs=out_specs, check_vma=False
    )
```

```python
import functools
import math

import jax
import jax.numpy as jnp
from jax import lax
from jax.experimental import pallas as pl
from jax.experimental.pallas import tpu as pltpu
from jax.sharding import PartitionSpec as P

HDIM = 64
DHDIM = 32
BLOCK = 128
LANES = 128
TILE = 256
EPSILON = 1e-06
NEGATIVE = -1e30
LOG2E = math.log2(math.e)
AXES = ("dp", "fsdp")
F32 = jnp.float32
LOW = jnp.bfloat16
PARAMS = pltpu.CompilerParams(vmem_limit_bytes=56 * 1024 * 1024)


def mm(left, right):
    return jnp.dot(left, right, preferred_element_type=F32)


def mm_tn(left, right):
    return lax.dot_general(left, right, (((0,), (0,)), ((), ())), preferred_element_type=F32)


def mm_nt(left, right):
    return lax.dot_general(left, right, (((1,), (1,)), ((), ())), preferred_element_type=F32)


def col_sum(values):
    return jnp.sum(values, axis=0, keepdims=True)


def norm_parts(values):
    centred = values - jnp.mean(values, axis=-1, keepdims=True)
    variance = jnp.mean(centred * centred, axis=-1, keepdims=True)
    scale = lax.rsqrt(variance + EPSILON)
    return centred * scale, scale


def norm_back(grad, unit, scale, gain):
    inner = grad * gain
    mean_inner = jnp.mean(inner, axis=-1, keepdims=True)
    mean_cross = jnp.mean(inner * unit, axis=-1, keepdims=True)
    return scale * (inner - mean_inner - unit * mean_cross)


def gelu_parts(hidden):
    cdf = 0.5 + 0.5 * lax.erf(hidden * (0.5**0.5))
    density = jnp.exp(hidden * hidden * -0.5) * (1.0 / math.sqrt(2.0 * math.pi))
    return hidden * cdf, cdf + hidden * density


CHEAP = pl.CostEstimate(flops=1 << 20, bytes_accessed=1 << 16, transcendentals=0)


def full(shape):
    return pl.BlockSpec(shape, lambda *_: (0,) * len(shape))


def at_col(rows, cols, index):
    return pl.BlockSpec((rows, cols), lambda *_: (0, index))


def shape(dims, kind):
    return jax.ShapeDtypeStruct(dims, kind)


def lane_mask(head, head_dim, kind):
    lane = lax.broadcasted_iota(jnp.int32, (1, LANES), 1)
    inside = (lane >= head * head_dim) & (lane < (head + 1) * head_dim)
    return inside.astype(F32).astype(kind)


def stack_heads(stacked, index, rows, head_dim):
    for h in range(LANES // head_dim):
        stacked[index, h * TILE : (h + 1) * TILE, :] = rows * lane_mask(h, head_dim, LOW)


def tile_range(seg_ref, here, tiles):
    first = seg_ref[0, here * TILE]
    last = seg_ref[0, here * TILE + TILE - 1]
    low = jnp.int32(0)
    high = jnp.int32(tiles)
    for other in range(tiles):
        low += (seg_ref[0, other * TILE + TILE - 1] < first).astype(jnp.int32)
        high -= (seg_ref[0, other * TILE] > last).astype(jnp.int32)
    return low, high


def attend_kernel(
    head_dim,
    tiles,
    seg_ref,
    q_ref,
    k_ref,
    v_ref,
    row_ref,
    col_ref,
    out_ref,
    inv_ref,
    exp_ref,
    km,
    vt,
    held,
    acc,
    top,
    tot,
):
    heads = LANES // head_dim
    here = pl.program_id(1)
    factor = head_dim ** (-0.5) * LOG2E

    @pl.when(here == 0)
    def _():
        for u in range(tiles):
            rows = slice(u * TILE, (u + 1) * TILE)
            vt[u] = v_ref[rows, :].astype(F32).T.astype(LOW)
            stack_heads(km, u, k_ref[rows, :], head_dim)

    acc[...] = jnp.zeros_like(acc)
    top[...] = jnp.full_like(top, NEGATIVE)
    tot[...] = jnp.zeros_like(tot)
    query = q_ref[...]
    row = row_ref[...]

    def score(u, carry):
        start = pl.multiple_of(u * TILE, TILE)
        same = col_ref[pl.ds(start, TILE), :] == row
        every = mm_nt(km[u], query)
        for h in range(heads):
            scores = jnp.where(same, every[h * TILE : (h + 1) * TILE, :], NEGATIVE)
            held[u, h] = scores
            top[h : h + 1, :] = jnp.maximum(
                top[h : h + 1, :], jnp.max(scores, axis=0, keepdims=True)
            )
        return carry

    def mix(u, carry):
        for h in range(heads):
            weights = jnp.exp2((held[u, h] - top[h : h + 1, :]) * factor)
            tot[h : h + 1, :] += col_sum(weights)
            span = slice(h * head_dim, (h + 1) * head_dim)
            weights = weights.astype(LOW)
            exp_ref[0, 0, u, :, h * TILE : (h + 1) * TILE] = weights
            acc[span, :] += mm(vt[u, span, :], weights)
        return carry

    low, high = tile_range(seg_ref, here, tiles)
    lax.fori_loop(low, high, score, 0)
    lax.fori_loop(low, high, mix, 0)
    for h in range(heads):
        span = slice(h * head_dim, (h + 1) * head_dim)
        inverse = jnp.broadcast_to(1.0 / tot[h : h + 1, :], (head_dim, TILE))
        acc[span, :] = acc[span, :] * inverse
        held[0, 0, span, :] = inverse
    out_ref[...] = acc[...].T.astype(LOW)
    inv_ref[...] = held[0, 0, :LANES, :].T


def attend(qkv, segments, seg_col, head_dim):
    rows, width = qkv.shape[0], qkv.shape[1] // 3
    groups, tiles, heads = width // LANES, rows // TILE, LANES // head_dim
    return pl.pallas_call(
        functools.partial(attend_kernel, head_dim, tiles),
        grid_spec=pltpu.PrefetchScalarGridSpec(
            num_scalar_prefetch=1,
            grid=(groups, tiles),
            in_specs=[
                pl.BlockSpec((TILE, LANES), lambda g, t, s: (t, g)),
                pl.BlockSpec((rows, LANES), lambda g, t, s: (0, groups + g)),
                pl.BlockSpec((rows, LANES), lambda g, t, s: (0, 2 * groups + g)),
                pl.BlockSpec((1, TILE), lambda g, t, s: (0, t)),
                pl.BlockSpec((rows, 1), lambda g, t, s: (0, 0)),
            ],
            out_specs=[
                pl.BlockSpec((TILE, LANES), lambda g, t, s: (t, g)),
                pl.BlockSpec((TILE, LANES), lambda g, t, s: (t, g)),
                pl.BlockSpec((1, 1, tiles, TILE, heads * TILE), lambda g, t, s: (g, t, 0, 0, 0)),
            ],
            scratch_shapes=[
                pltpu.VMEM((tiles, heads * TILE, LANES), LOW),
                pltpu.VMEM((tiles, LANES, TILE), LOW),
                pltpu.VMEM((tiles, heads, TILE, TILE), F32),
                pltpu.VMEM((LANES, TILE), F32),
                pltpu.VMEM((8, TILE), F32),
                pltpu.VMEM((8, TILE), F32),
            ],
        ),
        out_shape=[
            shape((rows, width), LOW),
            shape((rows, width), F32),
            shape((groups, tiles, tiles, TILE, heads * TILE), LOW),
        ],
        compiler_params=PARAMS,
        cost_estimate=CHEAP,
        name="attend",
    )(segments, qkv, qkv, qkv, segments, seg_col)


def attend_back_kernel(
    head_dim,
    tiles,
    seg_ref,
    q_ref,
    k_ref,
    v_ref,
    o_ref,
    g_ref,
    exp_ref,
    dq_ref,
    dk_ref,
    dv_ref,
    qm,
    gm,
    vm,
    dqt,
    delta,
    dk_acc,
    dv_acc,
):
    heads = LANES // head_dim
    here = pl.program_id(1)
    scale = head_dim ** (-0.5)

    @pl.when(here == 0)
    def _():
        dqt[...] = jnp.zeros_like(dqt)
        for t in range(tiles):
            rows = slice(t * TILE, (t + 1) * TILE)
            stack_heads(qm, t, q_ref[rows, :], head_dim)
            stack_heads(gm, t, g_ref[rows, :], head_dim)
            both = (g_ref[rows, :].astype(F32) * o_ref[rows, :].astype(F32)).T
            for h in range(heads):
                delta[t, h : h + 1, :] = col_sum(both[h * head_dim : (h + 1) * head_dim, :])

    keys_t = k_ref[...].astype(F32).T.astype(LOW)
    stack_heads(vm, 0, v_ref[...], head_dim)
    dk_acc[...] = jnp.zeros_like(dk_acc)
    dv_acc[...] = jnp.zeros_like(dv_acc)

    def step(t, carry):
        start = pl.multiple_of(t * TILE, TILE)
        every = mm_nt(vm[0], g_ref[pl.ds(start, TILE), :])
        dv_acc[...] += mm(exp_ref[0, t, 0], gm[t])
        pieces = []
        for h in range(heads):
            grad_probs = every[h * TILE : (h + 1) * TILE, :] - delta[t, h : h + 1, :]
            weights = exp_ref[0, t, 0, :, h * TILE : (h + 1) * TILE]
            pieces.append((weights.astype(F32) * grad_probs).astype(LOW))
        for h in range(heads):
            span = slice(h * head_dim, (h + 1) * head_dim)
            dqt[t, span, :] += mm(keys_t[span, :], pieces[h])
        dk_acc[...] += mm(jnp.concatenate(pieces, axis=1), qm[t])
        return carry

    low, high = tile_range(seg_ref, here, tiles)
    lax.fori_loop(low, high, step, 0)
    dk_ref[...] = (dk_acc[...] * scale).astype(LOW)
    dv_ref[...] = dv_acc[...].astype(LOW)

    @pl.when(here == tiles - 1)
    def _():
        for t in range(tiles):
            dq_ref[t * TILE : (t + 1) * TILE, :] = (dqt[t] * scale).T.astype(LOW)


def attend_back(qkv, attended, grad, weights, segments, head_dim):
    rows, width = attended.shape
    groups, tiles, heads = width // LANES, rows // TILE, LANES // head_dim
    whole = pl.BlockSpec((rows, LANES), lambda g, u, s: (0, g))
    piece = pl.BlockSpec((TILE, LANES), lambda g, u, s: (u, g))
    return pl.pallas_call(
        functools.partial(attend_back_kernel, head_dim, tiles),
        grid_spec=pltpu.PrefetchScalarGridSpec(
            num_scalar_prefetch=1,
            grid=(groups, tiles),
            in_specs=[
                whole,
                pl.BlockSpec((TILE, LANES), lambda g, u, s: (u, groups + g)),
                pl.BlockSpec((TILE, LANES), lambda g, u, s: (u, 2 * groups + g)),
                whole,
                whole,
                pl.BlockSpec((1, tiles, 1, TILE, heads * TILE), lambda g, u, s: (g, 0, u, 0, 0)),
            ],
            out_specs=[whole, piece, piece],
            scratch_shapes=[
                pltpu.VMEM((tiles, heads * TILE, LANES), LOW),
                pltpu.VMEM((tiles, heads * TILE, LANES), LOW),
                pltpu.VMEM((1, heads * TILE, LANES), LOW),
                pltpu.VMEM((tiles, LANES, TILE), F32),
                pltpu.VMEM((tiles, 8, TILE), F32),
                pltpu.VMEM((TILE, LANES), F32),
                pltpu.VMEM((TILE, LANES), F32),
            ],
        ),
        out_shape=[shape((rows, width), LOW)] * 3,
        compiler_params=PARAMS,
        cost_estimate=CHEAP,
        name="attend_back",
    )(segments, qkv, qkv, qkv, attended, grad, weights)


def pack_kernel(*refs):
    ins, outs = refs[: len(refs) * 2 // 3], refs[len(refs) * 2 // 3 :]
    for up, down, out in zip(ins[::2], ins[1::2], outs):
        rows, cols = up.shape
        out[:, :cols] = up[...]
        wide = down[...].astype(F32)
        width = down.shape[1]
        for part in range(4):
            piece = wide[part * rows : (part + 1) * rows, :].astype(LOW)
            out[:, cols + part * width : cols + (part + 1) * width] = piece


def pack_shards(*shards):
    outs = [shape((u.shape[0], u.shape[1] + 4 * d.shape[1]), LOW) for u, d in zip(shards[::2], shards[1::2])]
    return pl.pallas_call(
        pack_kernel,
        in_specs=[full(s.shape) for s in shards],
        out_specs=[full(o.shape) for o in outs],
        out_shape=outs,
        grid=(1,),
        compiler_params=PARAMS,
        cost_estimate=CHEAP,
        name="pack",
    )(*shards)


def natural_rows(block, group, kind):
    width = block.shape[1] // 4
    parts = [
        block[:, i * width : (i + 1) * width].astype(kind).reshape(-1, group, width)
        for i in range(4)
    ]
    return jnp.stack(parts, axis=1).reshape(-1, width).astype(LOW)


def enc_qkv_kernel(x_ref, vec_ref, w_ref, out_ref, normed):
    part = pl.program_id(0)

    @pl.when(part == 0)
    def _():
        unit, _ = norm_parts(x_ref[...].astype(F32))
        normed[...] = (unit * vec_ref[0:1, :] + vec_ref[3:4, :]).astype(LOW)

    bias = jnp.where(part == 0, vec_ref[4:5, :], jnp.where(part == 2, vec_ref[5:6, :], 0.0))
    out_ref[...] = (mm(normed[...], w_ref[...]) + bias).astype(LOW)


def enc_qkv_call(rows_in, vecs, weight):
    rows, width = rows_in.shape
    return pl.pallas_call(
        enc_qkv_kernel,
        grid=(3,),
        in_specs=[
            full((rows, width)),
            full(vecs.shape),
            pl.BlockSpec((width, width), lambda i: (0, i)),
        ],
        out_specs=pl.BlockSpec((rows, width), lambda i: (0, i)),
        out_shape=shape((rows, 3 * width), LOW),
        scratch_shapes=[pltpu.VMEM((rows, width), LOW)],
        compiler_params=PARAMS,
        cost_estimate=CHEAP,
        name="enc_qkv",
    )(rows_in, vecs, weight)


def enc_mid_kernel(
    chunks,
    packed,
    x_ref,
    att_ref,
    vec_ref,
    b1_ref,
    eb_ref,
    wo_ref,
    we_ref,
    *refs,
):
    up_ref, down_ref, *refs = refs
    mid_ref, out_ref, final_ref, act_ref, slope_ref, emb_ref, *refs = refs
    naturals, (normed, acc) = refs[:-2], refs[-2:]
    part = pl.program_id(0)

    @pl.when(part == 0)
    def _():
        middle = x_ref[...].astype(F32) + mm(att_ref[...], wo_ref[...]) + vec_ref[6:7, :]
        mid_ref[...] = middle
        unit, _ = norm_parts(middle)
        normed[...] = (unit * vec_ref[1:2, :] + vec_ref[7:8, :]).astype(LOW)
        acc[...] = middle + vec_ref[8:9, :]

    down = down_ref[...]
    if packed:
        down = natural_rows(down, packed, F32)
        naturals[0][...] = down
    hidden = mm(normed[...], up_ref[...]) + b1_ref[...]
    value, slope = gelu_parts(hidden)
    value = value.astype(LOW)
    act_ref[...] = value
    slope_ref[...] = slope
    acc[...] += mm(value, down)

    @pl.when(part == chunks - 1)
    def _():
        result = acc[...]
        out_ref[...] = result
        unit, _ = norm_parts(result)
        final = (unit * vec_ref[2:3, :] + vec_ref[9:10, :]).astype(LOW)
        final_ref[...] = final
        emb_ref[...] = (mm(final, we_ref[...]) + eb_ref[...]).astype(LOW)


def enc_mid(rows_in, attended, vecs, up_bias, emb_bias, wide, weights, proj_at, emb_at):
    rows, width = rows_in.shape
    hidden = up_bias.shape[1]
    emb_width = emb_bias.shape[1]
    chunks = hidden // width
    by_row = pl.BlockSpec((width, width), lambda i: (i, 0))
    specs = [pl.BlockSpec((width, width), lambda i: (0, i))]
    if len(weights) == 1:
        packed = width // (lax.axis_size("dp") * lax.axis_size("fsdp"))
        specs.append(pl.BlockSpec((width // 4, hidden), lambda i: (i, 1)))
        operands = [weights[0]] * 2
        natural_specs, natural_shapes = [by_row], [shape((hidden, width), LOW)]
    else:
        packed = 0
        specs.append(by_row)
        operands, natural_specs, natural_shapes = list(weights), [], []
    outs = pl.pallas_call(
        functools.partial(enc_mid_kernel, chunks, packed),
        grid=(chunks,),
        in_specs=[
            full((rows, width)),
            full((rows, width)),
            full(vecs.shape),
            pl.BlockSpec((1, width), lambda i: (0, i)),
            full((1, emb_width)),
            at_col(width, width, proj_at // width),
            at_col(width, emb_width, emb_at // emb_width),
        ]
        + specs,
        out_specs=[
            full((rows, width)),
            full((rows, width)),
            full((rows, width)),
            pl.BlockSpec((rows, width), lambda i: (0, i)),
            pl.BlockSpec((rows, width), lambda i: (0, i)),
            full((rows, emb_width)),
        ]
        + natural_specs,
        out_shape=[
            shape((rows, width), F32),
            shape((rows, width), F32),
            shape((rows, width), LOW),
            shape((rows, hidden), LOW),
            shape((rows, hidden), F32),
            shape((rows, emb_width), LOW),
        ]
        + natural_shapes,
        scratch_shapes=[pltpu.VMEM((rows, width), LOW), pltpu.VMEM((rows, width), F32)],
        compiler_params=PARAMS,
        cost_estimate=CHEAP,
        name="enc_mid",
    )(rows_in, attended, vecs, up_bias, emb_bias, wide, wide, *operands)
    return outs if packed else list(outs) + [weights[1]]


def enc_mid_back_kernel(
    chunks,
    elow_ref,
    final_ref,
    out_ref,
    mid_ref,
    att_ref,
    act_ref,
    slope_ref,
    vec_ref,
    wo_ref,
    w1_ref,
    w2_ref,
    we_ref,
    inv_ref,
    dpe_ref,
    dw2_ref,
    dw1_ref,
    db1_ref,
    esum_ref,
    sum_ref,
    gmid_ref,
    gatt_ref,
    grad,
    grad_low,
    unit_two,
    scale_two,
    normed,
    dnorm,
):
    part = pl.program_id(0)

    @pl.when(part == 0)
    def _():
        elow = elow_ref[...]
        width = final_ref.shape[1]
        dpe_ref[:, width:] = mm_tn(final_ref[...], elow).astype(LOW)
        esum_ref[...] = jnp.zeros_like(esum_ref)
        esum_ref[0:1, :] = col_sum(elow.astype(F32))
        unit, scale = norm_parts(out_ref[...])
        dfinal = mm_nt(elow, we_ref[...])
        sum_ref[...] = jnp.zeros_like(sum_ref)
        sum_ref[0:1, :] = col_sum(dfinal * unit)
        sum_ref[1:2, :] = col_sum(dfinal)
        total = norm_back(dfinal, unit, scale, vec_ref[2:3, :])
        grad[...] = total
        low = total.astype(LOW)
        grad_low[...] = low
        sum_ref[2:3, :] = col_sum(low.astype(F32))
        unit, scale = norm_parts(mid_ref[...])
        unit_two[...] = unit
        scale_two[...] = jnp.broadcast_to(scale, scale_two.shape)
        normed[...] = (unit * vec_ref[1:2, :] + vec_ref[7:8, :]).astype(LOW)
        dnorm[...] = jnp.zeros_like(dnorm)

    low = grad_low[...]
    dw2_ref[...] = mm_tn(act_ref[...], low).astype(LOW)
    dhid = (slope_ref[...] * mm_nt(low, w2_ref[...])).astype(LOW)
    dw1_ref[...] = mm_tn(normed[...], dhid).astype(LOW)
    db1_ref[...] = col_sum(dhid.astype(F32))
    dnorm[...] += mm_nt(dhid, w1_ref[...])

    @pl.when(part == chunks - 1)
    def _():
        dn = dnorm[...]
        unit = unit_two[...]
        sum_ref[3:4, :] = col_sum(dn * unit)
        sum_ref[4:5, :] = col_sum(dn)
        gmid = grad[...] + norm_back(dn, unit, scale_two[:, 0:1], vec_ref[1:2, :])
        gmid_ref[...] = gmid
        mlow = gmid.astype(LOW)
        sum_ref[5:6, :] = col_sum(mlow.astype(F32))
        dpe_ref[:, : mlow.shape[1]] = mm_tn(att_ref[...], mlow).astype(LOW)
        gatt_ref[...] = (mm_nt(mlow, wo_ref[...]) * inv_ref[...]).astype(LOW)


def enc_mid_back(
    elow, final, out, mid, attended, act, slope, inverse, vecs, wide, up_w, down_w, proj_at, emb_at
):
    rows, width = mid.shape
    hidden = down_w.shape[0]
    emb_width = elow.shape[1]
    chunks = hidden // width
    by_col = pl.BlockSpec((rows, width), lambda i: (0, i))
    return pl.pallas_call(
        functools.partial(enc_mid_back_kernel, chunks),
        grid=(chunks,),
        in_specs=[
            full((rows, emb_width)),
            full((rows, width)),
            full((rows, width)),
            full((rows, width)),
            full((rows, width)),
            by_col,
            by_col,
            full(vecs.shape),
            at_col(width, width, proj_at // width),
            pl.BlockSpec((width, width), lambda i: (0, i)),
            pl.BlockSpec((width, width), lambda i: (i, 0)),
            at_col(width, emb_width, emb_at // emb_width),
            full((rows, width)),
        ],
        out_specs=[
            full((width, width + emb_width)),
            pl.BlockSpec((width, width), lambda i: (i, 0)),
            pl.BlockSpec((width, width), lambda i: (0, i)),
            pl.BlockSpec((1, width), lambda i: (0, i)),
            full((8, emb_width)),
            full((8, width)),
            full((rows, width)),
            full((rows, width)),
        ],
        out_shape=[
            shape((width, width + emb_width), LOW),
            shape((hidden, width), LOW),
            shape((width, hidden), LOW),
            shape((1, hidden), F32),
            shape((8, emb_width), F32),
            shape((8, width), F32),
            shape((rows, width), F32),
            shape((rows, width), LOW),
        ],
        scratch_shapes=[
            pltpu.VMEM((rows, width), F32),
            pltpu.VMEM((rows, width), LOW),
            pltpu.VMEM((rows, width), F32),
            pltpu.VMEM((rows, LANES), F32),
            pltpu.VMEM((rows, width), LOW),
            pltpu.VMEM((rows, width), F32),
        ],
        compiler_params=PARAMS,
        cost_estimate=CHEAP,
        name="enc_mid_back",
    )(elow, final, out, mid, attended, act, slope, vecs, wide, up_w, down_w, wide, inverse)


def enc_qkv_back_kernel(
    x_ref, dq_ref, dk_ref, dv_ref, gmid_ref, vec_ref, more_ref, w_ref, dw_ref, din_ref, sums
):
    width = x_ref.shape[1]
    unit, scale = norm_parts(x_ref[...].astype(F32))
    normed = (unit * vec_ref[0:1, :] + vec_ref[3:4, :]).astype(LOW)
    dn = None
    for i, ref in enumerate((dq_ref, dk_ref, dv_ref)):
        cols = slice(i * width, (i + 1) * width)
        grad = ref[...]
        dw_ref[:, cols] = mm_tn(normed, grad).astype(LOW)
        piece = mm_nt(grad, w_ref[:, cols])
        dn = piece if dn is None else dn + piece
    sums[...] = jnp.zeros_like(sums)
    sums[0:16, :] = more_ref[...]
    sums[0:1, :] = col_sum(dn * unit)
    sums[3:4, :] = col_sum(dn)
    sums[4:5, :] = col_sum(dq_ref[...].astype(F32))
    sums[5:6, :] = col_sum(dv_ref[...].astype(F32))
    dw_ref[:, 3 * width :] = sums[...].T.astype(LOW)
    din = gmid_ref[...] + norm_back(dn, unit, scale, vec_ref[0:1, :])
    din_ref[...] = din.astype(LOW)


def enc_qkv_back(rows_in, dq, dk, dv, gmid, vecs, more, weight):
    rows, width = rows_in.shape
    whole = full((rows, width))
    packed = (width, 3 * width + LANES)
    return pl.pallas_call(
        enc_qkv_back_kernel,
        grid=(1,),
        in_specs=[whole] * 5 + [full(vecs.shape), full((16, width)), at_col(width, 3 * width, 0)],
        out_specs=[full(packed), whole],
        out_shape=[shape(packed, LOW), shape((rows, width), LOW)],
        scratch_shapes=[pltpu.VMEM((LANES, width), F32)],
        compiler_params=PARAMS,
        cost_estimate=CHEAP,
        name="enc_qkv_back",
    )(rows_in, dq, dk, dv, gmid, vecs, more, weight)


def dec_in_kernel(limit, order_ref, one_ref, two_ref, pos_ref, vec_ref, w_ref, in_ref, qkv_ref):
    step = pl.program_id(0)
    width = in_ref.shape[1]
    for half, ref in enumerate((one_ref, two_ref)):
        visible = order_ref[0, 2 * step + half] < limit
        rows = slice(half * BLOCK, (half + 1) * BLOCK)
        in_ref[rows, :] = (
            jnp.where(visible, ref[...].astype(F32), vec_ref[9:10, :]) + pos_ref[rows, :]
        )
    unit, _ = norm_parts(in_ref[...])
    normed = (unit * vec_ref[0:1, :] + vec_ref[3:4, :]).astype(LOW)
    qkv = mm(normed, w_ref[...])
    qkv_ref[:, :width] = (qkv[:, :width] + vec_ref[4:5, :]).astype(LOW)
    qkv_ref[:, width : 2 * width] = qkv[:, width : 2 * width].astype(LOW)
    qkv_ref[:, 2 * width :] = (qkv[:, 2 * width :] + vec_ref[5:6, :]).astype(LOW)


def dec_in_call(order, gathered, pos, vecs, weight):
    rows, width = pos.shape
    limit = gathered.shape[0] // BLOCK

    def chosen(half):
        def index(i, order_ref):
            return (jnp.clip(order_ref[0, 2 * i + half], 0, limit - 1), 0)

        return pl.BlockSpec((BLOCK, width), index)

    return pl.pallas_call(
        functools.partial(dec_in_kernel, limit),
        grid_spec=pltpu.PrefetchScalarGridSpec(
            num_scalar_prefetch=1,
            grid=(rows // TILE,),
            in_specs=[
                chosen(0),
                chosen(1),
                pl.BlockSpec((TILE, width), lambda i, o: (i, 0)),
                full(vecs.shape),
                at_col(width, 3 * width, 0),
            ],
            out_specs=[
                pl.BlockSpec((TILE, width), lambda i, o: (i, 0)),
                pl.BlockSpec((TILE, 3 * width), lambda i, o: (i, 0)),
            ],
        ),
        out_shape=[shape((rows, width), F32), shape((rows, 3 * width), LOW)],
        compiler_params=PARAMS,
        cost_estimate=CHEAP,
        name="dec_in",
    )(order, gathered, gathered, pos, vecs, weight)


def dec_mid_kernel(
    steps,
    chunks,
    packed,
    x_ref,
    att_ref,
    cot_ref,
    inv_ref,
    vec_ref,
    b1_ref,
    wo_ref,
    up_ref,
    down_ref,
    out_ref,
    gmid_ref,
    gatt_ref,
    dw_ref,
    db1_ref,
    sum_ref,
    aw1,
    aw2,
    acc,
    dnorm,
):
    step = pl.program_id(0)
    width = x_ref.shape[1]
    hidden = chunks * width
    lead = width // 4

    @pl.when(step == 0)
    def _():
        aw1[...] = jnp.zeros_like(aw1)
        aw2[...] = jnp.zeros_like(aw2)
        db1_ref[...] = jnp.zeros_like(db1_ref)
        sum_ref[...] = jnp.zeros_like(sum_ref)

    att = att_ref[...]
    low = cot_ref[...]
    middle = x_ref[...] + mm(att, wo_ref[...]) + vec_ref[6:7, :]
    unit, scale = norm_parts(middle)
    normed = (unit * vec_ref[1:2, :] + vec_ref[7:8, :]).astype(LOW)
    acc[...] = middle + vec_ref[8:9, :]
    dnorm[...] = jnp.zeros_like(dnorm)

    def chunk(j, carry):
        cols = pl.ds(pl.multiple_of(j * width, width), width)
        some = pl.ds(pl.multiple_of(j * lead, lead), lead)
        up = up_ref[:, cols]
        down = natural_rows(down_ref[some, :], packed, LOW) if packed else down_ref[cols, :]
        value, slope = gelu_parts(mm(normed, up) + b1_ref[j])
        value = value.astype(LOW)
        acc[...] += mm(value, down)
        grad = mm_tn(value, low)
        if packed:
            grad = grad.reshape(-1, 4, packed, width)
            for part in range(4):
                piece = grad[:, part].reshape(lead, width)
                aw2[some, part * width : (part + 1) * width] += piece
        else:
            aw2[cols, :] += grad
        dhid = (slope * mm_nt(low, down)).astype(LOW)
        aw1[:, cols] += mm_tn(normed, dhid)
        db1_ref[j] += col_sum(dhid.astype(F32))
        dnorm[...] += mm_nt(dhid, up)
        return carry

    lax.fori_loop(0, chunks, chunk, 0)
    out_ref[...] = acc[...].astype(LOW)
    dn = dnorm[...]
    sum_ref[0:1, :] += col_sum(dn * unit)
    sum_ref[1:2, :] += col_sum(dn)
    gmid = low.astype(F32) + norm_back(dn, unit, scale, vec_ref[1:2, :])
    gmid_ref[...] = gmid
    mlow = gmid.astype(LOW)
    sum_ref[2:3, :] += col_sum(mlow.astype(F32))
    sum_ref[3:4, :] += col_sum(low.astype(F32))
    aw1[:, hidden:] += mm_tn(att, mlow)
    gatt_ref[...] = (mm_nt(mlow, wo_ref[...]) * inv_ref[...]).astype(LOW)

    @pl.when(step == steps - 1)
    def _():
        dw_ref[:, : hidden + width] = aw1[...].astype(LOW)
        if packed:
            dw_ref[:, hidden + width :] = aw2[...].astype(LOW)
        else:
            for c in range(chunks):
                col = hidden + (1 + c) * width
                dw_ref[:, col : col + width] = aw2[c * width : (c + 1) * width, :].astype(LOW)


def dec_mid(dec_in, attended, cotangent, inverse, vecs, up_bias, wide, weights, proj_at):
    rows, width = dec_in.shape
    hidden = up_bias.shape[1]
    chunks = hidden // width
    tile = 2 * TILE
    steps = rows // tile
    by_row = pl.BlockSpec((tile, width), lambda i: (i, 0))
    if len(weights) == 1:
        packed = width // (lax.axis_size("dp") * lax.axis_size("fsdp"))
        down_shape = (width, hidden)
        specs, operands = [at_col(width, hidden, 0), at_col(width, hidden, 1)], [weights[0]] * 2
    else:
        packed, down_shape = 0, (hidden, width)
        specs, operands = [full((width, hidden)), full(down_shape)], list(weights)
    return pl.pallas_call(
        functools.partial(dec_mid_kernel, steps, chunks, packed),
        grid=(steps,),
        in_specs=[
            by_row,
            by_row,
            by_row,
            by_row,
            full(vecs.shape),
            full((chunks, 1, width)),
            at_col(width, width, proj_at // width),
        ]
        + specs,
        out_specs=[
            by_row,
            by_row,
            by_row,
            full((width, 2 * hidden + width)),
            full((chunks, 1, width)),
            full((8, width)),
        ],
        out_shape=[
            shape((rows, width), LOW),
            shape((rows, width), F32),
            shape((rows, width), LOW),
            shape((width, 2 * hidden + width), LOW),
            shape((chunks, 1, width), F32),
            shape((8, width), F32),
        ],
        scratch_shapes=[
            pltpu.VMEM((width, hidden + width), F32),
            pltpu.VMEM(down_shape, F32),
            pltpu.VMEM((tile, width), F32),
            pltpu.VMEM((tile, width), F32),
        ],
        compiler_params=PARAMS,
        cost_estimate=CHEAP,
        name="dec_mid",
    )(
        dec_in,
        attended,
        cotangent,
        inverse,
        vecs,
        up_bias.reshape(chunks, 1, width),
        wide,
        *operands,
    )


def dec_back_kernel(
    limit,
    steps,
    order_ref,
    x_ref,
    dq_ref,
    dk_ref,
    dv_ref,
    gmid_ref,
    vec_ref,
    more_ref,
    w_ref,
    dw_ref,
    send_ref,
    acc,
    sums,
):
    step = pl.program_id(0)
    width = x_ref.shape[1]

    @pl.when(step == 0)
    def _():
        acc[...] = jnp.zeros_like(acc)
        sums[...] = jnp.zeros_like(sums)
        sums[0:16, :] = more_ref[...]
        send_ref[...] = jnp.zeros_like(send_ref)

    unit, scale = norm_parts(x_ref[...])
    normed = (unit * vec_ref[0:1, :] + vec_ref[3:4, :]).astype(LOW)
    grads = (dq_ref[...], dk_ref[...], dv_ref[...])
    dn = None
    for i, grad in enumerate(grads):
        cols = slice(i * width, (i + 1) * width)
        acc[:, cols] += mm_tn(normed, grad)
        piece = mm_nt(grad, w_ref[:, cols])
        dn = piece if dn is None else dn + piece
    sums[0:1, :] += col_sum(dn * unit)
    sums[2:3, :] += col_sum(dn)
    sums[3:4, :] += col_sum(grads[0].astype(F32))
    sums[4:5, :] += col_sum(grads[2].astype(F32))
    din = gmid_ref[...] + norm_back(dn, unit, scale, vec_ref[0:1, :])
    per = x_ref.shape[0] // BLOCK
    for b in range(per):
        place = order_ref[0, per * step + b]
        rows = din[b * BLOCK : (b + 1) * BLOCK, :]

        @pl.when(place < limit)
        def _():
            send_ref[pl.ds(pl.multiple_of(place * BLOCK, BLOCK), BLOCK), :] = rows.astype(LOW)

        @pl.when(place >= limit)
        def _():
            sums[8:9, :] += col_sum(rows)

    @pl.when(step == steps - 1)
    def _():
        dw_ref[:, : 3 * width] = acc[...].astype(LOW)
        dw_ref[:, 3 * width :] = sums[...].T.astype(LOW)


def dec_back(order, dec_in, dq, dk, dv, gmid, vecs, more, weight, limit):
    rows, width = dec_in.shape
    tile = 2 * TILE
    steps = rows // tile
    by_row = pl.BlockSpec((tile, width), lambda i, o: (i, 0))
    packed = (width, 3 * width + LANES)
    return pl.pallas_call(
        functools.partial(dec_back_kernel, limit, steps),
        grid_spec=pltpu.PrefetchScalarGridSpec(
            num_scalar_prefetch=1,
            grid=(steps,),
            in_specs=[by_row] * 5
            + [full(vecs.shape), full((16, width)), at_col(width, 3 * width, 0)],
            out_specs=[full(packed), full((limit * BLOCK, width))],
            scratch_shapes=[
                pltpu.VMEM((width, 3 * width), F32),
                pltpu.VMEM((LANES, width), F32),
            ],
        ),
        out_shape=[shape(packed, LOW), shape((limit * BLOCK, width), LOW)],
        compiler_params=PARAMS,
        cost_estimate=CHEAP,
        name="dec_back",
    )(order, dec_in, dq, dk, dv, gmid, vecs, more, weight)


def positions(count, width):
    places = jnp.arange(count, dtype=jnp.float32)[:, None]
    columns = jnp.arange(width)
    rates = jnp.exp((2 * (columns // 2)).astype(jnp.float32) * (-math.log(10000.0) / width))
    angles = places * rates[None, :]
    return jnp.where((columns % 2 == 0)[None, :], jnp.sin(angles), jnp.cos(angles))


def bits_of(axis):
    size, out = lax.axis_size(axis), []
    while size > 1:
        size //= 2
        out.append((axis, size))
    return out


def all_bits():
    return bits_of("dp") + bits_of("fsdp")


def bit_here(bit):
    axis, stride = bit
    return lax.axis_index(axis) // stride % 2


def swap(value, bit):
    axis, stride = bit
    return lax.ppermute(value, axis, [(i, i ^ stride) for i in range(lax.axis_size(axis))])


def pair(own, got, here, dim):
    dims = tuple(2 if d == dim else 1 for d in range(own.ndim + 1))
    mine = lax.broadcasted_iota(jnp.int32, dims, dim) == here
    return jnp.where(mine, jnp.expand_dims(own, dim), jnp.expand_dims(got, dim))


class Gather:
    def __init__(self, piece, order, held=()):
        self.piece, self.order, self.held = piece, list(order), list(held)

    def step(self):
        canon, bit = all_bits(), self.order.pop(0)
        got = swap(self.piece, bit)
        dim = sum(canon.index(b) < canon.index(bit) for b in self.held)
        self.piece = pair(self.piece, got, bit_here(bit), dim)
        self.held.append(bit)

    def rest(self):
        while self.order:
            self.step()
        return self.piece

    def tie(self, other):
        self.piece, other = lax.optimization_barrier((self.piece, other))
        return other


def gather(piece, order, held=()):
    return Gather(piece, order, held).rest()


def join(pieces, bit):
    both = [pair(own, swap(own, bit), bit_here(bit), own.ndim - 2) for own in pieces]
    both = both[0] if len(both) == 1 else jnp.concatenate(both, axis=-1)
    return both.reshape(-1, both.shape[-1])


def term_sum(terms, kind):
    total = terms[0].astype(F32)
    for term in terms[1:]:
        total = total + term.astype(F32)
    return total.astype(kind)


class Fold:
    def __init__(self, terms, order, held=None):
        self.terms, self.order = list(terms), list(order)
        self.left = list(all_bits() if held is None else held)

    def cut(self):
        bit = self.order[0]
        dim = self.left.index(bit)
        here = bit_here(bit)

        def half(index):
            return [lax.dynamic_index_in_dim(t, index, dim, keepdims=False) for t in self.terms]

        self.send, self.terms = term_sum(half(1 - here), LOW), half(here)

    def pass_on(self):
        bit = self.order.pop(0)
        self.left.remove(bit)
        self.terms.append(swap(self.send, bit))


def start_beside(folds, inputs):
    for fold in folds:
        fold.cut()
    sends, inputs = lax.optimization_barrier(([f.send for f in folds], inputs))
    for fold, send in zip(folds, sends):
        fold.send = send
        fold.pass_on()
    return inputs


def end_beside(folds, outputs):
    last, outputs = lax.optimization_barrier(([f.terms[-1] for f in folds], outputs))
    for fold, got in zip(folds, last):
        fold.terms[-1] = got
    return outputs


def one_round(folds):
    for fold in folds:
        fold.cut()
        fold.pass_on()
    end_beside(folds, ())


def by_bits(grads):
    bits = len(all_bits())
    rows = grads.shape[0] >> bits
    return grads.reshape((2,) * bits + (rows, grads.shape[1]))


def pack_vectors(pieces, rows):
    wide = jnp.concatenate([p.reshape(-1, rows) for p in pieces], axis=0)
    wide = jnp.pad(wide, ((0, LANES - wide.shape[0]), (0, 0)))
    return wide.T


def unpack_tall(columns, devices, width):
    rows = columns.shape[0] // devices
    parts = columns.shape[1] // width
    return (
        columns.reshape(devices, rows, parts, width)
        .transpose(0, 2, 1, 3)
        .reshape(devices * parts * rows, width)
    )


def repack_tall(weight, devices, rows):
    parts = weight.shape[0] // (devices * rows)
    width = weight.shape[1]
    return (
        weight.reshape(devices, parts, rows, width)
        .transpose(0, 2, 1, 3)
        .reshape(devices * rows, parts * width)
    )


def split_columns(array, widths):
    out, at = [], 0
    for w in widths:
        out.append(array[:, at : at + w])
        at += w
    return out


def long_vector(rows_of, devices):
    parts, total = rows_of.shape
    return rows_of.reshape(parts, devices, total // devices).transpose(1, 0, 2).reshape(1, -1)


def long_rows(vector, devices, rows):
    parts = vector.shape[0] // (devices * rows)
    return vector.reshape(devices, parts, rows).transpose(1, 0, 2).reshape(parts, -1)


def per_device(
    enc_input,
    enc_segments,
    dec_segments,
    block_order,
    dec_cotangent,
    enc_qkv,
    enc_proj,
    enc_fc1,
    enc_fc2,
    enc_gains,
    enc_biases,
    enc_fc1_bias,
    embed,
    mask_token,
    dec_qkv,
    dec_proj,
    dec_fc1,
    dec_fc2,
    dec_gains,
    dec_biases,
    dec_fc1_bias,
    dec_fc2_bias,
):
    devices = lax.axis_size("dp") * lax.axis_size("fsdp")
    enc_rows, width = enc_input.shape
    dec_rows, dwidth = dec_cotangent.shape
    erows = enc_qkv.shape[0]
    drows = dec_qkv.shape[0]
    ff = enc_fc1.shape[1]
    dff = dec_fc1.shape[1]
    emb_row = jnp.pad(dec_biases[0], (0, erows - drows))
    enc_first = jnp.concatenate(
        [
            enc_qkv,
            enc_proj,
            embed,
            pack_vectors([enc_gains, enc_biases, enc_fc1_bias, emb_row], erows),
        ],
        axis=1,
    )
    dec_first = jnp.concatenate(
        [
            dec_qkv,
            dec_proj,
            pack_vectors(
                [dec_gains, dec_biases, dec_fc2_bias[None], mask_token[None], dec_fc1_bias], drows
            ),
        ],
        axis=1,
    )
    proj_at, emb_at = 3 * width, 4 * width
    vec_at = emb_at + dwidth
    dproj_at, dvec_at = 3 * dwidth, 4 * dwidth
    ecut = vec_at // 2 // LANES * LANES
    dp, fsdp = bits_of("dp"), bits_of("fsdp")
    line, core = fsdp[:-1], fsdp[-1]
    packed = erows % 8 == 0 and drows % 16 == 0
    enc_rest, dec_rest = (enc_fc1, enc_fc2), (dec_fc1, dec_fc2)
    if packed:
        enc_rest, dec_rest = ((w,) for w in pack_shards(*enc_rest, *dec_rest))
    enc_rest = [lax.all_gather(w, AXES, axis=0, tiled=True) for w in enc_rest]
    lined = gather(enc_first, line)
    one = gather(lined[..., :ecut], dp[::-1], line)
    two = gather(lined[..., ecut:], dp, line)
    enc_all = join([one, two], core)
    evecs = enc_all[:, vec_at:].T[:16].astype(F32)
    up_bias = long_vector(evecs[10:14], devices)
    emb_bias = evecs[14].reshape(devices, erows)[:, :drows].reshape(1, -1)

    dec_gather = Gather(dec_first, line + dp)
    enc_all, evecs = dec_gather.tie((enc_all, evecs))
    dec_gather.step()
    pos = positions(dec_rows, dwidth)
    qkv = enc_qkv_call(enc_input, evecs, enc_all)
    enc_col = enc_segments.reshape(-1, 1)
    qkv, pos = dec_gather.tie((qkv, pos))
    dec_gather.step()
    attended, inverse, weights = attend(qkv, enc_segments, enc_col, HDIM)
    attended = dec_gather.tie(attended)
    while len(dec_gather.order) > 1:
        dec_gather.step()
    attended = dec_gather.tie(attended)
    dec_gather.step()
    mid, enc_out, final, act, slope, embedded, down_w = enc_mid(
        enc_input,
        attended,
        evecs,
        up_bias,
        emb_bias,
        enc_all,
        enc_rest,
        proj_at,
        emb_at,
    )
    emb_gather = Gather(embedded, fsdp)
    emb_gather.step()
    dec_rest = emb_gather.tie(dec_rest)
    dec_rest = [lax.all_gather(w, AXES, axis=0, tiled=True) for w in dec_rest]
    dec_all = join([dec_gather.piece], core)
    dvecs = dec_all[:, dvec_at:].T[:16].astype(F32)
    dup_bias = long_vector(dvecs[10:14], devices)
    gathered = emb_gather.rest().reshape(-1, dwidth)
    limit = gathered.shape[0] // BLOCK
    dec_in, dqkv = dec_in_call(block_order, gathered, pos, dvecs, dec_all)
    dec_col = dec_segments.reshape(-1, 1)
    dattended, dinverse, dweights = attend(dqkv, dec_segments, dec_col, DHDIM)
    dec_out, dgmid, dgatt, dw_rest, db1, dsum_mid = dec_mid(
        dec_in,
        dattended,
        dec_cotangent,
        dinverse,
        dvecs,
        dup_bias,
        dec_all,
        dec_rest,
        dproj_at,
    )
    if not packed:
        chunks = dff // dwidth
        tall = dw_rest[:, dff + dwidth :].reshape(dwidth, chunks, dwidth).transpose(1, 0, 2)
        tall = repack_tall(tall.reshape(dff, dwidth), devices, drows)
        dw_rest = jnp.concatenate([dw_rest[:, : dff + dwidth], tall], axis=1)
    dec_own = lax.psum_scatter(dw_rest, "dp", scatter_dimension=0, tiled=True)
    dec_more = jnp.concatenate(
        [
            jnp.zeros((1, dwidth), F32),
            dsum_mid[0:1],
            jnp.zeros((3, dwidth), F32),
            dsum_mid[2:3],
            dsum_mid[1:2],
            dsum_mid[3:4],
            jnp.zeros((1, dwidth), F32),
            long_rows(db1.reshape(-1), devices, drows),
            jnp.zeros((3, dwidth), F32),
        ],
        axis=0,
    )
    dgatt, dec_more = lax.optimization_barrier((dgatt, dec_more))
    ddq, ddk, ddv = attend_back(dqkv, dattended, dgatt, dweights, dec_segments, DHDIM)
    dec_grads, send = dec_back(
        block_order, dec_in, ddq, ddk, ddv, dgmid, dvecs, dec_more, dec_all, limit
    )
    dec_grads, send, dec_own = lax.optimization_barrier((dec_grads, send, dec_own))
    dec_own = lax.psum_scatter(dec_own, "fsdp", scatter_dimension=0, tiled=True)
    emb_fold = Fold([send.reshape((2,) * len(fsdp) + (enc_rows, dwidth))], fsdp[::-1], fsdp)
    dfirst = Fold([by_bits(dec_grads)], [core] + dp + line[::-1])
    emb_fold.cut()
    emb_fold.pass_on()
    for _ in line:
        one_round([emb_fold, dfirst])
    elow = start_beside([dfirst], term_sum(emb_fold.terms, LOW))
    dpe, ew2, ew1, eb1, esum_emb, esum_mid, gmid, gatt = enc_mid_back(
        elow,
        final,
        enc_out,
        mid,
        attended,
        act,
        slope,
        inverse,
        evecs,
        enc_all,
        enc_rest[0],
        down_w,
        proj_at,
        emb_at,
    )
    gatt, dec_own = end_beside([dfirst], (gatt, dec_own))
    eup = Fold([by_bits(ew1)], [core] + dp[:1] + line[::-1] + dp[1:])
    edown = Fold(
        [by_bits(ew2)],
        [core] + dp[::-1][:1] + line[::-1][:1] + dp[::-1][1:] + line[::-1][1:],
    )
    early = Fold([by_bits(dpe)], [core] + line[::-1] + dp)
    side = [eup, edown, early, dfirst]
    gatt = start_beside(side, gatt)
    emb_sum = jnp.pad(esum_emb[0].reshape(devices, drows), ((0, 0), (0, erows - drows)))
    enc_more = jnp.concatenate(
        [
            jnp.zeros((1, width), F32),
            esum_mid[3:4],
            esum_mid[0:1],
            jnp.zeros((3, width), F32),
            esum_mid[5:6],
            esum_mid[4:5],
            esum_mid[2:3],
            esum_mid[1:2],
            long_rows(eb1.reshape(-1), devices, erows),
            emb_sum.reshape(1, -1),
            jnp.zeros((1, width), F32),
        ],
        axis=0,
    )
    dq, dk, dv = attend_back(qkv, attended, gatt, weights, enc_segments, HDIM)
    dq, dk, dv = end_beside(side, (dq, dk, dv))
    dq, dk, dv = start_beside(side, (dq, dk, dv))
    enc_grads, enc_in_grad = enc_qkv_back(
        enc_input, dq, dk, dv, gmid, evecs, enc_more, enc_all
    )
    chip = Fold([by_bits(enc_grads)], [core])
    chip.cut()
    chip.pass_on()
    end_beside(side + [chip], ())
    gcut = 10 * LANES * width // 768
    one = Fold([t[..., :gcut] for t in chip.terms], dp + line[::-1], all_bits()[:-1])
    two = Fold([t[..., gcut:] for t in chip.terms], dp[::-1] + line[::-1], all_bits()[:-1])
    one_round([one, two, eup, early])
    while any(f.order for f in [one, two] + side):
        one_round([f for f in [one, two] + side if f.order])
    rfirst, eu, ed, epe = (term_sum(f.terms, F32) for f in (dfirst, eup, edown, early))
    efirst = jnp.concatenate([term_sum(one.terms, F32), term_sum(two.terms, F32)], axis=-1)
    rq, rv = split_columns(rfirst, [3 * dwidth, LANES])
    ru, rp, rd = split_columns(dec_own.astype(F32), [dff, dwidth, dff])
    rd = unpack_tall(rd, 1, dwidth)
    ep, em = split_columns(epe, [width, dwidth])
    eq, ev = split_columns(efirst, [3 * width, LANES])
    rv = rv.T
    ev = ev.T
    return (
        dec_out,
        enc_in_grad,
        eq,
        ep,
        eu,
        ed,
        ev[:3],
        ev[3:10],
        ev[10:14].reshape(-1),
        em,
        rv[8],
        rq,
        rp,
        ru,
        rd,
        rv[:2],
        jnp.concatenate([ev[14:15, :drows], rv[2:7]], axis=0),
        rv[9:13].reshape(-1),
        rv[7],
    )


def solution(mesh):
    in_specs = (
        P(("dp", "fsdp"), None),
        P(("dp", "fsdp"), None),
        P(("dp", "fsdp"), None),
        P("dp", "fsdp"),
        P(("dp", "fsdp"), None),
        P(("dp", "fsdp"), None),
        P(("dp", "fsdp"), None),
        P(("dp", "fsdp"), None),
        P(("dp", "fsdp"), None),
        P(None, ("dp", "fsdp")),
        P(None, ("dp", "fsdp")),
        P(("dp", "fsdp")),
        P(("dp", "fsdp"), None),
        P(("dp", "fsdp")),
        P(("dp", "fsdp"), None),
        P(("dp", "fsdp"), None),
        P(("dp", "fsdp"), None),
        P(("dp", "fsdp"), None),
        P(None, ("dp", "fsdp")),
        P(None, ("dp", "fsdp")),
        P(("dp", "fsdp")),
        P(("dp", "fsdp")),
    )
    out_specs = (
        P(("dp", "fsdp"), None),
        P(("dp", "fsdp"), None),
        P(("dp", "fsdp"), None),
        P(("dp", "fsdp"), None),
        P(("dp", "fsdp"), None),
        P(("dp", "fsdp"), None),
        P(None, ("dp", "fsdp")),
        P(None, ("dp", "fsdp")),
        P(("dp", "fsdp")),
        P(("dp", "fsdp"), None),
        P(("dp", "fsdp")),
        P(("dp", "fsdp"), None),
        P(("dp", "fsdp"), None),
        P(("dp", "fsdp"), None),
        P(("dp", "fsdp"), None),
        P(None, ("dp", "fsdp")),
        P(None, ("dp", "fsdp")),
        P(("dp", "fsdp")),
        P(("dp", "fsdp")),
    )
    return jax.shard_map(
        per_device, mesh=mesh, in_specs=in_specs, out_specs=out_specs, check_vma=False
    )
```

```python
import functools
import math

import jax
import jax.numpy as jnp
from jax import lax
from jax.experimental import pallas as pl
from jax.experimental.pallas import tpu as pltpu
from jax.sharding import PartitionSpec as P

HDIM = 64
DHDIM = 32
BLOCK = 128
LANES = 128
TILE = 256
EPSILON = 1e-06
NEGATIVE = -1e30
LOG2E = math.log2(math.e)
AXES = ("dp", "fsdp")
F32 = jnp.float32
LOW = jnp.bfloat16
PARAMS = pltpu.CompilerParams(vmem_limit_bytes=56 * 1024 * 1024)


def mm(left, right):
    return jnp.dot(left, right, preferred_element_type=F32)


def mm_tn(left, right):
    return lax.dot_general(left, right, (((0,), (0,)), ((), ())), preferred_element_type=F32)


def mm_nt(left, right):
    return lax.dot_general(left, right, (((1,), (1,)), ((), ())), preferred_element_type=F32)


def col_sum(values):
    return jnp.sum(values, axis=0, keepdims=True)


def norm_parts(values):
    centred = values - jnp.mean(values, axis=-1, keepdims=True)
    variance = jnp.mean(centred * centred, axis=-1, keepdims=True)
    scale = lax.rsqrt(variance + EPSILON)
    return centred * scale, scale


def norm_back(grad, unit, scale, gain):
    inner = grad * gain
    mean_inner = jnp.mean(inner, axis=-1, keepdims=True)
    mean_cross = jnp.mean(inner * unit, axis=-1, keepdims=True)
    return scale * (inner - mean_inner - unit * mean_cross)


def gelu_parts(hidden):
    cdf = 0.5 + 0.5 * lax.erf(hidden * (0.5**0.5))
    density = jnp.exp(hidden * hidden * -0.5) * (1.0 / math.sqrt(2.0 * math.pi))
    return hidden * cdf, cdf + hidden * density


CHEAP = pl.CostEstimate(flops=1 << 20, bytes_accessed=1 << 16, transcendentals=0)


def full(shape):
    return pl.BlockSpec(shape, lambda *_: (0,) * len(shape))


def at_col(rows, cols, index):
    return pl.BlockSpec((rows, cols), lambda *_: (0, index))


def shape(dims, kind):
    return jax.ShapeDtypeStruct(dims, kind)


def lane_mask(head, head_dim, kind):
    lane = lax.broadcasted_iota(jnp.int32, (1, LANES), 1)
    inside = (lane >= head * head_dim) & (lane < (head + 1) * head_dim)
    return inside.astype(F32).astype(kind)


def stack_heads(stacked, index, rows, head_dim):
    for h in range(LANES // head_dim):
        stacked[index, h * TILE : (h + 1) * TILE, :] = rows * lane_mask(h, head_dim, LOW)


def tile_range(seg_ref, here, tiles):
    first = seg_ref[0, here * TILE]
    last = seg_ref[0, here * TILE + TILE - 1]
    low = jnp.int32(0)
    high = jnp.int32(tiles)
    for other in range(tiles):
        low += (seg_ref[0, other * TILE + TILE - 1] < first).astype(jnp.int32)
        high -= (seg_ref[0, other * TILE] > last).astype(jnp.int32)
    return low, high


def attend_kernel(
    head_dim,
    tiles,
    seg_ref,
    q_ref,
    k_ref,
    v_ref,
    row_ref,
    col_ref,
    out_ref,
    inv_ref,
    exp_ref,
    km,
    vt,
    held,
    acc,
    top,
    tot,
):
    heads = LANES // head_dim
    here = pl.program_id(1)
    factor = head_dim ** (-0.5) * LOG2E

    @pl.when(here == 0)
    def _():
        for u in range(tiles):
            rows = slice(u * TILE, (u + 1) * TILE)
            vt[u] = v_ref[rows, :].astype(F32).T.astype(LOW)
            stack_heads(km, u, k_ref[rows, :], head_dim)

    acc[...] = jnp.zeros_like(acc)
    top[...] = jnp.full_like(top, NEGATIVE)
    tot[...] = jnp.zeros_like(tot)
    query = q_ref[...]
    row = row_ref[...]

    def score(u, carry):
        start = pl.multiple_of(u * TILE, TILE)
        same = col_ref[pl.ds(start, TILE), :] == row
        every = mm_nt(km[u], query)
        for h in range(heads):
            scores = jnp.where(same, every[h * TILE : (h + 1) * TILE, :], NEGATIVE)
            held[u, h] = scores
            top[h : h + 1, :] = jnp.maximum(
                top[h : h + 1, :], jnp.max(scores, axis=0, keepdims=True)
            )
        return carry

    def mix(u, carry):
        for h in range(heads):
            weights = jnp.exp2((held[u, h] - top[h : h + 1, :]) * factor)
            tot[h : h + 1, :] += col_sum(weights)
            span = slice(h * head_dim, (h + 1) * head_dim)
            weights = weights.astype(LOW)
            exp_ref[0, 0, u, :, h * TILE : (h + 1) * TILE] = weights
            acc[span, :] += mm(vt[u, span, :], weights)
        return carry

    low, high = tile_range(seg_ref, here, tiles)
    lax.fori_loop(low, high, score, 0)
    lax.fori_loop(low, high, mix, 0)
    for h in range(heads):
        span = slice(h * head_dim, (h + 1) * head_dim)
        inverse = jnp.broadcast_to(1.0 / tot[h : h + 1, :], (head_dim, TILE))
        acc[span, :] = acc[span, :] * inverse
        held[0, 0, span, :] = inverse
    out_ref[...] = acc[...].T.astype(LOW)
    inv_ref[...] = held[0, 0, :LANES, :].T


def attend(qkv, segments, seg_col, head_dim):
    rows, width = qkv.shape[0], qkv.shape[1] // 3
    groups, tiles, heads = width // LANES, rows // TILE, LANES // head_dim
    return pl.pallas_call(
        functools.partial(attend_kernel, head_dim, tiles),
        grid_spec=pltpu.PrefetchScalarGridSpec(
            num_scalar_prefetch=1,
            grid=(groups, tiles),
            in_specs=[
                pl.BlockSpec((TILE, LANES), lambda g, t, s: (t, g)),
                pl.BlockSpec((rows, LANES), lambda g, t, s: (0, groups + g)),
                pl.BlockSpec((rows, LANES), lambda g, t, s: (0, 2 * groups + g)),
                pl.BlockSpec((1, TILE), lambda g, t, s: (0, t)),
                pl.BlockSpec((rows, 1), lambda g, t, s: (0, 0)),
            ],
            out_specs=[
                pl.BlockSpec((TILE, LANES), lambda g, t, s: (t, g)),
                pl.BlockSpec((TILE, LANES), lambda g, t, s: (t, g)),
                pl.BlockSpec((1, 1, tiles, TILE, heads * TILE), lambda g, t, s: (g, t, 0, 0, 0)),
            ],
            scratch_shapes=[
                pltpu.VMEM((tiles, heads * TILE, LANES), LOW),
                pltpu.VMEM((tiles, LANES, TILE), LOW),
                pltpu.VMEM((tiles, heads, TILE, TILE), F32),
                pltpu.VMEM((LANES, TILE), F32),
                pltpu.VMEM((8, TILE), F32),
                pltpu.VMEM((8, TILE), F32),
            ],
        ),
        out_shape=[
            shape((rows, width), LOW),
            shape((rows, width), F32),
            shape((groups, tiles, tiles, TILE, heads * TILE), LOW),
        ],
        compiler_params=PARAMS,
        cost_estimate=CHEAP,
        name="attend",
    )(segments, qkv, qkv, qkv, segments, seg_col)


def attend_back_kernel(
    head_dim,
    tiles,
    seg_ref,
    q_ref,
    k_ref,
    v_ref,
    o_ref,
    g_ref,
    exp_ref,
    dq_ref,
    dk_ref,
    dv_ref,
    qm,
    gm,
    vm,
    dqt,
    delta,
    dk_acc,
    dv_acc,
):
    heads = LANES // head_dim
    here = pl.program_id(1)
    scale = head_dim ** (-0.5)

    @pl.when(here == 0)
    def _():
        dqt[...] = jnp.zeros_like(dqt)
        for t in range(tiles):
            rows = slice(t * TILE, (t + 1) * TILE)
            stack_heads(qm, t, q_ref[rows, :], head_dim)
            stack_heads(gm, t, g_ref[rows, :], head_dim)
            both = (g_ref[rows, :].astype(F32) * o_ref[rows, :].astype(F32)).T
            for h in range(heads):
                delta[t, h : h + 1, :] = col_sum(both[h * head_dim : (h + 1) * head_dim, :])

    keys_t = k_ref[...].astype(F32).T.astype(LOW)
    stack_heads(vm, 0, v_ref[...], head_dim)
    dk_acc[...] = jnp.zeros_like(dk_acc)
    dv_acc[...] = jnp.zeros_like(dv_acc)

    def step(t, carry):
        start = pl.multiple_of(t * TILE, TILE)
        every = mm_nt(vm[0], g_ref[pl.ds(start, TILE), :])
        dv_acc[...] += mm(exp_ref[0, t, 0], gm[t])
        pieces = []
        for h in range(heads):
            grad_probs = every[h * TILE : (h + 1) * TILE, :] - delta[t, h : h + 1, :]
            weights = exp_ref[0, t, 0, :, h * TILE : (h + 1) * TILE]
            pieces.append((weights.astype(F32) * grad_probs).astype(LOW))
        for h in range(heads):
            span = slice(h * head_dim, (h + 1) * head_dim)
            dqt[t, span, :] += mm(keys_t[span, :], pieces[h])
        dk_acc[...] += mm(jnp.concatenate(pieces, axis=1), qm[t])
        return carry

    low, high = tile_range(seg_ref, here, tiles)
    lax.fori_loop(low, high, step, 0)
    dk_ref[...] = (dk_acc[...] * scale).astype(LOW)
    dv_ref[...] = dv_acc[...].astype(LOW)

    @pl.when(here == tiles - 1)
    def _():
        for t in range(tiles):
            dq_ref[t * TILE : (t + 1) * TILE, :] = (dqt[t] * scale).T.astype(LOW)


def attend_back(qkv, attended, grad, weights, segments, head_dim):
    rows, width = attended.shape
    groups, tiles, heads = width // LANES, rows // TILE, LANES // head_dim
    whole = pl.BlockSpec((rows, LANES), lambda g, u, s: (0, g))
    piece = pl.BlockSpec((TILE, LANES), lambda g, u, s: (u, g))
    return pl.pallas_call(
        functools.partial(attend_back_kernel, head_dim, tiles),
        grid_spec=pltpu.PrefetchScalarGridSpec(
            num_scalar_prefetch=1,
            grid=(groups, tiles),
            in_specs=[
                whole,
                pl.BlockSpec((TILE, LANES), lambda g, u, s: (u, groups + g)),
                pl.BlockSpec((TILE, LANES), lambda g, u, s: (u, 2 * groups + g)),
                whole,
                whole,
                pl.BlockSpec((1, tiles, 1, TILE, heads * TILE), lambda g, u, s: (g, 0, u, 0, 0)),
            ],
            out_specs=[whole, piece, piece],
            scratch_shapes=[
                pltpu.VMEM((tiles, heads * TILE, LANES), LOW),
                pltpu.VMEM((tiles, heads * TILE, LANES), LOW),
                pltpu.VMEM((1, heads * TILE, LANES), LOW),
                pltpu.VMEM((tiles, LANES, TILE), F32),
                pltpu.VMEM((tiles, 8, TILE), F32),
                pltpu.VMEM((TILE, LANES), F32),
                pltpu.VMEM((TILE, LANES), F32),
            ],
        ),
        out_shape=[shape((rows, width), LOW)] * 3,
        compiler_params=PARAMS,
        cost_estimate=CHEAP,
        name="attend_back",
    )(segments, qkv, qkv, qkv, attended, grad, weights)


def pack_kernel(*refs):
    ins, outs = refs[: len(refs) * 2 // 3], refs[len(refs) * 2 // 3 :]
    for up, down, out in zip(ins[::2], ins[1::2], outs):
        rows, cols = up.shape
        out[:, :cols] = up[...]
        wide = down[...].astype(F32)
        width = down.shape[1]
        for part in range(4):
            piece = wide[part * rows : (part + 1) * rows, :].astype(LOW)
            out[:, cols + part * width : cols + (part + 1) * width] = piece


def pack_shards(*shards):
    outs = [shape((u.shape[0], u.shape[1] + 4 * d.shape[1]), LOW) for u, d in zip(shards[::2], shards[1::2])]
    return pl.pallas_call(
        pack_kernel,
        in_specs=[full(s.shape) for s in shards],
        out_specs=[full(o.shape) for o in outs],
        out_shape=outs,
        grid=(1,),
        compiler_params=PARAMS,
        cost_estimate=CHEAP,
        name="pack",
    )(*shards)


def natural_rows(block, group, kind):
    width = block.shape[1] // 4
    parts = [
        block[:, i * width : (i + 1) * width].astype(kind).reshape(-1, group, width)
        for i in range(4)
    ]
    return jnp.stack(parts, axis=1).reshape(-1, width).astype(LOW)


def enc_qkv_kernel(x_ref, vec_ref, w_ref, out_ref, normed):
    part = pl.program_id(0)

    @pl.when(part == 0)
    def _():
        unit, _ = norm_parts(x_ref[...].astype(F32))
        normed[...] = (unit * vec_ref[0:1, :] + vec_ref[3:4, :]).astype(LOW)

    bias = jnp.where(part == 0, vec_ref[4:5, :], jnp.where(part == 2, vec_ref[5:6, :], 0.0))
    out_ref[...] = (mm(normed[...], w_ref[...]) + bias).astype(LOW)


def enc_qkv_call(rows_in, vecs, weight):
    rows, width = rows_in.shape
    return pl.pallas_call(
        enc_qkv_kernel,
        grid=(3,),
        in_specs=[
            full((rows, width)),
            full(vecs.shape),
            pl.BlockSpec((width, width), lambda i: (0, i)),
        ],
        out_specs=pl.BlockSpec((rows, width), lambda i: (0, i)),
        out_shape=shape((rows, 3 * width), LOW),
        scratch_shapes=[pltpu.VMEM((rows, width), LOW)],
        compiler_params=PARAMS,
        cost_estimate=CHEAP,
        name="enc_qkv",
    )(rows_in, vecs, weight)


def enc_mid_kernel(
    chunks,
    packed,
    x_ref,
    att_ref,
    vec_ref,
    b1_ref,
    eb_ref,
    wo_ref,
    we_ref,
    *refs,
):
    up_ref, down_ref, *refs = refs
    mid_ref, out_ref, final_ref, act_ref, slope_ref, emb_ref, *refs = refs
    naturals, (normed, acc) = refs[:-2], refs[-2:]
    part = pl.program_id(0)

    @pl.when(part == 0)
    def _():
        middle = x_ref[...].astype(F32) + mm(att_ref[...], wo_ref[...]) + vec_ref[6:7, :]
        mid_ref[...] = middle
        unit, _ = norm_parts(middle)
        normed[...] = (unit * vec_ref[1:2, :] + vec_ref[7:8, :]).astype(LOW)
        acc[...] = middle + vec_ref[8:9, :]

    down = down_ref[...]
    if packed:
        down = natural_rows(down, packed, F32)
        naturals[0][...] = down
    hidden = mm(normed[...], up_ref[...]) + b1_ref[...]
    value, slope = gelu_parts(hidden)
    value = value.astype(LOW)
    act_ref[...] = value
    slope_ref[...] = slope
    acc[...] += mm(value, down)

    @pl.when(part == chunks - 1)
    def _():
        result = acc[...]
        out_ref[...] = result
        unit, _ = norm_parts(result)
        final = (unit * vec_ref[2:3, :] + vec_ref[9:10, :]).astype(LOW)
        final_ref[...] = final
        emb_ref[...] = (mm(final, we_ref[...]) + eb_ref[...]).astype(LOW)


def enc_mid(rows_in, attended, vecs, up_bias, emb_bias, wide, weights, proj_at, emb_at):
    rows, width = rows_in.shape
    hidden = up_bias.shape[1]
    emb_width = emb_bias.shape[1]
    chunks = hidden // width
    by_row = pl.BlockSpec((width, width), lambda i: (i, 0))
    specs = [pl.BlockSpec((width, width), lambda i: (0, i))]
    if len(weights) == 1:
        packed = width // (lax.axis_size("dp") * lax.axis_size("fsdp"))
        specs.append(pl.BlockSpec((width // 4, hidden), lambda i: (i, 1)))
        operands = [weights[0]] * 2
        natural_specs, natural_shapes = [by_row], [shape((hidden, width), LOW)]
    else:
        packed = 0
        specs.append(by_row)
        operands, natural_specs, natural_shapes = list(weights), [], []
    outs = pl.pallas_call(
        functools.partial(enc_mid_kernel, chunks, packed),
        grid=(chunks,),
        in_specs=[
            full((rows, width)),
            full((rows, width)),
            full(vecs.shape),
            pl.BlockSpec((1, width), lambda i: (0, i)),
            full((1, emb_width)),
            at_col(width, width, proj_at // width),
            at_col(width, emb_width, emb_at // emb_width),
        ]
        + specs,
        out_specs=[
            full((rows, width)),
            full((rows, width)),
            full((rows, width)),
            pl.BlockSpec((rows, width), lambda i: (0, i)),
            pl.BlockSpec((rows, width), lambda i: (0, i)),
            full((rows, emb_width)),
        ]
        + natural_specs,
        out_shape=[
            shape((rows, width), F32),
            shape((rows, width), F32),
            shape((rows, width), LOW),
            shape((rows, hidden), LOW),
            shape((rows, hidden), F32),
            shape((rows, emb_width), LOW),
        ]
        + natural_shapes,
        scratch_shapes=[pltpu.VMEM((rows, width), LOW), pltpu.VMEM((rows, width), F32)],
        compiler_params=PARAMS,
        cost_estimate=CHEAP,
        name="enc_mid",
    )(rows_in, attended, vecs, up_bias, emb_bias, wide, wide, *operands)
    return outs if packed else list(outs) + [weights[1]]


def enc_mid_back_kernel(
    chunks,
    packed,
    elow_ref,
    final_ref,
    out_ref,
    mid_ref,
    att_ref,
    act_ref,
    slope_ref,
    vec_ref,
    wo_ref,
    w1_ref,
    w2_ref,
    we_ref,
    inv_ref,
    dpe_ref,
    dw2_ref,
    dw1_ref,
    db1_ref,
    esum_ref,
    sum_ref,
    gmid_ref,
    gatt_ref,
    grad,
    grad_low,
    unit_two,
    scale_two,
    normed,
    dnorm,
):
    part = pl.program_id(0)

    @pl.when(part == 0)
    def _():
        elow = elow_ref[...]
        width = final_ref.shape[1]
        dpe_ref[:, width:] = mm_tn(final_ref[...], elow).astype(LOW)
        esum_ref[...] = jnp.zeros_like(esum_ref)
        esum_ref[0:1, :] = col_sum(elow.astype(F32))
        unit, scale = norm_parts(out_ref[...])
        dfinal = mm_nt(elow, we_ref[...])
        sum_ref[...] = jnp.zeros_like(sum_ref)
        sum_ref[0:1, :] = col_sum(dfinal * unit)
        sum_ref[1:2, :] = col_sum(dfinal)
        total = norm_back(dfinal, unit, scale, vec_ref[2:3, :])
        grad[...] = total
        low = total.astype(LOW)
        grad_low[...] = low
        sum_ref[2:3, :] = col_sum(low.astype(F32))
        unit, scale = norm_parts(mid_ref[...])
        unit_two[...] = unit
        scale_two[...] = jnp.broadcast_to(scale, scale_two.shape)
        normed[...] = (unit * vec_ref[1:2, :] + vec_ref[7:8, :]).T.astype(LOW)
        dnorm[...] = jnp.zeros_like(dnorm)

    low = grad_low[...]
    down = mm_tn(act_ref[...], low)
    if packed:
        width = low.shape[1]
        down = down.reshape(-1, 4, packed, width)
        for i in range(4):
            piece = down[:, i].reshape(-1, width).astype(LOW)
            dw2_ref[:, i * width : (i + 1) * width] = piece
    else:
        dw2_ref[...] = down.astype(LOW)
    dhid = (slope_ref[...] * mm_nt(low, w2_ref[...])).astype(LOW)
    dw1_ref[...] = mm(normed[...], dhid).astype(LOW)
    db1_ref[...] = col_sum(dhid.astype(F32))
    dnorm[...] += mm_nt(dhid, w1_ref[...])

    @pl.when(part == chunks - 1)
    def _():
        dn = dnorm[...]
        unit = unit_two[...]
        sum_ref[3:4, :] = col_sum(dn * unit)
        sum_ref[4:5, :] = col_sum(dn)
        gmid = grad[...] + norm_back(dn, unit, scale_two[:, 0:1], vec_ref[1:2, :])
        gmid_ref[...] = gmid
        mlow = gmid.astype(LOW)
        sum_ref[5:6, :] = col_sum(mlow.astype(F32))
        dpe_ref[:, : mlow.shape[1]] = mm_tn(att_ref[...], mlow).astype(LOW)
        gatt_ref[...] = (mm_nt(mlow, wo_ref[...]) * inv_ref[...]).astype(LOW)


def enc_mid_back(
    elow, final, out, mid, attended, act, slope, inverse, vecs, wide, up_w, down_w, proj_at, emb_at
):
    rows, width = mid.shape
    hidden = down_w.shape[0]
    emb_width = elow.shape[1]
    chunks = hidden // width
    packed = width // (lax.axis_size("dp") * lax.axis_size("fsdp"))
    packed = packed if packed % 8 == 0 else 0
    by_col = pl.BlockSpec((rows, width), lambda i: (0, i))
    return pl.pallas_call(
        functools.partial(enc_mid_back_kernel, chunks, packed),
        grid=(chunks,),
        in_specs=[
            full((rows, emb_width)),
            full((rows, width)),
            full((rows, width)),
            full((rows, width)),
            full((rows, width)),
            by_col,
            by_col,
            full(vecs.shape),
            at_col(width, width, proj_at // width),
            pl.BlockSpec((width, width), lambda i: (0, i)),
            pl.BlockSpec((width, width), lambda i: (i, 0)),
            at_col(width, emb_width, emb_at // emb_width),
            full((rows, width)),
        ],
        out_specs=[
            full((width, width + emb_width)),
            pl.BlockSpec((width // 4, hidden) if packed else (width, width), lambda i: (i, 0)),
            pl.BlockSpec((width, width), lambda i: (0, i)),
            pl.BlockSpec((1, width), lambda i: (0, i)),
            full((8, emb_width)),
            full((8, width)),
            full((rows, width)),
            full((rows, width)),
        ],
        out_shape=[
            shape((width, width + emb_width), LOW),
            shape((width, hidden) if packed else (hidden, width), LOW),
            shape((width, hidden), LOW),
            shape((1, hidden), F32),
            shape((8, emb_width), F32),
            shape((8, width), F32),
            shape((rows, width), F32),
            shape((rows, width), LOW),
        ],
        scratch_shapes=[
            pltpu.VMEM((rows, width), F32),
            pltpu.VMEM((rows, width), LOW),
            pltpu.VMEM((rows, width), F32),
            pltpu.VMEM((rows, LANES), F32),
            pltpu.VMEM((width, rows), LOW),
            pltpu.VMEM((rows, width), F32),
        ],
        compiler_params=PARAMS,
        cost_estimate=CHEAP,
        name="enc_mid_back",
    )(elow, final, out, mid, attended, act, slope, vecs, wide, up_w, down_w, wide, inverse)


def enc_qkv_back_kernel(
    x_ref,
    dq_ref,
    dk_ref,
    dv_ref,
    gmid_ref,
    vec_ref,
    more_ref,
    dpe_ref,
    w_ref,
    dw_ref,
    din_ref,
    sums,
):
    width = x_ref.shape[1]
    unit, scale = norm_parts(x_ref[...].astype(F32))
    normed = (unit * vec_ref[0:1, :] + vec_ref[3:4, :]).astype(LOW)
    grads = jnp.concatenate([dq_ref[...], dk_ref[...], dv_ref[...]], axis=1)
    dw_ref[:, : 3 * width] = mm_tn(normed, grads).astype(LOW)
    dw_ref[:, 3 * width : 3 * width + dpe_ref.shape[1]] = dpe_ref[...]
    dn = mm_nt(grads, w_ref[...])
    sums[...] = jnp.zeros_like(sums)
    sums[0:16, :] = more_ref[...]
    sums[0:1, :] = col_sum(dn * unit)
    sums[3:4, :] = col_sum(dn)
    sums[4:5, :] = col_sum(dq_ref[...].astype(F32))
    sums[5:6, :] = col_sum(dv_ref[...].astype(F32))
    dw_ref[:, 3 * width + dpe_ref.shape[1] :] = sums[...].T.astype(LOW)
    din = gmid_ref[...] + norm_back(dn, unit, scale, vec_ref[0:1, :])
    din_ref[...] = din.astype(LOW)


def enc_qkv_back(rows_in, dq, dk, dv, gmid, vecs, more, dpe, weight):
    rows, width = rows_in.shape
    whole = full((rows, width))
    packed = (width, 3 * width + dpe.shape[1] + LANES)
    return pl.pallas_call(
        enc_qkv_back_kernel,
        grid=(1,),
        in_specs=[whole] * 5
        + [full(vecs.shape), full((16, width)), full(dpe.shape), at_col(width, 3 * width, 0)],
        out_specs=[full(packed), whole],
        out_shape=[shape(packed, LOW), shape((rows, width), LOW)],
        scratch_shapes=[pltpu.VMEM((LANES, width), F32)],
        compiler_params=PARAMS,
        cost_estimate=CHEAP,
        name="enc_qkv_back",
    )(rows_in, dq, dk, dv, gmid, vecs, more, dpe, weight)


def dec_in_kernel(limit, order_ref, one_ref, two_ref, pos_ref, vec_ref, w_ref, in_ref, qkv_ref):
    step = pl.program_id(0)
    width = in_ref.shape[1]
    for half, ref in enumerate((one_ref, two_ref)):
        visible = order_ref[0, 2 * step + half] < limit
        rows = slice(half * BLOCK, (half + 1) * BLOCK)
        in_ref[rows, :] = (
            jnp.where(visible, ref[...].astype(F32), vec_ref[9:10, :]) + pos_ref[rows, :]
        )
    unit, _ = norm_parts(in_ref[...])
    normed = (unit * vec_ref[0:1, :] + vec_ref[3:4, :]).astype(LOW)
    qkv = mm(normed, w_ref[...])
    qkv_ref[:, :width] = (qkv[:, :width] + vec_ref[4:5, :]).astype(LOW)
    qkv_ref[:, width : 2 * width] = qkv[:, width : 2 * width].astype(LOW)
    qkv_ref[:, 2 * width :] = (qkv[:, 2 * width :] + vec_ref[5:6, :]).astype(LOW)


def dec_in_call(order, gathered, pos, vecs, weight):
    rows, width = pos.shape
    limit = gathered.shape[0] // BLOCK

    def chosen(half):
        def index(i, order_ref):
            return (jnp.clip(order_ref[0, 2 * i + half], 0, limit - 1), 0)

        return pl.BlockSpec((BLOCK, width), index)

    return pl.pallas_call(
        functools.partial(dec_in_kernel, limit),
        grid_spec=pltpu.PrefetchScalarGridSpec(
            num_scalar_prefetch=1,
            grid=(rows // TILE,),
            in_specs=[
                chosen(0),
                chosen(1),
                pl.BlockSpec((TILE, width), lambda i, o: (i, 0)),
                full(vecs.shape),
                at_col(width, 3 * width, 0),
            ],
            out_specs=[
                pl.BlockSpec((TILE, width), lambda i, o: (i, 0)),
                pl.BlockSpec((TILE, 3 * width), lambda i, o: (i, 0)),
            ],
        ),
        out_shape=[shape((rows, width), F32), shape((rows, 3 * width), LOW)],
        compiler_params=PARAMS,
        cost_estimate=CHEAP,
        name="dec_in",
    )(order, gathered, gathered, pos, vecs, weight)


def dec_mid_kernel(
    steps,
    chunks,
    packed,
    x_ref,
    att_ref,
    cot_ref,
    inv_ref,
    vec_ref,
    b1_ref,
    wo_ref,
    up_ref,
    down_ref,
    out_ref,
    gmid_ref,
    gatt_ref,
    dw_ref,
    db1_ref,
    sum_ref,
    aw1,
    aw2,
    acc,
    dnorm,
    turned,
):
    step = pl.program_id(0)
    width = x_ref.shape[1]
    hidden = chunks * width
    lead = width // 4

    @pl.when(step == 0)
    def _():
        aw1[...] = jnp.zeros_like(aw1)
        aw2[...] = jnp.zeros_like(aw2)
        db1_ref[...] = jnp.zeros_like(db1_ref)
        sum_ref[...] = jnp.zeros_like(sum_ref)

    att = att_ref[...]
    low = cot_ref[...]
    middle = x_ref[...] + mm(att, wo_ref[...]) + vec_ref[6:7, :]
    unit, scale = norm_parts(middle)
    normed = unit * vec_ref[1:2, :] + vec_ref[7:8, :]
    turned[...] = normed.T.astype(LOW)
    normed = normed.astype(LOW)
    acc[...] = middle + vec_ref[8:9, :]
    dnorm[...] = jnp.zeros_like(dnorm)

    def chunk(j, carry):
        cols = pl.ds(pl.multiple_of(j * width, width), width)
        some = pl.ds(pl.multiple_of(j * lead, lead), lead)
        up = up_ref[:, cols]
        down = natural_rows(down_ref[some, :], packed, LOW) if packed else down_ref[cols, :]
        value, slope = gelu_parts(mm(normed, up) + b1_ref[j])
        value = value.astype(LOW)
        acc[...] += mm(value, down)
        grad = mm_tn(value, low)
        if packed:
            grad = grad.reshape(-1, 4, packed, width)
            for part in range(4):
                piece = grad[:, part].reshape(lead, width)
                aw2[some, part * width : (part + 1) * width] += piece
        else:
            aw2[cols, :] += grad
        dhid = (slope * mm_nt(low, down)).astype(LOW)
        aw1[:, cols] += mm(turned[...], dhid)
        db1_ref[j] += col_sum(dhid.astype(F32))
        dnorm[...] += mm_nt(dhid, up)
        return carry

    lax.fori_loop(0, chunks, chunk, 0)
    out_ref[...] = acc[...].astype(LOW)
    dn = dnorm[...]
    sum_ref[0:1, :] += col_sum(dn * unit)
    sum_ref[1:2, :] += col_sum(dn)
    gmid = low.astype(F32) + norm_back(dn, unit, scale, vec_ref[1:2, :])
    gmid_ref[...] = gmid
    mlow = gmid.astype(LOW)
    sum_ref[2:3, :] += col_sum(mlow.astype(F32))
    sum_ref[3:4, :] += col_sum(low.astype(F32))
    aw1[:, hidden:] += mm_tn(att, mlow)
    gatt_ref[...] = (mm_nt(mlow, wo_ref[...]) * inv_ref[...]).astype(LOW)

    @pl.when(step == steps - 1)
    def _():
        dw_ref[:, : hidden + width] = aw1[...].astype(LOW)
        if packed:
            dw_ref[:, hidden + width :] = aw2[...].astype(LOW)
        else:
            for c in range(chunks):
                col = hidden + (1 + c) * width
                dw_ref[:, col : col + width] = aw2[c * width : (c + 1) * width, :].astype(LOW)


def dec_mid(dec_in, attended, cotangent, inverse, vecs, up_bias, wide, weights, proj_at):
    rows, width = dec_in.shape
    hidden = up_bias.shape[1]
    chunks = hidden // width
    tile = 2 * TILE
    steps = rows // tile
    by_row = pl.BlockSpec((tile, width), lambda i: (i, 0))
    if len(weights) == 1:
        packed = width // (lax.axis_size("dp") * lax.axis_size("fsdp"))
        down_shape = (width, hidden)
        specs, operands = [at_col(width, hidden, 0), at_col(width, hidden, 1)], [weights[0]] * 2
    else:
        packed, down_shape = 0, (hidden, width)
        specs, operands = [full((width, hidden)), full(down_shape)], list(weights)
    return pl.pallas_call(
        functools.partial(dec_mid_kernel, steps, chunks, packed),
        grid=(steps,),
        in_specs=[
            by_row,
            by_row,
            by_row,
            by_row,
            full(vecs.shape),
            full((chunks, 1, width)),
            at_col(width, width, proj_at // width),
        ]
        + specs,
        out_specs=[
            by_row,
            by_row,
            by_row,
            full((width, 2 * hidden + width)),
            full((chunks, 1, width)),
            full((8, width)),
        ],
        out_shape=[
            shape((rows, width), LOW),
            shape((rows, width), F32),
            shape((rows, width), LOW),
            shape((width, 2 * hidden + width), LOW),
            shape((chunks, 1, width), F32),
            shape((8, width), F32),
        ],
        scratch_shapes=[
            pltpu.VMEM((width, hidden + width), F32),
            pltpu.VMEM(down_shape, F32),
            pltpu.VMEM((tile, width), F32),
            pltpu.VMEM((tile, width), F32),
            pltpu.VMEM((width, tile), LOW),
        ],
        compiler_params=PARAMS,
        cost_estimate=CHEAP,
        name="dec_mid",
    )(
        dec_in,
        attended,
        cotangent,
        inverse,
        vecs,
        up_bias.reshape(chunks, 1, width),
        wide,
        *operands,
    )


def dec_back_kernel(
    limit,
    order_ref,
    x_ref,
    dq_ref,
    dk_ref,
    dv_ref,
    gmid_ref,
    vec_ref,
    more_ref,
    w_ref,
    sum_ref,
    send_ref,
):
    step = pl.program_id(0)

    @pl.when(step == 0)
    def _():
        sum_ref[...] = more_ref[...]
        send_ref[...] = jnp.zeros_like(send_ref)

    unit, scale = norm_parts(x_ref[...])
    grads = jnp.concatenate([dq_ref[...], dk_ref[...], dv_ref[...]], axis=1)
    dn = mm_nt(grads, w_ref[...])
    sum_ref[0:1, :] += col_sum(dn * unit)
    sum_ref[2:3, :] += col_sum(dn)
    sum_ref[3:4, :] += col_sum(dq_ref[...].astype(F32))
    sum_ref[4:5, :] += col_sum(dv_ref[...].astype(F32))
    din = gmid_ref[...] + norm_back(dn, unit, scale, vec_ref[0:1, :])
    per = x_ref.shape[0] // BLOCK
    for b in range(per):
        place = order_ref[0, per * step + b]
        rows = din[b * BLOCK : (b + 1) * BLOCK, :]

        @pl.when(place < limit)
        def _():
            send_ref[pl.ds(pl.multiple_of(place * BLOCK, BLOCK), BLOCK), :] = rows.astype(LOW)

        @pl.when(place >= limit)
        def _():
            sum_ref[8:9, :] += col_sum(rows)


def dec_back(order, dec_in, dq, dk, dv, gmid, vecs, more, weight, limit):
    rows, width = dec_in.shape
    tile = TILE
    by_row = pl.BlockSpec((tile, width), lambda i, o: (i, 0))
    return pl.pallas_call(
        functools.partial(dec_back_kernel, limit),
        grid_spec=pltpu.PrefetchScalarGridSpec(
            num_scalar_prefetch=1,
            grid=(rows // tile,),
            in_specs=[by_row] * 5
            + [full(vecs.shape), full((16, width)), at_col(width, 3 * width, 0)],
            out_specs=[full((16, width)), full((limit * BLOCK, width))],
        ),
        out_shape=[shape((16, width), F32), shape((limit * BLOCK, width), LOW)],
        compiler_params=PARAMS,
        cost_estimate=CHEAP,
        name="dec_back",
    )(order, dec_in, dq, dk, dv, gmid, vecs, more, weight)


def dec_grad_kernel(x_ref, dq_ref, dk_ref, dv_ref, vec_ref, sum_ref, dw_ref, acc, sums):
    step = pl.program_id(0)
    width = x_ref.shape[1]

    @pl.when(step == 0)
    def _():
        acc[...] = jnp.zeros_like(acc)

    unit, _ = norm_parts(x_ref[...])
    normed = (unit * vec_ref[0:1, :] + vec_ref[3:4, :]).astype(LOW)
    grads = jnp.concatenate([dq_ref[...], dk_ref[...], dv_ref[...]], axis=1)
    acc[...] += mm_tn(normed, grads)

    @pl.when(step == pl.num_programs(0) - 1)
    def _():
        dw_ref[:, : 3 * width] = acc[...].astype(LOW)
        sums[...] = jnp.zeros_like(sums)
        sums[0:16, :] = sum_ref[...]
        dw_ref[:, 3 * width :] = sums[...].T.astype(LOW)


def dec_grad(dec_in, dq, dk, dv, vecs, sums):
    rows, width = dec_in.shape
    tile = 2 * TILE
    by_row = pl.BlockSpec((tile, width), lambda i: (i, 0))
    packed = (width, 3 * width + LANES)
    return pl.pallas_call(
        dec_grad_kernel,
        grid=(rows // tile,),
        in_specs=[by_row] * 4 + [full(vecs.shape), full((16, width))],
        out_specs=full(packed),
        out_shape=shape(packed, LOW),
        scratch_shapes=[pltpu.VMEM((width, 3 * width), F32), pltpu.VMEM((LANES, width), F32)],
        compiler_params=PARAMS,
        cost_estimate=CHEAP,
        name="dec_grad",
    )(dec_in, dq, dk, dv, vecs, sums)


def positions(count, width):
    places = jnp.arange(count, dtype=jnp.float32)[:, None]
    columns = jnp.arange(width)
    rates = jnp.exp((2 * (columns // 2)).astype(jnp.float32) * (-math.log(10000.0) / width))
    angles = places * rates[None, :]
    return jnp.where((columns % 2 == 0)[None, :], jnp.sin(angles), jnp.cos(angles))


def bits_of(axis):
    size, out = lax.axis_size(axis), []
    while size > 1:
        size //= 2
        out.append((axis, size))
    return out


def all_bits():
    return bits_of("dp") + bits_of("fsdp")


def bit_here(bit):
    axis, stride = bit
    return lax.axis_index(axis) // stride % 2


def swap(value, bit):
    axis, stride = bit
    return lax.ppermute(value, axis, [(i, i ^ stride) for i in range(lax.axis_size(axis))])


def pair(own, got, here, dim):
    dims = tuple(2 if d == dim else 1 for d in range(own.ndim + 1))
    mine = lax.broadcasted_iota(jnp.int32, dims, dim) == here
    return jnp.where(mine, jnp.expand_dims(own, dim), jnp.expand_dims(got, dim))


class Gather:
    def __init__(self, piece, order, held=()):
        self.piece, self.order, self.held = piece, list(order), list(held)

    def step(self):
        canon, bit = all_bits(), self.order.pop(0)
        got = swap(self.piece, bit)
        dim = sum(canon.index(b) < canon.index(bit) for b in self.held)
        self.piece = pair(self.piece, got, bit_here(bit), dim)
        self.held.append(bit)

    def rest(self):
        while self.order:
            self.step()
        return self.piece

    def tie(self, other):
        self.piece, other = lax.optimization_barrier((self.piece, other))
        return other


def gather(piece, order, held=()):
    return Gather(piece, order, held).rest()


def join(pieces, bit):
    both = [pair(own, swap(own, bit), bit_here(bit), own.ndim - 2) for own in pieces]
    both = both[0] if len(both) == 1 else jnp.concatenate(both, axis=-1)
    return both.reshape(-1, both.shape[-1])


def term_sum(terms, kind):
    total = terms[0].astype(F32)
    for term in terms[1:]:
        total = total + term.astype(F32)
    return total.astype(kind)


class Fold:
    def __init__(self, terms, order, held=None):
        self.terms, self.order = list(terms), list(order)
        self.left = list(all_bits() if held is None else held)

    def cut(self):
        bit = self.order[0]
        dim = self.left.index(bit)
        here = bit_here(bit)

        def half(index):
            return [lax.dynamic_index_in_dim(t, index, dim, keepdims=False) for t in self.terms]

        self.send, self.terms = term_sum(half(1 - here), LOW), half(here)

    def pass_on(self):
        bit = self.order.pop(0)
        self.left.remove(bit)
        self.terms.append(swap(self.send, bit))


def start_beside(folds, inputs):
    for fold in folds:
        fold.cut()
    sends, inputs = lax.optimization_barrier(([f.send for f in folds], inputs))
    for fold, send in zip(folds, sends):
        fold.send = send
        fold.pass_on()
    return inputs


def end_beside(folds, outputs):
    last, outputs = lax.optimization_barrier(([f.terms[-1] for f in folds], outputs))
    for fold, got in zip(folds, last):
        fold.terms[-1] = got
    return outputs


def one_round(folds):
    for fold in folds:
        fold.cut()
        fold.pass_on()
    end_beside(folds, ())


def joined(folds, line):
    terms = [term_sum(f.terms, F32) for f in folds]
    return Fold([jnp.concatenate(terms, axis=-1)], line[::-1], line)


def by_bits(grads):
    bits = len(all_bits())
    rows = grads.shape[0] >> bits
    return grads.reshape((2,) * bits + (rows, grads.shape[1]))


def pack_vectors(pieces, rows):
    wide = jnp.concatenate([p.reshape(-1, rows) for p in pieces], axis=0)
    wide = jnp.pad(wide, ((0, LANES - wide.shape[0]), (0, 0)))
    return wide.T


def unpack_tall(columns, devices, width):
    rows = columns.shape[0] // devices
    parts = columns.shape[1] // width
    return (
        columns.reshape(devices, rows, parts, width)
        .transpose(0, 2, 1, 3)
        .reshape(devices * parts * rows, width)
    )


def repack_tall(weight, devices, rows):
    parts = weight.shape[0] // (devices * rows)
    width = weight.shape[1]
    return (
        weight.reshape(devices, parts, rows, width)
        .transpose(0, 2, 1, 3)
        .reshape(devices * rows, parts * width)
    )


def split_columns(array, widths):
    out, at = [], 0
    for w in widths:
        out.append(array[:, at : at + w])
        at += w
    return out


def long_vector(rows_of, devices):
    parts, total = rows_of.shape
    return rows_of.reshape(parts, devices, total // devices).transpose(1, 0, 2).reshape(1, -1)


def long_rows(vector, devices, rows):
    parts = vector.shape[0] // (devices * rows)
    return vector.reshape(devices, parts, rows).transpose(1, 0, 2).reshape(parts, -1)


def per_device(
    enc_input,
    enc_segments,
    dec_segments,
    block_order,
    dec_cotangent,
    enc_qkv,
    enc_proj,
    enc_fc1,
    enc_fc2,
    enc_gains,
    enc_biases,
    enc_fc1_bias,
    embed,
    mask_token,
    dec_qkv,
    dec_proj,
    dec_fc1,
    dec_fc2,
    dec_gains,
    dec_biases,
    dec_fc1_bias,
    dec_fc2_bias,
):
    devices = lax.axis_size("dp") * lax.axis_size("fsdp")
    enc_rows, width = enc_input.shape
    dec_rows, dwidth = dec_cotangent.shape
    erows = enc_qkv.shape[0]
    drows = dec_qkv.shape[0]
    ff = enc_fc1.shape[1]
    dff = dec_fc1.shape[1]
    emb_row = jnp.pad(dec_biases[0], (0, erows - drows))
    enc_first = jnp.concatenate(
        [
            enc_qkv,
            enc_proj,
            embed,
            pack_vectors([enc_gains, enc_biases, enc_fc1_bias, emb_row], erows),
        ],
        axis=1,
    )
    dec_first = jnp.concatenate(
        [
            dec_qkv,
            dec_proj,
            pack_vectors(
                [dec_gains, dec_biases, dec_fc2_bias[None], mask_token[None], dec_fc1_bias], drows
            ),
        ],
        axis=1,
    )
    proj_at, emb_at = 3 * width, 4 * width
    vec_at = emb_at + dwidth
    dproj_at, dvec_at = 3 * dwidth, 4 * dwidth
    ecut = vec_at // 2 // LANES * LANES
    dp, fsdp = bits_of("dp"), bits_of("fsdp")
    line, core = fsdp[:-1], fsdp[-1]
    packed = erows % 8 == 0 and drows % 16 == 0
    enc_rest, dec_rest = (enc_fc1, enc_fc2), (dec_fc1, dec_fc2)
    if packed:
        enc_rest, dec_rest = ((w,) for w in pack_shards(*enc_rest, *dec_rest))
    enc_rest = [lax.all_gather(w, AXES, axis=0, tiled=True) for w in enc_rest]
    lined = gather(enc_first, line)
    one = gather(lined[..., :ecut], dp[::-1], line)
    two = gather(lined[..., ecut:], dp, line)
    enc_all = join([one, two], core)
    evecs = enc_all[:, vec_at:].T[:16].astype(F32)
    up_bias = long_vector(evecs[10:14], devices)
    emb_bias = evecs[14].reshape(devices, erows)[:, :drows].reshape(1, -1)

    dec_gather = Gather(dec_first, line + dp)
    enc_all, evecs = dec_gather.tie((enc_all, evecs))
    dec_gather.step()
    qkv = enc_qkv_call(enc_input, evecs, enc_all)
    enc_col = enc_segments.reshape(-1, 1)
    qkv = dec_gather.tie(qkv)
    dec_gather.step()
    attended, inverse, weights = attend(qkv, enc_segments, enc_col, HDIM)
    attended = dec_gather.tie(attended)
    while len(dec_gather.order) > 1:
        dec_gather.step()
    mid, enc_out, final, act, slope, embedded, down_w = enc_mid(
        enc_input,
        attended,
        evecs,
        up_bias,
        emb_bias,
        enc_all,
        enc_rest,
        proj_at,
        emb_at,
    )
    embedded = dec_gather.tie(embedded)
    emb_gather = Gather(embedded, fsdp)
    emb_gather.step()
    dec_gather.step()
    pos = positions(dec_rows, dwidth)
    dec_rest, pos, dec_gather.piece = emb_gather.tie((dec_rest, pos, dec_gather.piece))
    dec_rest = [lax.all_gather(w, AXES, axis=0, tiled=True) for w in dec_rest]
    dec_all = join([dec_gather.piece], core)
    dvecs = dec_all[:, dvec_at:].T[:16].astype(F32)
    dup_bias = long_vector(dvecs[10:14], devices)
    gathered = emb_gather.rest().reshape(-1, dwidth)
    limit = gathered.shape[0] // BLOCK
    dec_in, dqkv = dec_in_call(block_order, gathered, pos, dvecs, dec_all)
    dec_col = dec_segments.reshape(-1, 1)
    dattended, dinverse, dweights = attend(dqkv, dec_segments, dec_col, DHDIM)
    dec_out, dgmid, dgatt, dw_rest, db1, dsum_mid = dec_mid(
        dec_in,
        dattended,
        dec_cotangent,
        dinverse,
        dvecs,
        dup_bias,
        dec_all,
        dec_rest,
        dproj_at,
    )
    if not packed:
        chunks = dff // dwidth
        tall = dw_rest[:, dff + dwidth :].reshape(dwidth, chunks, dwidth).transpose(1, 0, 2)
        tall = repack_tall(tall.reshape(dff, dwidth), devices, drows)
        dw_rest = jnp.concatenate([dw_rest[:, : dff + dwidth], tall], axis=1)
    dec_own = lax.psum_scatter(dw_rest, "dp", scatter_dimension=0, tiled=True)
    dec_more = jnp.concatenate(
        [
            jnp.zeros((1, dwidth), F32),
            dsum_mid[0:1],
            jnp.zeros((3, dwidth), F32),
            dsum_mid[2:3],
            dsum_mid[1:2],
            dsum_mid[3:4],
            jnp.zeros((1, dwidth), F32),
            long_rows(db1.reshape(-1), devices, drows),
            jnp.zeros((3, dwidth), F32),
        ],
        axis=0,
    )
    dgatt, dec_more = lax.optimization_barrier((dgatt, dec_more))
    ddq, ddk, ddv = attend_back(dqkv, dattended, dgatt, dweights, dec_segments, DHDIM)
    dsum, send = dec_back(
        block_order, dec_in, ddq, ddk, ddv, dgmid, dvecs, dec_more, dec_all, limit
    )
    emb_fold = Fold([send.reshape((2,) * len(fsdp) + (enc_rows, dwidth))], fsdp[::-1], fsdp)
    emb_fold.cut()
    emb_fold.pass_on()
    dec_grads = dec_grad(dec_in, ddq, ddk, ddv, dvecs, dsum)
    dec_grads, dec_own = end_beside([emb_fold], (dec_grads, dec_own))
    dec_grads = lax.psum_scatter(dec_grads, "dp", scatter_dimension=0, tiled=True)
    for _ in line:
        one_round([emb_fold])
    elow = term_sum(emb_fold.terms, LOW)
    dpe, ew2, ew1, eb1, esum_emb, esum_mid, gmid, gatt = enc_mid_back(
        elow,
        final,
        enc_out,
        mid,
        attended,
        act,
        slope,
        inverse,
        evecs,
        enc_all,
        enc_rest[0],
        down_w,
        proj_at,
        emb_at,
    )
    gatt, dec_own, dec_grads = lax.optimization_barrier((gatt, dec_own, dec_grads))
    dec_own = jnp.concatenate([dec_own, dec_grads], axis=1)
    dec_own = lax.psum_scatter(dec_own, "fsdp", scatter_dimension=0, tiled=True)
    if not packed:
        ew2 = repack_tall(ew2, devices, erows)
    eup = Fold([by_bits(ew1)], [core] + dp)
    edown = Fold([by_bits(ew2)], [core] + dp[::-1])
    gatt = start_beside([eup, edown], gatt)
    gatt = end_beside([eup, edown], gatt)
    gatt = start_beside([eup, edown], gatt)
    emb_sum = jnp.pad(esum_emb[0].reshape(devices, drows), ((0, 0), (0, erows - drows)))
    enc_more = jnp.concatenate(
        [
            jnp.zeros((1, width), F32),
            esum_mid[3:4],
            esum_mid[0:1],
            jnp.zeros((3, width), F32),
            esum_mid[5:6],
            esum_mid[4:5],
            esum_mid[2:3],
            esum_mid[1:2],
            long_rows(eb1.reshape(-1), devices, erows),
            emb_sum.reshape(1, -1),
            jnp.zeros((1, width), F32),
        ],
        axis=0,
    )
    dq, dk, dv = attend_back(qkv, attended, gatt, weights, enc_segments, HDIM)
    enc_grads, enc_in_grad = enc_qkv_back(
        enc_input, dq, dk, dv, gmid, evecs, enc_more, dpe, enc_all
    )
    chip = Fold([by_bits(enc_grads)], [core])
    chip.cut()
    chip.send, dec_own = end_beside([eup, edown], (chip.send, dec_own))
    chip.pass_on()
    while eup.order:
        one_round([eup, edown, chip] if chip.order else [eup, edown])
    end_beside([chip], ())
    gcut = enc_grads.shape[1] // 2 // LANES * LANES
    one = Fold([t[..., :gcut] for t in chip.terms], dp, all_bits()[:-1])
    two = Fold([t[..., gcut:] for t in chip.terms], dp[::-1], all_bits()[:-1])
    rest = joined([eup, edown], line)
    while one.order:
        one_round([one, two] + ([rest] if rest.order else []))
    first = joined([one, two], line)
    while first.order or rest.order:
        one_round([f for f in (first, rest) if f.order])
    eu, ed = split_columns(term_sum(rest.terms, F32), [ff, ff])
    ed = unpack_tall(ed, 1, width)
    eq, ep, em, ev = split_columns(term_sum(first.terms, F32), [3 * width, width, dwidth, LANES])
    ru, rp, rd, rq, rv = split_columns(
        dec_own.astype(F32), [dff, dwidth, dff, 3 * dwidth, LANES]
    )
    rd = unpack_tall(rd, 1, dwidth)
    rv = rv.T
    ev = ev.T
    return (
        dec_out,
        enc_in_grad,
        eq,
        ep,
        eu,
        ed,
        ev[:3],
        ev[3:10],
        ev[10:14].reshape(-1),
        em,
        rv[8],
        rq,
        rp,
        ru,
        rd,
        rv[:2],
        jnp.concatenate([ev[14:15, :drows], rv[2:7]], axis=0),
        rv[9:13].reshape(-1),
        rv[7],
    )


def solution(mesh):
    in_specs = (
        P(("dp", "fsdp"), None),
        P(("dp", "fsdp"), None),
        P(("dp", "fsdp"), None),
        P("dp", "fsdp"),
        P(("dp", "fsdp"), None),
        P(("dp", "fsdp"), None),
        P(("dp", "fsdp"), None),
        P(("dp", "fsdp"), None),
        P(("dp", "fsdp"), None),
        P(None, ("dp", "fsdp")),
        P(None, ("dp", "fsdp")),
        P(("dp", "fsdp")),
        P(("dp", "fsdp"), None),
        P(("dp", "fsdp")),
        P(("dp", "fsdp"), None),
        P(("dp", "fsdp"), None),
        P(("dp", "fsdp"), None),
        P(("dp", "fsdp"), None),
        P(None, ("dp", "fsdp")),
        P(None, ("dp", "fsdp")),
        P(("dp", "fsdp")),
        P(("dp", "fsdp")),
    )
    out_specs = (
        P(("dp", "fsdp"), None),
        P(("dp", "fsdp"), None),
        P(("dp", "fsdp"), None),
        P(("dp", "fsdp"), None),
        P(("dp", "fsdp"), None),
        P(("dp", "fsdp"), None),
        P(None, ("dp", "fsdp")),
        P(None, ("dp", "fsdp")),
        P(("dp", "fsdp")),
        P(("dp", "fsdp"), None),
        P(("dp", "fsdp")),
        P(("dp", "fsdp"), None),
        P(("dp", "fsdp"), None),
        P(("dp", "fsdp"), None),
        P(("dp", "fsdp"), None),
        P(None, ("dp", "fsdp")),
        P(None, ("dp", "fsdp")),
        P(("dp", "fsdp")),
        P(("dp", "fsdp")),
    )
    return jax.shard_map(
        per_device, mesh=mesh, in_specs=in_specs, out_specs=out_specs, check_vma=False
    )
```

```python
import functools
import math

import jax
import jax.numpy as jnp
from jax import lax
from jax.experimental import pallas as pl
from jax.experimental.pallas import tpu as pltpu
from jax.sharding import PartitionSpec as P

HDIM = 64
DHDIM = 32
BLOCK = 128
LANES = 128
TILE = 256
EPSILON = 1e-06
NEGATIVE = -1e30
LOG2E = math.log2(math.e)
AXES = ("dp", "fsdp")
F32 = jnp.float32
LOW = jnp.bfloat16
PARAMS = pltpu.CompilerParams(vmem_limit_bytes=56 * 1024 * 1024)


def mm(left, right):
    return jnp.dot(left, right, preferred_element_type=F32)


def mm_tn(left, right):
    return lax.dot_general(left, right, (((0,), (0,)), ((), ())), preferred_element_type=F32)


def mm_nt(left, right):
    return lax.dot_general(left, right, (((1,), (1,)), ((), ())), preferred_element_type=F32)


def col_sum(values):
    return jnp.sum(values, axis=0, keepdims=True)


def norm_parts(values):
    centred = values - jnp.mean(values, axis=-1, keepdims=True)
    variance = jnp.mean(centred * centred, axis=-1, keepdims=True)
    scale = lax.rsqrt(variance + EPSILON)
    return centred * scale, scale


def norm_back(grad, unit, scale, gain):
    inner = grad * gain
    mean_inner = jnp.mean(inner, axis=-1, keepdims=True)
    mean_cross = jnp.mean(inner * unit, axis=-1, keepdims=True)
    return scale * (inner - mean_inner - unit * mean_cross)


def gelu_parts(hidden):
    cdf = 0.5 + 0.5 * lax.erf(hidden * (0.5**0.5))
    density = jnp.exp(hidden * hidden * -0.5) * (1.0 / math.sqrt(2.0 * math.pi))
    return hidden * cdf, cdf + hidden * density


CHEAP = pl.CostEstimate(flops=1 << 20, bytes_accessed=1 << 16, transcendentals=0)


def full(shape):
    return pl.BlockSpec(shape, lambda *_: (0,) * len(shape))


def at_col(rows, cols, index):
    return pl.BlockSpec((rows, cols), lambda *_: (0, index))


def shape(dims, kind):
    return jax.ShapeDtypeStruct(dims, kind)


def lane_mask(head, head_dim, kind):
    lane = lax.broadcasted_iota(jnp.int32, (1, LANES), 1)
    inside = (lane >= head * head_dim) & (lane < (head + 1) * head_dim)
    return inside.astype(F32).astype(kind)


def stack_heads(stacked, index, rows, head_dim):
    for h in range(LANES // head_dim):
        stacked[index, h * TILE : (h + 1) * TILE, :] = rows * lane_mask(h, head_dim, LOW)


def tile_range(seg_ref, here, tiles):
    first = seg_ref[0, here * TILE]
    last = seg_ref[0, here * TILE + TILE - 1]
    low = jnp.int32(0)
    high = jnp.int32(tiles)
    for other in range(tiles):
        low += (seg_ref[0, other * TILE + TILE - 1] < first).astype(jnp.int32)
        high -= (seg_ref[0, other * TILE] > last).astype(jnp.int32)
    return low, high


def attend_kernel(
    head_dim,
    tiles,
    seg_ref,
    q_ref,
    k_ref,
    v_ref,
    row_ref,
    col_ref,
    out_ref,
    inv_ref,
    exp_ref,
    km,
    vt,
    held,
    acc,
    top,
    tot,
):
    heads = LANES // head_dim
    here = pl.program_id(1)
    factor = head_dim ** (-0.5) * LOG2E

    @pl.when(here == 0)
    def _():
        for u in range(tiles):
            rows = slice(u * TILE, (u + 1) * TILE)
            vt[u] = v_ref[rows, :].astype(F32).T.astype(LOW)
            stack_heads(km, u, k_ref[rows, :], head_dim)

    acc[...] = jnp.zeros_like(acc)
    top[...] = jnp.full_like(top, NEGATIVE)
    tot[...] = jnp.zeros_like(tot)
    query = q_ref[...]
    row = row_ref[...]

    def score(u, carry):
        start = pl.multiple_of(u * TILE, TILE)
        same = col_ref[pl.ds(start, TILE), :] == row
        every = mm_nt(km[u], query)
        for h in range(heads):
            scores = jnp.where(same, every[h * TILE : (h + 1) * TILE, :], NEGATIVE)
            held[u, h] = scores
            top[h : h + 1, :] = jnp.maximum(
                top[h : h + 1, :], jnp.max(scores, axis=0, keepdims=True)
            )
        return carry

    def mix(u, carry):
        for h in range(heads):
            weights = jnp.exp2((held[u, h] - top[h : h + 1, :]) * factor)
            tot[h : h + 1, :] += col_sum(weights)
            span = slice(h * head_dim, (h + 1) * head_dim)
            weights = weights.astype(LOW)
            exp_ref[0, 0, u, :, h * TILE : (h + 1) * TILE] = weights
            acc[span, :] += mm(vt[u, span, :], weights)
        return carry

    low, high = tile_range(seg_ref, here, tiles)
    lax.fori_loop(low, high, score, 0)
    lax.fori_loop(low, high, mix, 0)
    for h in range(heads):
        span = slice(h * head_dim, (h + 1) * head_dim)
        inverse = jnp.broadcast_to(1.0 / tot[h : h + 1, :], (head_dim, TILE))
        acc[span, :] = acc[span, :] * inverse
        held[0, 0, span, :] = inverse
    out_ref[...] = acc[...].T.astype(LOW)
    inv_ref[...] = held[0, 0, :LANES, :].T


def attend(qkv, segments, seg_col, head_dim):
    rows, width = qkv.shape[0], qkv.shape[1] // 3
    groups, tiles, heads = width // LANES, rows // TILE, LANES // head_dim
    return pl.pallas_call(
        functools.partial(attend_kernel, head_dim, tiles),
        grid_spec=pltpu.PrefetchScalarGridSpec(
            num_scalar_prefetch=1,
            grid=(groups, tiles),
            in_specs=[
                pl.BlockSpec((TILE, LANES), lambda g, t, s: (t, g)),
                pl.BlockSpec((rows, LANES), lambda g, t, s: (0, groups + g)),
                pl.BlockSpec((rows, LANES), lambda g, t, s: (0, 2 * groups + g)),
                pl.BlockSpec((1, TILE), lambda g, t, s: (0, t)),
                pl.BlockSpec((rows, 1), lambda g, t, s: (0, 0)),
            ],
            out_specs=[
                pl.BlockSpec((TILE, LANES), lambda g, t, s: (t, g)),
                pl.BlockSpec((TILE, LANES), lambda g, t, s: (t, g)),
                pl.BlockSpec((1, 1, tiles, TILE, heads * TILE), lambda g, t, s: (g, t, 0, 0, 0)),
            ],
            scratch_shapes=[
                pltpu.VMEM((tiles, heads * TILE, LANES), LOW),
                pltpu.VMEM((tiles, LANES, TILE), LOW),
                pltpu.VMEM((tiles, heads, TILE, TILE), F32),
                pltpu.VMEM((LANES, TILE), F32),
                pltpu.VMEM((8, TILE), F32),
                pltpu.VMEM((8, TILE), F32),
            ],
        ),
        out_shape=[
            shape((rows, width), LOW),
            shape((rows, width), F32),
            shape((groups, tiles, tiles, TILE, heads * TILE), LOW),
        ],
        compiler_params=PARAMS,
        cost_estimate=CHEAP,
        name="attend",
    )(segments, qkv, qkv, qkv, segments, seg_col)


def attend_back_kernel(
    head_dim,
    tiles,
    seg_ref,
    q_ref,
    k_ref,
    v_ref,
    o_ref,
    g_ref,
    exp_ref,
    dq_ref,
    dk_ref,
    dv_ref,
    qm,
    gm,
    vm,
    dqt,
    delta,
    dk_acc,
    dv_acc,
):
    heads = LANES // head_dim
    here = pl.program_id(1)
    scale = head_dim ** (-0.5)

    @pl.when(here == 0)
    def _():
        dqt[...] = jnp.zeros_like(dqt)
        for t in range(tiles):
            rows = slice(t * TILE, (t + 1) * TILE)
            stack_heads(qm, t, q_ref[rows, :], head_dim)
            stack_heads(gm, t, g_ref[rows, :], head_dim)
            both = (g_ref[rows, :].astype(F32) * o_ref[rows, :].astype(F32)).T
            for h in range(heads):
                delta[t, h : h + 1, :] = col_sum(both[h * head_dim : (h + 1) * head_dim, :])

    keys_t = k_ref[...].astype(F32).T.astype(LOW)
    stack_heads(vm, 0, v_ref[...], head_dim)
    dk_acc[...] = jnp.zeros_like(dk_acc)
    dv_acc[...] = jnp.zeros_like(dv_acc)

    def step(t, carry):
        start = pl.multiple_of(t * TILE, TILE)
        every = mm_nt(vm[0], g_ref[pl.ds(start, TILE), :])
        dv_acc[...] += mm(exp_ref[0, t, 0], gm[t])
        pieces = []
        for h in range(heads):
            grad_probs = every[h * TILE : (h + 1) * TILE, :] - delta[t, h : h + 1, :]
            weights = exp_ref[0, t, 0, :, h * TILE : (h + 1) * TILE]
            pieces.append((weights.astype(F32) * grad_probs).astype(LOW))
        for h in range(heads):
            span = slice(h * head_dim, (h + 1) * head_dim)
            dqt[t, span, :] += mm(keys_t[span, :], pieces[h])
        dk_acc[...] += mm(jnp.concatenate(pieces, axis=1), qm[t])
        return carry

    low, high = tile_range(seg_ref, here, tiles)
    lax.fori_loop(low, high, step, 0)
    dk_ref[...] = (dk_acc[...] * scale).astype(LOW)
    dv_ref[...] = dv_acc[...].astype(LOW)

    @pl.when(here == tiles - 1)
    def _():
        for t in range(tiles):
            dq_ref[t * TILE : (t + 1) * TILE, :] = (dqt[t] * scale).T.astype(LOW)


def attend_back(qkv, attended, grad, weights, segments, head_dim):
    rows, width = attended.shape
    groups, tiles, heads = width // LANES, rows // TILE, LANES // head_dim
    whole = pl.BlockSpec((rows, LANES), lambda g, u, s: (0, g))
    piece = pl.BlockSpec((TILE, LANES), lambda g, u, s: (u, g))
    return pl.pallas_call(
        functools.partial(attend_back_kernel, head_dim, tiles),
        grid_spec=pltpu.PrefetchScalarGridSpec(
            num_scalar_prefetch=1,
            grid=(groups, tiles),
            in_specs=[
                whole,
                pl.BlockSpec((TILE, LANES), lambda g, u, s: (u, groups + g)),
                pl.BlockSpec((TILE, LANES), lambda g, u, s: (u, 2 * groups + g)),
                whole,
                whole,
                pl.BlockSpec((1, tiles, 1, TILE, heads * TILE), lambda g, u, s: (g, 0, u, 0, 0)),
            ],
            out_specs=[whole, piece, piece],
            scratch_shapes=[
                pltpu.VMEM((tiles, heads * TILE, LANES), LOW),
                pltpu.VMEM((tiles, heads * TILE, LANES), LOW),
                pltpu.VMEM((1, heads * TILE, LANES), LOW),
                pltpu.VMEM((tiles, LANES, TILE), F32),
                pltpu.VMEM((tiles, 8, TILE), F32),
                pltpu.VMEM((TILE, LANES), F32),
                pltpu.VMEM((TILE, LANES), F32),
            ],
        ),
        out_shape=[shape((rows, width), LOW)] * 3,
        compiler_params=PARAMS,
        cost_estimate=CHEAP,
        name="attend_back",
    )(segments, qkv, qkv, qkv, attended, grad, weights)


def pack_kernel(up_ref, down_ref, proj_ref, embed_ref, dup_ref, ddown_ref, out_ref, dout_ref):
    for up, down, out in ((up_ref, down_ref, out_ref), (dup_ref, ddown_ref, dout_ref)):
        rows, cols = up.shape
        out[:, :cols] = up[...]
        wide = down[...].astype(F32)
        width = down.shape[1]
        for part in range(4):
            piece = wide[part * rows : (part + 1) * rows, :].astype(LOW)
            out[:, cols + part * width : cols + (part + 1) * width] = piece
    at = 2 * up_ref.shape[1]
    width, emb_width = proj_ref.shape[1], embed_ref.shape[1]
    out_ref[:, at : at + width] = proj_ref[...]
    out_ref[:, at + width :] = jnp.zeros((out_ref.shape[0], out_ref.shape[1] - at - width), LOW)
    out_ref[:, out_ref.shape[1] - emb_width :] = embed_ref[...]


def gap_of(width, emb_width):
    return -width % emb_width


def pack_shards(up, down, proj, embed, dup, ddown):
    rows, cols = up.shape
    more = proj.shape[1] + gap_of(proj.shape[1], embed.shape[1]) + embed.shape[1]
    ins = (up, down, proj, embed, dup, ddown)
    outs = [shape((rows, 2 * cols + more), LOW), shape((dup.shape[0], 2 * dup.shape[1]), LOW)]
    return pl.pallas_call(
        pack_kernel,
        in_specs=[full(s.shape) for s in ins],
        out_specs=[full(o.shape) for o in outs],
        out_shape=outs,
        grid=(1,),
        compiler_params=PARAMS,
        cost_estimate=CHEAP,
        name="pack",
    )(*ins)


def by_core(grads, group):
    pairs = grads.reshape(-1, 2, group, grads.shape[1])
    return pairs[:, 0], pairs[:, 1]


def natural_rows(block, group, kind):
    width = block.shape[1] // 4
    parts = [
        block[:, i * width : (i + 1) * width].astype(kind).reshape(-1, group, width)
        for i in range(4)
    ]
    return jnp.stack(parts, axis=1).reshape(-1, width).astype(LOW)


def enc_qkv_kernel(x_ref, vec_ref, w_ref, out_ref, normed):
    part = pl.program_id(0)

    @pl.when(part == 0)
    def _():
        unit, _ = norm_parts(x_ref[...].astype(F32))
        normed[...] = (unit * vec_ref[0:1, :] + vec_ref[3:4, :]).astype(LOW)

    bias = jnp.where(part == 0, vec_ref[4:5, :], jnp.where(part == 2, vec_ref[5:6, :], 0.0))
    out_ref[...] = (mm(normed[...], w_ref[...]) + bias).astype(LOW)


def enc_qkv_call(rows_in, vecs, weight):
    rows, width = rows_in.shape
    return pl.pallas_call(
        enc_qkv_kernel,
        grid=(3,),
        in_specs=[
            full((rows, width)),
            full(vecs.shape),
            pl.BlockSpec((width, width), lambda i: (0, i)),
        ],
        out_specs=pl.BlockSpec((rows, width), lambda i: (0, i)),
        out_shape=shape((rows, 3 * width), LOW),
        scratch_shapes=[pltpu.VMEM((rows, width), LOW)],
        compiler_params=PARAMS,
        cost_estimate=CHEAP,
        name="enc_qkv",
    )(rows_in, vecs, weight)


def enc_mid_kernel(
    chunks,
    packed,
    x_ref,
    att_ref,
    vec_ref,
    b1_ref,
    eb_ref,
    wo_ref,
    we_ref,
    *refs,
):
    up_ref, down_ref, *refs = refs
    mid_ref, out_ref, final_ref, act_ref, slope_ref, emb_ref, *refs = refs
    naturals, (normed, acc) = refs[:-2], refs[-2:]
    part = pl.program_id(0)

    @pl.when(part == 0)
    def _():
        middle = x_ref[...].astype(F32) + mm(att_ref[...], wo_ref[...]) + vec_ref[6:7, :]
        mid_ref[...] = middle
        unit, _ = norm_parts(middle)
        normed[...] = (unit * vec_ref[1:2, :] + vec_ref[7:8, :]).astype(LOW)
        acc[...] = middle + vec_ref[8:9, :]

    down = down_ref[...]
    if packed:
        down = natural_rows(down, packed, F32)
        naturals[0][...] = down
    hidden = mm(normed[...], up_ref[...]) + b1_ref[...]
    value, slope = gelu_parts(hidden)
    value = value.astype(LOW)
    act_ref[...] = value
    slope_ref[...] = slope
    acc[...] += mm(value, down)

    @pl.when(part == chunks - 1)
    def _():
        result = acc[...]
        out_ref[...] = result
        unit, _ = norm_parts(result)
        final = (unit * vec_ref[2:3, :] + vec_ref[9:10, :]).astype(LOW)
        final_ref[...] = final
        emb_ref[...] = (mm(final, we_ref[...]) + eb_ref[...]).astype(LOW)


def enc_mid(rows_in, attended, vecs, up_bias, emb_bias, wide, weights, proj_at, emb_at):
    rows, width = rows_in.shape
    hidden = up_bias.shape[1]
    emb_width = emb_bias.shape[1]
    chunks = hidden // width
    by_row = pl.BlockSpec((width, width), lambda i: (i, 0))
    specs = [pl.BlockSpec((width, width), lambda i: (0, i))]
    if len(weights) == 1:
        packed = width // (lax.axis_size("dp") * lax.axis_size("fsdp"))
        specs.append(pl.BlockSpec((width // 4, hidden), lambda i: (i, 1)))
        operands = [weights[0]] * 2
        natural_specs, natural_shapes = [by_row], [shape((hidden, width), LOW)]
    else:
        packed = 0
        specs.append(by_row)
        operands, natural_specs, natural_shapes = list(weights), [], []
    outs = pl.pallas_call(
        functools.partial(enc_mid_kernel, chunks, packed),
        grid=(chunks,),
        in_specs=[
            full((rows, width)),
            full((rows, width)),
            full(vecs.shape),
            pl.BlockSpec((1, width), lambda i: (0, i)),
            full((1, emb_width)),
            at_col(width, width, proj_at // width),
            at_col(width, emb_width, emb_at // emb_width),
        ]
        + specs,
        out_specs=[
            full((rows, width)),
            full((rows, width)),
            full((rows, width)),
            pl.BlockSpec((rows, width), lambda i: (0, i)),
            pl.BlockSpec((rows, width), lambda i: (0, i)),
            full((rows, emb_width)),
        ]
        + natural_specs,
        out_shape=[
            shape((rows, width), F32),
            shape((rows, width), F32),
            shape((rows, width), LOW),
            shape((rows, hidden), LOW),
            shape((rows, hidden), F32),
            shape((rows, emb_width), LOW),
        ]
        + natural_shapes,
        scratch_shapes=[pltpu.VMEM((rows, width), LOW), pltpu.VMEM((rows, width), F32)],
        compiler_params=PARAMS,
        cost_estimate=CHEAP,
        name="enc_mid",
    )(rows_in, attended, vecs, up_bias, emb_bias, wide, wide, *operands)
    return outs if packed else list(outs) + [weights[1]]


def enc_mid_back_kernel(
    chunks,
    packed,
    core_ref,
    elow_ref,
    final_ref,
    out_ref,
    mid_ref,
    att_ref,
    act_ref,
    slope_ref,
    vec_ref,
    wo_ref,
    w1_ref,
    w2_ref,
    we_ref,
    inv_ref,
    dpe_ref,
    *refs,
):
    if packed:
        keep2_ref, send2_ref, keep1_ref, send1_ref, *refs = refs
    else:
        dw2_ref, dw1_ref, *refs = refs
    (
        db1_ref,
    esum_ref,
    sum_ref,
    gmid_ref,
    gatt_ref,
    grad,
    grad_low,
    unit_two,
    scale_two,
    normed,
        dnorm,
    ) = refs
    first = core_ref[0] == 0
    part = pl.program_id(0)

    @pl.when(part == 0)
    def _():
        elow = elow_ref[...]
        width = final_ref.shape[1]
        dpe_ref[:, width:] = mm_tn(final_ref[...], elow).astype(LOW)
        esum_ref[...] = jnp.zeros_like(esum_ref)
        esum_ref[0:1, :] = col_sum(elow.astype(F32))
        unit, scale = norm_parts(out_ref[...])
        dfinal = mm_nt(elow, we_ref[...])
        sum_ref[...] = jnp.zeros_like(sum_ref)
        sum_ref[0:1, :] = col_sum(dfinal * unit)
        sum_ref[1:2, :] = col_sum(dfinal)
        total = norm_back(dfinal, unit, scale, vec_ref[2:3, :])
        grad[...] = total
        low = total.astype(LOW)
        grad_low[...] = low
        sum_ref[2:3, :] = col_sum(low.astype(F32))
        unit, scale = norm_parts(mid_ref[...])
        unit_two[...] = unit
        scale_two[...] = jnp.broadcast_to(scale, scale_two.shape)
        normed[...] = (unit * vec_ref[1:2, :] + vec_ref[7:8, :]).T.astype(LOW)
        dnorm[...] = jnp.zeros_like(dnorm)

    low = grad_low[...]
    down = mm_tn(act_ref[...], low)
    if packed:
        width = low.shape[1]
        down = down.reshape(-1, 4, packed, width)
        for i in range(4):
            zero, one = by_core(down[:, i].reshape(-1, width), packed)
            cols = slice(i * width, (i + 1) * width)
            keep2_ref[:, :, cols] = jnp.where(first, zero, one).astype(LOW)
            send2_ref[:, :, cols] = jnp.where(first, one, zero).astype(LOW)
    else:
        dw2_ref[...] = down.astype(LOW)
    dhid = (slope_ref[...] * mm_nt(low, w2_ref[...])).astype(LOW)
    up = mm(normed[...], dhid)
    if packed:
        zero, one = by_core(up, packed)
        keep1_ref[...] = jnp.where(first, zero, one).astype(LOW)
        send1_ref[...] = jnp.where(first, one, zero).astype(LOW)
    else:
        dw1_ref[...] = up.astype(LOW)
    db1_ref[...] = col_sum(dhid.astype(F32))
    dnorm[...] += mm_nt(dhid, w1_ref[...])

    @pl.when(part == chunks - 1)
    def _():
        dn = dnorm[...]
        unit = unit_two[...]
        sum_ref[3:4, :] = col_sum(dn * unit)
        sum_ref[4:5, :] = col_sum(dn)
        gmid = grad[...] + norm_back(dn, unit, scale_two[:, 0:1], vec_ref[1:2, :])
        gmid_ref[...] = gmid
        mlow = gmid.astype(LOW)
        sum_ref[5:6, :] = col_sum(mlow.astype(F32))
        dpe_ref[:, : mlow.shape[1]] = mm_tn(att_ref[...], mlow).astype(LOW)
        gatt_ref[...] = (mm_nt(mlow, wo_ref[...]) * inv_ref[...]).astype(LOW)


def enc_mid_back(
    core, elow, final, out, mid, attended, act, slope, inverse, vecs, wide, up_w, down_w, proj_at, emb_at
):
    rows, width = mid.shape
    hidden = down_w.shape[0]
    emb_width = elow.shape[1]
    chunks = hidden // width
    packed = width // (lax.axis_size("dp") * lax.axis_size("fsdp"))
    packed = packed if packed % 8 == 0 else 0
    by_col = pl.BlockSpec((rows, width), lambda i: (0, i))
    if packed:
        chips = width // packed // 2
        two = pl.BlockSpec((chips // chunks, packed, hidden), lambda i: (i, 0, 0))
        one = pl.BlockSpec((chips, packed, width), lambda i: (0, 0, i))
        specs = [two, two, one, one]
        shapes = [shape((chips, packed, hidden), LOW)] * 4
    else:
        specs = [
            pl.BlockSpec((width, width), lambda i: (i, 0)),
            pl.BlockSpec((width, width), lambda i: (0, i)),
        ]
        shapes = [shape((hidden, width), LOW), shape((width, hidden), LOW)]
    return pl.pallas_call(
        functools.partial(enc_mid_back_kernel, chunks, packed),
        grid=(chunks,),
        in_specs=[
            pl.BlockSpec(memory_space=pltpu.SMEM),
            full((rows, emb_width)),
            full((rows, width)),
            full((rows, width)),
            full((rows, width)),
            full((rows, width)),
            by_col,
            by_col,
            full(vecs.shape),
            at_col(width, width, proj_at // width),
            pl.BlockSpec((width, width), lambda i: (0, i)),
            pl.BlockSpec((width, width), lambda i: (i, 0)),
            at_col(width, emb_width, emb_at // emb_width),
            full((rows, width)),
        ],
        out_specs=[
            full((width, width + emb_width)),
            *specs,
            pl.BlockSpec((1, width), lambda i: (0, i)),
            full((8, emb_width)),
            full((8, width)),
            full((rows, width)),
            full((rows, width)),
        ],
        out_shape=[
            shape((width, width + emb_width), LOW),
            *shapes,
            shape((1, hidden), F32),
            shape((8, emb_width), F32),
            shape((8, width), F32),
            shape((rows, width), F32),
            shape((rows, width), LOW),
        ],
        scratch_shapes=[
            pltpu.VMEM((rows, width), F32),
            pltpu.VMEM((rows, width), LOW),
            pltpu.VMEM((rows, width), F32),
            pltpu.VMEM((rows, LANES), F32),
            pltpu.VMEM((width, rows), LOW),
            pltpu.VMEM((rows, width), F32),
        ],
        compiler_params=PARAMS,
        cost_estimate=CHEAP,
        name="enc_mid_back",
    )(core, elow, final, out, mid, attended, act, slope, vecs, wide, up_w, down_w, wide, inverse)


def enc_qkv_back_kernel(
    packed,
    core_ref,
    x_ref,
    dq_ref,
    dk_ref,
    dv_ref,
    gmid_ref,
    vec_ref,
    more_ref,
    dpe_ref,
    w_ref,
    din_ref,
    *refs,
):
    outs, sums = refs[:-1], refs[-1]
    first = core_ref[0] == 0
    width = x_ref.shape[1]

    def put(cols, grads):
        if packed:
            zero, one = by_core(grads, packed)
            outs[0][:, :, cols] = jnp.where(first, zero, one).astype(LOW)
            outs[1][:, :, cols] = jnp.where(first, one, zero).astype(LOW)
        else:
            outs[0][:, cols] = grads.astype(LOW)

    unit, scale = norm_parts(x_ref[...].astype(F32))
    normed = (unit * vec_ref[0:1, :] + vec_ref[3:4, :]).astype(LOW)
    grads = jnp.concatenate([dq_ref[...], dk_ref[...], dv_ref[...]], axis=1)
    put(slice(0, 3 * width), mm_tn(normed, grads))
    end = 3 * width + dpe_ref.shape[1]
    put(slice(3 * width, end), dpe_ref[...].astype(F32))
    dn = mm_nt(grads, w_ref[...])
    sums[...] = jnp.zeros_like(sums)
    sums[0:16, :] = more_ref[...]
    sums[0:1, :] = col_sum(dn * unit)
    sums[3:4, :] = col_sum(dn)
    sums[4:5, :] = col_sum(dq_ref[...].astype(F32))
    sums[5:6, :] = col_sum(dv_ref[...].astype(F32))
    put(slice(end, end + LANES), sums[...].T)
    din = gmid_ref[...] + norm_back(dn, unit, scale, vec_ref[0:1, :])
    din_ref[...] = din.astype(LOW)


def enc_qkv_back(core, rows_in, dq, dk, dv, gmid, vecs, more, dpe, weight):
    rows, width = rows_in.shape
    whole = full((rows, width))
    cols = 3 * width + dpe.shape[1] + LANES
    packed = width // (lax.axis_size("dp") * lax.axis_size("fsdp"))
    packed = packed if packed % 8 == 0 else 0
    outs = [(width // packed // 2, packed, cols)] * 2 if packed else [(width, cols)]
    return pl.pallas_call(
        functools.partial(enc_qkv_back_kernel, packed),
        grid=(1,),
        in_specs=[pl.BlockSpec(memory_space=pltpu.SMEM)]
        + [whole] * 5
        + [full(vecs.shape), full((16, width)), full(dpe.shape), at_col(width, 3 * width, 0)],
        out_specs=[whole] + [full(o) for o in outs],
        out_shape=[shape((rows, width), LOW)] + [shape(o, LOW) for o in outs],
        scratch_shapes=[pltpu.VMEM((LANES, width), F32)],
        compiler_params=PARAMS,
        cost_estimate=CHEAP,
        name="enc_qkv_back",
    )(core, rows_in, dq, dk, dv, gmid, vecs, more, dpe, weight)


def dec_in_kernel(limit, order_ref, one_ref, two_ref, pos_ref, vec_ref, w_ref, in_ref, qkv_ref):
    step = pl.program_id(0)
    width = in_ref.shape[1]
    for half, ref in enumerate((one_ref, two_ref)):
        visible = order_ref[0, 2 * step + half] < limit
        rows = slice(half * BLOCK, (half + 1) * BLOCK)
        in_ref[rows, :] = (
            jnp.where(visible, ref[...].astype(F32), vec_ref[9:10, :]) + pos_ref[rows, :]
        )
    unit, _ = norm_parts(in_ref[...])
    normed = (unit * vec_ref[0:1, :] + vec_ref[3:4, :]).astype(LOW)
    qkv = mm(normed, w_ref[...])
    qkv_ref[:, :width] = (qkv[:, :width] + vec_ref[4:5, :]).astype(LOW)
    qkv_ref[:, width : 2 * width] = qkv[:, width : 2 * width].astype(LOW)
    qkv_ref[:, 2 * width :] = (qkv[:, 2 * width :] + vec_ref[5:6, :]).astype(LOW)


def dec_in_call(order, gathered, pos, vecs, weight):
    rows, width = pos.shape
    limit = gathered.shape[0] // BLOCK

    def chosen(half):
        def index(i, order_ref):
            return (jnp.clip(order_ref[0, 2 * i + half], 0, limit - 1), 0)

        return pl.BlockSpec((BLOCK, width), index)

    return pl.pallas_call(
        functools.partial(dec_in_kernel, limit),
        grid_spec=pltpu.PrefetchScalarGridSpec(
            num_scalar_prefetch=1,
            grid=(rows // TILE,),
            in_specs=[
                chosen(0),
                chosen(1),
                pl.BlockSpec((TILE, width), lambda i, o: (i, 0)),
                full(vecs.shape),
                at_col(width, 3 * width, 0),
            ],
            out_specs=[
                pl.BlockSpec((TILE, width), lambda i, o: (i, 0)),
                pl.BlockSpec((TILE, 3 * width), lambda i, o: (i, 0)),
            ],
        ),
        out_shape=[shape((rows, width), F32), shape((rows, 3 * width), LOW)],
        compiler_params=PARAMS,
        cost_estimate=CHEAP,
        name="dec_in",
    )(order, gathered, gathered, pos, vecs, weight)


def dec_mid_kernel(
    steps,
    chunks,
    packed,
    x_ref,
    att_ref,
    cot_ref,
    inv_ref,
    vec_ref,
    b1_ref,
    wo_ref,
    up_ref,
    down_ref,
    out_ref,
    gmid_ref,
    gatt_ref,
    dw_ref,
    db1_ref,
    sum_ref,
    aw1,
    aw2,
    acc,
    dnorm,
    turned,
):
    step = pl.program_id(0)
    width = x_ref.shape[1]
    hidden = chunks * width
    lead = width // 4

    @pl.when(step == 0)
    def _():
        aw1[...] = jnp.zeros_like(aw1)
        aw2[...] = jnp.zeros_like(aw2)
        db1_ref[...] = jnp.zeros_like(db1_ref)
        sum_ref[...] = jnp.zeros_like(sum_ref)

    att = att_ref[...]
    low = cot_ref[...]
    middle = x_ref[...] + mm(att, wo_ref[...]) + vec_ref[6:7, :]
    unit, scale = norm_parts(middle)
    normed = unit * vec_ref[1:2, :] + vec_ref[7:8, :]
    turned[...] = normed.T.astype(LOW)
    normed = normed.astype(LOW)
    acc[...] = middle + vec_ref[8:9, :]
    dnorm[...] = jnp.zeros_like(dnorm)

    def chunk(j, carry):
        cols = pl.ds(pl.multiple_of(j * width, width), width)
        some = pl.ds(pl.multiple_of(j * lead, lead), lead)
        up = up_ref[:, cols]
        down = natural_rows(down_ref[some, :], packed, LOW) if packed else down_ref[cols, :]
        value, slope = gelu_parts(mm(normed, up) + b1_ref[j])
        value = value.astype(LOW)
        acc[...] += mm(value, down)
        grad = mm_tn(value, low)
        if packed:
            grad = grad.reshape(-1, 4, packed, width)
            for part in range(4):
                piece = grad[:, part].reshape(lead, width)
                aw2[some, part * width : (part + 1) * width] += piece
        else:
            aw2[cols, :] += grad
        dhid = (slope * mm_nt(low, down)).astype(LOW)
        aw1[:, cols] += mm(turned[...], dhid)
        db1_ref[j] += col_sum(dhid.astype(F32))
        dnorm[...] += mm_nt(dhid, up)
        return carry

    lax.fori_loop(0, chunks, chunk, 0, unroll=2)
    out_ref[...] = acc[...].astype(LOW)
    dn = dnorm[...]
    sum_ref[0:1, :] += col_sum(dn * unit)
    sum_ref[1:2, :] += col_sum(dn)
    gmid = low.astype(F32) + norm_back(dn, unit, scale, vec_ref[1:2, :])
    gmid_ref[...] = gmid
    mlow = gmid.astype(LOW)
    sum_ref[2:3, :] += col_sum(mlow.astype(F32))
    sum_ref[3:4, :] += col_sum(low.astype(F32))
    aw1[:, hidden:] += mm_tn(att, mlow)
    gatt_ref[...] = (mm_nt(mlow, wo_ref[...]) * inv_ref[...]).astype(LOW)

    @pl.when(step == steps - 1)
    def _():
        dw_ref[:, : hidden + width] = aw1[...].astype(LOW)
        if packed:
            dw_ref[:, hidden + width :] = aw2[...].astype(LOW)
        else:
            for c in range(chunks):
                col = hidden + (1 + c) * width
                dw_ref[:, col : col + width] = aw2[c * width : (c + 1) * width, :].astype(LOW)


def dec_mid(dec_in, attended, cotangent, inverse, vecs, up_bias, wide, weights, proj_at):
    rows, width = dec_in.shape
    hidden = up_bias.shape[1]
    chunks = hidden // width
    tile = 2 * TILE
    steps = rows // tile
    by_row = pl.BlockSpec((tile, width), lambda i: (i, 0))
    if len(weights) == 1:
        packed = width // (lax.axis_size("dp") * lax.axis_size("fsdp"))
        down_shape = (width, hidden)
        specs, operands = [at_col(width, hidden, 0), at_col(width, hidden, 1)], [weights[0]] * 2
    else:
        packed, down_shape = 0, (hidden, width)
        specs, operands = [full((width, hidden)), full(down_shape)], list(weights)
    return pl.pallas_call(
        functools.partial(dec_mid_kernel, steps, chunks, packed),
        grid=(steps,),
        in_specs=[
            by_row,
            by_row,
            by_row,
            by_row,
            full(vecs.shape),
            full((chunks, 1, width)),
            at_col(width, width, proj_at // width),
        ]
        + specs,
        out_specs=[
            by_row,
            by_row,
            by_row,
            full((width, 2 * hidden + width)),
            full((chunks, 1, width)),
            full((8, width)),
        ],
        out_shape=[
            shape((rows, width), LOW),
            shape((rows, width), F32),
            shape((rows, width), LOW),
            shape((width, 2 * hidden + width), LOW),
            shape((chunks, 1, width), F32),
            shape((8, width), F32),
        ],
        scratch_shapes=[
            pltpu.VMEM((width, hidden + width), F32),
            pltpu.VMEM(down_shape, F32),
            pltpu.VMEM((tile, width), F32),
            pltpu.VMEM((tile, width), F32),
            pltpu.VMEM((width, tile), LOW),
        ],
        compiler_params=PARAMS,
        cost_estimate=CHEAP,
        name="dec_mid",
    )(
        dec_in,
        attended,
        cotangent,
        inverse,
        vecs,
        up_bias.reshape(chunks, 1, width),
        wide,
        *operands,
    )


def dec_back_kernel(
    limit,
    each,
    order_ref,
    core_ref,
    x_ref,
    dq_ref,
    dk_ref,
    dv_ref,
    gmid_ref,
    vec_ref,
    more_ref,
    w_ref,
    sum_ref,
    keep_ref,
    send_ref,
):
    step = pl.program_id(0)

    @pl.when(step == 0)
    def _():
        sum_ref[...] = more_ref[...]
        keep_ref[...] = jnp.zeros_like(keep_ref)
        send_ref[...] = jnp.zeros_like(send_ref)

    unit, scale = norm_parts(x_ref[...])
    grads = jnp.concatenate([dq_ref[...], dk_ref[...], dv_ref[...]], axis=1)
    dn = mm_nt(grads, w_ref[...])
    sum_ref[0:1, :] += col_sum(dn * unit)
    sum_ref[2:3, :] += col_sum(dn)
    sum_ref[3:4, :] += col_sum(dq_ref[...].astype(F32))
    sum_ref[4:5, :] += col_sum(dv_ref[...].astype(F32))
    din = gmid_ref[...] + norm_back(dn, unit, scale, vec_ref[0:1, :])
    per = x_ref.shape[0] // BLOCK
    for b in range(per):
        place = order_ref[0, per * step + b]
        rows = din[b * BLOCK : (b + 1) * BLOCK, :]

        owner = place // each
        spot = pl.ds(pl.multiple_of(place % each * BLOCK, BLOCK), BLOCK)

        @pl.when((place < limit) & (owner % 2 == core_ref[0]))
        def _():
            keep_ref[owner // 2, spot, :] = rows.astype(LOW)

        @pl.when((place < limit) & (owner % 2 != core_ref[0]))
        def _():
            send_ref[owner // 2, spot, :] = rows.astype(LOW)

        @pl.when(place >= limit)
        def _():
            sum_ref[8:9, :] += col_sum(rows)


def dec_back(order, core, dec_in, dq, dk, dv, gmid, vecs, more, weight, limit, each):
    rows, width = dec_in.shape
    tile = TILE
    by_row = pl.BlockSpec((tile, width), lambda i, o: (i, 0))
    side = (limit // each // 2, each * BLOCK, width)
    return pl.pallas_call(
        functools.partial(dec_back_kernel, limit, each),
        grid_spec=pltpu.PrefetchScalarGridSpec(
            num_scalar_prefetch=1,
            grid=(rows // tile,),
            in_specs=[pl.BlockSpec(memory_space=pltpu.SMEM)]
            + [by_row] * 5
            + [full(vecs.shape), full((16, width)), at_col(width, 3 * width, 0)],
            out_specs=[full((16, width)), full(side), full(side)],
        ),
        out_shape=[shape((16, width), F32), shape(side, LOW), shape(side, LOW)],
        compiler_params=PARAMS,
        cost_estimate=CHEAP,
        name="dec_back",
    )(order, core, dec_in, dq, dk, dv, gmid, vecs, more, weight)


def dec_grad_kernel(x_ref, dq_ref, dk_ref, dv_ref, vec_ref, sum_ref, dw_ref, acc, sums):
    step = pl.program_id(0)
    width = x_ref.shape[1]

    @pl.when(step == 0)
    def _():
        acc[...] = jnp.zeros_like(acc)

    unit, _ = norm_parts(x_ref[...])
    normed = (unit * vec_ref[0:1, :] + vec_ref[3:4, :]).astype(LOW)
    grads = jnp.concatenate([dq_ref[...], dk_ref[...], dv_ref[...]], axis=1)
    acc[...] += mm_tn(normed, grads)

    @pl.when(step == pl.num_programs(0) - 1)
    def _():
        dw_ref[:, : 3 * width] = acc[...].astype(LOW)
        sums[...] = jnp.zeros_like(sums)
        sums[0:16, :] = sum_ref[...]
        dw_ref[:, 3 * width :] = sums[...].T.astype(LOW)


def dec_grad(dec_in, dq, dk, dv, vecs, sums):
    rows, width = dec_in.shape
    tile = 2 * TILE
    by_row = pl.BlockSpec((tile, width), lambda i: (i, 0))
    packed = (width, 3 * width + LANES)
    return pl.pallas_call(
        dec_grad_kernel,
        grid=(rows // tile,),
        in_specs=[by_row] * 4 + [full(vecs.shape), full((16, width))],
        out_specs=full(packed),
        out_shape=shape(packed, LOW),
        scratch_shapes=[pltpu.VMEM((width, 3 * width), F32), pltpu.VMEM((LANES, width), F32)],
        compiler_params=PARAMS,
        cost_estimate=CHEAP,
        name="dec_grad",
    )(dec_in, dq, dk, dv, vecs, sums)


def positions(count, width):
    places = jnp.arange(count, dtype=jnp.float32)[:, None]
    columns = jnp.arange(width)
    rates = jnp.exp((2 * (columns // 2)).astype(jnp.float32) * (-math.log(10000.0) / width))
    angles = places * rates[None, :]
    return jnp.where((columns % 2 == 0)[None, :], jnp.sin(angles), jnp.cos(angles))


def bits_of(axis):
    size, out = lax.axis_size(axis), []
    while size > 1:
        size //= 2
        out.append((axis, size))
    return out


def all_bits():
    return bits_of("dp") + bits_of("fsdp")


def bit_here(bit):
    axis, stride = bit
    return lax.axis_index(axis) // stride % 2


def swap(value, bit):
    axis, stride = bit
    return lax.ppermute(value, axis, [(i, i ^ stride) for i in range(lax.axis_size(axis))])


def pair(own, got, here, dim):
    dims = tuple(2 if d == dim else 1 for d in range(own.ndim + 1))
    mine = lax.broadcasted_iota(jnp.int32, dims, dim) == here
    return jnp.where(mine, jnp.expand_dims(own, dim), jnp.expand_dims(got, dim))


class Gather:
    def __init__(self, piece, order, held=()):
        self.piece, self.order, self.held = piece, list(order), list(held)

    def step(self):
        canon, bit = all_bits(), self.order.pop(0)
        got = swap(self.piece, bit)
        dim = sum(canon.index(b) < canon.index(bit) for b in self.held)
        self.piece = pair(self.piece, got, bit_here(bit), dim)
        self.held.append(bit)

    def rest(self):
        while self.order:
            self.step()
        return self.piece

    def tie(self, other):
        self.piece, other = lax.optimization_barrier((self.piece, other))
        return other


def gather(piece, order, held=()):
    return Gather(piece, order, held).rest()


def join(pieces, bit):
    both = [pair(own, swap(own, bit), bit_here(bit), own.ndim - 2) for own in pieces]
    both = both[0] if len(both) == 1 else jnp.concatenate(both, axis=-1)
    return both.reshape(-1, both.shape[-1])


def term_sum(terms, kind):
    total = terms[0].astype(F32)
    for term in terms[1:]:
        total = total + term.astype(F32)
    return total.astype(kind)


class Fold:
    def __init__(self, terms, order, held=None):
        self.terms, self.order, self.send = list(terms), list(order), None
        self.left = list(all_bits() if held is None else held)

    def cut(self):
        if self.send is not None:
            return
        bit = self.order[0]
        dim = self.left.index(bit)
        here = bit_here(bit)

        def half(index):
            return [lax.dynamic_index_in_dim(t, index, dim, keepdims=False) for t in self.terms]

        self.send, self.terms = term_sum(half(1 - here), LOW), half(here)

    def pass_on(self):
        bit = self.order.pop(0)
        self.left.remove(bit)
        self.terms.append(swap(self.send, bit))
        self.send = None


def split_fold(keep, send, order, held=None):
    held = all_bits() if held is None else held
    dims = (2,) * (len(held) - 1) + keep.shape[-2:]
    fold = Fold([keep.reshape(dims)], order, held)
    fold.send = send.reshape(dims)
    return fold


def start_beside(folds, inputs):
    for fold in folds:
        fold.cut()
    sends, inputs = lax.optimization_barrier(([f.send for f in folds], inputs))
    for fold, send in zip(folds, sends):
        fold.send = send
        fold.pass_on()
    return inputs


def end_beside(folds, outputs):
    last, outputs = lax.optimization_barrier(([f.terms[-1] for f in folds], outputs))
    for fold, got in zip(folds, last):
        fold.terms[-1] = got
    return outputs


def one_round(folds):
    for fold in folds:
        fold.cut()
        fold.pass_on()
    end_beside(folds, ())


def joined(folds, line):
    terms = [term_sum(f.terms, F32) for f in folds]
    return Fold([jnp.concatenate(terms, axis=-1)], line[::-1], line)


def by_bits(grads):
    bits = len(all_bits())
    rows = grads.shape[0] >> bits
    return grads.reshape((2,) * bits + (rows, grads.shape[1]))


def pack_vectors(pieces, rows):
    wide = jnp.concatenate([p.reshape(-1, rows) for p in pieces], axis=0)
    wide = jnp.pad(wide, ((0, LANES - wide.shape[0]), (0, 0)))
    return wide.T


def unpack_tall(columns, devices, width):
    rows = columns.shape[0] // devices
    parts = columns.shape[1] // width
    return (
        columns.reshape(devices, rows, parts, width)
        .transpose(0, 2, 1, 3)
        .reshape(devices * parts * rows, width)
    )


def repack_tall(weight, devices, rows):
    parts = weight.shape[0] // (devices * rows)
    width = weight.shape[1]
    return (
        weight.reshape(devices, parts, rows, width)
        .transpose(0, 2, 1, 3)
        .reshape(devices * rows, parts * width)
    )


def split_columns(array, widths):
    out, at = [], 0
    for w in widths:
        out.append(array[:, at : at + w])
        at += w
    return out


def long_vector(rows_of, devices):
    parts, total = rows_of.shape
    return rows_of.reshape(parts, devices, total // devices).transpose(1, 0, 2).reshape(1, -1)


def long_rows(vector, devices, rows):
    parts = vector.shape[0] // (devices * rows)
    return vector.reshape(devices, parts, rows).transpose(1, 0, 2).reshape(parts, -1)


def per_device(
    enc_input,
    enc_segments,
    dec_segments,
    block_order,
    dec_cotangent,
    enc_qkv,
    enc_proj,
    enc_fc1,
    enc_fc2,
    enc_gains,
    enc_biases,
    enc_fc1_bias,
    embed,
    mask_token,
    dec_qkv,
    dec_proj,
    dec_fc1,
    dec_fc2,
    dec_gains,
    dec_biases,
    dec_fc1_bias,
    dec_fc2_bias,
):
    devices = lax.axis_size("dp") * lax.axis_size("fsdp")
    enc_rows, width = enc_input.shape
    dec_rows, dwidth = dec_cotangent.shape
    erows = enc_qkv.shape[0]
    drows = dec_qkv.shape[0]
    ff = enc_fc1.shape[1]
    dff = dec_fc1.shape[1]
    emb_row = jnp.pad(dec_biases[0], (0, erows - drows))
    enc_first = jnp.concatenate(
        [
            enc_qkv,
            pack_vectors([enc_gains, enc_biases, enc_fc1_bias, emb_row], erows),
        ],
        axis=1,
    )
    dec_first = jnp.concatenate(
        [
            dec_qkv,
            dec_proj,
            pack_vectors(
                [dec_gains, dec_biases, dec_fc2_bias[None], mask_token[None], dec_fc1_bias], drows
            ),
        ],
        axis=1,
    )
    vec_at = 3 * width
    dproj_at, dvec_at = 3 * dwidth, 4 * dwidth
    ecut = (vec_at + LANES) // 2 // LANES * LANES
    gap = gap_of(width, dwidth)
    here = bit_here(bits_of("fsdp")[-1]).reshape(1)
    dp, fsdp = bits_of("dp"), bits_of("fsdp")
    line, core = fsdp[:-1], fsdp[-1]
    packed = erows % 8 == 0 and drows % 16 == 0
    if packed:
        enc_rest, dec_rest = pack_shards(enc_fc1, enc_fc2, enc_proj, embed, dec_fc1, dec_fc2)
        enc_rest = [lax.all_gather(enc_rest, AXES, axis=0, tiled=True)]
        dec_rest = [dec_rest]
        outer, proj_at = enc_rest[0], 2 * ff
    else:
        outer = jnp.concatenate([enc_proj, jnp.zeros((erows, gap), LOW), embed], axis=1)
        enc_rest = [lax.all_gather(w, AXES, axis=0, tiled=True) for w in (enc_fc1, enc_fc2, outer)]
        dec_rest = [dec_fc1, dec_fc2]
        outer, proj_at = enc_rest.pop(), 0
    emb_at = proj_at + width + gap
    lined = gather(enc_first, line)
    one = gather(lined[..., :ecut], dp[::-1], line)
    two = gather(lined[..., ecut:], dp, line)
    enc_all = join([one, two], core)
    evecs = enc_all[:, vec_at:].T[:16].astype(F32)
    up_bias = long_vector(evecs[10:14], devices)
    emb_bias = evecs[14].reshape(devices, erows)[:, :drows].reshape(1, -1)

    dec_gather = Gather(dec_first, line + dp)
    enc_all, evecs = dec_gather.tie((enc_all, evecs))
    dec_gather.step()
    qkv = enc_qkv_call(enc_input, evecs, enc_all)
    enc_col = enc_segments.reshape(-1, 1)
    qkv = dec_gather.tie(qkv)
    dec_gather.step()
    attended, inverse, weights = attend(qkv, enc_segments, enc_col, HDIM)
    attended = dec_gather.tie(attended)
    dec_all = join([dec_gather.rest()], core)
    dvecs = dec_all[:, dvec_at:].T[:16].astype(F32)
    dup_bias = long_vector(dvecs[10:14], devices)
    pos = positions(dec_rows, dwidth)
    attended, dec_all, dvecs, dup_bias, pos = lax.optimization_barrier(
        (attended, dec_all, dvecs, dup_bias, pos)
    )
    mid, enc_out, final, act, slope, embedded, down_w = enc_mid(
        enc_input,
        attended,
        evecs,
        up_bias,
        emb_bias,
        outer,
        enc_rest,
        proj_at,
        emb_at,
    )
    emb_gather = Gather(embedded, fsdp)
    emb_gather.step()
    dec_rest = emb_gather.tie(dec_rest)
    dec_rest = [lax.all_gather(w, AXES, axis=0, tiled=True) for w in dec_rest]
    gathered = emb_gather.rest().reshape(-1, dwidth)
    limit = gathered.shape[0] // BLOCK
    dec_in, dqkv = dec_in_call(block_order, gathered, pos, dvecs, dec_all)
    dec_col = dec_segments.reshape(-1, 1)
    dattended, dinverse, dweights = attend(dqkv, dec_segments, dec_col, DHDIM)
    dec_out, dgmid, dgatt, dw_rest, db1, dsum_mid = dec_mid(
        dec_in,
        dattended,
        dec_cotangent,
        dinverse,
        dvecs,
        dup_bias,
        dec_all,
        dec_rest,
        dproj_at,
    )
    if not packed:
        chunks = dff // dwidth
        tall = dw_rest[:, dff + dwidth :].reshape(dwidth, chunks, dwidth).transpose(1, 0, 2)
        tall = repack_tall(tall.reshape(dff, dwidth), devices, drows)
        dw_rest = jnp.concatenate([dw_rest[:, : dff + dwidth], tall], axis=1)
    dec_own = lax.psum_scatter(dw_rest, "dp", scatter_dimension=0, tiled=True)
    dec_more = jnp.concatenate(
        [
            jnp.zeros((1, dwidth), F32),
            dsum_mid[0:1],
            jnp.zeros((3, dwidth), F32),
            dsum_mid[2:3],
            dsum_mid[1:2],
            dsum_mid[3:4],
            jnp.zeros((1, dwidth), F32),
            long_rows(db1.reshape(-1), devices, drows),
            jnp.zeros((3, dwidth), F32),
        ],
        axis=0,
    )
    dgatt, dec_more = lax.optimization_barrier((dgatt, dec_more))
    ddq, ddk, ddv = attend_back(dqkv, dattended, dgatt, dweights, dec_segments, DHDIM)
    dsum, keep, send = dec_back(
        block_order,
        here,
        dec_in,
        ddq,
        ddk,
        ddv,
        dgmid,
        dvecs,
        dec_more,
        dec_all,
        limit,
        enc_rows // BLOCK,
    )
    emb_fold = split_fold(keep, send, fsdp[::-1], fsdp)
    emb_fold.pass_on()
    dsum = end_beside([emb_fold], dsum)
    emb_fold.cut()
    emb_fold.pass_on()
    dec_grads = dec_grad(dec_in, ddq, ddk, ddv, dvecs, dsum)
    dec_grads, dec_own = end_beside([emb_fold], (dec_grads, dec_own))
    dec_grads = lax.psum_scatter(dec_grads, "dp", scatter_dimension=0, tiled=True)
    for _ in line[1:]:
        one_round([emb_fold])
    elow = term_sum(emb_fold.terms, LOW)
    dpe, *ew, eb1, esum_emb, esum_mid, gmid, gatt = enc_mid_back(
        here,
        elow,
        final,
        enc_out,
        mid,
        attended,
        act,
        slope,
        inverse,
        evecs,
        outer,
        enc_rest[0],
        down_w,
        proj_at,
        emb_at,
    )
    gatt, dec_own, dec_grads = lax.optimization_barrier((gatt, dec_own, dec_grads))
    dec_own = jnp.concatenate([dec_own, dec_grads], axis=1)
    dec_own = lax.psum_scatter(dec_own, "fsdp", scatter_dimension=0, tiled=True)
    if packed:
        edown = split_fold(ew[0], ew[1], [core] + dp[::-1])
        eup = split_fold(ew[2], ew[3], [core] + dp)
    else:
        edown = Fold([by_bits(repack_tall(ew[0], devices, erows))], [core] + dp[::-1])
        eup = Fold([by_bits(ew[1])], [core] + dp)
    gatt = start_beside([eup, edown], gatt)
    gatt = end_beside([eup, edown], gatt)
    gatt = start_beside([eup, edown], gatt)
    emb_sum = jnp.pad(esum_emb[0].reshape(devices, drows), ((0, 0), (0, erows - drows)))
    enc_more = jnp.concatenate(
        [
            jnp.zeros((1, width), F32),
            esum_mid[3:4],
            esum_mid[0:1],
            jnp.zeros((3, width), F32),
            esum_mid[5:6],
            esum_mid[4:5],
            esum_mid[2:3],
            esum_mid[1:2],
            long_rows(eb1.reshape(-1), devices, erows),
            emb_sum.reshape(1, -1),
            jnp.zeros((1, width), F32),
        ],
        axis=0,
    )
    dq, dk, dv = attend_back(qkv, attended, gatt, weights, enc_segments, HDIM)
    enc_in_grad, *enc_grads = enc_qkv_back(
        here, enc_input, dq, dk, dv, gmid, evecs, enc_more, dpe, enc_all
    )
    if packed:
        chip = split_fold(enc_grads[0], enc_grads[1], [core])
    else:
        chip = Fold([by_bits(enc_grads[0])], [core])
        chip.cut()
    chip.send, dec_own = end_beside([eup, edown], (chip.send, dec_own))
    chip.pass_on()
    while eup.order:
        one_round([eup, edown, chip] if chip.order else [eup, edown])
    end_beside([chip], ())
    gcut = enc_grads[0].shape[-1] // 2 // LANES * LANES
    one = Fold([t[..., :gcut] for t in chip.terms], dp, all_bits()[:-1])
    two = Fold([t[..., gcut:] for t in chip.terms], dp[::-1], all_bits()[:-1])
    rest = joined([eup, edown], line)
    while one.order:
        one_round([one, two] + ([rest] if rest.order else []))
    first = joined([one, two], line)
    while first.order or rest.order:
        one_round([f for f in (first, rest) if f.order])
    eu, ed = split_columns(term_sum(rest.terms, F32), [ff, ff])
    ed = unpack_tall(ed, 1, width)
    eq, ep, em, ev = split_columns(term_sum(first.terms, F32), [3 * width, width, dwidth, LANES])
    ru, rp, rd, rq, rv = split_columns(
        dec_own.astype(F32), [dff, dwidth, dff, 3 * dwidth, LANES]
    )
    rd = unpack_tall(rd, 1, dwidth)
    rv = rv.T
    ev = ev.T
    return (
        dec_out,
        enc_in_grad,
        eq,
        ep,
        eu,
        ed,
        ev[:3],
        ev[3:10],
        ev[10:14].reshape(-1),
        em,
        rv[8],
        rq,
        rp,
        ru,
        rd,
        rv[:2],
        jnp.concatenate([ev[14:15, :drows], rv[2:7]], axis=0),
        rv[9:13].reshape(-1),
        rv[7],
    )


def solution(mesh):
    in_specs = (
        P(("dp", "fsdp"), None),
        P(("dp", "fsdp"), None),
        P(("dp", "fsdp"), None),
        P("dp", "fsdp"),
        P(("dp", "fsdp"), None),
        P(("dp", "fsdp"), None),
        P(("dp", "fsdp"), None),
        P(("dp", "fsdp"), None),
        P(("dp", "fsdp"), None),
        P(None, ("dp", "fsdp")),
        P(None, ("dp", "fsdp")),
        P(("dp", "fsdp")),
        P(("dp", "fsdp"), None),
        P(("dp", "fsdp")),
        P(("dp", "fsdp"), None),
        P(("dp", "fsdp"), None),
        P(("dp", "fsdp"), None),
        P(("dp", "fsdp"), None),
        P(None, ("dp", "fsdp")),
        P(None, ("dp", "fsdp")),
        P(("dp", "fsdp")),
        P(("dp", "fsdp")),
    )
    out_specs = (
        P(("dp", "fsdp"), None),
        P(("dp", "fsdp"), None),
        P(("dp", "fsdp"), None),
        P(("dp", "fsdp"), None),
        P(("dp", "fsdp"), None),
        P(("dp", "fsdp"), None),
        P(None, ("dp", "fsdp")),
        P(None, ("dp", "fsdp")),
        P(("dp", "fsdp")),
        P(("dp", "fsdp"), None),
        P(("dp", "fsdp")),
        P(("dp", "fsdp"), None),
        P(("dp", "fsdp"), None),
        P(("dp", "fsdp"), None),
        P(("dp", "fsdp"), None),
        P(None, ("dp", "fsdp")),
        P(None, ("dp", "fsdp")),
        P(("dp", "fsdp")),
        P(("dp", "fsdp")),
    )
    return jax.shard_map(
        per_device, mesh=mesh, in_specs=in_specs, out_specs=out_specs, check_vma=False
    )
```

```python
import functools
import math

import jax
import jax.numpy as jnp
from jax import lax
from jax.experimental import pallas as pl
from jax.experimental.pallas import tpu as pltpu
from jax.sharding import PartitionSpec as P

HDIM = 64
DHDIM = 32
BLOCK = 128
LANES = 128
TILE = 256
SPAN = 128
GROUP = 256
EPSILON = 1e-06
NEGATIVE = -1e30
LOG2E = math.log2(math.e)
AXES = ("dp", "fsdp")
F32 = jnp.float32
LOW = jnp.bfloat16
PARAMS = pltpu.CompilerParams(vmem_limit_bytes=56 * 1024 * 1024)


def mm(left, right):
    return jnp.dot(left, right, preferred_element_type=F32)


def mm_tn(left, right):
    return lax.dot_general(left, right, (((0,), (0,)), ((), ())), preferred_element_type=F32)


def mm_nt(left, right):
    return lax.dot_general(left, right, (((1,), (1,)), ((), ())), preferred_element_type=F32)


def col_sum(values):
    return jnp.sum(values, axis=0, keepdims=True)


def norm_parts(values):
    centred = values - jnp.mean(values, axis=-1, keepdims=True)
    variance = jnp.mean(centred * centred, axis=-1, keepdims=True)
    scale = lax.rsqrt(variance + EPSILON)
    return centred * scale, scale


def norm_back(grad, unit, scale, gain):
    inner = grad * gain
    mean_inner = jnp.mean(inner, axis=-1, keepdims=True)
    mean_cross = jnp.mean(inner * unit, axis=-1, keepdims=True)
    return scale * (inner - mean_inner - unit * mean_cross)


def gelu_parts(hidden):
    cdf = 0.5 + 0.5 * lax.erf(hidden * (0.5**0.5))
    density = jnp.exp(hidden * hidden * -0.5) * (1.0 / math.sqrt(2.0 * math.pi))
    return hidden * cdf, cdf + hidden * density


CHEAP = pl.CostEstimate(flops=1 << 20, bytes_accessed=1 << 16, transcendentals=0)


def full(shape):
    return pl.BlockSpec(shape, lambda *_: (0,) * len(shape))


def at_col(rows, cols, index):
    return pl.BlockSpec((rows, cols), lambda *_: (0, index))


def shape(dims, kind):
    return jax.ShapeDtypeStruct(dims, kind)


def lane_mask(head, head_dim, kind):
    lane = lax.broadcasted_iota(jnp.int32, (1, GROUP), 1)
    inside = (lane >= head * head_dim) & (lane < (head + 1) * head_dim)
    return inside.astype(F32).astype(kind)


def stack_heads(stacked, index, rows, head_dim):
    count = rows.shape[0]
    for h in range(GROUP // head_dim):
        stacked[index, h * count : (h + 1) * count, :] = rows * lane_mask(h, head_dim, LOW)


def tile_range(seg_ref, start, size, other, count):
    first, last = seg_ref[0, start], seg_ref[0, start + size - 1]
    low, high = jnp.int32(0), jnp.int32(count)
    for tile in range(count):
        low += (seg_ref[0, tile * other + other - 1] < first).astype(jnp.int32)
        high -= (seg_ref[0, tile * other] > last).astype(jnp.int32)
    return low, high


def attend_kernel(
    head_dim,
    tiles,
    seg_ref,
    q_ref,
    k_ref,
    v_ref,
    row_ref,
    col_ref,
    out_ref,
    inv_ref,
    exp_ref,
    km,
    vt,
    held,
    acc,
    inverse,
    top,
    tot,
):
    heads = GROUP // head_dim
    here = pl.program_id(1)
    factor = head_dim ** (-0.5) * LOG2E

    @pl.when(here == 0)
    def _():
        for u in range(tiles):
            rows = slice(u * SPAN, (u + 1) * SPAN)
            vt[u] = v_ref[rows, :].astype(F32).T.astype(LOW)
            stack_heads(km, u, k_ref[rows, :], head_dim)

    acc[...] = jnp.zeros_like(acc)
    top[...] = jnp.full_like(top, NEGATIVE)
    tot[...] = jnp.zeros_like(tot)
    query = q_ref[...]
    row = row_ref[...]

    def score(u, carry):
        start = pl.multiple_of(u * SPAN, SPAN)
        same = col_ref[pl.ds(start, SPAN), :] == row
        every = mm_nt(km[u], query)
        for h in range(heads):
            scores = jnp.where(same, every[h * SPAN : (h + 1) * SPAN, :], NEGATIVE)
            held[u, h] = scores
            top[h : h + 1, :] = jnp.maximum(
                top[h : h + 1, :], jnp.max(scores, axis=0, keepdims=True)
            )
        return carry

    def mix(u, carry):
        for h in range(heads):
            weights = jnp.exp2((held[u, h] - top[h : h + 1, :]) * factor)
            tot[h : h + 1, :] += col_sum(weights)
            span = slice(h * head_dim, (h + 1) * head_dim)
            weights = weights.astype(LOW)
            exp_ref[0, 0, u, :, h * TILE : (h + 1) * TILE] = weights
            acc[span, :] += mm(vt[u, span, :], weights)
        return carry

    low, high = tile_range(seg_ref, here * TILE, TILE, SPAN, tiles)
    lax.fori_loop(low, high, score, 0)
    lax.fori_loop(low, high, mix, 0)
    for h in range(heads):
        span = slice(h * head_dim, (h + 1) * head_dim)
        inverse[span, :] = jnp.broadcast_to(1.0 / tot[h : h + 1, :], (head_dim, TILE))
    out_ref[...] = (acc[...] * inverse[...]).T.astype(LOW)
    inv_ref[...] = inverse[...].T


def attend(qkv, segments, seg_col, head_dim):
    rows, width = qkv.shape[0], qkv.shape[1] // 3
    groups, steps, tiles, heads = width // GROUP, rows // TILE, rows // SPAN, GROUP // head_dim
    return pl.pallas_call(
        functools.partial(attend_kernel, head_dim, tiles),
        grid_spec=pltpu.PrefetchScalarGridSpec(
            num_scalar_prefetch=1,
            grid=(groups, steps),
            in_specs=[
                pl.BlockSpec((TILE, GROUP), lambda g, t, s: (t, g)),
                pl.BlockSpec((rows, GROUP), lambda g, t, s: (0, groups + g)),
                pl.BlockSpec((rows, GROUP), lambda g, t, s: (0, 2 * groups + g)),
                pl.BlockSpec((1, TILE), lambda g, t, s: (0, t)),
                pl.BlockSpec((rows, 1), lambda g, t, s: (0, 0)),
            ],
            out_specs=[
                pl.BlockSpec((TILE, GROUP), lambda g, t, s: (t, g)),
                pl.BlockSpec((TILE, GROUP), lambda g, t, s: (t, g)),
                pl.BlockSpec((1, 1, tiles, SPAN, heads * TILE), lambda g, t, s: (g, t, 0, 0, 0)),
            ],
            scratch_shapes=[
                pltpu.VMEM((tiles, heads * SPAN, GROUP), LOW),
                pltpu.VMEM((tiles, GROUP, SPAN), LOW),
                pltpu.VMEM((tiles, heads, SPAN, TILE), F32),
                pltpu.VMEM((GROUP, TILE), F32),
                pltpu.VMEM((GROUP, TILE), F32),
                pltpu.VMEM((8, TILE), F32),
                pltpu.VMEM((8, TILE), F32),
            ],
        ),
        out_shape=[
            shape((rows, width), LOW),
            shape((rows, width), F32),
            shape((groups, steps, tiles, SPAN, heads * TILE), LOW),
        ],
        compiler_params=PARAMS,
        cost_estimate=CHEAP,
        name="attend",
    )(segments, qkv, qkv, qkv, segments, seg_col)


def attend_back_kernel(
    head_dim,
    steps,
    seg_ref,
    q_ref,
    k_ref,
    v_ref,
    o_ref,
    g_ref,
    exp_ref,
    dq_ref,
    dk_ref,
    dv_ref,
    qm,
    gm,
    vm,
    dqt,
    delta,
    dk_acc,
    dv_acc,
):
    heads = GROUP // head_dim
    here = pl.program_id(1)
    scale = head_dim ** (-0.5)

    @pl.when(here == 0)
    def _():
        dqt[...] = jnp.zeros_like(dqt)
        for t in range(steps):
            rows = slice(t * TILE, (t + 1) * TILE)
            stack_heads(qm, t, q_ref[rows, :], head_dim)
            stack_heads(gm, t, g_ref[rows, :], head_dim)
            both = (g_ref[rows, :].astype(F32) * o_ref[rows, :].astype(F32)).T
            for h in range(heads):
                delta[t, h : h + 1, :] = col_sum(both[h * head_dim : (h + 1) * head_dim, :])

    keys_t = k_ref[...].astype(F32).T.astype(LOW)
    stack_heads(vm, 0, v_ref[...], head_dim)
    dk_acc[...] = jnp.zeros_like(dk_acc)
    dv_acc[...] = jnp.zeros_like(dv_acc)

    def step(t, carry):
        start = pl.multiple_of(t * TILE, TILE)
        every = mm_nt(vm[0], g_ref[pl.ds(start, TILE), :])
        dv_acc[...] += mm(exp_ref[0, t, 0], gm[t])
        pieces = []
        for h in range(heads):
            grad_probs = every[h * SPAN : (h + 1) * SPAN, :] - delta[t, h : h + 1, :]
            weights = exp_ref[0, t, 0, :, h * TILE : (h + 1) * TILE]
            pieces.append((weights.astype(F32) * grad_probs).astype(LOW))
        for h in range(heads):
            span = slice(h * head_dim, (h + 1) * head_dim)
            dqt[t, span, :] += mm(keys_t[span, :], pieces[h])
        dk_acc[...] += mm(jnp.concatenate(pieces, axis=1), qm[t])
        return carry

    low, high = tile_range(seg_ref, here * SPAN, SPAN, TILE, steps)
    lax.fori_loop(low, high, step, 0)
    dk_ref[...] = (dk_acc[...] * scale).astype(LOW)
    dv_ref[...] = dv_acc[...].astype(LOW)

    @pl.when(here == pl.num_programs(1) - 1)
    def _():
        for t in range(steps):
            dq_ref[t * TILE : (t + 1) * TILE, :] = (dqt[t] * scale).T.astype(LOW)


def attend_back(qkv, attended, grad, weights, segments, head_dim):
    rows, width = attended.shape
    groups, steps, tiles, heads = width // GROUP, rows // TILE, rows // SPAN, GROUP // head_dim
    whole = pl.BlockSpec((rows, GROUP), lambda g, u, s: (0, g))
    piece = pl.BlockSpec((SPAN, GROUP), lambda g, u, s: (u, g))
    return pl.pallas_call(
        functools.partial(attend_back_kernel, head_dim, steps),
        grid_spec=pltpu.PrefetchScalarGridSpec(
            num_scalar_prefetch=1,
            grid=(groups, tiles),
            in_specs=[
                whole,
                pl.BlockSpec((SPAN, GROUP), lambda g, u, s: (u, groups + g)),
                pl.BlockSpec((SPAN, GROUP), lambda g, u, s: (u, 2 * groups + g)),
                whole,
                whole,
                pl.BlockSpec((1, steps, 1, SPAN, heads * TILE), lambda g, u, s: (g, 0, u, 0, 0)),
            ],
            out_specs=[whole, piece, piece],
            scratch_shapes=[
                pltpu.VMEM((steps, heads * TILE, GROUP), LOW),
                pltpu.VMEM((steps, heads * TILE, GROUP), LOW),
                pltpu.VMEM((1, heads * SPAN, GROUP), LOW),
                pltpu.VMEM((steps, GROUP, TILE), F32),
                pltpu.VMEM((steps, 8, TILE), F32),
                pltpu.VMEM((SPAN, GROUP), F32),
                pltpu.VMEM((SPAN, GROUP), F32),
            ],
        ),
        out_shape=[shape((rows, width), LOW)] * 3,
        compiler_params=PARAMS,
        cost_estimate=CHEAP,
        name="attend_back",
    )(segments, qkv, qkv, qkv, attended, grad, weights)


def pack_kernel(up_ref, down_ref, dup_ref, ddown_ref, out_ref, dout_ref):
    for up, down, out in ((up_ref, down_ref, out_ref), (dup_ref, ddown_ref, dout_ref)):
        rows, cols = up.shape
        out[:, :cols] = up[...]
        wide = down[...].astype(F32)
        width = down.shape[1]
        for part in range(4):
            piece = wide[part * rows : (part + 1) * rows, :].astype(LOW)
            out[:, cols + part * width : cols + (part + 1) * width] = piece


def pack_shards(*shards):
    outs = [shape((w.shape[0], 2 * w.shape[1]), LOW) for w in shards[::2]]
    return pl.pallas_call(
        pack_kernel,
        in_specs=[full(s.shape) for s in shards],
        out_specs=[full(o.shape) for o in outs],
        out_shape=outs,
        grid=(1,),
        compiler_params=PARAMS,
        cost_estimate=CHEAP,
        name="pack",
    )(*shards)


def by_core(grads, group):
    pairs = grads.reshape(-1, 2, group, grads.shape[1])
    return pairs[:, 0], pairs[:, 1]


def natural_rows(block, group, kind):
    width = block.shape[1] // 4
    parts = [
        block[:, i * width : (i + 1) * width].astype(kind).reshape(-1, group, width)
        for i in range(4)
    ]
    return jnp.stack(parts, axis=1).reshape(-1, width).astype(LOW)


def enc_qkv_kernel(x_ref, vec_ref, w_ref, out_ref, normed):
    part = pl.program_id(0)

    @pl.when(part == 0)
    def _():
        unit, _ = norm_parts(x_ref[...].astype(F32))
        normed[...] = (unit * vec_ref[0:1, :] + vec_ref[3:4, :]).astype(LOW)

    bias = jnp.where(part == 0, vec_ref[4:5, :], jnp.where(part == 2, vec_ref[5:6, :], 0.0))
    out_ref[...] = (mm(normed[...], w_ref[...]) + bias).astype(LOW)


def enc_qkv_call(rows_in, vecs, weight):
    rows, width = rows_in.shape
    return pl.pallas_call(
        enc_qkv_kernel,
        grid=(3,),
        in_specs=[
            full((rows, width)),
            full(vecs.shape),
            pl.BlockSpec((width, width), lambda i: (0, i)),
        ],
        out_specs=pl.BlockSpec((rows, width), lambda i: (0, i)),
        out_shape=shape((rows, 3 * width), LOW),
        scratch_shapes=[pltpu.VMEM((rows, width), LOW)],
        compiler_params=PARAMS,
        cost_estimate=CHEAP,
        name="enc_qkv",
    )(rows_in, vecs, weight)


def enc_mid_kernel(
    chunks,
    packed,
    x_ref,
    att_ref,
    vec_ref,
    b1_ref,
    eb_ref,
    wo_ref,
    we_ref,
    *refs,
):
    up_ref, down_ref, *refs = refs
    mid_ref, out_ref, final_ref, act_ref, slope_ref, emb_ref, *refs = refs
    naturals, (normed, acc) = refs[:-2], refs[-2:]
    part = pl.program_id(0)

    @pl.when(part == 0)
    def _():
        middle = x_ref[...].astype(F32) + mm(att_ref[...], wo_ref[...]) + vec_ref[6:7, :]
        mid_ref[...] = middle
        unit, _ = norm_parts(middle)
        normed[...] = (unit * vec_ref[1:2, :] + vec_ref[7:8, :]).astype(LOW)
        acc[...] = middle + vec_ref[8:9, :]

    down = down_ref[...]
    if packed:
        down = natural_rows(down, packed, F32)
        naturals[0][...] = down
    hidden = mm(normed[...], up_ref[...]) + b1_ref[...]
    value, slope = gelu_parts(hidden)
    value = value.astype(LOW)
    act_ref[...] = value
    slope_ref[...] = slope
    acc[...] += mm(value, down)

    @pl.when(part == chunks - 1)
    def _():
        result = acc[...]
        out_ref[...] = result
        unit, _ = norm_parts(result)
        final = (unit * vec_ref[2:3, :] + vec_ref[9:10, :]).astype(LOW)
        final_ref[...] = final
        emb_ref[...] = (mm(final, we_ref[...]) + eb_ref[...]).astype(LOW)


def enc_mid(rows_in, attended, vecs, up_bias, emb_bias, wide, weights, proj_at, emb_at):
    rows, width = rows_in.shape
    hidden = up_bias.shape[1]
    emb_width = emb_bias.shape[1]
    chunks = hidden // width
    by_row = pl.BlockSpec((width, width), lambda i: (i, 0))
    specs = [pl.BlockSpec((width, width), lambda i: (0, i))]
    if len(weights) == 1:
        packed = width // (lax.axis_size("dp") * lax.axis_size("fsdp"))
        specs.append(pl.BlockSpec((width // 4, hidden), lambda i: (i, 1)))
        operands = [weights[0]] * 2
        natural_specs, natural_shapes = [by_row], [shape((hidden, width), LOW)]
    else:
        packed = 0
        specs.append(by_row)
        operands, natural_specs, natural_shapes = list(weights), [], []
    outs = pl.pallas_call(
        functools.partial(enc_mid_kernel, chunks, packed),
        grid=(chunks,),
        in_specs=[
            full((rows, width)),
            full((rows, width)),
            full(vecs.shape),
            pl.BlockSpec((1, width), lambda i: (0, i)),
            full((1, emb_width)),
            at_col(width, width, proj_at // width),
            at_col(width, emb_width, emb_at // emb_width),
        ]
        + specs,
        out_specs=[
            full((rows, width)),
            full((rows, width)),
            full((rows, width)),
            pl.BlockSpec((rows, width), lambda i: (0, i)),
            pl.BlockSpec((rows, width), lambda i: (0, i)),
            full((rows, emb_width)),
        ]
        + natural_specs,
        out_shape=[
            shape((rows, width), F32),
            shape((rows, width), F32),
            shape((rows, width), LOW),
            shape((rows, hidden), LOW),
            shape((rows, hidden), F32),
            shape((rows, emb_width), LOW),
        ]
        + natural_shapes,
        scratch_shapes=[pltpu.VMEM((rows, width), LOW), pltpu.VMEM((rows, width), F32)],
        compiler_params=PARAMS,
        cost_estimate=CHEAP,
        name="enc_mid",
    )(rows_in, attended, vecs, up_bias, emb_bias, wide, wide, *operands)
    return outs if packed else list(outs) + [weights[1]]


def enc_mid_back_kernel(
    chunks,
    packed,
    core_ref,
    elow_ref,
    final_ref,
    out_ref,
    mid_ref,
    att_ref,
    act_ref,
    slope_ref,
    vec_ref,
    wo_ref,
    w1_ref,
    w2_ref,
    we_ref,
    inv_ref,
    *refs,
):
    if packed:
        keep_ref, send_ref, keep2_ref, send2_ref, keep1_ref, send1_ref, *refs = refs
    else:
        keep_ref, dw2_ref, dw1_ref, *refs = refs
    (
        db1_ref,
    esum_ref,
    sum_ref,
    gmid_ref,
    gatt_ref,
    grad,
    grad_low,
    unit_two,
    scale_two,
    normed,
        dnorm,
    ) = refs
    first = core_ref[0] == 0

    def put(cols, grads):
        if packed:
            zero, one = by_core(grads, packed)
            keep_ref[:, :, cols] = jnp.where(first, zero, one).astype(LOW)
            send_ref[:, :, cols] = jnp.where(first, one, zero).astype(LOW)
        else:
            keep_ref[:, cols] = grads.astype(LOW)

    part = pl.program_id(0)

    @pl.when(part == 0)
    def _():
        elow = elow_ref[...]
        width = final_ref.shape[1]
        put(slice(width, width + elow.shape[1]), mm_tn(final_ref[...], elow))
        esum_ref[...] = jnp.zeros_like(esum_ref)
        esum_ref[0:1, :] = col_sum(elow.astype(F32))
        unit, scale = norm_parts(out_ref[...])
        dfinal = mm_nt(elow, we_ref[...])
        sum_ref[...] = jnp.zeros_like(sum_ref)
        sum_ref[0:1, :] = col_sum(dfinal * unit)
        sum_ref[1:2, :] = col_sum(dfinal)
        total = norm_back(dfinal, unit, scale, vec_ref[2:3, :])
        grad[...] = total
        low = total.astype(LOW)
        grad_low[...] = low
        sum_ref[2:3, :] = col_sum(low.astype(F32))
        unit, scale = norm_parts(mid_ref[...])
        unit_two[...] = unit
        scale_two[...] = jnp.broadcast_to(scale, scale_two.shape)
        normed[...] = (unit * vec_ref[1:2, :] + vec_ref[7:8, :]).T.astype(LOW)
        dnorm[...] = jnp.zeros_like(dnorm)

    low = grad_low[...]
    down = mm_tn(act_ref[...], low)
    if packed:
        width = low.shape[1]
        down = down.reshape(-1, 4, packed, width)
        for i in range(4):
            zero, one = by_core(down[:, i].reshape(-1, width), packed)
            cols = slice(i * width, (i + 1) * width)
            keep2_ref[:, :, cols] = jnp.where(first, zero, one).astype(LOW)
            send2_ref[:, :, cols] = jnp.where(first, one, zero).astype(LOW)
    else:
        dw2_ref[...] = down.astype(LOW)
    dhid = (slope_ref[...] * mm_nt(low, w2_ref[...])).astype(LOW)
    up = mm(normed[...], dhid)
    if packed:
        zero, one = by_core(up, packed)
        keep1_ref[...] = jnp.where(first, zero, one).astype(LOW)
        send1_ref[...] = jnp.where(first, one, zero).astype(LOW)
    else:
        dw1_ref[...] = up.astype(LOW)
    db1_ref[...] = col_sum(dhid.astype(F32))
    dnorm[...] += mm_nt(dhid, w1_ref[...])

    @pl.when(part == chunks - 1)
    def _():
        dn = dnorm[...]
        unit = unit_two[...]
        sum_ref[3:4, :] = col_sum(dn * unit)
        sum_ref[4:5, :] = col_sum(dn)
        gmid = grad[...] + norm_back(dn, unit, scale_two[:, 0:1], vec_ref[1:2, :])
        gmid_ref[...] = gmid
        mlow = gmid.astype(LOW)
        sum_ref[5:6, :] = col_sum(mlow.astype(F32))
        put(slice(0, mlow.shape[1]), mm_tn(att_ref[...], mlow))
        gatt_ref[...] = (mm_nt(mlow, wo_ref[...]) * inv_ref[...]).astype(LOW)


def enc_mid_back(
    core, elow, final, out, mid, attended, act, slope, inverse, vecs, wide, up_w, down_w, proj_at, emb_at
):
    rows, width = mid.shape
    hidden = down_w.shape[0]
    emb_width = elow.shape[1]
    chunks = hidden // width
    packed = width // (lax.axis_size("dp") * lax.axis_size("fsdp"))
    packed = packed if packed % 8 == 0 else 0
    by_col = pl.BlockSpec((rows, width), lambda i: (0, i))
    if packed:
        chips = width // packed // 2
        two = pl.BlockSpec((chips // chunks, packed, hidden), lambda i: (i, 0, 0))
        one = pl.BlockSpec((chips, packed, width), lambda i: (0, 0, i))
        side = (chips, packed, width + emb_width)
        specs = [full(side), full(side), two, two, one, one]
        shapes = [shape(side, LOW)] * 2 + [shape((chips, packed, hidden), LOW)] * 4
    else:
        specs = [
            full((width, width + emb_width)),
            pl.BlockSpec((width, width), lambda i: (i, 0)),
            pl.BlockSpec((width, width), lambda i: (0, i)),
        ]
        shapes = [
            shape((width, width + emb_width), LOW),
            shape((hidden, width), LOW),
            shape((width, hidden), LOW),
        ]
    return pl.pallas_call(
        functools.partial(enc_mid_back_kernel, chunks, packed),
        grid=(chunks,),
        in_specs=[
            pl.BlockSpec(memory_space=pltpu.SMEM),
            full((rows, emb_width)),
            full((rows, width)),
            full((rows, width)),
            full((rows, width)),
            full((rows, width)),
            by_col,
            by_col,
            full(vecs.shape),
            at_col(width, width, proj_at // width),
            pl.BlockSpec((width, width), lambda i: (0, i)),
            pl.BlockSpec((width, width), lambda i: (i, 0)),
            at_col(width, emb_width, emb_at // emb_width),
            full((rows, width)),
        ],
        out_specs=[
            *specs,
            pl.BlockSpec((1, width), lambda i: (0, i)),
            full((8, emb_width)),
            full((8, width)),
            full((rows, width)),
            full((rows, width)),
        ],
        out_shape=[
            *shapes,
            shape((1, hidden), F32),
            shape((8, emb_width), F32),
            shape((8, width), F32),
            shape((rows, width), F32),
            shape((rows, width), LOW),
        ],
        scratch_shapes=[
            pltpu.VMEM((rows, width), F32),
            pltpu.VMEM((rows, width), LOW),
            pltpu.VMEM((rows, width), F32),
            pltpu.VMEM((rows, LANES), F32),
            pltpu.VMEM((width, rows), LOW),
            pltpu.VMEM((rows, width), F32),
        ],
        compiler_params=PARAMS,
        cost_estimate=CHEAP,
        name="enc_mid_back",
    )(core, elow, final, out, mid, attended, act, slope, vecs, wide, up_w, down_w, wide, inverse)


def enc_qkv_back_kernel(
    packed,
    core_ref,
    x_ref,
    dq_ref,
    dk_ref,
    dv_ref,
    gmid_ref,
    vec_ref,
    more_ref,
    w_ref,
    din_ref,
    *refs,
):
    outs, sums = refs[:-1], refs[-1]
    first = core_ref[0] == 0
    width = x_ref.shape[1]

    def put(cols, grads):
        if packed:
            zero, one = by_core(grads, packed)
            outs[0][:, :, cols] = jnp.where(first, zero, one).astype(LOW)
            outs[1][:, :, cols] = jnp.where(first, one, zero).astype(LOW)
        else:
            outs[0][:, cols] = grads.astype(LOW)

    unit, scale = norm_parts(x_ref[...].astype(F32))
    normed = (unit * vec_ref[0:1, :] + vec_ref[3:4, :]).astype(LOW)
    grads = jnp.concatenate([dq_ref[...], dk_ref[...], dv_ref[...]], axis=1)
    put(slice(0, 3 * width), mm_tn(normed, grads))
    dn = mm_nt(grads, w_ref[...])
    sums[...] = jnp.zeros_like(sums)
    sums[0:16, :] = more_ref[...]
    sums[0:1, :] = col_sum(dn * unit)
    sums[3:4, :] = col_sum(dn)
    sums[4:5, :] = col_sum(dq_ref[...].astype(F32))
    sums[5:6, :] = col_sum(dv_ref[...].astype(F32))
    put(slice(3 * width, 3 * width + LANES), sums[...].T)
    din = gmid_ref[...] + norm_back(dn, unit, scale, vec_ref[0:1, :])
    din_ref[...] = din.astype(LOW)


def enc_qkv_back(core, rows_in, dq, dk, dv, gmid, vecs, more, weight):
    rows, width = rows_in.shape
    whole = full((rows, width))
    cols = 3 * width + LANES
    packed = width // (lax.axis_size("dp") * lax.axis_size("fsdp"))
    packed = packed if packed % 8 == 0 else 0
    outs = [(width // packed // 2, packed, cols)] * 2 if packed else [(width, cols)]
    return pl.pallas_call(
        functools.partial(enc_qkv_back_kernel, packed),
        grid=(1,),
        in_specs=[pl.BlockSpec(memory_space=pltpu.SMEM)]
        + [whole] * 5
        + [full(vecs.shape), full((16, width)), at_col(width, 3 * width, 0)],
        out_specs=[whole] + [full(o) for o in outs],
        out_shape=[shape((rows, width), LOW)] + [shape(o, LOW) for o in outs],
        scratch_shapes=[pltpu.VMEM((LANES, width), F32)],
        compiler_params=PARAMS,
        cost_estimate=CHEAP,
        name="enc_qkv_back",
    )(core, rows_in, dq, dk, dv, gmid, vecs, more, weight)


def dec_in_kernel(limit, order_ref, one_ref, two_ref, pos_ref, vec_ref, w_ref, in_ref, qkv_ref):
    step = pl.program_id(0)
    width = in_ref.shape[1]
    for half, ref in enumerate((one_ref, two_ref)):
        visible = order_ref[0, 2 * step + half] < limit
        rows = slice(half * BLOCK, (half + 1) * BLOCK)
        in_ref[rows, :] = (
            jnp.where(visible, ref[...].astype(F32), vec_ref[9:10, :]) + pos_ref[rows, :]
        )
    unit, _ = norm_parts(in_ref[...])
    normed = (unit * vec_ref[0:1, :] + vec_ref[3:4, :]).astype(LOW)
    qkv = mm(normed, w_ref[...])
    qkv_ref[:, :width] = (qkv[:, :width] + vec_ref[4:5, :]).astype(LOW)
    qkv_ref[:, width : 2 * width] = qkv[:, width : 2 * width].astype(LOW)
    qkv_ref[:, 2 * width :] = (qkv[:, 2 * width :] + vec_ref[5:6, :]).astype(LOW)


def dec_in_call(order, gathered, pos, vecs, weight):
    rows, width = pos.shape
    limit = gathered.shape[0] // BLOCK

    def chosen(half):
        def index(i, order_ref):
            return (jnp.clip(order_ref[0, 2 * i + half], 0, limit - 1), 0)

        return pl.BlockSpec((BLOCK, width), index)

    return pl.pallas_call(
        functools.partial(dec_in_kernel, limit),
        grid_spec=pltpu.PrefetchScalarGridSpec(
            num_scalar_prefetch=1,
            grid=(rows // TILE,),
            in_specs=[
                chosen(0),
                chosen(1),
                pl.BlockSpec((TILE, width), lambda i, o: (i, 0)),
                full(vecs.shape),
                at_col(width, 3 * width, 0),
            ],
            out_specs=[
                pl.BlockSpec((TILE, width), lambda i, o: (i, 0)),
                pl.BlockSpec((TILE, 3 * width), lambda i, o: (i, 0)),
            ],
        ),
        out_shape=[shape((rows, width), F32), shape((rows, 3 * width), LOW)],
        compiler_params=PARAMS,
        cost_estimate=CHEAP,
        name="dec_in",
    )(order, gathered, gathered, pos, vecs, weight)


def dec_mid_kernel(
    steps,
    chunks,
    packed,
    x_ref,
    att_ref,
    cot_ref,
    inv_ref,
    vec_ref,
    b1_ref,
    wo_ref,
    up_ref,
    down_ref,
    out_ref,
    gmid_ref,
    gatt_ref,
    dw_ref,
    db1_ref,
    sum_ref,
    aw1,
    aw2,
    acc,
    dnorm,
    turned,
):
    step = pl.program_id(0)
    width = x_ref.shape[1]
    hidden = chunks * width
    lead = width // 4

    @pl.when(step == 0)
    def _():
        aw1[...] = jnp.zeros_like(aw1)
        aw2[...] = jnp.zeros_like(aw2)
        db1_ref[...] = jnp.zeros_like(db1_ref)
        sum_ref[...] = jnp.zeros_like(sum_ref)

    att = att_ref[...]
    low = cot_ref[...]
    middle = x_ref[...] + mm(att, wo_ref[...]) + vec_ref[6:7, :]
    unit, scale = norm_parts(middle)
    normed = unit * vec_ref[1:2, :] + vec_ref[7:8, :]
    turned[...] = normed.T.astype(LOW)
    normed = normed.astype(LOW)
    acc[...] = middle + vec_ref[8:9, :]
    dnorm[...] = jnp.zeros_like(dnorm)

    def chunk(j, carry):
        cols = pl.ds(pl.multiple_of(j * width, width), width)
        some = pl.ds(pl.multiple_of(j * lead, lead), lead)
        up = up_ref[:, cols]
        down = natural_rows(down_ref[some, :], packed, LOW) if packed else down_ref[cols, :]
        value, slope = gelu_parts(mm(normed, up) + b1_ref[j])
        value = value.astype(LOW)
        acc[...] += mm(value, down)
        grad = mm_tn(value, low)
        if packed:
            grad = grad.reshape(-1, 4, packed, width)
            for part in range(4):
                piece = grad[:, part].reshape(lead, width)
                aw2[some, part * width : (part + 1) * width] += piece
        else:
            aw2[cols, :] += grad
        dhid = (slope * mm_nt(low, down)).astype(LOW)
        aw1[:, cols] += mm(turned[...], dhid)
        db1_ref[j] += col_sum(dhid.astype(F32))
        dnorm[...] += mm_nt(dhid, up)
        return carry

    lax.fori_loop(0, chunks, chunk, 0, unroll=2)
    out_ref[...] = acc[...].astype(LOW)
    dn = dnorm[...]
    sum_ref[0:1, :] += col_sum(dn * unit)
    sum_ref[1:2, :] += col_sum(dn)
    gmid = low.astype(F32) + norm_back(dn, unit, scale, vec_ref[1:2, :])
    gmid_ref[...] = gmid
    mlow = gmid.astype(LOW)
    sum_ref[2:3, :] += col_sum(mlow.astype(F32))
    sum_ref[3:4, :] += col_sum(low.astype(F32))
    aw1[:, hidden:] += mm_tn(att, mlow)
    gatt_ref[...] = (mm_nt(mlow, wo_ref[...]) * inv_ref[...]).astype(LOW)

    @pl.when(step == steps - 1)
    def _():
        dw_ref[:, : hidden + width] = aw1[...].astype(LOW)
        if packed:
            dw_ref[:, hidden + width :] = aw2[...].astype(LOW)
        else:
            for c in range(chunks):
                col = hidden + (1 + c) * width
                dw_ref[:, col : col + width] = aw2[c * width : (c + 1) * width, :].astype(LOW)


def dec_mid(dec_in, attended, cotangent, inverse, vecs, up_bias, wide, weights, proj_at):
    rows, width = dec_in.shape
    hidden = up_bias.shape[1]
    chunks = hidden // width
    tile = 2 * TILE
    steps = rows // tile
    by_row = pl.BlockSpec((tile, width), lambda i: (i, 0))
    if len(weights) == 1:
        packed = width // (lax.axis_size("dp") * lax.axis_size("fsdp"))
        down_shape = (width, hidden)
        specs, operands = [at_col(width, hidden, 0), at_col(width, hidden, 1)], [weights[0]] * 2
    else:
        packed, down_shape = 0, (hidden, width)
        specs, operands = [full((width, hidden)), full(down_shape)], list(weights)
    return pl.pallas_call(
        functools.partial(dec_mid_kernel, steps, chunks, packed),
        grid=(steps,),
        in_specs=[
            by_row,
            by_row,
            by_row,
            by_row,
            full(vecs.shape),
            full((chunks, 1, width)),
            at_col(width, width, proj_at // width),
        ]
        + specs,
        out_specs=[
            by_row,
            by_row,
            by_row,
            full((width, 2 * hidden + width)),
            full((chunks, 1, width)),
            full((8, width)),
        ],
        out_shape=[
            shape((rows, width), LOW),
            shape((rows, width), F32),
            shape((rows, width), LOW),
            shape((width, 2 * hidden + width), LOW),
            shape((chunks, 1, width), F32),
            shape((8, width), F32),
        ],
        scratch_shapes=[
            pltpu.VMEM((width, hidden + width), F32),
            pltpu.VMEM(down_shape, F32),
            pltpu.VMEM((tile, width), F32),
            pltpu.VMEM((tile, width), F32),
            pltpu.VMEM((width, tile), LOW),
        ],
        compiler_params=PARAMS,
        cost_estimate=CHEAP,
        name="dec_mid",
    )(
        dec_in,
        attended,
        cotangent,
        inverse,
        vecs,
        up_bias.reshape(chunks, 1, width),
        wide,
        *operands,
    )


def dec_back_kernel(
    limit,
    each,
    order_ref,
    core_ref,
    x_ref,
    dq_ref,
    dk_ref,
    dv_ref,
    gmid_ref,
    vec_ref,
    more_ref,
    w_ref,
    sum_ref,
    keep_ref,
    send_ref,
):
    step = pl.program_id(0)

    @pl.when(step == 0)
    def _():
        sum_ref[...] = more_ref[...]
        keep_ref[...] = jnp.zeros_like(keep_ref)
        send_ref[...] = jnp.zeros_like(send_ref)

    unit, scale = norm_parts(x_ref[...])
    grads = jnp.concatenate([dq_ref[...], dk_ref[...], dv_ref[...]], axis=1)
    dn = mm_nt(grads, w_ref[...])
    sum_ref[0:1, :] += col_sum(dn * unit)
    sum_ref[2:3, :] += col_sum(dn)
    sum_ref[3:4, :] += col_sum(dq_ref[...].astype(F32))
    sum_ref[4:5, :] += col_sum(dv_ref[...].astype(F32))
    din = gmid_ref[...] + norm_back(dn, unit, scale, vec_ref[0:1, :])
    per = x_ref.shape[0] // BLOCK
    for b in range(per):
        place = order_ref[0, per * step + b]
        rows = din[b * BLOCK : (b + 1) * BLOCK, :]

        owner = place // each
        spot = pl.ds(pl.multiple_of(place % each * BLOCK, BLOCK), BLOCK)

        @pl.when((place < limit) & (owner % 2 == core_ref[0]))
        def _():
            keep_ref[owner // 2, spot, :] = rows.astype(LOW)

        @pl.when((place < limit) & (owner % 2 != core_ref[0]))
        def _():
            send_ref[owner // 2, spot, :] = rows.astype(LOW)

        @pl.when(place >= limit)
        def _():
            sum_ref[8:9, :] += col_sum(rows)


def dec_back(order, core, dec_in, dq, dk, dv, gmid, vecs, more, weight, limit, each):
    rows, width = dec_in.shape
    tile = TILE
    by_row = pl.BlockSpec((tile, width), lambda i, o: (i, 0))
    side = (limit // each // 2, each * BLOCK, width)
    return pl.pallas_call(
        functools.partial(dec_back_kernel, limit, each),
        grid_spec=pltpu.PrefetchScalarGridSpec(
            num_scalar_prefetch=1,
            grid=(rows // tile,),
            in_specs=[pl.BlockSpec(memory_space=pltpu.SMEM)]
            + [by_row] * 5
            + [full(vecs.shape), full((16, width)), at_col(width, 3 * width, 0)],
            out_specs=[full((16, width)), full(side), full(side)],
        ),
        out_shape=[shape((16, width), F32), shape(side, LOW), shape(side, LOW)],
        compiler_params=PARAMS,
        cost_estimate=CHEAP,
        name="dec_back",
    )(order, core, dec_in, dq, dk, dv, gmid, vecs, more, weight)


def dec_grad_kernel(x_ref, dq_ref, dk_ref, dv_ref, vec_ref, sum_ref, dw_ref, acc, sums):
    step = pl.program_id(0)
    width = x_ref.shape[1]

    @pl.when(step == 0)
    def _():
        acc[...] = jnp.zeros_like(acc)

    unit, _ = norm_parts(x_ref[...])
    normed = (unit * vec_ref[0:1, :] + vec_ref[3:4, :]).astype(LOW)
    grads = jnp.concatenate([dq_ref[...], dk_ref[...], dv_ref[...]], axis=1)
    acc[...] += mm_tn(normed, grads)

    @pl.when(step == pl.num_programs(0) - 1)
    def _():
        dw_ref[:, : 3 * width] = acc[...].astype(LOW)
        sums[...] = jnp.zeros_like(sums)
        sums[0:16, :] = sum_ref[...]
        dw_ref[:, 3 * width :] = sums[...].T.astype(LOW)


def dec_grad(dec_in, dq, dk, dv, vecs, sums):
    rows, width = dec_in.shape
    tile = 2 * TILE
    by_row = pl.BlockSpec((tile, width), lambda i: (i, 0))
    packed = (width, 3 * width + LANES)
    return pl.pallas_call(
        dec_grad_kernel,
        grid=(rows // tile,),
        in_specs=[by_row] * 4 + [full(vecs.shape), full((16, width))],
        out_specs=full(packed),
        out_shape=shape(packed, LOW),
        scratch_shapes=[pltpu.VMEM((width, 3 * width), F32), pltpu.VMEM((LANES, width), F32)],
        compiler_params=PARAMS,
        cost_estimate=CHEAP,
        name="dec_grad",
    )(dec_in, dq, dk, dv, vecs, sums)


def positions(count, width):
    places = jnp.arange(count, dtype=jnp.float32)[:, None]
    columns = jnp.arange(width)
    rates = jnp.exp((2 * (columns // 2)).astype(jnp.float32) * (-math.log(10000.0) / width))
    angles = places * rates[None, :]
    return jnp.where((columns % 2 == 0)[None, :], jnp.sin(angles), jnp.cos(angles))


def bits_of(axis):
    size, out = lax.axis_size(axis), []
    while size > 1:
        size //= 2
        out.append((axis, size))
    return out


def all_bits():
    return bits_of("dp") + bits_of("fsdp")


def bit_here(bit):
    axis, stride = bit
    return lax.axis_index(axis) // stride % 2


def swap(value, bit):
    axis, stride = bit
    return lax.ppermute(value, axis, [(i, i ^ stride) for i in range(lax.axis_size(axis))])


def pair(own, got, here, dim):
    dims = tuple(2 if d == dim else 1 for d in range(own.ndim + 1))
    mine = lax.broadcasted_iota(jnp.int32, dims, dim) == here
    return jnp.where(mine, jnp.expand_dims(own, dim), jnp.expand_dims(got, dim))


class Gather:
    def __init__(self, piece, order, held=()):
        self.piece, self.order, self.held = piece, list(order), list(held)

    def step(self):
        canon, bit = all_bits(), self.order.pop(0)
        got = swap(self.piece, bit)
        dim = sum(canon.index(b) < canon.index(bit) for b in self.held)
        self.piece = pair(self.piece, got, bit_here(bit), dim)
        self.held.append(bit)

    def rest(self):
        while self.order:
            self.step()
        return self.piece

    def tie(self, other):
        self.piece, other = lax.optimization_barrier((self.piece, other))
        return other


def gather(piece, order, held=()):
    return Gather(piece, order, held).rest()


def join(pieces, bit):
    both = [pair(own, swap(own, bit), bit_here(bit), own.ndim - 2) for own in pieces]
    both = both[0] if len(both) == 1 else jnp.concatenate(both, axis=-1)
    return both.reshape(-1, both.shape[-1])


def term_sum(terms, kind):
    total = terms[0].astype(F32)
    for term in terms[1:]:
        total = total + term.astype(F32)
    return total.astype(kind)


class Fold:
    def __init__(self, terms, order, held=None):
        self.terms, self.order, self.send = list(terms), list(order), None
        self.left = list(all_bits() if held is None else held)

    def cut(self):
        if self.send is not None:
            return
        bit = self.order[0]
        dim = self.left.index(bit)
        here = bit_here(bit)

        def half(index):
            return [lax.dynamic_index_in_dim(t, index, dim, keepdims=False) for t in self.terms]

        self.send, self.terms = term_sum(half(1 - here), LOW), half(here)

    def pass_on(self):
        bit = self.order.pop(0)
        self.left.remove(bit)
        self.terms.append(swap(self.send, bit))
        self.send = None


def split_fold(keep, send, order, held=None):
    held = all_bits() if held is None else held
    dims = (2,) * (len(held) - 1) + keep.shape[-2:]
    fold = Fold([keep.reshape(dims)], order, held)
    fold.send = send.reshape(dims)
    return fold


def start_beside(folds, inputs):
    for fold in folds:
        fold.cut()
    sends, inputs = lax.optimization_barrier(([f.send for f in folds], inputs))
    for fold, send in zip(folds, sends):
        fold.send = send
        fold.pass_on()
    return inputs


def end_beside(folds, outputs):
    last, outputs = lax.optimization_barrier(([f.terms[-1] for f in folds], outputs))
    for fold, got in zip(folds, last):
        fold.terms[-1] = got
    return outputs


def one_round(folds):
    for fold in folds:
        fold.cut()
        fold.pass_on()
    end_beside(folds, ())


def joined(folds, line):
    terms = [term_sum(f.terms, F32) for f in folds]
    return Fold([jnp.concatenate(terms, axis=-1)], line[::-1], line)


def by_bits(grads):
    bits = len(all_bits())
    rows = grads.shape[0] >> bits
    return grads.reshape((2,) * bits + (rows, grads.shape[1]))


def pack_vectors(pieces, rows):
    wide = jnp.concatenate([p.reshape(-1, rows) for p in pieces], axis=0)
    wide = jnp.pad(wide, ((0, LANES - wide.shape[0]), (0, 0)))
    return wide.T


def unpack_tall(columns, devices, width):
    rows = columns.shape[0] // devices
    parts = columns.shape[1] // width
    return (
        columns.reshape(devices, rows, parts, width)
        .transpose(0, 2, 1, 3)
        .reshape(devices * parts * rows, width)
    )


def repack_tall(weight, devices, rows):
    parts = weight.shape[0] // (devices * rows)
    width = weight.shape[1]
    return (
        weight.reshape(devices, parts, rows, width)
        .transpose(0, 2, 1, 3)
        .reshape(devices * rows, parts * width)
    )


def split_columns(array, widths):
    out, at = [], 0
    for w in widths:
        out.append(array[:, at : at + w])
        at += w
    return out


def long_vector(rows_of, devices):
    parts, total = rows_of.shape
    return rows_of.reshape(parts, devices, total // devices).transpose(1, 0, 2).reshape(1, -1)


def long_rows(vector, devices, rows):
    parts = vector.shape[0] // (devices * rows)
    return vector.reshape(devices, parts, rows).transpose(1, 0, 2).reshape(parts, -1)


def per_device(
    enc_input,
    enc_segments,
    dec_segments,
    block_order,
    dec_cotangent,
    enc_qkv,
    enc_proj,
    enc_fc1,
    enc_fc2,
    enc_gains,
    enc_biases,
    enc_fc1_bias,
    embed,
    mask_token,
    dec_qkv,
    dec_proj,
    dec_fc1,
    dec_fc2,
    dec_gains,
    dec_biases,
    dec_fc1_bias,
    dec_fc2_bias,
):
    devices = lax.axis_size("dp") * lax.axis_size("fsdp")
    enc_rows, width = enc_input.shape
    dec_rows, dwidth = dec_cotangent.shape
    erows = enc_qkv.shape[0]
    drows = dec_qkv.shape[0]
    ff = enc_fc1.shape[1]
    dff = dec_fc1.shape[1]
    emb_row = jnp.pad(dec_biases[0], (0, erows - drows))
    enc_first = jnp.concatenate(
        [
            enc_qkv,
            enc_proj,
            embed,
            pack_vectors([enc_gains, enc_biases, enc_fc1_bias, emb_row], erows),
        ],
        axis=1,
    )
    dec_first = jnp.concatenate(
        [
            dec_qkv,
            dec_proj,
            pack_vectors(
                [dec_gains, dec_biases, dec_fc2_bias[None], mask_token[None], dec_fc1_bias], drows
            ),
        ],
        axis=1,
    )
    proj_at, emb_at = 3 * width, 4 * width
    vec_at = emb_at + dwidth
    dproj_at, dvec_at = 3 * dwidth, 4 * dwidth
    ecut = (vec_at + LANES) // 2 // LANES * LANES
    here = bit_here(bits_of("fsdp")[-1]).reshape(1)
    dp, fsdp = bits_of("dp"), bits_of("fsdp")
    line, core = fsdp[:-1], fsdp[-1]
    packed = erows % 8 == 0 and drows % 16 == 0
    enc_rest, dec_rest = [enc_fc1, enc_fc2], [dec_fc1, dec_fc2]
    if packed:
        enc_rest, dec_rest = ([w] for w in pack_shards(*enc_rest, *dec_rest))
    enc_rest = [lax.all_gather(w, AXES, axis=0, tiled=True) for w in enc_rest]
    lined = gather(enc_first, line)
    one = Gather(lined[..., :ecut], dp[::-1], line)
    two = Gather(lined[..., ecut:], dp, line)
    dec_gather = Gather(dec_first, line + dp)
    one.piece = dec_gather.tie(one.piece)
    while one.order:
        one.step()
        two.step()
        if len(dec_gather.order) > 2:
            dec_gather.step()
        one.piece, two.piece = dec_gather.tie((one.piece, two.piece))
    enc_all = join([one.piece, two.piece], core)
    evecs = enc_all[:, vec_at:].T[:16].astype(F32)
    up_bias = long_vector(evecs[10:14], devices)
    emb_bias = evecs[14].reshape(devices, erows)[:, :drows].reshape(1, -1)

    enc_all, evecs = dec_gather.tie((enc_all, evecs))
    while len(dec_gather.order) > 1:
        dec_gather.step()
    qkv = enc_qkv_call(enc_input, evecs, enc_all)
    enc_col = enc_segments.reshape(-1, 1)
    qkv = dec_gather.tie(qkv)
    dec_gather.step()
    attended, inverse, weights = attend(qkv, enc_segments, enc_col, HDIM)
    attended = dec_gather.tie(attended)
    dec_got = swap(dec_gather.piece, core)
    mid, enc_out, final, act, slope, embedded, down_w = enc_mid(
        enc_input,
        attended,
        evecs,
        up_bias,
        emb_bias,
        enc_all,
        enc_rest,
        proj_at,
        emb_at,
    )
    dec_got, embedded = lax.optimization_barrier((dec_got, embedded))
    emb_gather = Gather(embedded, fsdp)
    emb_gather.step()
    pos = positions(dec_rows, dwidth)
    dec_rest, pos = emb_gather.tie((dec_rest, pos))
    dec_rest = [lax.all_gather(w, AXES, axis=0, tiled=True) for w in dec_rest]
    emb_gather.step()
    dec_all = pair(dec_gather.piece, dec_got, bit_here(core), dec_got.ndim - 2)
    dec_all = dec_all.reshape(-1, dec_got.shape[-1])
    dvecs = dec_all[:, dvec_at:].T[:16].astype(F32)
    dup_bias = long_vector(dvecs[10:14], devices)
    dec_all, dvecs, dup_bias = emb_gather.tie((dec_all, dvecs, dup_bias))
    gathered = emb_gather.rest().reshape(-1, dwidth)
    limit = gathered.shape[0] // BLOCK
    dec_in, dqkv = dec_in_call(block_order, gathered, pos, dvecs, dec_all)
    dec_col = dec_segments.reshape(-1, 1)
    dattended, dinverse, dweights = attend(dqkv, dec_segments, dec_col, DHDIM)
    dec_out, dgmid, dgatt, dw_rest, db1, dsum_mid = dec_mid(
        dec_in,
        dattended,
        dec_cotangent,
        dinverse,
        dvecs,
        dup_bias,
        dec_all,
        dec_rest,
        dproj_at,
    )
    if not packed:
        chunks = dff // dwidth
        tall = dw_rest[:, dff + dwidth :].reshape(dwidth, chunks, dwidth).transpose(1, 0, 2)
        tall = repack_tall(tall.reshape(dff, dwidth), devices, drows)
        dw_rest = jnp.concatenate([dw_rest[:, : dff + dwidth], tall], axis=1)
    dec_own = lax.psum_scatter(dw_rest, "dp", scatter_dimension=0, tiled=True)
    dec_more = jnp.concatenate(
        [
            jnp.zeros((1, dwidth), F32),
            dsum_mid[0:1],
            jnp.zeros((3, dwidth), F32),
            dsum_mid[2:3],
            dsum_mid[1:2],
            dsum_mid[3:4],
            jnp.zeros((1, dwidth), F32),
            long_rows(db1.reshape(-1), devices, drows),
            jnp.zeros((3, dwidth), F32),
        ],
        axis=0,
    )
    dgatt, dec_more = lax.optimization_barrier((dgatt, dec_more))
    ddq, ddk, ddv = attend_back(dqkv, dattended, dgatt, dweights, dec_segments, DHDIM)
    dsum, keep, send = dec_back(
        block_order,
        here,
        dec_in,
        ddq,
        ddk,
        ddv,
        dgmid,
        dvecs,
        dec_more,
        dec_all,
        limit,
        enc_rows // BLOCK,
    )
    emb_fold = split_fold(keep, send, fsdp[::-1], fsdp)
    emb_fold.pass_on()
    dsum = end_beside([emb_fold], dsum)
    emb_fold.cut()
    emb_fold.pass_on()
    dec_grads = dec_grad(dec_in, ddq, ddk, ddv, dvecs, dsum)
    dec_grads, dec_own = end_beside([emb_fold], (dec_grads, dec_own))
    dec_grads = lax.psum_scatter(dec_grads, "dp", scatter_dimension=0, tiled=True)
    for _ in line[1:]:
        one_round([emb_fold])
    elow = term_sum(emb_fold.terms, LOW)
    *ew, eb1, esum_emb, esum_mid, gmid, gatt = enc_mid_back(
        here,
        elow,
        final,
        enc_out,
        mid,
        attended,
        act,
        slope,
        inverse,
        evecs,
        enc_all,
        enc_rest[0],
        down_w,
        proj_at,
        emb_at,
    )
    gatt, dec_own, dec_grads = lax.optimization_barrier((gatt, dec_own, dec_grads))
    dec_own = jnp.concatenate([dec_own, dec_grads], axis=1)
    dec_own = lax.psum_scatter(dec_own, "fsdp", scatter_dimension=0, tiled=True)
    spread = [core] + line[::-1] + dp
    if packed:
        early = split_fold(ew[0], ew[1], spread)
        edown = split_fold(ew[2], ew[3], [core] + dp[::-1])
        eup = split_fold(ew[4], ew[5], [core] + dp)
    else:
        early = Fold([by_bits(ew[0])], spread)
        edown = Fold([by_bits(repack_tall(ew[1], devices, erows))], [core] + dp[::-1])
        eup = Fold([by_bits(ew[2])], [core] + dp)
    side = [eup, edown, early]
    gatt = start_beside(side, gatt)
    gatt = end_beside(side, gatt)
    gatt = start_beside(side, gatt)
    emb_sum = jnp.pad(esum_emb[0].reshape(devices, drows), ((0, 0), (0, erows - drows)))
    enc_more = jnp.concatenate(
        [
            jnp.zeros((1, width), F32),
            esum_mid[3:4],
            esum_mid[0:1],
            jnp.zeros((3, width), F32),
            esum_mid[5:6],
            esum_mid[4:5],
            esum_mid[2:3],
            esum_mid[1:2],
            long_rows(eb1.reshape(-1), devices, erows),
            emb_sum.reshape(1, -1),
            jnp.zeros((1, width), F32),
        ],
        axis=0,
    )
    dq, dk, dv = attend_back(qkv, attended, gatt, weights, enc_segments, HDIM)
    enc_in_grad, *enc_grads = enc_qkv_back(
        here, enc_input, dq, dk, dv, gmid, evecs, enc_more, enc_all
    )
    if packed:
        chip = split_fold(enc_grads[0], enc_grads[1], [core])
    else:
        chip = Fold([by_bits(enc_grads[0])], [core])
        chip.cut()
    chip.send, dec_own = end_beside(side, (chip.send, dec_own))
    chip.pass_on()
    while eup.order:
        one_round(side)
    end_beside([chip], ())
    gcut = (3 * width + LANES) // 2 // LANES * LANES
    one = Fold([t[..., :gcut] for t in chip.terms], dp, all_bits()[:-1])
    two = Fold([t[..., gcut:] for t in chip.terms], dp[::-1], all_bits()[:-1])
    rest = joined([eup, edown], line)
    one_round([one, two, rest, early])
    if rest.order:
        rest.cut()
        rest.pass_on()
    while one.order or early.order:
        one_round([f for f in (one, two, early) if f.order])
    first = joined([one, two], line)
    first.cut()
    first.pass_on()
    end_beside([first, rest], ())
    while first.order or rest.order:
        one_round([f for f in (first, rest) if f.order])
    ep, em = split_columns(term_sum(early.terms, F32), [width, dwidth])
    eu, ed = split_columns(term_sum(rest.terms, F32), [ff, ff])
    ed = unpack_tall(ed, 1, width)
    eq, ev = split_columns(term_sum(first.terms, F32), [3 * width, LANES])
    ru, rp, rd, rq, rv = split_columns(
        dec_own.astype(F32), [dff, dwidth, dff, 3 * dwidth, LANES]
    )
    rd = unpack_tall(rd, 1, dwidth)
    rv = rv.T
    ev = ev.T
    return (
        dec_out,
        enc_in_grad,
        eq,
        ep,
        eu,
        ed,
        ev[:3],
        ev[3:10],
        ev[10:14].reshape(-1),
        em,
        rv[8],
        rq,
        rp,
        ru,
        rd,
        rv[:2],
        jnp.concatenate([ev[14:15, :drows], rv[2:7]], axis=0),
        rv[9:13].reshape(-1),
        rv[7],
    )


def solution(mesh):
    in_specs = (
        P(("dp", "fsdp"), None),
        P(("dp", "fsdp"), None),
        P(("dp", "fsdp"), None),
        P("dp", "fsdp"),
        P(("dp", "fsdp"), None),
        P(("dp", "fsdp"), None),
        P(("dp", "fsdp"), None),
        P(("dp", "fsdp"), None),
        P(("dp", "fsdp"), None),
        P(None, ("dp", "fsdp")),
        P(None, ("dp", "fsdp")),
        P(("dp", "fsdp")),
        P(("dp", "fsdp"), None),
        P(("dp", "fsdp")),
        P(("dp", "fsdp"), None),
        P(("dp", "fsdp"), None),
        P(("dp", "fsdp"), None),
        P(("dp", "fsdp"), None),
        P(None, ("dp", "fsdp")),
        P(None, ("dp", "fsdp")),
        P(("dp", "fsdp")),
        P(("dp", "fsdp")),
    )
    out_specs = (
        P(("dp", "fsdp"), None),
        P(("dp", "fsdp"), None),
        P(("dp", "fsdp"), None),
        P(("dp", "fsdp"), None),
        P(("dp", "fsdp"), None),
        P(("dp", "fsdp"), None),
        P(None, ("dp", "fsdp")),
        P(None, ("dp", "fsdp")),
        P(("dp", "fsdp")),
        P(("dp", "fsdp"), None),
        P(("dp", "fsdp")),
        P(("dp", "fsdp"), None),
        P(("dp", "fsdp"), None),
        P(("dp", "fsdp"), None),
        P(("dp", "fsdp"), None),
        P(None, ("dp", "fsdp")),
        P(None, ("dp", "fsdp")),
        P(("dp", "fsdp")),
        P(("dp", "fsdp")),
    )
    return jax.shard_map(
        per_device, mesh=mesh, in_specs=in_specs, out_specs=out_specs, check_vma=False
    )
```

```python
import functools
import math

import jax
import jax.numpy as jnp
from jax import lax
from jax.experimental import pallas as pl
from jax.experimental.pallas import tpu as pltpu
from jax.sharding import PartitionSpec as P

HDIM = 64
DHDIM = 32
BLOCK = 128
LANES = 128
TILE = 256
SPAN = 128
GROUP = 256
EPSILON = 1e-06
NEGATIVE = -1e30
LOG2E = math.log2(math.e)
AXES = ("dp", "fsdp")
F32 = jnp.float32
LOW = jnp.bfloat16
PARAMS = pltpu.CompilerParams(vmem_limit_bytes=56 * 1024 * 1024)


def mm(left, right):
    return jnp.dot(left, right, preferred_element_type=F32)


def mm_tn(left, right):
    return lax.dot_general(left, right, (((0,), (0,)), ((), ())), preferred_element_type=F32)


def mm_nt(left, right):
    return lax.dot_general(left, right, (((1,), (1,)), ((), ())), preferred_element_type=F32)


def col_sum(values):
    return jnp.sum(values, axis=0, keepdims=True)


def norm_parts(values):
    centred = values - jnp.mean(values, axis=-1, keepdims=True)
    variance = jnp.mean(centred * centred, axis=-1, keepdims=True)
    scale = lax.rsqrt(variance + EPSILON)
    return centred * scale, scale


def norm_back(grad, unit, scale, gain):
    inner = grad * gain
    mean_inner = jnp.mean(inner, axis=-1, keepdims=True)
    mean_cross = jnp.mean(inner * unit, axis=-1, keepdims=True)
    return scale * (inner - mean_inner - unit * mean_cross)


def gelu_parts(hidden):
    cdf = 0.5 + 0.5 * lax.erf(hidden * (0.5**0.5))
    density = jnp.exp(hidden * hidden * -0.5) * (1.0 / math.sqrt(2.0 * math.pi))
    return hidden * cdf, cdf + hidden * density


CHEAP = pl.CostEstimate(flops=1 << 20, bytes_accessed=1 << 16, transcendentals=0)


def full(shape):
    return pl.BlockSpec(shape, lambda *_: (0,) * len(shape))


def at_col(rows, cols, index):
    return pl.BlockSpec((rows, cols), lambda *_: (0, index))


def shape(dims, kind):
    return jax.ShapeDtypeStruct(dims, kind)


def lane_mask(head, head_dim, kind):
    lane = lax.broadcasted_iota(jnp.int32, (1, GROUP), 1)
    inside = (lane >= head * head_dim) & (lane < (head + 1) * head_dim)
    return inside.astype(F32).astype(kind)


def stack_heads(stacked, index, rows, head_dim):
    count = rows.shape[0]
    for h in range(GROUP // head_dim):
        stacked[index, h * count : (h + 1) * count, :] = rows * lane_mask(h, head_dim, LOW)


def tile_range(seg_ref, start, size, other, count):
    first, last = seg_ref[0, start], seg_ref[0, start + size - 1]
    low, high = jnp.int32(0), jnp.int32(count)
    for tile in range(count):
        low += (seg_ref[0, tile * other + other - 1] < first).astype(jnp.int32)
        high -= (seg_ref[0, tile * other] > last).astype(jnp.int32)
    return low, high


def attend_kernel(
    head_dim,
    tiles,
    seg_ref,
    q_ref,
    k_ref,
    v_ref,
    row_ref,
    col_ref,
    out_ref,
    inv_ref,
    exp_ref,
    km,
    vt,
    held,
    acc,
    inverse,
    top,
    tot,
):
    heads = GROUP // head_dim
    here = pl.program_id(1)
    factor = head_dim ** (-0.5) * LOG2E

    @pl.when(here == 0)
    def _():
        for u in range(tiles):
            rows = slice(u * SPAN, (u + 1) * SPAN)
            vt[u] = v_ref[rows, :].astype(F32).T.astype(LOW)
            stack_heads(km, u, k_ref[rows, :], head_dim)

    acc[...] = jnp.zeros_like(acc)
    top[...] = jnp.full_like(top, NEGATIVE)
    tot[...] = jnp.zeros_like(tot)
    query = q_ref[...]
    row = row_ref[...]

    def score(u, carry):
        start = pl.multiple_of(u * SPAN, SPAN)
        same = col_ref[pl.ds(start, SPAN), :] == row
        every = mm_nt(km[u], query)
        for h in range(heads):
            scores = jnp.where(same, every[h * SPAN : (h + 1) * SPAN, :], NEGATIVE)
            held[u, h] = scores
            top[h : h + 1, :] = jnp.maximum(
                top[h : h + 1, :], jnp.max(scores, axis=0, keepdims=True)
            )
        return carry

    def mix(u, carry):
        for h in range(heads):
            weights = jnp.exp2((held[u, h] - top[h : h + 1, :]) * factor)
            tot[h : h + 1, :] += col_sum(weights)
            span = slice(h * head_dim, (h + 1) * head_dim)
            weights = weights.astype(LOW)
            exp_ref[0, 0, u, :, h * TILE : (h + 1) * TILE] = weights
            acc[span, :] += mm(vt[u, span, :], weights)
        return carry

    low, high = tile_range(seg_ref, here * TILE, TILE, SPAN, tiles)
    lax.fori_loop(low, high, score, 0)
    lax.fori_loop(low, high, mix, 0)
    for h in range(heads):
        span = slice(h * head_dim, (h + 1) * head_dim)
        inverse[span, :] = jnp.broadcast_to(1.0 / tot[h : h + 1, :], (head_dim, TILE))
    out_ref[...] = (acc[...] * inverse[...]).T.astype(LOW)
    inv_ref[...] = inverse[...].T


def attend(qkv, segments, seg_col, head_dim):
    rows, width = qkv.shape[0], qkv.shape[1] // 3
    groups, steps, tiles, heads = width // GROUP, rows // TILE, rows // SPAN, GROUP // head_dim
    return pl.pallas_call(
        functools.partial(attend_kernel, head_dim, tiles),
        grid_spec=pltpu.PrefetchScalarGridSpec(
            num_scalar_prefetch=1,
            grid=(groups, steps),
            in_specs=[
                pl.BlockSpec((TILE, GROUP), lambda g, t, s: (t, g)),
                pl.BlockSpec((rows, GROUP), lambda g, t, s: (0, groups + g)),
                pl.BlockSpec((rows, GROUP), lambda g, t, s: (0, 2 * groups + g)),
                pl.BlockSpec((1, TILE), lambda g, t, s: (0, t)),
                pl.BlockSpec((rows, 1), lambda g, t, s: (0, 0)),
            ],
            out_specs=[
                pl.BlockSpec((TILE, GROUP), lambda g, t, s: (t, g)),
                pl.BlockSpec((TILE, GROUP), lambda g, t, s: (t, g)),
                pl.BlockSpec((1, 1, tiles, SPAN, heads * TILE), lambda g, t, s: (g, t, 0, 0, 0)),
            ],
            scratch_shapes=[
                pltpu.VMEM((tiles, heads * SPAN, GROUP), LOW),
                pltpu.VMEM((tiles, GROUP, SPAN), LOW),
                pltpu.VMEM((tiles, heads, SPAN, TILE), F32),
                pltpu.VMEM((GROUP, TILE), F32),
                pltpu.VMEM((GROUP, TILE), F32),
                pltpu.VMEM((8, TILE), F32),
                pltpu.VMEM((8, TILE), F32),
            ],
        ),
        out_shape=[
            shape((rows, width), LOW),
            shape((rows, width), F32),
            shape((groups, steps, tiles, SPAN, heads * TILE), LOW),
        ],
        compiler_params=PARAMS,
        cost_estimate=CHEAP,
        name="attend",
    )(segments, qkv, qkv, qkv, segments, seg_col)


def attend_back_kernel(
    head_dim,
    tiles,
    seg_ref,
    q_ref,
    k_ref,
    v_ref,
    o_ref,
    g_ref,
    exp_ref,
    dq_ref,
    dk_ref,
    dv_ref,
    kt,
    vm,
    qm,
    gm,
    dqt,
    delta,
    dk_acc,
    dv_acc,
):
    heads = GROUP // head_dim
    here = pl.program_id(1)
    scale = head_dim ** (-0.5)

    @pl.when(here == 0)
    def _():
        dk_acc[...] = jnp.zeros_like(dk_acc)
        dv_acc[...] = jnp.zeros_like(dv_acc)
        for u in range(tiles):
            rows = slice(u * SPAN, (u + 1) * SPAN)
            kt[u] = k_ref[rows, :].astype(F32).T.astype(LOW)
            stack_heads(vm, u, v_ref[rows, :], head_dim)

    grads = g_ref[...]
    both = (grads.astype(F32) * o_ref[...].astype(F32)).T
    for h in range(heads):
        delta[h : h + 1, :] = col_sum(both[h * head_dim : (h + 1) * head_dim, :])
    stack_heads(qm, 0, q_ref[...], head_dim)
    stack_heads(gm, 0, grads, head_dim)
    dqt[...] = jnp.zeros_like(dqt)

    def step(u, carry):
        rows = pl.ds(pl.multiple_of(u * SPAN, SPAN), SPAN)
        every = mm_nt(vm[u], grads)
        dv_acc[rows, :] += mm(exp_ref[0, 0, u], gm[0])
        pieces = []
        for h in range(heads):
            grad_probs = every[h * SPAN : (h + 1) * SPAN, :] - delta[h : h + 1, :]
            weights = exp_ref[0, 0, u, :, h * TILE : (h + 1) * TILE]
            pieces.append((weights.astype(F32) * grad_probs).astype(LOW))
        for h in range(heads):
            span = slice(h * head_dim, (h + 1) * head_dim)
            dqt[span, :] += mm(kt[u, span, :], pieces[h])
        dk_acc[rows, :] += mm(jnp.concatenate(pieces, axis=1), qm[0])
        return carry

    low, high = tile_range(seg_ref, here * TILE, TILE, SPAN, tiles)
    lax.fori_loop(low, high, step, 0)
    dq_ref[...] = (dqt[...] * scale).T.astype(LOW)

    @pl.when(here == pl.num_programs(1) - 1)
    def _():
        dk_ref[...] = (dk_acc[...] * scale).astype(LOW)
        dv_ref[...] = dv_acc[...].astype(LOW)


def attend_back(qkv, attended, grad, weights, segments, head_dim):
    rows, width = attended.shape
    groups, steps, tiles, heads = width // GROUP, rows // TILE, rows // SPAN, GROUP // head_dim
    whole = pl.BlockSpec((rows, GROUP), lambda g, t, s: (0, g))
    piece = pl.BlockSpec((TILE, GROUP), lambda g, t, s: (t, g))
    return pl.pallas_call(
        functools.partial(attend_back_kernel, head_dim, tiles),
        grid_spec=pltpu.PrefetchScalarGridSpec(
            num_scalar_prefetch=1,
            grid=(groups, steps),
            in_specs=[
                piece,
                pl.BlockSpec((rows, GROUP), lambda g, t, s: (0, groups + g)),
                pl.BlockSpec((rows, GROUP), lambda g, t, s: (0, 2 * groups + g)),
                piece,
                piece,
                pl.BlockSpec((1, 1, tiles, SPAN, heads * TILE), lambda g, t, s: (g, t, 0, 0, 0)),
            ],
            out_specs=[piece, whole, whole],
            scratch_shapes=[
                pltpu.VMEM((tiles, GROUP, SPAN), LOW),
                pltpu.VMEM((tiles, heads * SPAN, GROUP), LOW),
                pltpu.VMEM((1, heads * TILE, GROUP), LOW),
                pltpu.VMEM((1, heads * TILE, GROUP), LOW),
                pltpu.VMEM((GROUP, TILE), F32),
                pltpu.VMEM((8, TILE), F32),
                pltpu.VMEM((rows, GROUP), F32),
                pltpu.VMEM((rows, GROUP), F32),
            ],
        ),
        out_shape=[shape((rows, width), LOW)] * 3,
        compiler_params=PARAMS,
        cost_estimate=CHEAP,
        name="attend_back",
    )(segments, qkv, qkv, qkv, attended, grad, weights)


def pack_kernel(up_ref, down_ref, dup_ref, ddown_ref, out_ref, dout_ref):
    for up, down, out in ((up_ref, down_ref, out_ref), (dup_ref, ddown_ref, dout_ref)):
        rows, cols = up.shape
        out[:, :cols] = up[...]
        wide = down[...].astype(F32)
        width = down.shape[1]
        for part in range(4):
            piece = wide[part * rows : (part + 1) * rows, :].astype(LOW)
            out[:, cols + part * width : cols + (part + 1) * width] = piece


def pack_shards(*shards):
    outs = [shape((w.shape[0], 2 * w.shape[1]), LOW) for w in shards[::2]]
    return pl.pallas_call(
        pack_kernel,
        in_specs=[full(s.shape) for s in shards],
        out_specs=[full(o.shape) for o in outs],
        out_shape=outs,
        grid=(1,),
        compiler_params=PARAMS,
        cost_estimate=CHEAP,
        name="pack",
    )(*shards)


def by_core(grads, group):
    pairs = grads.reshape(-1, 2, group, grads.shape[1])
    return pairs[:, 0], pairs[:, 1]


def natural_rows(block, group, kind):
    width = block.shape[1] // 4
    parts = [
        block[:, i * width : (i + 1) * width].astype(kind).reshape(-1, group, width)
        for i in range(4)
    ]
    return jnp.stack(parts, axis=1).reshape(-1, width).astype(LOW)


def enc_qkv_kernel(x_ref, vec_ref, w_ref, out_ref, normed):
    part = pl.program_id(0)

    @pl.when(part == 0)
    def _():
        unit, _ = norm_parts(x_ref[...].astype(F32))
        normed[...] = (unit * vec_ref[0:1, :] + vec_ref[3:4, :]).astype(LOW)

    bias = jnp.where(part == 0, vec_ref[4:5, :], jnp.where(part == 2, vec_ref[5:6, :], 0.0))
    out_ref[...] = (mm(normed[...], w_ref[...]) + bias).astype(LOW)


def enc_qkv_call(rows_in, vecs, weight):
    rows, width = rows_in.shape
    return pl.pallas_call(
        enc_qkv_kernel,
        grid=(3,),
        in_specs=[
            full((rows, width)),
            full(vecs.shape),
            pl.BlockSpec((width, width), lambda i: (0, i)),
        ],
        out_specs=pl.BlockSpec((rows, width), lambda i: (0, i)),
        out_shape=shape((rows, 3 * width), LOW),
        scratch_shapes=[pltpu.VMEM((rows, width), LOW)],
        compiler_params=PARAMS,
        cost_estimate=CHEAP,
        name="enc_qkv",
    )(rows_in, vecs, weight)


def enc_mid_kernel(
    chunks,
    packed,
    x_ref,
    att_ref,
    vec_ref,
    b1_ref,
    eb_ref,
    wo_ref,
    we_ref,
    *refs,
):
    up_ref, down_ref, *refs = refs
    mid_ref, out_ref, final_ref, act_ref, slope_ref, emb_ref, *refs = refs
    naturals, (normed, acc) = refs[:-2], refs[-2:]
    part = pl.program_id(0)

    @pl.when(part == 0)
    def _():
        middle = x_ref[...].astype(F32) + mm(att_ref[...], wo_ref[...]) + vec_ref[6:7, :]
        mid_ref[...] = middle
        unit, _ = norm_parts(middle)
        normed[...] = (unit * vec_ref[1:2, :] + vec_ref[7:8, :]).astype(LOW)
        acc[...] = middle + vec_ref[8:9, :]

    down = down_ref[...]
    if packed:
        down = natural_rows(down, packed, F32)
        naturals[0][...] = down
    hidden = mm(normed[...], up_ref[...]) + b1_ref[...]
    value, slope = gelu_parts(hidden)
    value = value.astype(LOW)
    act_ref[...] = value
    slope_ref[...] = slope
    acc[...] += mm(value, down)

    @pl.when(part == chunks - 1)
    def _():
        result = acc[...]
        out_ref[...] = result
        unit, _ = norm_parts(result)
        final = (unit * vec_ref[2:3, :] + vec_ref[9:10, :]).astype(LOW)
        final_ref[...] = final
        emb_ref[...] = (mm(final, we_ref[...]) + eb_ref[...]).astype(LOW)


def enc_mid(rows_in, attended, vecs, up_bias, emb_bias, wide, weights, proj_at, emb_at):
    rows, width = rows_in.shape
    hidden = up_bias.shape[1]
    emb_width = emb_bias.shape[1]
    chunks = hidden // width
    by_row = pl.BlockSpec((width, width), lambda i: (i, 0))
    specs = [pl.BlockSpec((width, width), lambda i: (0, i))]
    if len(weights) == 1:
        packed = width // (lax.axis_size("dp") * lax.axis_size("fsdp"))
        specs.append(pl.BlockSpec((width // 4, hidden), lambda i: (i, 1)))
        operands = [weights[0]] * 2
        natural_specs, natural_shapes = [by_row], [shape((hidden, width), LOW)]
    else:
        packed = 0
        specs.append(by_row)
        operands, natural_specs, natural_shapes = list(weights), [], []
    outs = pl.pallas_call(
        functools.partial(enc_mid_kernel, chunks, packed),
        grid=(chunks,),
        in_specs=[
            full((rows, width)),
            full((rows, width)),
            full(vecs.shape),
            pl.BlockSpec((1, width), lambda i: (0, i)),
            full((1, emb_width)),
            at_col(width, width, proj_at // width),
            at_col(width, emb_width, emb_at // emb_width),
        ]
        + specs,
        out_specs=[
            full((rows, width)),
            full((rows, width)),
            full((rows, width)),
            pl.BlockSpec((rows, width), lambda i: (0, i)),
            pl.BlockSpec((rows, width), lambda i: (0, i)),
            full((rows, emb_width)),
        ]
        + natural_specs,
        out_shape=[
            shape((rows, width), F32),
            shape((rows, width), F32),
            shape((rows, width), LOW),
            shape((rows, hidden), LOW),
            shape((rows, hidden), F32),
            shape((rows, emb_width), LOW),
        ]
        + natural_shapes,
        scratch_shapes=[pltpu.VMEM((rows, width), LOW), pltpu.VMEM((rows, width), F32)],
        compiler_params=PARAMS,
        cost_estimate=CHEAP,
        name="enc_mid",
    )(rows_in, attended, vecs, up_bias, emb_bias, wide, wide, *operands)
    return outs if packed else list(outs) + [weights[1]]


def enc_mid_back_kernel(
    chunks,
    packed,
    core_ref,
    elow_ref,
    final_ref,
    out_ref,
    mid_ref,
    att_ref,
    act_ref,
    slope_ref,
    vec_ref,
    wo_ref,
    w1_ref,
    w2_ref,
    we_ref,
    inv_ref,
    *refs,
):
    if packed:
        keep_ref, send_ref, keep2_ref, send2_ref, keep1_ref, send1_ref, *refs = refs
    else:
        keep_ref, dw2_ref, dw1_ref, *refs = refs
    (
        db1_ref,
    esum_ref,
    sum_ref,
    gmid_ref,
    gatt_ref,
    grad,
    grad_low,
    unit_two,
    scale_two,
    normed,
        dnorm,
    ) = refs
    first = core_ref[0] == 0

    def put(cols, grads):
        if packed:
            zero, one = by_core(grads, packed)
            keep_ref[:, :, cols] = jnp.where(first, zero, one).astype(LOW)
            send_ref[:, :, cols] = jnp.where(first, one, zero).astype(LOW)
        else:
            keep_ref[:, cols] = grads.astype(LOW)

    part = pl.program_id(0)

    @pl.when(part == 0)
    def _():
        elow = elow_ref[...]
        width = final_ref.shape[1]
        put(slice(width, width + elow.shape[1]), mm_tn(final_ref[...], elow))
        esum_ref[...] = jnp.zeros_like(esum_ref)
        esum_ref[0:1, :] = col_sum(elow.astype(F32))
        unit, scale = norm_parts(out_ref[...])
        dfinal = mm_nt(elow, we_ref[...])
        sum_ref[...] = jnp.zeros_like(sum_ref)
        sum_ref[0:1, :] = col_sum(dfinal * unit)
        sum_ref[1:2, :] = col_sum(dfinal)
        total = norm_back(dfinal, unit, scale, vec_ref[2:3, :])
        grad[...] = total
        low = total.astype(LOW)
        grad_low[...] = low
        sum_ref[2:3, :] = col_sum(low.astype(F32))
        unit, scale = norm_parts(mid_ref[...])
        unit_two[...] = unit
        scale_two[...] = jnp.broadcast_to(scale, scale_two.shape)
        normed[...] = (unit * vec_ref[1:2, :] + vec_ref[7:8, :]).T.astype(LOW)
        dnorm[...] = jnp.zeros_like(dnorm)

    low = grad_low[...]
    down = mm_tn(act_ref[...], low)
    if packed:
        width = low.shape[1]
        down = down.reshape(-1, 4, packed, width)
        for i in range(4):
            zero, one = by_core(down[:, i].reshape(-1, width), packed)
            cols = slice(i * width, (i + 1) * width)
            keep2_ref[:, :, cols] = jnp.where(first, zero, one).astype(LOW)
            send2_ref[:, :, cols] = jnp.where(first, one, zero).astype(LOW)
    else:
        dw2_ref[...] = down.astype(LOW)
    dhid = (slope_ref[...] * mm_nt(low, w2_ref[...])).astype(LOW)
    up = mm(normed[...], dhid)
    if packed:
        zero, one = by_core(up, packed)
        keep1_ref[...] = jnp.where(first, zero, one).astype(LOW)
        send1_ref[...] = jnp.where(first, one, zero).astype(LOW)
    else:
        dw1_ref[...] = up.astype(LOW)
    db1_ref[...] = col_sum(dhid.astype(F32))
    dnorm[...] += mm_nt(dhid, w1_ref[...])

    @pl.when(part == chunks - 1)
    def _():
        dn = dnorm[...]
        unit = unit_two[...]
        sum_ref[3:4, :] = col_sum(dn * unit)
        sum_ref[4:5, :] = col_sum(dn)
        gmid = grad[...] + norm_back(dn, unit, scale_two[:, 0:1], vec_ref[1:2, :])
        gmid_ref[...] = gmid
        mlow = gmid.astype(LOW)
        sum_ref[5:6, :] = col_sum(mlow.astype(F32))
        put(slice(0, mlow.shape[1]), mm_tn(att_ref[...], mlow))
        gatt_ref[...] = (mm_nt(mlow, wo_ref[...]) * inv_ref[...]).astype(LOW)


def enc_mid_back(
    core, elow, final, out, mid, attended, act, slope, inverse, vecs, wide, up_w, down_w, proj_at, emb_at
):
    rows, width = mid.shape
    hidden = down_w.shape[0]
    emb_width = elow.shape[1]
    chunks = hidden // width
    packed = width // (lax.axis_size("dp") * lax.axis_size("fsdp"))
    packed = packed if packed % 8 == 0 else 0
    by_col = pl.BlockSpec((rows, width), lambda i: (0, i))
    if packed:
        chips = width // packed // 2
        two = pl.BlockSpec((chips // chunks, packed, hidden), lambda i: (i, 0, 0))
        one = pl.BlockSpec((chips, packed, width), lambda i: (0, 0, i))
        side = (chips, packed, width + emb_width)
        specs = [full(side), full(side), two, two, one, one]
        shapes = [shape(side, LOW)] * 2 + [shape((chips, packed, hidden), LOW)] * 4
    else:
        specs = [
            full((width, width + emb_width)),
            pl.BlockSpec((width, width), lambda i: (i, 0)),
            pl.BlockSpec((width, width), lambda i: (0, i)),
        ]
        shapes = [
            shape((width, width + emb_width), LOW),
            shape((hidden, width), LOW),
            shape((width, hidden), LOW),
        ]
    return pl.pallas_call(
        functools.partial(enc_mid_back_kernel, chunks, packed),
        grid=(chunks,),
        in_specs=[
            pl.BlockSpec(memory_space=pltpu.SMEM),
            full((rows, emb_width)),
            full((rows, width)),
            full((rows, width)),
            full((rows, width)),
            full((rows, width)),
            by_col,
            by_col,
            full(vecs.shape),
            at_col(width, width, proj_at // width),
            pl.BlockSpec((width, width), lambda i: (0, i)),
            pl.BlockSpec((width, width), lambda i: (i, 0)),
            at_col(width, emb_width, emb_at // emb_width),
            full((rows, width)),
        ],
        out_specs=[
            *specs,
            pl.BlockSpec((1, width), lambda i: (0, i)),
            full((8, emb_width)),
            full((8, width)),
            full((rows, width)),
            full((rows, width)),
        ],
        out_shape=[
            *shapes,
            shape((1, hidden), F32),
            shape((8, emb_width), F32),
            shape((8, width), F32),
            shape((rows, width), F32),
            shape((rows, width), LOW),
        ],
        scratch_shapes=[
            pltpu.VMEM((rows, width), F32),
            pltpu.VMEM((rows, width), LOW),
            pltpu.VMEM((rows, width), F32),
            pltpu.VMEM((rows, LANES), F32),
            pltpu.VMEM((width, rows), LOW),
            pltpu.VMEM((rows, width), F32),
        ],
        compiler_params=PARAMS,
        cost_estimate=CHEAP,
        name="enc_mid_back",
    )(core, elow, final, out, mid, attended, act, slope, vecs, wide, up_w, down_w, wide, inverse)


def enc_qkv_back_kernel(
    packed,
    core_ref,
    x_ref,
    dq_ref,
    dk_ref,
    dv_ref,
    gmid_ref,
    vec_ref,
    more_ref,
    w_ref,
    din_ref,
    *refs,
):
    outs, sums = refs[:-1], refs[-1]
    first = core_ref[0] == 0
    width = x_ref.shape[1]

    cut = outs[0].shape[-1]

    def put(ref, cols, grads):
        if packed:
            zero, one = by_core(grads, packed)
            outs[ref][:, :, cols] = jnp.where(first, zero, one).astype(LOW)
            outs[ref + 2][:, :, cols] = jnp.where(first, one, zero).astype(LOW)
        else:
            outs[ref][:, cols] = grads.astype(LOW)

    unit, scale = norm_parts(x_ref[...].astype(F32))
    normed = (unit * vec_ref[0:1, :] + vec_ref[3:4, :]).astype(LOW)
    grads = jnp.concatenate([dq_ref[...], dk_ref[...], dv_ref[...]], axis=1)
    weight_grad = mm_tn(normed, grads)
    put(0, slice(0, cut), weight_grad[:, :cut])
    put(1, slice(0, 3 * width - cut), weight_grad[:, cut:])
    dn = mm_nt(grads, w_ref[...])
    sums[...] = jnp.zeros_like(sums)
    sums[0:16, :] = more_ref[...]
    sums[0:1, :] = col_sum(dn * unit)
    sums[3:4, :] = col_sum(dn)
    sums[4:5, :] = col_sum(dq_ref[...].astype(F32))
    sums[5:6, :] = col_sum(dv_ref[...].astype(F32))
    put(1, slice(3 * width - cut, 3 * width - cut + LANES), sums[...].T)
    din = gmid_ref[...] + norm_back(dn, unit, scale, vec_ref[0:1, :])
    din_ref[...] = din.astype(LOW)


def enc_qkv_back(core, rows_in, dq, dk, dv, gmid, vecs, more, weight):
    rows, width = rows_in.shape
    whole = full((rows, width))
    cut = (3 * width + LANES) // 2 // LANES * LANES
    halves = [cut, 3 * width + LANES - cut]
    packed = width // (lax.axis_size("dp") * lax.axis_size("fsdp"))
    packed = packed if packed % 8 == 0 else 0
    if packed:
        outs = [(width // packed // 2, packed, cols) for cols in halves * 2]
    else:
        outs = [(width, cols) for cols in halves]
    return pl.pallas_call(
        functools.partial(enc_qkv_back_kernel, packed),
        grid=(1,),
        in_specs=[pl.BlockSpec(memory_space=pltpu.SMEM)]
        + [whole] * 5
        + [full(vecs.shape), full((16, width)), at_col(width, 3 * width, 0)],
        out_specs=[whole] + [full(o) for o in outs],
        out_shape=[shape((rows, width), LOW)] + [shape(o, LOW) for o in outs],
        scratch_shapes=[pltpu.VMEM((LANES, width), F32)],
        compiler_params=PARAMS,
        cost_estimate=CHEAP,
        name="enc_qkv_back",
    )(core, rows_in, dq, dk, dv, gmid, vecs, more, weight)


def dec_in_kernel(limit, order_ref, one_ref, two_ref, pos_ref, vec_ref, w_ref, in_ref, qkv_ref):
    step = pl.program_id(0)
    width = in_ref.shape[1]
    for half, ref in enumerate((one_ref, two_ref)):
        visible = order_ref[0, 2 * step + half] < limit
        rows = slice(half * BLOCK, (half + 1) * BLOCK)
        in_ref[rows, :] = (
            jnp.where(visible, ref[...].astype(F32), vec_ref[9:10, :]) + pos_ref[rows, :]
        )
    unit, _ = norm_parts(in_ref[...])
    normed = (unit * vec_ref[0:1, :] + vec_ref[3:4, :]).astype(LOW)
    qkv = mm(normed, w_ref[...])
    qkv_ref[:, :width] = (qkv[:, :width] + vec_ref[4:5, :]).astype(LOW)
    qkv_ref[:, width : 2 * width] = qkv[:, width : 2 * width].astype(LOW)
    qkv_ref[:, 2 * width :] = (qkv[:, 2 * width :] + vec_ref[5:6, :]).astype(LOW)


def dec_in_call(order, gathered, pos, vecs, weight):
    rows, width = pos.shape
    limit = gathered.shape[0] // BLOCK

    def chosen(half):
        def index(i, order_ref):
            return (jnp.clip(order_ref[0, 2 * i + half], 0, limit - 1), 0)

        return pl.BlockSpec((BLOCK, width), index)

    return pl.pallas_call(
        functools.partial(dec_in_kernel, limit),
        grid_spec=pltpu.PrefetchScalarGridSpec(
            num_scalar_prefetch=1,
            grid=(rows // TILE,),
            in_specs=[
                chosen(0),
                chosen(1),
                pl.BlockSpec((TILE, width), lambda i, o: (i, 0)),
                full(vecs.shape),
                at_col(width, 3 * width, 0),
            ],
            out_specs=[
                pl.BlockSpec((TILE, width), lambda i, o: (i, 0)),
                pl.BlockSpec((TILE, 3 * width), lambda i, o: (i, 0)),
            ],
        ),
        out_shape=[shape((rows, width), F32), shape((rows, 3 * width), LOW)],
        compiler_params=PARAMS,
        cost_estimate=CHEAP,
        name="dec_in",
    )(order, gathered, gathered, pos, vecs, weight)


def dec_mid_kernel(
    steps,
    chunks,
    packed,
    x_ref,
    att_ref,
    cot_ref,
    inv_ref,
    vec_ref,
    b1_ref,
    wo_ref,
    up_ref,
    down_ref,
    out_ref,
    gmid_ref,
    gatt_ref,
    dw_ref,
    db1_ref,
    sum_ref,
    aw1,
    aw2,
    acc,
    dnorm,
    turned,
):
    step = pl.program_id(0)
    width = x_ref.shape[1]
    hidden = chunks * width
    lead = width // 4

    @pl.when(step == 0)
    def _():
        aw1[...] = jnp.zeros_like(aw1)
        aw2[...] = jnp.zeros_like(aw2)
        db1_ref[...] = jnp.zeros_like(db1_ref)
        sum_ref[...] = jnp.zeros_like(sum_ref)

    att = att_ref[...]
    low = cot_ref[...]
    middle = x_ref[...] + mm(att, wo_ref[...]) + vec_ref[6:7, :]
    unit, scale = norm_parts(middle)
    normed = unit * vec_ref[1:2, :] + vec_ref[7:8, :]
    turned[...] = normed.T.astype(LOW)
    normed = normed.astype(LOW)
    acc[...] = middle + vec_ref[8:9, :]
    dnorm[...] = jnp.zeros_like(dnorm)

    def chunk(j, carry):
        cols = pl.ds(pl.multiple_of(j * width, width), width)
        some = pl.ds(pl.multiple_of(j * lead, lead), lead)
        up = up_ref[:, cols]
        down = natural_rows(down_ref[some, :], packed, LOW) if packed else down_ref[cols, :]
        value, slope = gelu_parts(mm(normed, up) + b1_ref[j])
        value = value.astype(LOW)
        acc[...] += mm(value, down)
        grad = mm_tn(value, low)
        if packed:
            grad = grad.reshape(-1, 4, packed, width)
            for part in range(4):
                piece = grad[:, part].reshape(lead, width)
                aw2[some, part * width : (part + 1) * width] += piece
        else:
            aw2[cols, :] += grad
        dhid = (slope * mm_nt(low, down)).astype(LOW)
        aw1[:, cols] += mm(turned[...], dhid)
        db1_ref[j] += col_sum(dhid.astype(F32))
        dnorm[...] += mm_nt(dhid, up)
        return carry

    lax.fori_loop(0, chunks, chunk, 0, unroll=2)
    out_ref[...] = acc[...].astype(LOW)
    dn = dnorm[...]
    sum_ref[0:1, :] += col_sum(dn * unit)
    sum_ref[1:2, :] += col_sum(dn)
    gmid = low.astype(F32) + norm_back(dn, unit, scale, vec_ref[1:2, :])
    gmid_ref[...] = gmid
    mlow = gmid.astype(LOW)
    sum_ref[2:3, :] += col_sum(mlow.astype(F32))
    sum_ref[3:4, :] += col_sum(low.astype(F32))
    aw1[:, hidden:] += mm_tn(att, mlow)
    gatt_ref[...] = (mm_nt(mlow, wo_ref[...]) * inv_ref[...]).astype(LOW)

    @pl.when(step == steps - 1)
    def _():
        dw_ref[:, : hidden + width] = aw1[...].astype(LOW)
        if packed:
            dw_ref[:, hidden + width :] = aw2[...].astype(LOW)
        else:
            for c in range(chunks):
                col = hidden + (1 + c) * width
                dw_ref[:, col : col + width] = aw2[c * width : (c + 1) * width, :].astype(LOW)


def dec_mid(dec_in, attended, cotangent, inverse, vecs, up_bias, wide, weights, proj_at):
    rows, width = dec_in.shape
    hidden = up_bias.shape[1]
    chunks = hidden // width
    tile = 2 * TILE
    steps = rows // tile
    by_row = pl.BlockSpec((tile, width), lambda i: (i, 0))
    if len(weights) == 1:
        packed = width // (lax.axis_size("dp") * lax.axis_size("fsdp"))
        down_shape = (width, hidden)
        specs, operands = [at_col(width, hidden, 0), at_col(width, hidden, 1)], [weights[0]] * 2
    else:
        packed, down_shape = 0, (hidden, width)
        specs, operands = [full((width, hidden)), full(down_shape)], list(weights)
    return pl.pallas_call(
        functools.partial(dec_mid_kernel, steps, chunks, packed),
        grid=(steps,),
        in_specs=[
            by_row,
            by_row,
            by_row,
            by_row,
            full(vecs.shape),
            full((chunks, 1, width)),
            at_col(width, width, proj_at // width),
        ]
        + specs,
        out_specs=[
            by_row,
            by_row,
            by_row,
            full((width, 2 * hidden + width)),
            full((chunks, 1, width)),
            full((8, width)),
        ],
        out_shape=[
            shape((rows, width), LOW),
            shape((rows, width), F32),
            shape((rows, width), LOW),
            shape((width, 2 * hidden + width), LOW),
            shape((chunks, 1, width), F32),
            shape((8, width), F32),
        ],
        scratch_shapes=[
            pltpu.VMEM((width, hidden + width), F32),
            pltpu.VMEM(down_shape, F32),
            pltpu.VMEM((tile, width), F32),
            pltpu.VMEM((tile, width), F32),
            pltpu.VMEM((width, tile), LOW),
        ],
        compiler_params=PARAMS,
        cost_estimate=CHEAP,
        name="dec_mid",
    )(
        dec_in,
        attended,
        cotangent,
        inverse,
        vecs,
        up_bias.reshape(chunks, 1, width),
        wide,
        *operands,
    )


def dec_back_kernel(
    limit,
    each,
    order_ref,
    core_ref,
    x_ref,
    dq_ref,
    dk_ref,
    dv_ref,
    gmid_ref,
    vec_ref,
    more_ref,
    w_ref,
    sum_ref,
    keep_ref,
    send_ref,
):
    step = pl.program_id(0)

    @pl.when(step == 0)
    def _():
        sum_ref[...] = more_ref[...]
        keep_ref[...] = jnp.zeros_like(keep_ref)
        send_ref[...] = jnp.zeros_like(send_ref)

    unit, scale = norm_parts(x_ref[...])
    grads = jnp.concatenate([dq_ref[...], dk_ref[...], dv_ref[...]], axis=1)
    dn = mm_nt(grads, w_ref[...])
    sum_ref[0:1, :] += col_sum(dn * unit)
    sum_ref[2:3, :] += col_sum(dn)
    sum_ref[3:4, :] += col_sum(dq_ref[...].astype(F32))
    sum_ref[4:5, :] += col_sum(dv_ref[...].astype(F32))
    din = gmid_ref[...] + norm_back(dn, unit, scale, vec_ref[0:1, :])
    per = x_ref.shape[0] // BLOCK
    for b in range(per):
        place = order_ref[0, per * step + b]
        rows = din[b * BLOCK : (b + 1) * BLOCK, :]

        owner = place // each
        spot = pl.ds(pl.multiple_of(place % each * BLOCK, BLOCK), BLOCK)

        @pl.when((place < limit) & (owner % 2 == core_ref[0]))
        def _():
            keep_ref[owner // 2, spot, :] = rows.astype(LOW)

        @pl.when((place < limit) & (owner % 2 != core_ref[0]))
        def _():
            send_ref[owner // 2, spot, :] = rows.astype(LOW)

        @pl.when(place >= limit)
        def _():
            sum_ref[8:9, :] += col_sum(rows)


def dec_back(order, core, dec_in, dq, dk, dv, gmid, vecs, more, weight, limit, each):
    rows, width = dec_in.shape
    tile = TILE
    by_row = pl.BlockSpec((tile, width), lambda i, o: (i, 0))
    side = (limit // each // 2, each * BLOCK, width)
    return pl.pallas_call(
        functools.partial(dec_back_kernel, limit, each),
        grid_spec=pltpu.PrefetchScalarGridSpec(
            num_scalar_prefetch=1,
            grid=(rows // tile,),
            in_specs=[pl.BlockSpec(memory_space=pltpu.SMEM)]
            + [by_row] * 5
            + [full(vecs.shape), full((16, width)), at_col(width, 3 * width, 0)],
            out_specs=[full((16, width)), full(side), full(side)],
        ),
        out_shape=[shape((16, width), F32), shape(side, LOW), shape(side, LOW)],
        compiler_params=PARAMS,
        cost_estimate=CHEAP,
        name="dec_back",
    )(order, core, dec_in, dq, dk, dv, gmid, vecs, more, weight)


def dec_grad_kernel(x_ref, dq_ref, dk_ref, dv_ref, vec_ref, sum_ref, dw_ref, acc, sums):
    step = pl.program_id(0)
    width = x_ref.shape[1]

    @pl.when(step == 0)
    def _():
        acc[...] = jnp.zeros_like(acc)

    unit, _ = norm_parts(x_ref[...])
    normed = (unit * vec_ref[0:1, :] + vec_ref[3:4, :]).astype(LOW)
    grads = jnp.concatenate([dq_ref[...], dk_ref[...], dv_ref[...]], axis=1)
    acc[...] += mm_tn(normed, grads)

    @pl.when(step == pl.num_programs(0) - 1)
    def _():
        dw_ref[:, : 3 * width] = acc[...].astype(LOW)
        sums[...] = jnp.zeros_like(sums)
        sums[0:16, :] = sum_ref[...]
        dw_ref[:, 3 * width :] = sums[...].T.astype(LOW)


def dec_grad(dec_in, dq, dk, dv, vecs, sums):
    rows, width = dec_in.shape
    tile = 2 * TILE
    by_row = pl.BlockSpec((tile, width), lambda i: (i, 0))
    packed = (width, 3 * width + LANES)
    return pl.pallas_call(
        dec_grad_kernel,
        grid=(rows // tile,),
        in_specs=[by_row] * 4 + [full(vecs.shape), full((16, width))],
        out_specs=full(packed),
        out_shape=shape(packed, LOW),
        scratch_shapes=[pltpu.VMEM((width, 3 * width), F32), pltpu.VMEM((LANES, width), F32)],
        compiler_params=PARAMS,
        cost_estimate=CHEAP,
        name="dec_grad",
    )(dec_in, dq, dk, dv, vecs, sums)


def positions(count, width):
    places = jnp.arange(count, dtype=jnp.float32)[:, None]
    columns = jnp.arange(width)
    rates = jnp.exp((2 * (columns // 2)).astype(jnp.float32) * (-math.log(10000.0) / width))
    angles = places * rates[None, :]
    return jnp.where((columns % 2 == 0)[None, :], jnp.sin(angles), jnp.cos(angles))


def bits_of(axis):
    size, out = lax.axis_size(axis), []
    while size > 1:
        size //= 2
        out.append((axis, size))
    return out


def all_bits():
    return bits_of("dp") + bits_of("fsdp")


def bit_here(bit):
    axis, stride = bit
    return lax.axis_index(axis) // stride % 2


def swap(value, bit):
    axis, stride = bit
    return lax.ppermute(value, axis, [(i, i ^ stride) for i in range(lax.axis_size(axis))])


def pair(own, got, here, dim):
    dims = tuple(2 if d == dim else 1 for d in range(own.ndim + 1))
    mine = lax.broadcasted_iota(jnp.int32, dims, dim) == here
    return jnp.where(mine, jnp.expand_dims(own, dim), jnp.expand_dims(got, dim))


class Gather:
    def __init__(self, piece, order, held=()):
        self.piece, self.order, self.held = piece, list(order), list(held)

    def begin(self):
        self.got = swap(self.piece, self.order[0])

    def finish(self):
        canon, bit = all_bits(), self.order.pop(0)
        dim = sum(canon.index(b) < canon.index(bit) for b in self.held)
        self.piece = pair(self.piece, self.got, bit_here(bit), dim)
        self.held.append(bit)

    def step(self):
        self.begin()
        self.finish()

    def end_beside(self, outputs):
        self.got, outputs = lax.optimization_barrier((self.got, outputs))
        self.finish()
        return outputs

    def rest(self):
        while self.order:
            self.step()
        return self.piece

    def tie(self, other):
        self.piece, other = lax.optimization_barrier((self.piece, other))
        return other


def gather(piece, order, held=()):
    return Gather(piece, order, held).rest()


def join(pieces, bit):
    both = [pair(own, swap(own, bit), bit_here(bit), own.ndim - 2) for own in pieces]
    both = both[0] if len(both) == 1 else jnp.concatenate(both, axis=-1)
    return both.reshape(-1, both.shape[-1])


def term_sum(terms, kind):
    total = terms[0].astype(F32)
    for term in terms[1:]:
        total = total + term.astype(F32)
    return total.astype(kind)


class Fold:
    def __init__(self, terms, order, held=None):
        self.terms, self.order, self.send = list(terms), list(order), None
        self.left = list(all_bits() if held is None else held)

    def cut(self):
        if self.send is not None:
            return
        bit = self.order[0]
        dim = self.left.index(bit)
        here = bit_here(bit)

        def half(index):
            return [lax.dynamic_index_in_dim(t, index, dim, keepdims=False) for t in self.terms]

        self.send, self.terms = term_sum(half(1 - here), LOW), half(here)

    def pass_on(self):
        bit = self.order.pop(0)
        self.left.remove(bit)
        self.terms.append(swap(self.send, bit))
        self.send = None


def split_fold(keep, send, order, held=None):
    held = all_bits() if held is None else held
    dims = (2,) * (len(held) - 1) + keep.shape[-2:]
    fold = Fold([keep.reshape(dims)], order, held)
    fold.send = send.reshape(dims)
    return fold


def start_beside(folds, inputs):
    for fold in folds:
        fold.cut()
    sends, inputs = lax.optimization_barrier(([f.send for f in folds], inputs))
    for fold, send in zip(folds, sends):
        fold.send = send
        fold.pass_on()
    return inputs


def end_beside(folds, outputs):
    last, outputs = lax.optimization_barrier(([f.terms[-1] for f in folds], outputs))
    for fold, got in zip(folds, last):
        fold.terms[-1] = got
    return outputs


def one_round(folds):
    for fold in folds:
        fold.cut()
        fold.pass_on()
    end_beside(folds, ())


def joined(folds, line):
    terms = [term_sum(f.terms, F32) for f in folds]
    return Fold([jnp.concatenate(terms, axis=-1)], line[::-1], line)


def by_bits(grads):
    bits = len(all_bits())
    rows = grads.shape[0] >> bits
    return grads.reshape((2,) * bits + (rows, grads.shape[1]))


def pack_vectors(pieces, rows):
    wide = jnp.concatenate([p.reshape(-1, rows) for p in pieces], axis=0)
    wide = jnp.pad(wide, ((0, LANES - wide.shape[0]), (0, 0)))
    return wide.T


def unpack_tall(columns, devices, width):
    rows = columns.shape[0] // devices
    parts = columns.shape[1] // width
    return (
        columns.reshape(devices, rows, parts, width)
        .transpose(0, 2, 1, 3)
        .reshape(devices * parts * rows, width)
    )


def repack_tall(weight, devices, rows):
    parts = weight.shape[0] // (devices * rows)
    width = weight.shape[1]
    return (
        weight.reshape(devices, parts, rows, width)
        .transpose(0, 2, 1, 3)
        .reshape(devices * rows, parts * width)
    )


def split_columns(array, widths):
    out, at = [], 0
    for w in widths:
        out.append(array[:, at : at + w])
        at += w
    return out


def long_vector(rows_of, devices):
    parts, total = rows_of.shape
    return rows_of.reshape(parts, devices, total // devices).transpose(1, 0, 2).reshape(1, -1)


def long_rows(vector, devices, rows):
    parts = vector.shape[0] // (devices * rows)
    return vector.reshape(devices, parts, rows).transpose(1, 0, 2).reshape(parts, -1)


def per_device(
    enc_input,
    enc_segments,
    dec_segments,
    block_order,
    dec_cotangent,
    enc_qkv,
    enc_proj,
    enc_fc1,
    enc_fc2,
    enc_gains,
    enc_biases,
    enc_fc1_bias,
    embed,
    mask_token,
    dec_qkv,
    dec_proj,
    dec_fc1,
    dec_fc2,
    dec_gains,
    dec_biases,
    dec_fc1_bias,
    dec_fc2_bias,
):
    devices = lax.axis_size("dp") * lax.axis_size("fsdp")
    enc_rows, width = enc_input.shape
    dec_rows, dwidth = dec_cotangent.shape
    erows = enc_qkv.shape[0]
    drows = dec_qkv.shape[0]
    ff = enc_fc1.shape[1]
    dff = dec_fc1.shape[1]
    emb_row = jnp.pad(dec_biases[0], (0, erows - drows))
    enc_first = jnp.concatenate(
        [
            enc_qkv,
            enc_proj,
            embed,
            pack_vectors([enc_gains, enc_biases, enc_fc1_bias, emb_row], erows),
        ],
        axis=1,
    )
    dec_first = jnp.concatenate(
        [
            dec_qkv,
            dec_proj,
            pack_vectors(
                [dec_gains, dec_biases, dec_fc2_bias[None], mask_token[None], dec_fc1_bias], drows
            ),
        ],
        axis=1,
    )
    proj_at, emb_at = 3 * width, 4 * width
    vec_at = emb_at + dwidth
    dproj_at, dvec_at = 3 * dwidth, 4 * dwidth
    ecut = (vec_at + LANES) // 2 // LANES * LANES
    here = bit_here(bits_of("fsdp")[-1]).reshape(1)
    dp, fsdp = bits_of("dp"), bits_of("fsdp")
    line, core = fsdp[:-1], fsdp[-1]
    packed = erows % 8 == 0 and drows % 16 == 0
    enc_rest, dec_rest = [enc_fc1, enc_fc2], [dec_fc1, dec_fc2]
    if packed:
        enc_rest, dec_rest = ([w] for w in pack_shards(*enc_rest, *dec_rest))
    enc_rest = [lax.all_gather(w, AXES, axis=0, tiled=True) for w in enc_rest]
    lined = gather(enc_first, line)
    one = Gather(lined[..., :ecut], dp[::-1], line)
    two = Gather(lined[..., ecut:], dp, line)
    while one.order:
        one.step()
        two.step()
    enc_all = join([one.piece, two.piece], core)
    evecs = enc_all[:, vec_at:].T[:16].astype(F32)
    up_bias = long_vector(evecs[10:14], devices)
    emb_bias = evecs[14].reshape(devices, erows)[:, :drows].reshape(1, -1)

    dec_gather = Gather(dec_first, line + dp)
    enc_all, evecs = dec_gather.tie((enc_all, evecs))
    dec_gather.begin()
    qkv = enc_qkv_call(enc_input, evecs, enc_all)
    enc_col = enc_segments.reshape(-1, 1)
    qkv = dec_gather.end_beside(qkv)
    dec_gather.begin()
    attended, inverse, weights = attend(qkv, enc_segments, enc_col, HDIM)
    attended = dec_gather.end_beside(attended)
    while len(dec_gather.order) > 2:
        dec_gather.step()
    dec_gather.begin()
    mid, enc_out, final, act, slope, embedded, down_w = enc_mid(
        enc_input,
        attended,
        evecs,
        up_bias,
        emb_bias,
        enc_all,
        enc_rest,
        proj_at,
        emb_at,
    )
    embedded = dec_gather.end_beside(embedded)
    emb_gather = Gather(embedded, fsdp)
    emb_gather.begin()
    dec_gather.begin()
    pos = positions(dec_rows, dwidth)
    dec_gather.got, pos, dec_rest = emb_gather.end_beside((dec_gather.got, pos, dec_rest))
    dec_rest = [lax.all_gather(w, AXES, axis=0, tiled=True) for w in dec_rest]
    while len(emb_gather.order) > 2:
        emb_gather.step()
    emb_gather.begin()
    dec_gather.finish()
    dec_got = emb_gather.end_beside(swap(dec_gather.piece, core))
    emb_gather.begin()
    dim = dec_got.ndim - 2
    dec_all = pair(dec_gather.piece, dec_got, bit_here(core), dim)
    dec_all = dec_all.reshape(-1, dec_got.shape[-1])
    dvecs = pair(dec_gather.piece[..., dvec_at:], dec_got[..., dvec_at:], bit_here(core), dim)
    dvecs = dvecs.reshape(-1, LANES).T[:16].astype(F32)
    dup_bias = long_vector(dvecs[10:14], devices)
    emb_gather.finish()
    gathered = emb_gather.piece.reshape(-1, dwidth)
    limit = gathered.shape[0] // BLOCK
    dec_in, dqkv = dec_in_call(block_order, gathered, pos, dvecs, dec_all)
    dec_col = dec_segments.reshape(-1, 1)
    dattended, dinverse, dweights = attend(dqkv, dec_segments, dec_col, DHDIM)
    dec_out, dgmid, dgatt, dw_rest, db1, dsum_mid = dec_mid(
        dec_in,
        dattended,
        dec_cotangent,
        dinverse,
        dvecs,
        dup_bias,
        dec_all,
        dec_rest,
        dproj_at,
    )
    if not packed:
        chunks = dff // dwidth
        tall = dw_rest[:, dff + dwidth :].reshape(dwidth, chunks, dwidth).transpose(1, 0, 2)
        tall = repack_tall(tall.reshape(dff, dwidth), devices, drows)
        dw_rest = jnp.concatenate([dw_rest[:, : dff + dwidth], tall], axis=1)
    dec_own = lax.psum_scatter(dw_rest, "dp", scatter_dimension=0, tiled=True)
    dec_more = jnp.concatenate(
        [
            jnp.zeros((1, dwidth), F32),
            dsum_mid[0:1],
            jnp.zeros((3, dwidth), F32),
            dsum_mid[2:3],
            dsum_mid[1:2],
            dsum_mid[3:4],
            jnp.zeros((1, dwidth), F32),
            long_rows(db1.reshape(-1), devices, drows),
            jnp.zeros((3, dwidth), F32),
        ],
        axis=0,
    )
    dgatt, dec_more = lax.optimization_barrier((dgatt, dec_more))
    ddq, ddk, ddv = attend_back(dqkv, dattended, dgatt, dweights, dec_segments, DHDIM)
    dsum, keep, send = dec_back(
        block_order,
        here,
        dec_in,
        ddq,
        ddk,
        ddv,
        dgmid,
        dvecs,
        dec_more,
        dec_all,
        limit,
        enc_rows // BLOCK,
    )
    emb_fold = split_fold(keep, send, fsdp[::-1], fsdp)
    emb_fold.pass_on()
    dsum = end_beside([emb_fold], dsum)
    emb_fold.cut()
    emb_fold.pass_on()
    dec_grads = dec_grad(dec_in, ddq, ddk, ddv, dvecs, dsum)
    dec_grads, dec_own = end_beside([emb_fold], (dec_grads, dec_own))
    dec_grads = lax.psum_scatter(dec_grads, "dp", scatter_dimension=0, tiled=True)
    for _ in line[1:]:
        one_round([emb_fold])
    elow = term_sum(emb_fold.terms, LOW)
    *ew, eb1, esum_emb, esum_mid, gmid, gatt = enc_mid_back(
        here,
        elow,
        final,
        enc_out,
        mid,
        attended,
        act,
        slope,
        inverse,
        evecs,
        enc_all,
        enc_rest[0],
        down_w,
        proj_at,
        emb_at,
    )
    gatt, dec_own, dec_grads = lax.optimization_barrier((gatt, dec_own, dec_grads))
    dec_own = jnp.concatenate([dec_own, dec_grads], axis=1)
    dec_own = lax.psum_scatter(dec_own, "fsdp", scatter_dimension=0, tiled=True)
    spread = [core] + line[::-1] + dp
    if packed:
        early = split_fold(ew[0], ew[1], spread)
        edown = split_fold(ew[2], ew[3], [core] + dp[::-1])
        eup = split_fold(ew[4], ew[5], [core] + dp)
    else:
        early = Fold([by_bits(ew[0])], spread)
        edown = Fold([by_bits(repack_tall(ew[1], devices, erows))], [core] + dp[::-1])
        eup = Fold([by_bits(ew[2])], [core] + dp)
    side = [eup, edown, early]
    for fold in side:
        fold.cut()
        fold.pass_on()
    emb_sum = jnp.pad(esum_emb[0].reshape(devices, drows), ((0, 0), (0, erows - drows)))
    enc_more = jnp.concatenate(
        [
            jnp.zeros((1, width), F32),
            esum_mid[3:4],
            esum_mid[0:1],
            jnp.zeros((3, width), F32),
            esum_mid[5:6],
            esum_mid[4:5],
            esum_mid[2:3],
            esum_mid[1:2],
            long_rows(eb1.reshape(-1), devices, erows),
            emb_sum.reshape(1, -1),
            jnp.zeros((1, width), F32),
        ],
        axis=0,
    )
    gatt, enc_more = end_beside(side, (gatt, enc_more))
    gatt = start_beside(side, gatt)
    dq, dk, dv = attend_back(qkv, attended, gatt, weights, enc_segments, HDIM)
    enc_in_grad, *enc_grads = enc_qkv_back(
        here, enc_input, dq, dk, dv, gmid, evecs, enc_more, enc_all
    )
    if packed:
        halves = [split_fold(enc_grads[i], enc_grads[i + 2], [core]) for i in range(2)]
    else:
        halves = [Fold([by_bits(grads)], [core]) for grads in enc_grads]
        for half in halves:
            half.cut()
    sends, dec_own = end_beside(side, ([half.send for half in halves], dec_own))
    for half, half.send in zip(halves, sends):
        half.pass_on()
    while eup.order:
        one_round(side)
    end_beside(halves, ())
    one = Fold(halves[0].terms, dp, all_bits()[:-1])
    two = Fold(halves[1].terms, dp[::-1], all_bits()[:-1])
    rest = joined([eup, edown], line)
    one_round([one, two, rest, early])
    if rest.order:
        rest.cut()
        rest.pass_on()
    while one.order or early.order:
        one_round([f for f in (one, two, early) if f.order])
    first = joined([one, two], line)
    first.cut()
    first.pass_on()
    end_beside([first, rest], ())
    while first.order or rest.order:
        one_round([f for f in (first, rest) if f.order])
    ep, em = split_columns(term_sum(early.terms, F32), [width, dwidth])
    eu, ed = split_columns(term_sum(rest.terms, F32), [ff, ff])
    ed = unpack_tall(ed, 1, width)
    eq, ev = split_columns(term_sum(first.terms, F32), [3 * width, LANES])
    ru, rp, rd, rq, rv = split_columns(
        dec_own.astype(F32), [dff, dwidth, dff, 3 * dwidth, LANES]
    )
    rd = unpack_tall(rd, 1, dwidth)
    rv = rv.T
    ev = ev.T
    return (
        dec_out,
        enc_in_grad,
        eq,
        ep,
        eu,
        ed,
        ev[:3],
        ev[3:10],
        ev[10:14].reshape(-1),
        em,
        rv[8],
        rq,
        rp,
        ru,
        rd,
        rv[:2],
        jnp.concatenate([ev[14:15, :drows], rv[2:7]], axis=0),
        rv[9:13].reshape(-1),
        rv[7],
    )


def solution(mesh):
    in_specs = (
        P(("dp", "fsdp"), None),
        P(("dp", "fsdp"), None),
        P(("dp", "fsdp"), None),
        P("dp", "fsdp"),
        P(("dp", "fsdp"), None),
        P(("dp", "fsdp"), None),
        P(("dp", "fsdp"), None),
        P(("dp", "fsdp"), None),
        P(("dp", "fsdp"), None),
        P(None, ("dp", "fsdp")),
        P(None, ("dp", "fsdp")),
        P(("dp", "fsdp")),
        P(("dp", "fsdp"), None),
        P(("dp", "fsdp")),
        P(("dp", "fsdp"), None),
        P(("dp", "fsdp"), None),
        P(("dp", "fsdp"), None),
        P(("dp", "fsdp"), None),
        P(None, ("dp", "fsdp")),
        P(None, ("dp", "fsdp")),
        P(("dp", "fsdp")),
        P(("dp", "fsdp")),
    )
    out_specs = (
        P(("dp", "fsdp"), None),
        P(("dp", "fsdp"), None),
        P(("dp", "fsdp"), None),
        P(("dp", "fsdp"), None),
        P(("dp", "fsdp"), None),
        P(("dp", "fsdp"), None),
        P(None, ("dp", "fsdp")),
        P(None, ("dp", "fsdp")),
        P(("dp", "fsdp")),
        P(("dp", "fsdp"), None),
        P(("dp", "fsdp")),
        P(("dp", "fsdp"), None),
        P(("dp", "fsdp"), None),
        P(("dp", "fsdp"), None),
        P(("dp", "fsdp"), None),
        P(None, ("dp", "fsdp")),
        P(None, ("dp", "fsdp")),
        P(("dp", "fsdp")),
        P(("dp", "fsdp")),
    )
    return jax.shard_map(
        per_device, mesh=mesh, in_specs=in_specs, out_specs=out_specs, check_vma=False
    )
```

```python
import functools
import math

import jax
import jax.numpy as jnp
from jax import lax
from jax.experimental import pallas as pl
from jax.experimental.pallas import tpu as pltpu
from jax.sharding import PartitionSpec as P

HDIM = 64
DHDIM = 32
BLOCK = 128
LANES = 128
TILE = 256
SPAN = 128
GROUP = 256
EPSILON = 1e-06
NEGATIVE = -1e30
LOG2E = math.log2(math.e)
AXES = ("dp", "fsdp")
F32 = jnp.float32
LOW = jnp.bfloat16
PARAMS = pltpu.CompilerParams(vmem_limit_bytes=56 * 1024 * 1024)


def mm(left, right):
    return jnp.dot(left, right, preferred_element_type=F32)


def mm_tn(left, right):
    return lax.dot_general(left, right, (((0,), (0,)), ((), ())), preferred_element_type=F32)


def mm_nt(left, right):
    return lax.dot_general(left, right, (((1,), (1,)), ((), ())), preferred_element_type=F32)


def col_sum(values):
    return jnp.sum(values, axis=0, keepdims=True)


def norm_parts(values):
    centred = values - jnp.mean(values, axis=-1, keepdims=True)
    variance = jnp.mean(centred * centred, axis=-1, keepdims=True)
    scale = lax.rsqrt(variance + EPSILON)
    return centred * scale, scale


def norm_back(grad, unit, scale, gain):
    inner = grad * gain
    mean_inner = jnp.mean(inner, axis=-1, keepdims=True)
    mean_cross = jnp.mean(inner * unit, axis=-1, keepdims=True)
    return scale * (inner - mean_inner - unit * mean_cross)


def gelu_parts(hidden):
    cdf = 0.5 + 0.5 * lax.erf(hidden * (0.5**0.5))
    density = jnp.exp(hidden * hidden * -0.5) * (1.0 / math.sqrt(2.0 * math.pi))
    return hidden * cdf, cdf + hidden * density


CHEAP = pl.CostEstimate(flops=1 << 20, bytes_accessed=1 << 16, transcendentals=0)


def full(shape):
    return pl.BlockSpec(shape, lambda *_: (0,) * len(shape))


def at_col(rows, cols, index):
    return pl.BlockSpec((rows, cols), lambda *_: (0, index))


def shape(dims, kind):
    return jax.ShapeDtypeStruct(dims, kind)


def lane_mask(head, head_dim, kind):
    lane = lax.broadcasted_iota(jnp.int32, (1, GROUP), 1)
    inside = (lane >= head * head_dim) & (lane < (head + 1) * head_dim)
    return inside.astype(F32).astype(kind)


def stack_heads(stacked, index, rows, head_dim):
    count = rows.shape[0]
    for h in range(GROUP // head_dim):
        stacked[index, h * count : (h + 1) * count, :] = rows * lane_mask(h, head_dim, LOW)


def tile_range(seg_ref, start, size, other, count):
    first, last = seg_ref[0, start], seg_ref[0, start + size - 1]
    low, high = jnp.int32(0), jnp.int32(count)
    for tile in range(count):
        low += (seg_ref[0, tile * other + other - 1] < first).astype(jnp.int32)
        high -= (seg_ref[0, tile * other] > last).astype(jnp.int32)
    return low, high


def attend_kernel(
    head_dim,
    tiles,
    seg_ref,
    q_ref,
    k_ref,
    v_ref,
    row_ref,
    col_ref,
    out_ref,
    inv_ref,
    exp_ref,
    km,
    vt,
    held,
    acc,
    inverse,
    top,
    tot,
):
    heads = GROUP // head_dim
    here = pl.program_id(1)
    factor = head_dim ** (-0.5) * LOG2E

    @pl.when(here == 0)
    def _():
        for u in range(tiles):
            rows = slice(u * SPAN, (u + 1) * SPAN)
            vt[u] = v_ref[rows, :].astype(F32).T.astype(LOW)
            stack_heads(km, u, k_ref[rows, :], head_dim)

    acc[...] = jnp.zeros_like(acc)
    top[...] = jnp.full_like(top, NEGATIVE)
    tot[...] = jnp.zeros_like(tot)
    query = q_ref[...]
    row = row_ref[...]

    def score(u, carry):
        start = pl.multiple_of(u * SPAN, SPAN)
        same = col_ref[pl.ds(start, SPAN), :] == row
        every = mm_nt(km[u], query)
        for h in range(heads):
            scores = jnp.where(same, every[h * SPAN : (h + 1) * SPAN, :], NEGATIVE)
            held[u, h] = scores
            top[h : h + 1, :] = jnp.maximum(
                top[h : h + 1, :], jnp.max(scores, axis=0, keepdims=True)
            )
        return carry

    def mix(u, carry):
        for h in range(heads):
            weights = jnp.exp2((held[u, h] - top[h : h + 1, :]) * factor)
            tot[h : h + 1, :] += col_sum(weights)
            span = slice(h * head_dim, (h + 1) * head_dim)
            weights = weights.astype(LOW)
            exp_ref[0, 0, u, :, h * TILE : (h + 1) * TILE] = weights
            acc[span, :] += mm(vt[u, span, :], weights)
        return carry

    low, high = tile_range(seg_ref, here * TILE, TILE, SPAN, tiles)
    lax.fori_loop(low, high, score, 0)
    lax.fori_loop(low, high, mix, 0)
    for h in range(heads):
        span = slice(h * head_dim, (h + 1) * head_dim)
        inverse[span, :] = jnp.broadcast_to(1.0 / tot[h : h + 1, :], (head_dim, TILE))
    out_ref[...] = (acc[...] * inverse[...]).T.astype(LOW)
    inv_ref[...] = inverse[...].T


def attend(qkv, segments, seg_col, head_dim):
    rows, width = qkv.shape[0], qkv.shape[1] // 3
    groups, steps, tiles, heads = width // GROUP, rows // TILE, rows // SPAN, GROUP // head_dim
    return pl.pallas_call(
        functools.partial(attend_kernel, head_dim, tiles),
        grid_spec=pltpu.PrefetchScalarGridSpec(
            num_scalar_prefetch=1,
            grid=(groups, steps),
            in_specs=[
                pl.BlockSpec((TILE, GROUP), lambda g, t, s: (t, g)),
                pl.BlockSpec((rows, GROUP), lambda g, t, s: (0, groups + g)),
                pl.BlockSpec((rows, GROUP), lambda g, t, s: (0, 2 * groups + g)),
                pl.BlockSpec((1, TILE), lambda g, t, s: (0, t)),
                pl.BlockSpec((rows, 1), lambda g, t, s: (0, 0)),
            ],
            out_specs=[
                pl.BlockSpec((TILE, GROUP), lambda g, t, s: (t, g)),
                pl.BlockSpec((TILE, GROUP), lambda g, t, s: (t, g)),
                pl.BlockSpec((1, 1, tiles, SPAN, heads * TILE), lambda g, t, s: (g, t, 0, 0, 0)),
            ],
            scratch_shapes=[
                pltpu.VMEM((tiles, heads * SPAN, GROUP), LOW),
                pltpu.VMEM((tiles, GROUP, SPAN), LOW),
                pltpu.VMEM((tiles, heads, SPAN, TILE), F32),
                pltpu.VMEM((GROUP, TILE), F32),
                pltpu.VMEM((GROUP, TILE), F32),
                pltpu.VMEM((8, TILE), F32),
                pltpu.VMEM((8, TILE), F32),
            ],
        ),
        out_shape=[
            shape((rows, width), LOW),
            shape((rows, width), F32),
            shape((groups, steps, tiles, SPAN, heads * TILE), LOW),
        ],
        compiler_params=PARAMS,
        cost_estimate=CHEAP,
        name="attend",
    )(segments, qkv, qkv, qkv, segments, seg_col)


def attend_back_kernel(
    head_dim,
    tiles,
    seg_ref,
    q_ref,
    k_ref,
    v_ref,
    o_ref,
    g_ref,
    exp_ref,
    dq_ref,
    dk_ref,
    dv_ref,
    kt,
    vm,
    qm,
    gm,
    dqt,
    delta,
    dk_acc,
    dv_acc,
):
    heads = GROUP // head_dim
    here = pl.program_id(1)
    scale = head_dim ** (-0.5)

    @pl.when(here == 0)
    def _():
        dk_acc[...] = jnp.zeros_like(dk_acc)
        dv_acc[...] = jnp.zeros_like(dv_acc)
        for u in range(tiles):
            rows = slice(u * SPAN, (u + 1) * SPAN)
            kt[u] = k_ref[rows, :].astype(F32).T.astype(LOW)
            stack_heads(vm, u, v_ref[rows, :], head_dim)

    grads = g_ref[...]
    both = (grads.astype(F32) * o_ref[...].astype(F32)).T
    for h in range(heads):
        delta[h : h + 1, :] = col_sum(both[h * head_dim : (h + 1) * head_dim, :])
    stack_heads(qm, 0, q_ref[...], head_dim)
    stack_heads(gm, 0, grads, head_dim)
    dqt[...] = jnp.zeros_like(dqt)

    def step(u, carry):
        rows = pl.ds(pl.multiple_of(u * SPAN, SPAN), SPAN)
        every = mm_nt(vm[u], grads)
        dv_acc[rows, :] += mm(exp_ref[0, 0, u], gm[0])
        pieces = []
        for h in range(heads):
            grad_probs = every[h * SPAN : (h + 1) * SPAN, :] - delta[h : h + 1, :]
            weights = exp_ref[0, 0, u, :, h * TILE : (h + 1) * TILE]
            pieces.append((weights.astype(F32) * grad_probs).astype(LOW))
        for h in range(heads):
            span = slice(h * head_dim, (h + 1) * head_dim)
            dqt[span, :] += mm(kt[u, span, :], pieces[h])
        dk_acc[rows, :] += mm(jnp.concatenate(pieces, axis=1), qm[0])
        return carry

    low, high = tile_range(seg_ref, here * TILE, TILE, SPAN, tiles)
    lax.fori_loop(low, high, step, 0)
    dq_ref[...] = (dqt[...] * scale).T.astype(LOW)

    @pl.when(here == pl.num_programs(1) - 1)
    def _():
        dk_ref[...] = (dk_acc[...] * scale).astype(LOW)
        dv_ref[...] = dv_acc[...].astype(LOW)


def attend_back(qkv, attended, grad, weights, segments, head_dim):
    rows, width = attended.shape
    groups, steps, tiles, heads = width // GROUP, rows // TILE, rows // SPAN, GROUP // head_dim
    whole = pl.BlockSpec((rows, GROUP), lambda g, t, s: (0, g))
    piece = pl.BlockSpec((TILE, GROUP), lambda g, t, s: (t, g))
    return pl.pallas_call(
        functools.partial(attend_back_kernel, head_dim, tiles),
        grid_spec=pltpu.PrefetchScalarGridSpec(
            num_scalar_prefetch=1,
            grid=(groups, steps),
            in_specs=[
                piece,
                pl.BlockSpec((rows, GROUP), lambda g, t, s: (0, groups + g)),
                pl.BlockSpec((rows, GROUP), lambda g, t, s: (0, 2 * groups + g)),
                piece,
                piece,
                pl.BlockSpec((1, 1, tiles, SPAN, heads * TILE), lambda g, t, s: (g, t, 0, 0, 0)),
            ],
            out_specs=[piece, whole, whole],
            scratch_shapes=[
                pltpu.VMEM((tiles, GROUP, SPAN), LOW),
                pltpu.VMEM((tiles, heads * SPAN, GROUP), LOW),
                pltpu.VMEM((1, heads * TILE, GROUP), LOW),
                pltpu.VMEM((1, heads * TILE, GROUP), LOW),
                pltpu.VMEM((GROUP, TILE), F32),
                pltpu.VMEM((8, TILE), F32),
                pltpu.VMEM((rows, GROUP), F32),
                pltpu.VMEM((rows, GROUP), F32),
            ],
        ),
        out_shape=[shape((rows, width), LOW)] * 3,
        compiler_params=PARAMS,
        cost_estimate=CHEAP,
        name="attend_back",
    )(segments, qkv, qkv, qkv, attended, grad, weights)


def pack_kernel(up_ref, down_ref, dup_ref, ddown_ref, out_ref, dout_ref):
    for up, down, out in ((up_ref, down_ref, out_ref), (dup_ref, ddown_ref, dout_ref)):
        rows, cols = up.shape
        out[:, :cols] = up[...]
        wide = down[...].astype(F32)
        width = down.shape[1]
        for part in range(4):
            piece = wide[part * rows : (part + 1) * rows, :].astype(LOW)
            out[:, cols + part * width : cols + (part + 1) * width] = piece


def pack_shards(*shards):
    outs = [shape((w.shape[0], 2 * w.shape[1]), LOW) for w in shards[::2]]
    return pl.pallas_call(
        pack_kernel,
        in_specs=[full(s.shape) for s in shards],
        out_specs=[full(o.shape) for o in outs],
        out_shape=outs,
        grid=(1,),
        compiler_params=PARAMS,
        cost_estimate=CHEAP,
        name="pack",
    )(*shards)


def by_core(grads, group):
    pairs = grads.reshape(-1, 2, group, grads.shape[1])
    return pairs[:, 0], pairs[:, 1]


def natural_rows(block, group, kind):
    width = block.shape[1] // 4
    parts = [
        block[:, i * width : (i + 1) * width].astype(kind).reshape(-1, group, width)
        for i in range(4)
    ]
    return jnp.stack(parts, axis=1).reshape(-1, width).astype(LOW)


def enc_qkv_kernel(x_ref, vec_ref, w_ref, out_ref, normed):
    part = pl.program_id(0)

    @pl.when(part == 0)
    def _():
        unit, _ = norm_parts(x_ref[...].astype(F32))
        normed[...] = (unit * vec_ref[0:1, :] + vec_ref[3:4, :]).astype(LOW)

    bias = jnp.where(part == 0, vec_ref[4:5, :], jnp.where(part == 2, vec_ref[5:6, :], 0.0))
    out_ref[...] = (mm(normed[...], w_ref[...]) + bias).astype(LOW)


def enc_qkv_call(rows_in, vecs, weight):
    rows, width = rows_in.shape
    return pl.pallas_call(
        enc_qkv_kernel,
        grid=(3,),
        in_specs=[
            full((rows, width)),
            full(vecs.shape),
            pl.BlockSpec((width, width), lambda i: (0, i)),
        ],
        out_specs=pl.BlockSpec((rows, width), lambda i: (0, i)),
        out_shape=shape((rows, 3 * width), LOW),
        scratch_shapes=[pltpu.VMEM((rows, width), LOW)],
        compiler_params=PARAMS,
        cost_estimate=CHEAP,
        name="enc_qkv",
    )(rows_in, vecs, weight)


def enc_mid_kernel(
    chunks,
    packed,
    x_ref,
    att_ref,
    vec_ref,
    b1_ref,
    eb_ref,
    wo_ref,
    we_ref,
    *refs,
):
    up_ref, down_ref, *refs = refs
    mid_ref, out_ref, final_ref, act_ref, slope_ref, emb_ref, *refs = refs
    naturals, (normed, acc) = refs[:-2], refs[-2:]
    part = pl.program_id(0)

    @pl.when(part == 0)
    def _():
        middle = x_ref[...].astype(F32) + mm(att_ref[...], wo_ref[...]) + vec_ref[6:7, :]
        mid_ref[...] = middle
        unit, _ = norm_parts(middle)
        normed[...] = (unit * vec_ref[1:2, :] + vec_ref[7:8, :]).astype(LOW)
        acc[...] = middle + vec_ref[8:9, :]

    down = down_ref[...]
    if packed:
        down = natural_rows(down, packed, F32)
        naturals[0][...] = down
    hidden = mm(normed[...], up_ref[...]) + b1_ref[...]
    value, slope = gelu_parts(hidden)
    value = value.astype(LOW)
    act_ref[...] = value
    slope_ref[...] = slope
    acc[...] += mm(value, down)

    @pl.when(part == chunks - 1)
    def _():
        result = acc[...]
        out_ref[...] = result
        unit, _ = norm_parts(result)
        final = (unit * vec_ref[2:3, :] + vec_ref[9:10, :]).astype(LOW)
        final_ref[...] = final
        emb_ref[...] = (mm(final, we_ref[...]) + eb_ref[...]).astype(LOW)


def enc_mid(rows_in, attended, vecs, up_bias, emb_bias, wide, weights, proj_at, emb_at):
    rows, width = rows_in.shape
    hidden = up_bias.shape[1]
    emb_width = emb_bias.shape[1]
    chunks = hidden // width
    by_row = pl.BlockSpec((width, width), lambda i: (i, 0))
    specs = [pl.BlockSpec((width, width), lambda i: (0, i))]
    if len(weights) == 1:
        packed = width // (lax.axis_size("dp") * lax.axis_size("fsdp"))
        specs.append(pl.BlockSpec((width // 4, hidden), lambda i: (i, 1)))
        operands = [weights[0]] * 2
        natural_specs, natural_shapes = [by_row], [shape((hidden, width), LOW)]
    else:
        packed = 0
        specs.append(by_row)
        operands, natural_specs, natural_shapes = list(weights), [], []
    outs = pl.pallas_call(
        functools.partial(enc_mid_kernel, chunks, packed),
        grid=(chunks,),
        in_specs=[
            full((rows, width)),
            full((rows, width)),
            full(vecs.shape),
            pl.BlockSpec((1, width), lambda i: (0, i)),
            full((1, emb_width)),
            at_col(width, width, proj_at // width),
            at_col(width, emb_width, emb_at // emb_width),
        ]
        + specs,
        out_specs=[
            full((rows, width)),
            full((rows, width)),
            full((rows, width)),
            pl.BlockSpec((rows, width), lambda i: (0, i)),
            pl.BlockSpec((rows, width), lambda i: (0, i)),
            full((rows, emb_width)),
        ]
        + natural_specs,
        out_shape=[
            shape((rows, width), F32),
            shape((rows, width), F32),
            shape((rows, width), LOW),
            shape((rows, hidden), LOW),
            shape((rows, hidden), F32),
            shape((rows, emb_width), LOW),
        ]
        + natural_shapes,
        scratch_shapes=[pltpu.VMEM((rows, width), LOW), pltpu.VMEM((rows, width), F32)],
        compiler_params=PARAMS,
        cost_estimate=CHEAP,
        name="enc_mid",
    )(rows_in, attended, vecs, up_bias, emb_bias, wide, wide, *operands)
    return outs if packed else list(outs) + [weights[1]]


def enc_mid_back_kernel(
    chunks,
    packed,
    core_ref,
    elow_ref,
    final_ref,
    out_ref,
    mid_ref,
    att_ref,
    act_ref,
    slope_ref,
    vec_ref,
    wo_ref,
    w1_ref,
    w2_ref,
    we_ref,
    inv_ref,
    *refs,
):
    if packed:
        keep_ref, send_ref, keep2_ref, send2_ref, keep1_ref, send1_ref, *refs = refs
    else:
        keep_ref, dw2_ref, dw1_ref, *refs = refs
    (
        db1_ref,
    esum_ref,
    sum_ref,
    gmid_ref,
    gatt_ref,
    grad,
    grad_low,
    unit_two,
    scale_two,
    normed,
        dnorm,
    ) = refs
    first = core_ref[0] == 0

    def put(cols, grads):
        if packed:
            zero, one = by_core(grads, packed)
            keep_ref[:, :, cols] = jnp.where(first, zero, one).astype(LOW)
            send_ref[:, :, cols] = jnp.where(first, one, zero).astype(LOW)
        else:
            keep_ref[:, cols] = grads.astype(LOW)

    part = pl.program_id(0)

    @pl.when(part == 0)
    def _():
        elow = elow_ref[...]
        width = final_ref.shape[1]
        put(slice(width, width + elow.shape[1]), mm_tn(final_ref[...], elow))
        esum_ref[...] = jnp.zeros_like(esum_ref)
        esum_ref[0:1, :] = col_sum(elow.astype(F32))
        unit, scale = norm_parts(out_ref[...])
        dfinal = mm_nt(elow, we_ref[...])
        sum_ref[...] = jnp.zeros_like(sum_ref)
        sum_ref[0:1, :] = col_sum(dfinal * unit)
        sum_ref[1:2, :] = col_sum(dfinal)
        total = norm_back(dfinal, unit, scale, vec_ref[2:3, :])
        grad[...] = total
        low = total.astype(LOW)
        grad_low[...] = low
        sum_ref[2:3, :] = col_sum(low.astype(F32))
        unit, scale = norm_parts(mid_ref[...])
        unit_two[...] = unit
        scale_two[...] = jnp.broadcast_to(scale, scale_two.shape)
        normed[...] = (unit * vec_ref[1:2, :] + vec_ref[7:8, :]).T.astype(LOW)
        dnorm[...] = jnp.zeros_like(dnorm)

    low = grad_low[...]
    down = mm_tn(act_ref[...], low)
    if packed:
        width = low.shape[1]
        down = down.reshape(-1, 4, packed, width)
        for i in range(4):
            zero, one = by_core(down[:, i].reshape(-1, width), packed)
            cols = slice(i * width, (i + 1) * width)
            keep2_ref[:, :, cols] = jnp.where(first, zero, one).astype(LOW)
            send2_ref[:, :, cols] = jnp.where(first, one, zero).astype(LOW)
    else:
        dw2_ref[...] = down.astype(LOW)
    dhid = (slope_ref[...] * mm_nt(low, w2_ref[...])).astype(LOW)
    up = mm(normed[...], dhid)
    if packed:
        zero, one = by_core(up, packed)
        keep1_ref[...] = jnp.where(first, zero, one).astype(LOW)
        send1_ref[...] = jnp.where(first, one, zero).astype(LOW)
    else:
        dw1_ref[...] = up.astype(LOW)
    db1_ref[...] = col_sum(dhid.astype(F32))
    dnorm[...] += mm_nt(dhid, w1_ref[...])

    @pl.when(part == chunks - 1)
    def _():
        dn = dnorm[...]
        unit = unit_two[...]
        sum_ref[3:4, :] = col_sum(dn * unit)
        sum_ref[4:5, :] = col_sum(dn)
        gmid = grad[...] + norm_back(dn, unit, scale_two[:, 0:1], vec_ref[1:2, :])
        gmid_ref[...] = gmid
        mlow = gmid.astype(LOW)
        sum_ref[5:6, :] = col_sum(mlow.astype(F32))
        put(slice(0, mlow.shape[1]), mm_tn(att_ref[...], mlow))
        gatt_ref[...] = (mm_nt(mlow, wo_ref[...]) * inv_ref[...]).astype(LOW)


def enc_mid_back(
    core, elow, final, out, mid, attended, act, slope, inverse, vecs, wide, up_w, down_w, proj_at, emb_at
):
    rows, width = mid.shape
    hidden = down_w.shape[0]
    emb_width = elow.shape[1]
    chunks = hidden // width
    packed = width // (lax.axis_size("dp") * lax.axis_size("fsdp"))
    packed = packed if packed % 8 == 0 else 0
    by_col = pl.BlockSpec((rows, width), lambda i: (0, i))
    if packed:
        chips = width // packed // 2
        two = pl.BlockSpec((chips // chunks, packed, hidden), lambda i: (i, 0, 0))
        one = pl.BlockSpec((chips, packed, width), lambda i: (0, 0, i))
        side = (chips, packed, width + emb_width)
        specs = [full(side), full(side), two, two, one, one]
        shapes = [shape(side, LOW)] * 2 + [shape((chips, packed, hidden), LOW)] * 4
    else:
        specs = [
            full((width, width + emb_width)),
            pl.BlockSpec((width, width), lambda i: (i, 0)),
            pl.BlockSpec((width, width), lambda i: (0, i)),
        ]
        shapes = [
            shape((width, width + emb_width), LOW),
            shape((hidden, width), LOW),
            shape((width, hidden), LOW),
        ]
    return pl.pallas_call(
        functools.partial(enc_mid_back_kernel, chunks, packed),
        grid=(chunks,),
        in_specs=[
            pl.BlockSpec(memory_space=pltpu.SMEM),
            full((rows, emb_width)),
            full((rows, width)),
            full((rows, width)),
            full((rows, width)),
            full((rows, width)),
            by_col,
            by_col,
            full(vecs.shape),
            at_col(width, width, proj_at // width),
            pl.BlockSpec((width, width), lambda i: (0, i)),
            pl.BlockSpec((width, width), lambda i: (i, 0)),
            at_col(width, emb_width, emb_at // emb_width),
            full((rows, width)),
        ],
        out_specs=[
            *specs,
            pl.BlockSpec((1, width), lambda i: (0, i)),
            full((8, emb_width)),
            full((8, width)),
            full((rows, width)),
            full((rows, width)),
        ],
        out_shape=[
            *shapes,
            shape((1, hidden), F32),
            shape((8, emb_width), F32),
            shape((8, width), F32),
            shape((rows, width), F32),
            shape((rows, width), LOW),
        ],
        scratch_shapes=[
            pltpu.VMEM((rows, width), F32),
            pltpu.VMEM((rows, width), LOW),
            pltpu.VMEM((rows, width), F32),
            pltpu.VMEM((rows, LANES), F32),
            pltpu.VMEM((width, rows), LOW),
            pltpu.VMEM((rows, width), F32),
        ],
        compiler_params=PARAMS,
        cost_estimate=CHEAP,
        name="enc_mid_back",
    )(core, elow, final, out, mid, attended, act, slope, vecs, wide, up_w, down_w, wide, inverse)


def enc_qkv_back_kernel(
    packed,
    core_ref,
    x_ref,
    dq_ref,
    dk_ref,
    dv_ref,
    gmid_ref,
    vec_ref,
    more_ref,
    w_ref,
    din_ref,
    *refs,
):
    outs, sums = refs[:-1], refs[-1]
    first = core_ref[0] == 0
    width = x_ref.shape[1]

    cut = outs[0].shape[-1]

    def put(ref, cols, grads):
        if packed:
            zero, one = by_core(grads, packed)
            outs[ref][:, :, cols] = jnp.where(first, zero, one).astype(LOW)
            outs[ref + 2][:, :, cols] = jnp.where(first, one, zero).astype(LOW)
        else:
            outs[ref][:, cols] = grads.astype(LOW)

    unit, scale = norm_parts(x_ref[...].astype(F32))
    normed = (unit * vec_ref[0:1, :] + vec_ref[3:4, :]).astype(LOW)
    grads = jnp.concatenate([dq_ref[...], dk_ref[...], dv_ref[...]], axis=1)
    weight_grad = mm_tn(normed, grads)
    put(0, slice(0, cut), weight_grad[:, :cut])
    put(1, slice(0, 3 * width - cut), weight_grad[:, cut:])
    dn = mm_nt(grads, w_ref[...])
    sums[...] = jnp.zeros_like(sums)
    sums[0:16, :] = more_ref[...]
    sums[0:1, :] = col_sum(dn * unit)
    sums[3:4, :] = col_sum(dn)
    sums[4:5, :] = col_sum(dq_ref[...].astype(F32))
    sums[5:6, :] = col_sum(dv_ref[...].astype(F32))
    put(1, slice(3 * width - cut, 3 * width - cut + LANES), sums[...].T)
    din = gmid_ref[...] + norm_back(dn, unit, scale, vec_ref[0:1, :])
    din_ref[...] = din.astype(LOW)


def enc_qkv_back(core, rows_in, dq, dk, dv, gmid, vecs, more, weight):
    rows, width = rows_in.shape
    whole = full((rows, width))
    cut = (3 * width + LANES) // 2 // LANES * LANES
    halves = [cut, 3 * width + LANES - cut]
    packed = width // (lax.axis_size("dp") * lax.axis_size("fsdp"))
    packed = packed if packed % 8 == 0 else 0
    if packed:
        outs = [(width // packed // 2, packed, cols) for cols in halves * 2]
    else:
        outs = [(width, cols) for cols in halves]
    return pl.pallas_call(
        functools.partial(enc_qkv_back_kernel, packed),
        grid=(1,),
        in_specs=[pl.BlockSpec(memory_space=pltpu.SMEM)]
        + [whole] * 5
        + [full(vecs.shape), full((16, width)), at_col(width, 3 * width, 0)],
        out_specs=[whole] + [full(o) for o in outs],
        out_shape=[shape((rows, width), LOW)] + [shape(o, LOW) for o in outs],
        scratch_shapes=[pltpu.VMEM((LANES, width), F32)],
        compiler_params=PARAMS,
        cost_estimate=CHEAP,
        name="enc_qkv_back",
    )(core, rows_in, dq, dk, dv, gmid, vecs, more, weight)


def dec_in_kernel(
    limit,
    each,
    order_ref,
    core_ref,
    own_one,
    own_two,
    got_one,
    got_two,
    pos_ref,
    vec_ref,
    w_ref,
    in_ref,
    qkv_ref,
):
    step = pl.program_id(0)
    width = in_ref.shape[1]
    for half, (own, got) in enumerate(((own_one, got_one), (own_two, got_two))):
        place = order_ref[0, 2 * step + half]
        rows = slice(half * BLOCK, (half + 1) * BLOCK)
        block = jnp.where(place // each % 2 == core_ref[0], own[0], got[0]).astype(F32)
        in_ref[rows, :] = jnp.where(place < limit, block, vec_ref[9:10, :]) + pos_ref[rows, :]
    unit, _ = norm_parts(in_ref[...])
    normed = (unit * vec_ref[0:1, :] + vec_ref[3:4, :]).astype(LOW)
    qkv = mm(normed, w_ref[...])
    qkv_ref[:, :width] = (qkv[:, :width] + vec_ref[4:5, :]).astype(LOW)
    qkv_ref[:, width : 2 * width] = qkv[:, width : 2 * width].astype(LOW)
    qkv_ref[:, 2 * width :] = (qkv[:, 2 * width :] + vec_ref[5:6, :]).astype(LOW)


def dec_in_call(order, core, own, got, pos, vecs, weight):
    rows, width = pos.shape
    each = own.shape[1] // BLOCK
    limit = 2 * own.shape[0] * each

    def chosen(half):
        def index(i, order_ref):
            place = jnp.clip(order_ref[0, 2 * i + half], 0, limit - 1)
            return (place // each // 2, place % each, 0)

        return pl.BlockSpec((1, BLOCK, width), index)

    return pl.pallas_call(
        functools.partial(dec_in_kernel, limit, each),
        grid_spec=pltpu.PrefetchScalarGridSpec(
            num_scalar_prefetch=1,
            grid=(rows // TILE,),
            in_specs=[
                pl.BlockSpec(memory_space=pltpu.SMEM),
                chosen(0),
                chosen(1),
                chosen(0),
                chosen(1),
                pl.BlockSpec((TILE, width), lambda i, o: (i, 0)),
                full(vecs.shape),
                at_col(width, 3 * width, 0),
            ],
            out_specs=[
                pl.BlockSpec((TILE, width), lambda i, o: (i, 0)),
                pl.BlockSpec((TILE, 3 * width), lambda i, o: (i, 0)),
            ],
        ),
        out_shape=[shape((rows, width), F32), shape((rows, 3 * width), LOW)],
        compiler_params=PARAMS,
        cost_estimate=CHEAP,
        name="dec_in",
    )(order, core, own, own, got, got, pos, vecs, weight)


def dec_mid_kernel(
    steps,
    chunks,
    packed,
    x_ref,
    att_ref,
    cot_ref,
    inv_ref,
    vec_ref,
    b1_ref,
    wo_ref,
    up_ref,
    down_ref,
    out_ref,
    gmid_ref,
    gatt_ref,
    dw_ref,
    db1_ref,
    sum_ref,
    aw1,
    aw2,
    acc,
    dnorm,
    turned,
):
    step = pl.program_id(0)
    width = x_ref.shape[1]
    hidden = chunks * width
    lead = width // 4

    @pl.when(step == 0)
    def _():
        aw1[...] = jnp.zeros_like(aw1)
        aw2[...] = jnp.zeros_like(aw2)
        db1_ref[...] = jnp.zeros_like(db1_ref)
        sum_ref[...] = jnp.zeros_like(sum_ref)

    att = att_ref[...]
    low = cot_ref[...]
    middle = x_ref[...] + mm(att, wo_ref[...]) + vec_ref[6:7, :]
    unit, scale = norm_parts(middle)
    normed = unit * vec_ref[1:2, :] + vec_ref[7:8, :]
    turned[...] = normed.T.astype(LOW)
    normed = normed.astype(LOW)
    acc[...] = middle + vec_ref[8:9, :]
    dnorm[...] = jnp.zeros_like(dnorm)

    def chunk(j, carry):
        cols = pl.ds(pl.multiple_of(j * width, width), width)
        some = pl.ds(pl.multiple_of(j * lead, lead), lead)
        up = up_ref[:, cols]
        down = natural_rows(down_ref[some, :], packed, LOW) if packed else down_ref[cols, :]
        value, slope = gelu_parts(mm(normed, up) + b1_ref[j])
        value = value.astype(LOW)
        acc[...] += mm(value, down)
        grad = mm_tn(value, low)
        if packed:
            grad = grad.reshape(-1, 4, packed, width)
            for part in range(4):
                piece = grad[:, part].reshape(lead, width)
                aw2[some, part * width : (part + 1) * width] += piece
        else:
            aw2[cols, :] += grad
        dhid = (slope * mm_nt(low, down)).astype(LOW)
        aw1[:, cols] += mm(turned[...], dhid)
        db1_ref[j] += col_sum(dhid.astype(F32))
        dnorm[...] += mm_nt(dhid, up)
        return carry

    lax.fori_loop(0, chunks, chunk, 0, unroll=2)
    out_ref[...] = acc[...].astype(LOW)
    dn = dnorm[...]
    sum_ref[0:1, :] += col_sum(dn * unit)
    sum_ref[1:2, :] += col_sum(dn)
    gmid = low.astype(F32) + norm_back(dn, unit, scale, vec_ref[1:2, :])
    gmid_ref[...] = gmid
    mlow = gmid.astype(LOW)
    sum_ref[2:3, :] += col_sum(mlow.astype(F32))
    sum_ref[3:4, :] += col_sum(low.astype(F32))
    aw1[:, hidden:] += mm_tn(att, mlow)
    gatt_ref[...] = (mm_nt(mlow, wo_ref[...]) * inv_ref[...]).astype(LOW)

    @pl.when(step == steps - 1)
    def _():
        dw_ref[:, : hidden + width] = aw1[...].astype(LOW)
        if packed:
            dw_ref[:, hidden + width :] = aw2[...].astype(LOW)
        else:
            for c in range(chunks):
                col = hidden + (1 + c) * width
                dw_ref[:, col : col + width] = aw2[c * width : (c + 1) * width, :].astype(LOW)


def dec_mid(dec_in, attended, cotangent, inverse, vecs, up_bias, wide, weights, proj_at):
    rows, width = dec_in.shape
    hidden = up_bias.shape[1]
    chunks = hidden // width
    tile = 2 * TILE
    steps = rows // tile
    by_row = pl.BlockSpec((tile, width), lambda i: (i, 0))
    if len(weights) == 1:
        packed = width // (lax.axis_size("dp") * lax.axis_size("fsdp"))
        down_shape = (width, hidden)
        specs, operands = [at_col(width, hidden, 0), at_col(width, hidden, 1)], [weights[0]] * 2
    else:
        packed, down_shape = 0, (hidden, width)
        specs, operands = [full((width, hidden)), full(down_shape)], list(weights)
    return pl.pallas_call(
        functools.partial(dec_mid_kernel, steps, chunks, packed),
        grid=(steps,),
        in_specs=[
            by_row,
            by_row,
            by_row,
            by_row,
            full(vecs.shape),
            full((chunks, 1, width)),
            at_col(width, width, proj_at // width),
        ]
        + specs,
        out_specs=[
            by_row,
            by_row,
            by_row,
            full((width, 2 * hidden + width)),
            full((chunks, 1, width)),
            full((8, width)),
        ],
        out_shape=[
            shape((rows, width), LOW),
            shape((rows, width), F32),
            shape((rows, width), LOW),
            shape((width, 2 * hidden + width), LOW),
            shape((chunks, 1, width), F32),
            shape((8, width), F32),
        ],
        scratch_shapes=[
            pltpu.VMEM((width, hidden + width), F32),
            pltpu.VMEM(down_shape, F32),
            pltpu.VMEM((tile, width), F32),
            pltpu.VMEM((tile, width), F32),
            pltpu.VMEM((width, tile), LOW),
        ],
        compiler_params=PARAMS,
        cost_estimate=CHEAP,
        name="dec_mid",
    )(
        dec_in,
        attended,
        cotangent,
        inverse,
        vecs,
        up_bias.reshape(chunks, 1, width),
        wide,
        *operands,
    )


def dec_back_kernel(
    limit,
    each,
    order_ref,
    core_ref,
    x_ref,
    dq_ref,
    dk_ref,
    dv_ref,
    gmid_ref,
    vec_ref,
    more_ref,
    w_ref,
    sum_ref,
    keep_ref,
    send_ref,
):
    step = pl.program_id(0)

    @pl.when(step == 0)
    def _():
        sum_ref[...] = more_ref[...]
        keep_ref[...] = jnp.zeros_like(keep_ref)
        send_ref[...] = jnp.zeros_like(send_ref)

    unit, scale = norm_parts(x_ref[...])
    grads = jnp.concatenate([dq_ref[...], dk_ref[...], dv_ref[...]], axis=1)
    dn = mm_nt(grads, w_ref[...])
    sum_ref[0:1, :] += col_sum(dn * unit)
    sum_ref[2:3, :] += col_sum(dn)
    sum_ref[3:4, :] += col_sum(dq_ref[...].astype(F32))
    sum_ref[4:5, :] += col_sum(dv_ref[...].astype(F32))
    din = gmid_ref[...] + norm_back(dn, unit, scale, vec_ref[0:1, :])
    per = x_ref.shape[0] // BLOCK
    for b in range(per):
        place = order_ref[0, per * step + b]
        rows = din[b * BLOCK : (b + 1) * BLOCK, :]

        owner = place // each
        spot = pl.ds(pl.multiple_of(place % each * BLOCK, BLOCK), BLOCK)

        @pl.when((place < limit) & (owner % 2 == core_ref[0]))
        def _():
            keep_ref[owner // 2, spot, :] = rows.astype(LOW)

        @pl.when((place < limit) & (owner % 2 != core_ref[0]))
        def _():
            send_ref[owner // 2, spot, :] = rows.astype(LOW)

        @pl.when(place >= limit)
        def _():
            sum_ref[8:9, :] += col_sum(rows)


def dec_back(order, core, dec_in, dq, dk, dv, gmid, vecs, more, weight, limit, each):
    rows, width = dec_in.shape
    tile = TILE
    by_row = pl.BlockSpec((tile, width), lambda i, o: (i, 0))
    side = (limit // each // 2, each * BLOCK, width)
    return pl.pallas_call(
        functools.partial(dec_back_kernel, limit, each),
        grid_spec=pltpu.PrefetchScalarGridSpec(
            num_scalar_prefetch=1,
            grid=(rows // tile,),
            in_specs=[pl.BlockSpec(memory_space=pltpu.SMEM)]
            + [by_row] * 5
            + [full(vecs.shape), full((16, width)), at_col(width, 3 * width, 0)],
            out_specs=[full((16, width)), full(side), full(side)],
        ),
        out_shape=[shape((16, width), F32), shape(side, LOW), shape(side, LOW)],
        compiler_params=PARAMS,
        cost_estimate=CHEAP,
        name="dec_back",
    )(order, core, dec_in, dq, dk, dv, gmid, vecs, more, weight)


def dec_grad_kernel(x_ref, dq_ref, dk_ref, dv_ref, vec_ref, sum_ref, dw_ref, acc, sums):
    step = pl.program_id(0)
    width = x_ref.shape[1]

    @pl.when(step == 0)
    def _():
        acc[...] = jnp.zeros_like(acc)

    unit, _ = norm_parts(x_ref[...])
    normed = (unit * vec_ref[0:1, :] + vec_ref[3:4, :]).astype(LOW)
    grads = jnp.concatenate([dq_ref[...], dk_ref[...], dv_ref[...]], axis=1)
    acc[...] += mm_tn(normed, grads)

    @pl.when(step == pl.num_programs(0) - 1)
    def _():
        dw_ref[:, : 3 * width] = acc[...].astype(LOW)
        sums[...] = jnp.zeros_like(sums)
        sums[0:16, :] = sum_ref[...]
        dw_ref[:, 3 * width :] = sums[...].T.astype(LOW)


def dec_grad(dec_in, dq, dk, dv, vecs, sums):
    rows, width = dec_in.shape
    tile = 2 * TILE
    by_row = pl.BlockSpec((tile, width), lambda i: (i, 0))
    packed = (width, 3 * width + LANES)
    return pl.pallas_call(
        dec_grad_kernel,
        grid=(rows // tile,),
        in_specs=[by_row] * 4 + [full(vecs.shape), full((16, width))],
        out_specs=full(packed),
        out_shape=shape(packed, LOW),
        scratch_shapes=[pltpu.VMEM((width, 3 * width), F32), pltpu.VMEM((LANES, width), F32)],
        compiler_params=PARAMS,
        cost_estimate=CHEAP,
        name="dec_grad",
    )(dec_in, dq, dk, dv, vecs, sums)


def positions(count, width):
    places = jnp.arange(count, dtype=jnp.float32)[:, None]
    columns = jnp.arange(width)
    rates = jnp.exp((2 * (columns // 2)).astype(jnp.float32) * (-math.log(10000.0) / width))
    angles = places * rates[None, :]
    return jnp.where((columns % 2 == 0)[None, :], jnp.sin(angles), jnp.cos(angles))


def bits_of(axis):
    size, out = lax.axis_size(axis), []
    while size > 1:
        size //= 2
        out.append((axis, size))
    return out


def all_bits():
    return bits_of("dp") + bits_of("fsdp")


def bit_here(bit):
    axis, stride = bit
    return lax.axis_index(axis) // stride % 2


def swap(value, bit):
    axis, stride = bit
    return lax.ppermute(value, axis, [(i, i ^ stride) for i in range(lax.axis_size(axis))])


def pair(own, got, here, dim):
    dims = tuple(2 if d == dim else 1 for d in range(own.ndim + 1))
    mine = lax.broadcasted_iota(jnp.int32, dims, dim) == here
    return jnp.where(mine, jnp.expand_dims(own, dim), jnp.expand_dims(got, dim))


class Gather:
    def __init__(self, piece, order, held=()):
        self.piece, self.order, self.held = piece, list(order), list(held)

    def begin(self):
        self.got = swap(self.piece, self.order[0])

    def finish(self):
        canon, bit = all_bits(), self.order.pop(0)
        dim = sum(canon.index(b) < canon.index(bit) for b in self.held)
        self.piece = pair(self.piece, self.got, bit_here(bit), dim)
        self.held.append(bit)

    def step(self):
        self.begin()
        self.finish()

    def end_beside(self, outputs):
        self.got, outputs = lax.optimization_barrier((self.got, outputs))
        self.finish()
        return outputs

    def rest(self):
        while self.order:
            self.step()
        return self.piece

    def tie(self, other):
        self.piece, other = lax.optimization_barrier((self.piece, other))
        return other


def gather(piece, order, held=()):
    return Gather(piece, order, held).rest()


def join(pieces, bit):
    both = [pair(own, swap(own, bit), bit_here(bit), own.ndim - 2) for own in pieces]
    both = both[0] if len(both) == 1 else jnp.concatenate(both, axis=-1)
    return both.reshape(-1, both.shape[-1])


def term_sum(terms, kind):
    total = terms[0].astype(F32)
    for term in terms[1:]:
        total = total + term.astype(F32)
    return total.astype(kind)


class Fold:
    def __init__(self, terms, order, held=None):
        self.terms, self.order, self.send = list(terms), list(order), None
        self.left = list(all_bits() if held is None else held)

    def cut(self):
        if self.send is not None:
            return
        bit = self.order[0]
        dim = self.left.index(bit)
        here = bit_here(bit)

        def half(index):
            return [lax.dynamic_index_in_dim(t, index, dim, keepdims=False) for t in self.terms]

        self.send, self.terms = term_sum(half(1 - here), LOW), half(here)

    def pass_on(self):
        bit = self.order.pop(0)
        self.left.remove(bit)
        self.terms.append(swap(self.send, bit))
        self.send = None


def split_fold(keep, send, order, held=None):
    held = all_bits() if held is None else held
    dims = (2,) * (len(held) - 1) + keep.shape[-2:]
    fold = Fold([keep.reshape(dims)], order, held)
    fold.send = send.reshape(dims)
    return fold


def start_beside(folds, inputs):
    for fold in folds:
        fold.cut()
    sends, inputs = lax.optimization_barrier(([f.send for f in folds], inputs))
    for fold, send in zip(folds, sends):
        fold.send = send
        fold.pass_on()
    return inputs


def end_beside(folds, outputs):
    last, outputs = lax.optimization_barrier(([f.terms[-1] for f in folds], outputs))
    for fold, got in zip(folds, last):
        fold.terms[-1] = got
    return outputs


def one_round(folds):
    for fold in folds:
        fold.cut()
        fold.pass_on()
    end_beside(folds, ())


def joined(folds, line):
    terms = [term_sum(f.terms, F32) for f in folds]
    return Fold([jnp.concatenate(terms, axis=-1)], line[::-1], line)


def by_bits(grads):
    bits = len(all_bits())
    rows = grads.shape[0] >> bits
    return grads.reshape((2,) * bits + (rows, grads.shape[1]))


def pack_vectors(pieces, rows):
    wide = jnp.concatenate([p.reshape(-1, rows) for p in pieces], axis=0)
    wide = jnp.pad(wide, ((0, LANES - wide.shape[0]), (0, 0)))
    return wide.T


def unpack_tall(columns, devices, width):
    rows = columns.shape[0] // devices
    parts = columns.shape[1] // width
    return (
        columns.reshape(devices, rows, parts, width)
        .transpose(0, 2, 1, 3)
        .reshape(devices * parts * rows, width)
    )


def repack_tall(weight, devices, rows):
    parts = weight.shape[0] // (devices * rows)
    width = weight.shape[1]
    return (
        weight.reshape(devices, parts, rows, width)
        .transpose(0, 2, 1, 3)
        .reshape(devices * rows, parts * width)
    )


def split_columns(array, widths):
    out, at = [], 0
    for w in widths:
        out.append(array[:, at : at + w])
        at += w
    return out


def long_vector(rows_of, devices):
    parts, total = rows_of.shape
    return rows_of.reshape(parts, devices, total // devices).transpose(1, 0, 2).reshape(1, -1)


def long_rows(vector, devices, rows):
    parts = vector.shape[0] // (devices * rows)
    return vector.reshape(devices, parts, rows).transpose(1, 0, 2).reshape(parts, -1)


def per_device(
    enc_input,
    enc_segments,
    dec_segments,
    block_order,
    dec_cotangent,
    enc_qkv,
    enc_proj,
    enc_fc1,
    enc_fc2,
    enc_gains,
    enc_biases,
    enc_fc1_bias,
    embed,
    mask_token,
    dec_qkv,
    dec_proj,
    dec_fc1,
    dec_fc2,
    dec_gains,
    dec_biases,
    dec_fc1_bias,
    dec_fc2_bias,
):
    devices = lax.axis_size("dp") * lax.axis_size("fsdp")
    enc_rows, width = enc_input.shape
    dec_rows, dwidth = dec_cotangent.shape
    erows = enc_qkv.shape[0]
    drows = dec_qkv.shape[0]
    ff = enc_fc1.shape[1]
    dff = dec_fc1.shape[1]
    emb_row = jnp.pad(dec_biases[0], (0, erows - drows))
    enc_first = jnp.concatenate(
        [
            enc_qkv,
            enc_proj,
            embed,
            pack_vectors([enc_gains, enc_biases, enc_fc1_bias, emb_row], erows),
        ],
        axis=1,
    )
    dec_first = jnp.concatenate(
        [
            dec_qkv,
            dec_proj,
            pack_vectors(
                [dec_gains, dec_biases, dec_fc2_bias[None], mask_token[None], dec_fc1_bias], drows
            ),
        ],
        axis=1,
    )
    proj_at, emb_at = 3 * width, 4 * width
    vec_at = emb_at + dwidth
    dproj_at, dvec_at = 3 * dwidth, 4 * dwidth
    ecut = (vec_at + LANES) // 2 // LANES * LANES
    here = bit_here(bits_of("fsdp")[-1]).reshape(1)
    dp, fsdp = bits_of("dp"), bits_of("fsdp")
    line, core = fsdp[:-1], fsdp[-1]
    packed = erows % 8 == 0 and drows % 16 == 0
    enc_rest, dec_rest = [enc_fc1, enc_fc2], [dec_fc1, dec_fc2]
    if packed:
        enc_rest, dec_rest = ([w] for w in pack_shards(*enc_rest, *dec_rest))
    enc_rest = [lax.all_gather(w, AXES, axis=0, tiled=True) for w in enc_rest]
    lined = gather(enc_first, line)
    one = Gather(lined[..., :ecut], dp[::-1], line)
    two = Gather(lined[..., ecut:], dp, line)
    while one.order:
        one.step()
        two.step()
    enc_all = join([one.piece, two.piece], core)
    evecs = enc_all[:, vec_at:].T[:16].astype(F32)
    up_bias = long_vector(evecs[10:14], devices)
    emb_bias = evecs[14].reshape(devices, erows)[:, :drows].reshape(1, -1)

    dec_gather = Gather(dec_first, line + dp)
    enc_all, evecs = dec_gather.tie((enc_all, evecs))
    dec_gather.begin()
    qkv = enc_qkv_call(enc_input, evecs, enc_all)
    enc_col = enc_segments.reshape(-1, 1)
    qkv = dec_gather.end_beside(qkv)
    dec_gather.begin()
    attended, inverse, weights = attend(qkv, enc_segments, enc_col, HDIM)
    attended = dec_gather.end_beside(attended)
    while len(dec_gather.order) > 2:
        dec_gather.step()
    dec_gather.begin()
    mid, enc_out, final, act, slope, embedded, down_w = enc_mid(
        enc_input,
        attended,
        evecs,
        up_bias,
        emb_bias,
        enc_all,
        enc_rest,
        proj_at,
        emb_at,
    )
    embedded = dec_gather.end_beside(embedded)
    emb_gather = Gather(embedded, fsdp)
    emb_gather.begin()
    dec_gather.begin()
    pos = positions(dec_rows, dwidth)
    dec_gather.got, pos, dec_rest = emb_gather.end_beside((dec_gather.got, pos, dec_rest))
    dec_rest = [lax.all_gather(w, AXES, axis=0, tiled=True) for w in dec_rest]
    while len(emb_gather.order) > 2:
        emb_gather.step()
    emb_gather.begin()
    dec_gather.finish()
    dec_got = emb_gather.end_beside(swap(dec_gather.piece, core))
    emb_gather.begin()
    dim = dec_got.ndim - 2
    dec_all = pair(dec_gather.piece, dec_got, bit_here(core), dim)
    dec_all = dec_all.reshape(-1, dec_got.shape[-1])
    dvecs = pair(dec_gather.piece[..., dvec_at:], dec_got[..., dvec_at:], bit_here(core), dim)
    dvecs = dvecs.reshape(-1, LANES).T[:16].astype(F32)
    dup_bias = long_vector(dvecs[10:14], devices)
    emb_own = emb_gather.piece.reshape(-1, enc_rows, dwidth)
    emb_got = emb_gather.got.reshape(-1, enc_rows, dwidth)
    limit = lax.axis_size("fsdp") * enc_rows // BLOCK
    dec_in, dqkv = dec_in_call(block_order, here, emb_own, emb_got, pos, dvecs, dec_all)
    dec_col = dec_segments.reshape(-1, 1)
    dattended, dinverse, dweights = attend(dqkv, dec_segments, dec_col, DHDIM)
    dec_out, dgmid, dgatt, dw_rest, db1, dsum_mid = dec_mid(
        dec_in,
        dattended,
        dec_cotangent,
        dinverse,
        dvecs,
        dup_bias,
        dec_all,
        dec_rest,
        dproj_at,
    )
    if not packed:
        chunks = dff // dwidth
        tall = dw_rest[:, dff + dwidth :].reshape(dwidth, chunks, dwidth).transpose(1, 0, 2)
        tall = repack_tall(tall.reshape(dff, dwidth), devices, drows)
        dw_rest = jnp.concatenate([dw_rest[:, : dff + dwidth], tall], axis=1)
    dec_own = lax.psum_scatter(dw_rest, "dp", scatter_dimension=0, tiled=True)
    dec_more = jnp.concatenate(
        [
            jnp.zeros((1, dwidth), F32),
            dsum_mid[0:1],
            jnp.zeros((3, dwidth), F32),
            dsum_mid[2:3],
            dsum_mid[1:2],
            dsum_mid[3:4],
            jnp.zeros((1, dwidth), F32),
            long_rows(db1.reshape(-1), devices, drows),
            jnp.zeros((3, dwidth), F32),
        ],
        axis=0,
    )
    dgatt, dec_more = lax.optimization_barrier((dgatt, dec_more))
    ddq, ddk, ddv = attend_back(dqkv, dattended, dgatt, dweights, dec_segments, DHDIM)
    dsum, keep, send = dec_back(
        block_order,
        here,
        dec_in,
        ddq,
        ddk,
        ddv,
        dgmid,
        dvecs,
        dec_more,
        dec_all,
        limit,
        enc_rows // BLOCK,
    )
    emb_fold = split_fold(keep, send, fsdp[::-1], fsdp)
    emb_fold.pass_on()
    dsum = end_beside([emb_fold], dsum)
    emb_fold.cut()
    emb_fold.pass_on()
    dec_grads = dec_grad(dec_in, ddq, ddk, ddv, dvecs, dsum)
    dec_grads, dec_own = end_beside([emb_fold], (dec_grads, dec_own))
    dec_grads = lax.psum_scatter(dec_grads, "dp", scatter_dimension=0, tiled=True)
    for _ in line[1:]:
        one_round([emb_fold])
    elow = term_sum(emb_fold.terms, LOW)
    *ew, eb1, esum_emb, esum_mid, gmid, gatt = enc_mid_back(
        here,
        elow,
        final,
        enc_out,
        mid,
        attended,
        act,
        slope,
        inverse,
        evecs,
        enc_all,
        enc_rest[0],
        down_w,
        proj_at,
        emb_at,
    )
    gatt, dec_own, dec_grads = lax.optimization_barrier((gatt, dec_own, dec_grads))
    dec_own = jnp.concatenate([dec_own, dec_grads], axis=1)
    dec_own = lax.psum_scatter(dec_own, "fsdp", scatter_dimension=0, tiled=True)
    spread = [core] + line[::-1] + dp
    if packed:
        early = split_fold(ew[0], ew[1], spread)
        edown = split_fold(ew[2], ew[3], [core] + dp[::-1])
        eup = split_fold(ew[4], ew[5], [core] + dp)
    else:
        early = Fold([by_bits(ew[0])], spread)
        edown = Fold([by_bits(repack_tall(ew[1], devices, erows))], [core] + dp[::-1])
        eup = Fold([by_bits(ew[2])], [core] + dp)
    side = [eup, edown, early]
    for fold in side:
        fold.cut()
        fold.pass_on()
    emb_sum = jnp.pad(esum_emb[0].reshape(devices, drows), ((0, 0), (0, erows - drows)))
    enc_more = jnp.concatenate(
        [
            jnp.zeros((1, width), F32),
            esum_mid[3:4],
            esum_mid[0:1],
            jnp.zeros((3, width), F32),
            esum_mid[5:6],
            esum_mid[4:5],
            esum_mid[2:3],
            esum_mid[1:2],
            long_rows(eb1.reshape(-1), devices, erows),
            emb_sum.reshape(1, -1),
            jnp.zeros((1, width), F32),
        ],
        axis=0,
    )
    gatt, enc_more = end_beside(side, (gatt, enc_more))
    gatt = start_beside(side, gatt)
    dq, dk, dv = attend_back(qkv, attended, gatt, weights, enc_segments, HDIM)
    enc_in_grad, *enc_grads = enc_qkv_back(
        here, enc_input, dq, dk, dv, gmid, evecs, enc_more, enc_all
    )
    if packed:
        halves = [split_fold(enc_grads[i], enc_grads[i + 2], [core]) for i in range(2)]
    else:
        halves = [Fold([by_bits(grads)], [core]) for grads in enc_grads]
        for half in halves:
            half.cut()
    sends, dec_own = end_beside(side, ([half.send for half in halves], dec_own))
    for half, half.send in zip(halves, sends):
        half.pass_on()
    while len(eup.order) > 1:
        one_round(side)
    for fold in side:
        fold.cut()
        fold.pass_on()
    end_beside(halves, ())
    one = Fold(halves[0].terms, dp, all_bits()[:-1])
    two = Fold(halves[1].terms, dp[::-1], all_bits()[:-1])
    for fold in (one, two):
        fold.cut()
        fold.pass_on()
    end_beside([one, two] + side, ())
    rest = joined([eup, edown], line)
    while one.order:
        one_round([f for f in (rest, one, two, early) if f.order])
    first = joined([one, two], line)
    while first.order or rest.order or early.order:
        one_round([f for f in (first, rest, early) if f.order])
    ep, em = split_columns(term_sum(early.terms, F32), [width, dwidth])
    eu, ed = split_columns(term_sum(rest.terms, F32), [ff, ff])
    ed = unpack_tall(ed, 1, width)
    eq, ev = split_columns(term_sum(first.terms, F32), [3 * width, LANES])
    ru, rp, rd, rq, rv = split_columns(
        dec_own.astype(F32), [dff, dwidth, dff, 3 * dwidth, LANES]
    )
    rd = unpack_tall(rd, 1, dwidth)
    rv = rv.T
    ev = ev.T
    return (
        dec_out,
        enc_in_grad,
        eq,
        ep,
        eu,
        ed,
        ev[:3],
        ev[3:10],
        ev[10:14].reshape(-1),
        em,
        rv[8],
        rq,
        rp,
        ru,
        rd,
        rv[:2],
        jnp.concatenate([ev[14:15, :drows], rv[2:7]], axis=0),
        rv[9:13].reshape(-1),
        rv[7],
    )


def solution(mesh):
    in_specs = (
        P(("dp", "fsdp"), None),
        P(("dp", "fsdp"), None),
        P(("dp", "fsdp"), None),
        P("dp", "fsdp"),
        P(("dp", "fsdp"), None),
        P(("dp", "fsdp"), None),
        P(("dp", "fsdp"), None),
        P(("dp", "fsdp"), None),
        P(("dp", "fsdp"), None),
        P(None, ("dp", "fsdp")),
        P(None, ("dp", "fsdp")),
        P(("dp", "fsdp")),
        P(("dp", "fsdp"), None),
        P(("dp", "fsdp")),
        P(("dp", "fsdp"), None),
        P(("dp", "fsdp"), None),
        P(("dp", "fsdp"), None),
        P(("dp", "fsdp"), None),
        P(None, ("dp", "fsdp")),
        P(None, ("dp", "fsdp")),
        P(("dp", "fsdp")),
        P(("dp", "fsdp")),
    )
    out_specs = (
        P(("dp", "fsdp"), None),
        P(("dp", "fsdp"), None),
        P(("dp", "fsdp"), None),
        P(("dp", "fsdp"), None),
        P(("dp", "fsdp"), None),
        P(("dp", "fsdp"), None),
        P(None, ("dp", "fsdp")),
        P(None, ("dp", "fsdp")),
        P(("dp", "fsdp")),
        P(("dp", "fsdp"), None),
        P(("dp", "fsdp")),
        P(("dp", "fsdp"), None),
        P(("dp", "fsdp"), None),
        P(("dp", "fsdp"), None),
        P(("dp", "fsdp"), None),
        P(None, ("dp", "fsdp")),
        P(None, ("dp", "fsdp")),
        P(("dp", "fsdp")),
        P(("dp", "fsdp")),
    )
    return jax.shard_map(
        per_device, mesh=mesh, in_specs=in_specs, out_specs=out_specs, check_vma=False
    )
```

```python
import functools
import math

import jax
import jax.numpy as jnp
from jax import lax
from jax.experimental import pallas as pl
from jax.experimental.pallas import tpu as pltpu
from jax.sharding import PartitionSpec as P

HDIM = 64
DHDIM = 32
BLOCK = 128
LANES = 128
TILE = 256
SPAN = 128
GROUP = 256
EPSILON = 1e-06
NEGATIVE = -1e30
LOG2E = math.log2(math.e)
AXES = ("dp", "fsdp")
F32 = jnp.float32
LOW = jnp.bfloat16
PARAMS = pltpu.CompilerParams(vmem_limit_bytes=56 * 1024 * 1024)


def mm(left, right):
    return jnp.dot(left, right, preferred_element_type=F32)


def mm_tn(left, right):
    return lax.dot_general(left, right, (((0,), (0,)), ((), ())), preferred_element_type=F32)


def mm_nt(left, right):
    return lax.dot_general(left, right, (((1,), (1,)), ((), ())), preferred_element_type=F32)


def col_sum(values):
    return jnp.sum(values, axis=0, keepdims=True)


def norm_parts(values):
    centred = values - jnp.mean(values, axis=-1, keepdims=True)
    variance = jnp.mean(centred * centred, axis=-1, keepdims=True)
    scale = lax.rsqrt(variance + EPSILON)
    return centred * scale, scale


def norm_back(grad, unit, scale, gain):
    inner = grad * gain
    mean_inner = jnp.mean(inner, axis=-1, keepdims=True)
    mean_cross = jnp.mean(inner * unit, axis=-1, keepdims=True)
    return scale * (inner - mean_inner - unit * mean_cross)


def gelu_parts(hidden):
    cdf = 0.5 + 0.5 * lax.erf(hidden * (0.5**0.5))
    density = jnp.exp(hidden * hidden * -0.5) * (1.0 / math.sqrt(2.0 * math.pi))
    return hidden * cdf, cdf + hidden * density


CHEAP = pl.CostEstimate(flops=1 << 20, bytes_accessed=1 << 16, transcendentals=0)


def full(shape):
    return pl.BlockSpec(shape, lambda *_: (0,) * len(shape))


def at_col(rows, cols, index):
    return pl.BlockSpec((rows, cols), lambda *_: (0, index))


def shape(dims, kind):
    return jax.ShapeDtypeStruct(dims, kind)


def lane_mask(head, head_dim, kind):
    lane = lax.broadcasted_iota(jnp.int32, (1, GROUP), 1)
    inside = (lane >= head * head_dim) & (lane < (head + 1) * head_dim)
    return inside.astype(F32).astype(kind)


def stack_heads(stacked, index, rows, head_dim):
    count = rows.shape[0]
    for h in range(GROUP // head_dim):
        stacked[index, h * count : (h + 1) * count, :] = rows * lane_mask(h, head_dim, LOW)


def tile_range(seg_ref, start, size, other, count):
    first, last = seg_ref[0, start], seg_ref[0, start + size - 1]
    low, high = jnp.int32(0), jnp.int32(count)
    for tile in range(count):
        low += (seg_ref[0, tile * other + other - 1] < first).astype(jnp.int32)
        high -= (seg_ref[0, tile * other] > last).astype(jnp.int32)
    return low, high


def attend_kernel(
    head_dim,
    tiles,
    seg_ref,
    q_ref,
    k_ref,
    v_ref,
    row_ref,
    col_ref,
    out_ref,
    inv_ref,
    exp_ref,
    km,
    vt,
    held,
    acc,
    inverse,
    top,
    tot,
):
    heads = GROUP // head_dim
    here = pl.program_id(1)
    factor = head_dim ** (-0.5) * LOG2E

    @pl.when(here == 0)
    def _():
        for u in range(tiles):
            rows = slice(u * SPAN, (u + 1) * SPAN)
            vt[u] = v_ref[rows, :].astype(F32).T.astype(LOW)
            stack_heads(km, u, k_ref[rows, :], head_dim)

    acc[...] = jnp.zeros_like(acc)
    top[...] = jnp.full_like(top, NEGATIVE)
    tot[...] = jnp.zeros_like(tot)
    query = q_ref[...]
    row = row_ref[...]

    def score(u, carry):
        start = pl.multiple_of(u * SPAN, SPAN)
        same = col_ref[pl.ds(start, SPAN), :] == row
        every = mm_nt(km[u], query)
        for h in range(heads):
            scores = jnp.where(same, every[h * SPAN : (h + 1) * SPAN, :], NEGATIVE)
            held[u, h] = scores
            top[h : h + 1, :] = jnp.maximum(
                top[h : h + 1, :], jnp.max(scores, axis=0, keepdims=True)
            )
        return carry

    def mix(u, carry):
        for h in range(heads):
            weights = jnp.exp2((held[u, h] - top[h : h + 1, :]) * factor)
            tot[h : h + 1, :] += col_sum(weights)
            span = slice(h * head_dim, (h + 1) * head_dim)
            weights = weights.astype(LOW)
            exp_ref[0, 0, u, :, h * TILE : (h + 1) * TILE] = weights
            acc[span, :] += mm(vt[u, span, :], weights)
        return carry

    low, high = tile_range(seg_ref, here * TILE, TILE, SPAN, tiles)
    lax.fori_loop(low, high, score, 0)
    lax.fori_loop(low, high, mix, 0)
    for h in range(heads):
        span = slice(h * head_dim, (h + 1) * head_dim)
        inverse[span, :] = jnp.broadcast_to(1.0 / tot[h : h + 1, :], (head_dim, TILE))
    out_ref[...] = (acc[...] * inverse[...]).T.astype(LOW)
    inv_ref[...] = inverse[...].T


def attend(qkv, segments, seg_col, head_dim):
    rows, width = qkv.shape[0], qkv.shape[1] // 3
    groups, steps, tiles, heads = width // GROUP, rows // TILE, rows // SPAN, GROUP // head_dim
    return pl.pallas_call(
        functools.partial(attend_kernel, head_dim, tiles),
        grid_spec=pltpu.PrefetchScalarGridSpec(
            num_scalar_prefetch=1,
            grid=(groups, steps),
            in_specs=[
                pl.BlockSpec((TILE, GROUP), lambda g, t, s: (t, g)),
                pl.BlockSpec((rows, GROUP), lambda g, t, s: (0, groups + g)),
                pl.BlockSpec((rows, GROUP), lambda g, t, s: (0, 2 * groups + g)),
                pl.BlockSpec((1, TILE), lambda g, t, s: (0, t)),
                pl.BlockSpec((rows, 1), lambda g, t, s: (0, 0)),
            ],
            out_specs=[
                pl.BlockSpec((TILE, GROUP), lambda g, t, s: (t, g)),
                pl.BlockSpec((TILE, GROUP), lambda g, t, s: (t, g)),
                pl.BlockSpec((1, 1, tiles, SPAN, heads * TILE), lambda g, t, s: (g, t, 0, 0, 0)),
            ],
            scratch_shapes=[
                pltpu.VMEM((tiles, heads * SPAN, GROUP), LOW),
                pltpu.VMEM((tiles, GROUP, SPAN), LOW),
                pltpu.VMEM((tiles, heads, SPAN, TILE), F32),
                pltpu.VMEM((GROUP, TILE), F32),
                pltpu.VMEM((GROUP, TILE), F32),
                pltpu.VMEM((8, TILE), F32),
                pltpu.VMEM((8, TILE), F32),
            ],
        ),
        out_shape=[
            shape((rows, width), LOW),
            shape((rows, width), F32),
            shape((groups, steps, tiles, SPAN, heads * TILE), LOW),
        ],
        compiler_params=PARAMS,
        cost_estimate=CHEAP,
        name="attend",
    )(segments, qkv, qkv, qkv, segments, seg_col)


def attend_back_kernel(
    head_dim,
    tiles,
    seg_ref,
    q_ref,
    k_ref,
    v_ref,
    o_ref,
    g_ref,
    exp_ref,
    dq_ref,
    dk_ref,
    dv_ref,
    kt,
    vm,
    qm,
    gm,
    dqt,
    delta,
    dk_acc,
    dv_acc,
):
    heads = GROUP // head_dim
    here = pl.program_id(1)
    scale = head_dim ** (-0.5)

    @pl.when(here == 0)
    def _():
        dk_acc[...] = jnp.zeros_like(dk_acc)
        dv_acc[...] = jnp.zeros_like(dv_acc)
        for u in range(tiles):
            rows = slice(u * SPAN, (u + 1) * SPAN)
            kt[u] = k_ref[rows, :].astype(F32).T.astype(LOW)
            stack_heads(vm, u, v_ref[rows, :], head_dim)

    grads = g_ref[...]
    both = (grads.astype(F32) * o_ref[...].astype(F32)).T
    for h in range(heads):
        delta[h : h + 1, :] = col_sum(both[h * head_dim : (h + 1) * head_dim, :])
    stack_heads(qm, 0, q_ref[...], head_dim)
    stack_heads(gm, 0, grads, head_dim)
    dqt[...] = jnp.zeros_like(dqt)

    def step(u, carry):
        rows = pl.ds(pl.multiple_of(u * SPAN, SPAN), SPAN)
        every = mm_nt(vm[u], grads)
        dv_acc[rows, :] += mm(exp_ref[0, 0, u], gm[0])
        pieces = []
        for h in range(heads):
            grad_probs = every[h * SPAN : (h + 1) * SPAN, :] - delta[h : h + 1, :]
            weights = exp_ref[0, 0, u, :, h * TILE : (h + 1) * TILE]
            pieces.append((weights.astype(F32) * grad_probs).astype(LOW))
        for h in range(heads):
            span = slice(h * head_dim, (h + 1) * head_dim)
            dqt[span, :] += mm(kt[u, span, :], pieces[h])
        dk_acc[rows, :] += mm(jnp.concatenate(pieces, axis=1), qm[0])
        return carry

    low, high = tile_range(seg_ref, here * TILE, TILE, SPAN, tiles)
    lax.fori_loop(low, high, step, 0)
    dq_ref[...] = (dqt[...] * scale).T.astype(LOW)

    @pl.when(here == pl.num_programs(1) - 1)
    def _():
        dk_ref[...] = (dk_acc[...] * scale).astype(LOW)
        dv_ref[...] = dv_acc[...].astype(LOW)


def attend_back(qkv, attended, grad, weights, segments, head_dim):
    rows, width = attended.shape
    groups, steps, tiles, heads = width // GROUP, rows // TILE, rows // SPAN, GROUP // head_dim
    whole = pl.BlockSpec((rows, GROUP), lambda g, t, s: (0, g))
    piece = pl.BlockSpec((TILE, GROUP), lambda g, t, s: (t, g))
    return pl.pallas_call(
        functools.partial(attend_back_kernel, head_dim, tiles),
        grid_spec=pltpu.PrefetchScalarGridSpec(
            num_scalar_prefetch=1,
            grid=(groups, steps),
            in_specs=[
                piece,
                pl.BlockSpec((rows, GROUP), lambda g, t, s: (0, groups + g)),
                pl.BlockSpec((rows, GROUP), lambda g, t, s: (0, 2 * groups + g)),
                piece,
                piece,
                pl.BlockSpec((1, 1, tiles, SPAN, heads * TILE), lambda g, t, s: (g, t, 0, 0, 0)),
            ],
            out_specs=[piece, whole, whole],
            scratch_shapes=[
                pltpu.VMEM((tiles, GROUP, SPAN), LOW),
                pltpu.VMEM((tiles, heads * SPAN, GROUP), LOW),
                pltpu.VMEM((1, heads * TILE, GROUP), LOW),
                pltpu.VMEM((1, heads * TILE, GROUP), LOW),
                pltpu.VMEM((GROUP, TILE), F32),
                pltpu.VMEM((8, TILE), F32),
                pltpu.VMEM((rows, GROUP), F32),
                pltpu.VMEM((rows, GROUP), F32),
            ],
        ),
        out_shape=[shape((rows, width), LOW)] * 3,
        compiler_params=PARAMS,
        cost_estimate=CHEAP,
        name="attend_back",
    )(segments, qkv, qkv, qkv, attended, grad, weights)


def pack_kernel(up_ref, down_ref, dup_ref, ddown_ref, out_ref, dout_ref):
    for up, down, out in ((up_ref, down_ref, out_ref), (dup_ref, ddown_ref, dout_ref)):
        rows, cols = up.shape
        out[:, :cols] = up[...]
        wide = down[...].astype(F32)
        width = down.shape[1]
        for part in range(4):
            piece = wide[part * rows : (part + 1) * rows, :].astype(LOW)
            out[:, cols + part * width : cols + (part + 1) * width] = piece


def pack_shards(*shards):
    outs = [shape((w.shape[0], 2 * w.shape[1]), LOW) for w in shards[::2]]
    return pl.pallas_call(
        pack_kernel,
        in_specs=[full(s.shape) for s in shards],
        out_specs=[full(o.shape) for o in outs],
        out_shape=outs,
        grid=(1,),
        compiler_params=PARAMS,
        cost_estimate=CHEAP,
        name="pack",
    )(*shards)


def by_core(grads, group):
    pairs = grads.reshape(-1, 2, group, grads.shape[1])
    return pairs[:, 0], pairs[:, 1]


def natural_rows(block, group, kind):
    width = block.shape[1] // 4
    parts = [
        block[:, i * width : (i + 1) * width].astype(kind).reshape(-1, group, width)
        for i in range(4)
    ]
    return jnp.stack(parts, axis=1).reshape(-1, width).astype(LOW)


def enc_qkv_kernel(x_ref, vec_ref, w_ref, out_ref, normed):
    part = pl.program_id(0)

    @pl.when(part == 0)
    def _():
        unit, _ = norm_parts(x_ref[...].astype(F32))
        normed[...] = (unit * vec_ref[0:1, :] + vec_ref[3:4, :]).astype(LOW)

    bias = jnp.where(part == 0, vec_ref[4:5, :], jnp.where(part == 2, vec_ref[5:6, :], 0.0))
    out_ref[...] = (mm(normed[...], w_ref[...]) + bias).astype(LOW)


def enc_qkv_call(rows_in, vecs, weight):
    rows, width = rows_in.shape
    return pl.pallas_call(
        enc_qkv_kernel,
        grid=(3,),
        in_specs=[
            full((rows, width)),
            full(vecs.shape),
            pl.BlockSpec((width, width), lambda i: (0, i)),
        ],
        out_specs=pl.BlockSpec((rows, width), lambda i: (0, i)),
        out_shape=shape((rows, 3 * width), LOW),
        scratch_shapes=[pltpu.VMEM((rows, width), LOW)],
        compiler_params=PARAMS,
        cost_estimate=CHEAP,
        name="enc_qkv",
    )(rows_in, vecs, weight)


def enc_mid_kernel(
    chunks,
    packed,
    x_ref,
    att_ref,
    vec_ref,
    b1_ref,
    eb_ref,
    wo_ref,
    we_ref,
    *refs,
):
    up_ref, down_ref, *refs = refs
    mid_ref, out_ref, final_ref, act_ref, slope_ref, emb_ref, *refs = refs
    naturals, (normed, acc) = refs[:-2], refs[-2:]
    part = pl.program_id(0)

    @pl.when(part == 0)
    def _():
        middle = x_ref[...].astype(F32) + mm(att_ref[...], wo_ref[...]) + vec_ref[6:7, :]
        mid_ref[...] = middle
        unit, _ = norm_parts(middle)
        normed[...] = (unit * vec_ref[1:2, :] + vec_ref[7:8, :]).astype(LOW)
        acc[...] = middle + vec_ref[8:9, :]

    down = down_ref[...]
    if packed:
        down = natural_rows(down, packed, F32)
        naturals[0][...] = down
    hidden = mm(normed[...], up_ref[...]) + b1_ref[...]
    value, slope = gelu_parts(hidden)
    value = value.astype(LOW)
    act_ref[...] = value
    slope_ref[...] = slope
    acc[...] += mm(value, down)

    @pl.when(part == chunks - 1)
    def _():
        result = acc[...]
        out_ref[...] = result
        unit, _ = norm_parts(result)
        final = (unit * vec_ref[2:3, :] + vec_ref[9:10, :]).astype(LOW)
        final_ref[...] = final
        emb_ref[...] = (mm(final, we_ref[...]) + eb_ref[...]).astype(LOW)


def enc_mid(rows_in, attended, vecs, up_bias, emb_bias, wide, weights, proj_at, emb_at):
    rows, width = rows_in.shape
    hidden = up_bias.shape[1]
    emb_width = emb_bias.shape[1]
    chunks = hidden // width
    by_row = pl.BlockSpec((width, width), lambda i: (i, 0))
    specs = [pl.BlockSpec((width, width), lambda i: (0, i))]
    if len(weights) == 1:
        packed = width // (lax.axis_size("dp") * lax.axis_size("fsdp"))
        specs.append(pl.BlockSpec((width // 4, hidden), lambda i: (i, 1)))
        operands = [weights[0]] * 2
        natural_specs, natural_shapes = [by_row], [shape((hidden, width), LOW)]
    else:
        packed = 0
        specs.append(by_row)
        operands, natural_specs, natural_shapes = list(weights), [], []
    outs = pl.pallas_call(
        functools.partial(enc_mid_kernel, chunks, packed),
        grid=(chunks,),
        in_specs=[
            full((rows, width)),
            full((rows, width)),
            full(vecs.shape),
            pl.BlockSpec((1, width), lambda i: (0, i)),
            full((1, emb_width)),
            at_col(width, width, proj_at // width),
            at_col(width, emb_width, emb_at // emb_width),
        ]
        + specs,
        out_specs=[
            full((rows, width)),
            full((rows, width)),
            full((rows, width)),
            pl.BlockSpec((rows, width), lambda i: (0, i)),
            pl.BlockSpec((rows, width), lambda i: (0, i)),
            full((rows, emb_width)),
        ]
        + natural_specs,
        out_shape=[
            shape((rows, width), F32),
            shape((rows, width), F32),
            shape((rows, width), LOW),
            shape((rows, hidden), LOW),
            shape((rows, hidden), F32),
            shape((rows, emb_width), LOW),
        ]
        + natural_shapes,
        scratch_shapes=[pltpu.VMEM((rows, width), LOW), pltpu.VMEM((rows, width), F32)],
        compiler_params=PARAMS,
        cost_estimate=CHEAP,
        name="enc_mid",
    )(rows_in, attended, vecs, up_bias, emb_bias, wide, wide, *operands)
    return outs if packed else list(outs) + [weights[1]]


def enc_mid_back_kernel(
    chunks,
    packed,
    core_ref,
    elow_ref,
    final_ref,
    out_ref,
    mid_ref,
    att_ref,
    act_ref,
    slope_ref,
    vec_ref,
    wo_ref,
    w1_ref,
    w2_ref,
    we_ref,
    inv_ref,
    *refs,
):
    if packed:
        keep_ref, send_ref, keep2_ref, send2_ref, keep1_ref, send1_ref, *refs = refs
    else:
        keep_ref, dw2_ref, dw1_ref, *refs = refs
    (
        db1_ref,
    esum_ref,
    sum_ref,
    gmid_ref,
    gatt_ref,
    grad,
    grad_low,
    unit_two,
    scale_two,
    normed,
        dnorm,
    ) = refs
    first = core_ref[0] == 0

    def put(cols, grads):
        if packed:
            zero, one = by_core(grads, packed)
            keep_ref[:, :, cols] = jnp.where(first, zero, one).astype(LOW)
            send_ref[:, :, cols] = jnp.where(first, one, zero).astype(LOW)
        else:
            keep_ref[:, cols] = grads.astype(LOW)

    part = pl.program_id(0)

    @pl.when(part == 0)
    def _():
        elow = elow_ref[...]
        width = final_ref.shape[1]
        put(slice(width, width + elow.shape[1]), mm_tn(final_ref[...], elow))
        esum_ref[...] = jnp.zeros_like(esum_ref)
        esum_ref[0:1, :] = col_sum(elow.astype(F32))
        unit, scale = norm_parts(out_ref[...])
        dfinal = mm_nt(elow, we_ref[...])
        sum_ref[...] = jnp.zeros_like(sum_ref)
        sum_ref[0:1, :] = col_sum(dfinal * unit)
        sum_ref[1:2, :] = col_sum(dfinal)
        total = norm_back(dfinal, unit, scale, vec_ref[2:3, :])
        grad[...] = total
        low = total.astype(LOW)
        grad_low[...] = low
        sum_ref[2:3, :] = col_sum(low.astype(F32))
        unit, scale = norm_parts(mid_ref[...])
        unit_two[...] = unit
        scale_two[...] = jnp.broadcast_to(scale, scale_two.shape)
        normed[...] = (unit * vec_ref[1:2, :] + vec_ref[7:8, :]).T.astype(LOW)
        dnorm[...] = jnp.zeros_like(dnorm)

    low = grad_low[...]
    down = mm_tn(act_ref[...], low)
    if packed:
        width = low.shape[1]
        down = down.reshape(-1, 4, packed, width)
        for i in range(4):
            zero, one = by_core(down[:, i].reshape(-1, width), packed)
            cols = slice(i * width, (i + 1) * width)
            keep2_ref[:, :, cols] = jnp.where(first, zero, one).astype(LOW)
            send2_ref[:, :, cols] = jnp.where(first, one, zero).astype(LOW)
    else:
        dw2_ref[...] = down.astype(LOW)
    dhid = (slope_ref[...] * mm_nt(low, w2_ref[...])).astype(LOW)
    up = mm(normed[...], dhid)
    if packed:
        zero, one = by_core(up, packed)
        keep1_ref[...] = jnp.where(first, zero, one).astype(LOW)
        send1_ref[...] = jnp.where(first, one, zero).astype(LOW)
    else:
        dw1_ref[...] = up.astype(LOW)
    db1_ref[...] = col_sum(dhid.astype(F32))
    dnorm[...] += mm_nt(dhid, w1_ref[...])

    @pl.when(part == chunks - 1)
    def _():
        dn = dnorm[...]
        unit = unit_two[...]
        sum_ref[3:4, :] = col_sum(dn * unit)
        sum_ref[4:5, :] = col_sum(dn)
        gmid = grad[...] + norm_back(dn, unit, scale_two[:, 0:1], vec_ref[1:2, :])
        gmid_ref[...] = gmid
        mlow = gmid.astype(LOW)
        sum_ref[5:6, :] = col_sum(mlow.astype(F32))
        put(slice(0, mlow.shape[1]), mm_tn(att_ref[...], mlow))
        gatt_ref[...] = (mm_nt(mlow, wo_ref[...]) * inv_ref[...]).astype(LOW)


def enc_mid_back(
    core, elow, final, out, mid, attended, act, slope, inverse, vecs, wide, up_w, down_w, proj_at, emb_at
):
    rows, width = mid.shape
    hidden = down_w.shape[0]
    emb_width = elow.shape[1]
    chunks = hidden // width
    packed = width // (lax.axis_size("dp") * lax.axis_size("fsdp"))
    packed = packed if packed % 8 == 0 else 0
    by_col = pl.BlockSpec((rows, width), lambda i: (0, i))
    if packed:
        chips = width // packed // 2
        two = pl.BlockSpec((chips // chunks, packed, hidden), lambda i: (i, 0, 0))
        one = pl.BlockSpec((chips, packed, width), lambda i: (0, 0, i))
        side = (chips, packed, width + emb_width)
        specs = [full(side), full(side), two, two, one, one]
        shapes = [shape(side, LOW)] * 2 + [shape((chips, packed, hidden), LOW)] * 4
    else:
        specs = [
            full((width, width + emb_width)),
            pl.BlockSpec((width, width), lambda i: (i, 0)),
            pl.BlockSpec((width, width), lambda i: (0, i)),
        ]
        shapes = [
            shape((width, width + emb_width), LOW),
            shape((hidden, width), LOW),
            shape((width, hidden), LOW),
        ]
    return pl.pallas_call(
        functools.partial(enc_mid_back_kernel, chunks, packed),
        grid=(chunks,),
        in_specs=[
            pl.BlockSpec(memory_space=pltpu.SMEM),
            full((rows, emb_width)),
            full((rows, width)),
            full((rows, width)),
            full((rows, width)),
            full((rows, width)),
            by_col,
            by_col,
            full(vecs.shape),
            at_col(width, width, proj_at // width),
            pl.BlockSpec((width, width), lambda i: (0, i)),
            pl.BlockSpec((width, width), lambda i: (i, 0)),
            at_col(width, emb_width, emb_at // emb_width),
            full((rows, width)),
        ],
        out_specs=[
            *specs,
            pl.BlockSpec((1, width), lambda i: (0, i)),
            full((8, emb_width)),
            full((8, width)),
            full((rows, width)),
            full((rows, width)),
        ],
        out_shape=[
            *shapes,
            shape((1, hidden), F32),
            shape((8, emb_width), F32),
            shape((8, width), F32),
            shape((rows, width), F32),
            shape((rows, width), LOW),
        ],
        scratch_shapes=[
            pltpu.VMEM((rows, width), F32),
            pltpu.VMEM((rows, width), LOW),
            pltpu.VMEM((rows, width), F32),
            pltpu.VMEM((rows, LANES), F32),
            pltpu.VMEM((width, rows), LOW),
            pltpu.VMEM((rows, width), F32),
        ],
        compiler_params=PARAMS,
        cost_estimate=CHEAP,
        name="enc_mid_back",
    )(core, elow, final, out, mid, attended, act, slope, vecs, wide, up_w, down_w, wide, inverse)


def enc_qkv_back_kernel(
    packed,
    core_ref,
    x_ref,
    dq_ref,
    dk_ref,
    dv_ref,
    gmid_ref,
    vec_ref,
    more_ref,
    w_ref,
    din_ref,
    *refs,
):
    outs, sums = refs[:-1], refs[-1]
    first = core_ref[0] == 0
    width = x_ref.shape[1]

    cut = outs[0].shape[-1]

    def put(ref, cols, grads):
        if packed:
            zero, one = by_core(grads, packed)
            outs[ref][:, :, cols] = jnp.where(first, zero, one).astype(LOW)
            outs[ref + 2][:, :, cols] = jnp.where(first, one, zero).astype(LOW)
        else:
            outs[ref][:, cols] = grads.astype(LOW)

    unit, scale = norm_parts(x_ref[...].astype(F32))
    normed = (unit * vec_ref[0:1, :] + vec_ref[3:4, :]).astype(LOW)
    grads = jnp.concatenate([dq_ref[...], dk_ref[...], dv_ref[...]], axis=1)
    weight_grad = mm_tn(normed, grads)
    put(0, slice(0, cut), weight_grad[:, :cut])
    put(1, slice(0, 3 * width - cut), weight_grad[:, cut:])
    dn = mm_nt(grads, w_ref[...])
    sums[...] = jnp.zeros_like(sums)
    sums[0:16, :] = more_ref[...]
    sums[0:1, :] = col_sum(dn * unit)
    sums[3:4, :] = col_sum(dn)
    sums[4:5, :] = col_sum(dq_ref[...].astype(F32))
    sums[5:6, :] = col_sum(dv_ref[...].astype(F32))
    put(1, slice(3 * width - cut, 3 * width - cut + LANES), sums[...].T)
    din = gmid_ref[...] + norm_back(dn, unit, scale, vec_ref[0:1, :])
    din_ref[...] = din.astype(LOW)


def enc_qkv_back(core, rows_in, dq, dk, dv, gmid, vecs, more, weight):
    rows, width = rows_in.shape
    whole = full((rows, width))
    cut = (3 * width + LANES) // 2 // LANES * LANES
    halves = [cut, 3 * width + LANES - cut]
    packed = width // (lax.axis_size("dp") * lax.axis_size("fsdp"))
    packed = packed if packed % 8 == 0 else 0
    if packed:
        outs = [(width // packed // 2, packed, cols) for cols in halves * 2]
    else:
        outs = [(width, cols) for cols in halves]
    return pl.pallas_call(
        functools.partial(enc_qkv_back_kernel, packed),
        grid=(1,),
        in_specs=[pl.BlockSpec(memory_space=pltpu.SMEM)]
        + [whole] * 5
        + [full(vecs.shape), full((16, width)), at_col(width, 3 * width, 0)],
        out_specs=[whole] + [full(o) for o in outs],
        out_shape=[shape((rows, width), LOW)] + [shape(o, LOW) for o in outs],
        scratch_shapes=[pltpu.VMEM((LANES, width), F32)],
        compiler_params=PARAMS,
        cost_estimate=CHEAP,
        name="enc_qkv_back",
    )(core, rows_in, dq, dk, dv, gmid, vecs, more, weight)


def dec_in_kernel(
    limit,
    each,
    order_ref,
    line_ref,
    core_ref,
    own_one,
    own_two,
    got_one,
    got_two,
    pos_ref,
    vec_ref,
    w_ref,
    in_ref,
    qkv_ref,
):
    step = pl.program_id(0)
    width = in_ref.shape[1]
    for half, (own, got) in enumerate(((own_one, got_one), (own_two, got_two))):
        place = order_ref[0, 2 * step + half]
        rows = slice(half * BLOCK, (half + 1) * BLOCK)
        block = jnp.where(place // each % 2 == core_ref[0], own[0], got[0]).astype(F32)
        in_ref[rows, :] = jnp.where(place < limit, block, vec_ref[9:10, :]) + pos_ref[rows, :]
    unit, _ = norm_parts(in_ref[...])
    normed = (unit * vec_ref[0:1, :] + vec_ref[3:4, :]).astype(LOW)
    qkv = mm(normed, w_ref[...])
    qkv_ref[:, :width] = (qkv[:, :width] + vec_ref[4:5, :]).astype(LOW)
    qkv_ref[:, width : 2 * width] = qkv[:, width : 2 * width].astype(LOW)
    qkv_ref[:, 2 * width :] = (qkv[:, 2 * width :] + vec_ref[5:6, :]).astype(LOW)


def dec_in_call(order, line, core, own, got, pos, vecs, weight):
    rows, width = pos.shape
    each = own.shape[1] // BLOCK
    limit = 2 * own.shape[0] * each

    def chosen(half):
        def index(i, order_ref, line_ref):
            place = jnp.clip(order_ref[0, 2 * i + half], 0, limit - 1)
            chip = lax.rem(line_ref[0] - place // each // 2 + own.shape[0], own.shape[0])
            return (chip, place % each, 0)

        return pl.BlockSpec((1, BLOCK, width), index)

    return pl.pallas_call(
        functools.partial(dec_in_kernel, limit, each),
        grid_spec=pltpu.PrefetchScalarGridSpec(
            num_scalar_prefetch=2,
            grid=(rows // TILE,),
            in_specs=[
                pl.BlockSpec(memory_space=pltpu.SMEM),
                chosen(0),
                chosen(1),
                chosen(0),
                chosen(1),
                pl.BlockSpec((TILE, width), lambda i, o, z: (i, 0)),
                full(vecs.shape),
                at_col(width, 3 * width, 0),
            ],
            out_specs=[
                pl.BlockSpec((TILE, width), lambda i, o, z: (i, 0)),
                pl.BlockSpec((TILE, 3 * width), lambda i, o, z: (i, 0)),
            ],
        ),
        out_shape=[shape((rows, width), F32), shape((rows, 3 * width), LOW)],
        compiler_params=PARAMS,
        cost_estimate=CHEAP,
        name="dec_in",
    )(order, line, core, own, own, got, got, pos, vecs, weight)


def dec_mid_kernel(
    steps,
    chunks,
    packed,
    x_ref,
    att_ref,
    cot_ref,
    inv_ref,
    vec_ref,
    b1_ref,
    wo_ref,
    up_ref,
    down_ref,
    out_ref,
    gmid_ref,
    gatt_ref,
    dw_ref,
    db1_ref,
    sum_ref,
    aw1,
    aw2,
    acc,
    dnorm,
    turned,
):
    step = pl.program_id(0)
    width = x_ref.shape[1]
    hidden = chunks * width
    lead = width // 4

    @pl.when(step == 0)
    def _():
        aw1[...] = jnp.zeros_like(aw1)
        aw2[...] = jnp.zeros_like(aw2)
        db1_ref[...] = jnp.zeros_like(db1_ref)
        sum_ref[...] = jnp.zeros_like(sum_ref)

    att = att_ref[...]
    low = cot_ref[...]
    middle = x_ref[...] + mm(att, wo_ref[...]) + vec_ref[6:7, :]
    unit, scale = norm_parts(middle)
    normed = unit * vec_ref[1:2, :] + vec_ref[7:8, :]
    turned[...] = normed.T.astype(LOW)
    normed = normed.astype(LOW)
    acc[...] = middle + vec_ref[8:9, :]
    dnorm[...] = jnp.zeros_like(dnorm)

    def chunk(j, carry):
        cols = pl.ds(pl.multiple_of(j * width, width), width)
        some = pl.ds(pl.multiple_of(j * lead, lead), lead)
        up = up_ref[:, cols]
        down = natural_rows(down_ref[some, :], packed, LOW) if packed else down_ref[cols, :]
        value, slope = gelu_parts(mm(normed, up) + b1_ref[j])
        value = value.astype(LOW)
        acc[...] += mm(value, down)
        grad = mm_tn(value, low)
        if packed:
            grad = grad.reshape(-1, 4, packed, width)
            for part in range(4):
                piece = grad[:, part].reshape(lead, width)
                aw2[some, part * width : (part + 1) * width] += piece
        else:
            aw2[cols, :] += grad
        dhid = (slope * mm_nt(low, down)).astype(LOW)
        aw1[:, cols] += mm(turned[...], dhid)
        db1_ref[j] += col_sum(dhid.astype(F32))
        dnorm[...] += mm_nt(dhid, up)
        return carry

    lax.fori_loop(0, chunks, chunk, 0, unroll=2)
    out_ref[...] = acc[...].astype(LOW)
    dn = dnorm[...]
    sum_ref[0:1, :] += col_sum(dn * unit)
    sum_ref[1:2, :] += col_sum(dn)
    gmid = low.astype(F32) + norm_back(dn, unit, scale, vec_ref[1:2, :])
    gmid_ref[...] = gmid
    mlow = gmid.astype(LOW)
    sum_ref[2:3, :] += col_sum(mlow.astype(F32))
    sum_ref[3:4, :] += col_sum(low.astype(F32))
    aw1[:, hidden:] += mm_tn(att, mlow)
    gatt_ref[...] = (mm_nt(mlow, wo_ref[...]) * inv_ref[...]).astype(LOW)

    @pl.when(step == steps - 1)
    def _():
        dw_ref[:, : hidden + width] = aw1[...].astype(LOW)
        if packed:
            dw_ref[:, hidden + width :] = aw2[...].astype(LOW)
        else:
            for c in range(chunks):
                col = hidden + (1 + c) * width
                dw_ref[:, col : col + width] = aw2[c * width : (c + 1) * width, :].astype(LOW)


def dec_mid(dec_in, attended, cotangent, inverse, vecs, up_bias, wide, weights, proj_at):
    rows, width = dec_in.shape
    hidden = up_bias.shape[1]
    chunks = hidden // width
    tile = 2 * TILE
    steps = rows // tile
    by_row = pl.BlockSpec((tile, width), lambda i: (i, 0))
    if len(weights) == 1:
        packed = width // (lax.axis_size("dp") * lax.axis_size("fsdp"))
        down_shape = (width, hidden)
        specs, operands = [at_col(width, hidden, 0), at_col(width, hidden, 1)], [weights[0]] * 2
    else:
        packed, down_shape = 0, (hidden, width)
        specs, operands = [full((width, hidden)), full(down_shape)], list(weights)
    return pl.pallas_call(
        functools.partial(dec_mid_kernel, steps, chunks, packed),
        grid=(steps,),
        in_specs=[
            by_row,
            by_row,
            by_row,
            by_row,
            full(vecs.shape),
            full((chunks, 1, width)),
            at_col(width, width, proj_at // width),
        ]
        + specs,
        out_specs=[
            by_row,
            by_row,
            by_row,
            full((width, 2 * hidden + width)),
            full((chunks, 1, width)),
            full((8, width)),
        ],
        out_shape=[
            shape((rows, width), LOW),
            shape((rows, width), F32),
            shape((rows, width), LOW),
            shape((width, 2 * hidden + width), LOW),
            shape((chunks, 1, width), F32),
            shape((8, width), F32),
        ],
        scratch_shapes=[
            pltpu.VMEM((width, hidden + width), F32),
            pltpu.VMEM(down_shape, F32),
            pltpu.VMEM((tile, width), F32),
            pltpu.VMEM((tile, width), F32),
            pltpu.VMEM((width, tile), LOW),
        ],
        compiler_params=PARAMS,
        cost_estimate=CHEAP,
        name="dec_mid",
    )(
        dec_in,
        attended,
        cotangent,
        inverse,
        vecs,
        up_bias.reshape(chunks, 1, width),
        wide,
        *operands,
    )


def dec_back_kernel(
    limit,
    each,
    order_ref,
    core_ref,
    x_ref,
    dq_ref,
    dk_ref,
    dv_ref,
    gmid_ref,
    vec_ref,
    more_ref,
    w_ref,
    sum_ref,
    keep_ref,
    send_ref,
):
    step = pl.program_id(0)

    @pl.when(step == 0)
    def _():
        sum_ref[...] = more_ref[...]
        keep_ref[...] = jnp.zeros_like(keep_ref)
        send_ref[...] = jnp.zeros_like(send_ref)

    unit, scale = norm_parts(x_ref[...])
    grads = jnp.concatenate([dq_ref[...], dk_ref[...], dv_ref[...]], axis=1)
    dn = mm_nt(grads, w_ref[...])
    sum_ref[0:1, :] += col_sum(dn * unit)
    sum_ref[2:3, :] += col_sum(dn)
    sum_ref[3:4, :] += col_sum(dq_ref[...].astype(F32))
    sum_ref[4:5, :] += col_sum(dv_ref[...].astype(F32))
    din = gmid_ref[...] + norm_back(dn, unit, scale, vec_ref[0:1, :])
    per = x_ref.shape[0] // BLOCK
    for b in range(per):
        place = order_ref[0, per * step + b]
        rows = din[b * BLOCK : (b + 1) * BLOCK, :]

        owner = place // each
        spot = pl.ds(pl.multiple_of(place % each * BLOCK, BLOCK), BLOCK)

        @pl.when((place < limit) & (owner % 2 == core_ref[0]))
        def _():
            keep_ref[owner // 2, spot, :] = rows.astype(LOW)

        @pl.when((place < limit) & (owner % 2 != core_ref[0]))
        def _():
            send_ref[owner // 2, spot, :] = rows.astype(LOW)

        @pl.when(place >= limit)
        def _():
            sum_ref[8:9, :] += col_sum(rows)


def dec_back(order, core, dec_in, dq, dk, dv, gmid, vecs, more, weight, limit, each):
    rows, width = dec_in.shape
    tile = TILE
    by_row = pl.BlockSpec((tile, width), lambda i, o: (i, 0))
    side = (limit // each // 2, each * BLOCK, width)
    return pl.pallas_call(
        functools.partial(dec_back_kernel, limit, each),
        grid_spec=pltpu.PrefetchScalarGridSpec(
            num_scalar_prefetch=1,
            grid=(rows // tile,),
            in_specs=[pl.BlockSpec(memory_space=pltpu.SMEM)]
            + [by_row] * 5
            + [full(vecs.shape), full((16, width)), at_col(width, 3 * width, 0)],
            out_specs=[full((16, width)), full(side), full(side)],
        ),
        out_shape=[shape((16, width), F32), shape(side, LOW), shape(side, LOW)],
        compiler_params=PARAMS,
        cost_estimate=CHEAP,
        name="dec_back",
    )(order, core, dec_in, dq, dk, dv, gmid, vecs, more, weight)


def dec_grad_kernel(x_ref, dq_ref, dk_ref, dv_ref, vec_ref, sum_ref, dw_ref, acc, sums):
    step = pl.program_id(0)
    width = x_ref.shape[1]

    @pl.when(step == 0)
    def _():
        acc[...] = jnp.zeros_like(acc)

    unit, _ = norm_parts(x_ref[...])
    normed = (unit * vec_ref[0:1, :] + vec_ref[3:4, :]).astype(LOW)
    grads = jnp.concatenate([dq_ref[...], dk_ref[...], dv_ref[...]], axis=1)
    acc[...] += mm_tn(normed, grads)

    @pl.when(step == pl.num_programs(0) - 1)
    def _():
        dw_ref[:, : 3 * width] = acc[...].astype(LOW)
        sums[...] = jnp.zeros_like(sums)
        sums[0:16, :] = sum_ref[...]
        dw_ref[:, 3 * width :] = sums[...].T.astype(LOW)


def dec_grad(dec_in, dq, dk, dv, vecs, sums):
    rows, width = dec_in.shape
    tile = 2 * TILE
    by_row = pl.BlockSpec((tile, width), lambda i: (i, 0))
    packed = (width, 3 * width + LANES)
    return pl.pallas_call(
        dec_grad_kernel,
        grid=(rows // tile,),
        in_specs=[by_row] * 4 + [full(vecs.shape), full((16, width))],
        out_specs=full(packed),
        out_shape=shape(packed, LOW),
        scratch_shapes=[pltpu.VMEM((width, 3 * width), F32), pltpu.VMEM((LANES, width), F32)],
        compiler_params=PARAMS,
        cost_estimate=CHEAP,
        name="dec_grad",
    )(dec_in, dq, dk, dv, vecs, sums)


def positions(count, width):
    places = jnp.arange(count, dtype=jnp.float32)[:, None]
    columns = jnp.arange(width)
    rates = jnp.exp((2 * (columns // 2)).astype(jnp.float32) * (-math.log(10000.0) / width))
    angles = places * rates[None, :]
    return jnp.where((columns % 2 == 0)[None, :], jnp.sin(angles), jnp.cos(angles))


def bits_of(axis):
    size, out = lax.axis_size(axis), []
    while size > 1:
        size //= 2
        out.append((axis, size))
    return out


def all_bits():
    return bits_of("dp") + bits_of("fsdp")


def bit_here(bit):
    axis, stride = bit
    return lax.axis_index(axis) // stride % 2


def swap(value, bit):
    axis, stride = bit
    return lax.ppermute(value, axis, [(i, i ^ stride) for i in range(lax.axis_size(axis))])


def pair(own, got, here, dim):
    dims = tuple(2 if d == dim else 1 for d in range(own.ndim + 1))
    mine = lax.broadcasted_iota(jnp.int32, dims, dim) == here
    return jnp.where(mine, jnp.expand_dims(own, dim), jnp.expand_dims(got, dim))


class Gather:
    def __init__(self, piece, order, held=()):
        self.piece, self.order, self.held = piece, list(order), list(held)

    def begin(self):
        self.got = swap(self.piece, self.order[0])

    def finish(self):
        canon, bit = all_bits(), self.order.pop(0)
        dim = sum(canon.index(b) < canon.index(bit) for b in self.held)
        self.piece = pair(self.piece, self.got, bit_here(bit), dim)
        self.held.append(bit)

    def step(self):
        self.begin()
        self.finish()

    def end_beside(self, outputs):
        self.got, outputs = lax.optimization_barrier((self.got, outputs))
        self.finish()
        return outputs

    def rest(self):
        while self.order:
            self.step()
        return self.piece

    def tie(self, other):
        self.piece, other = lax.optimization_barrier((self.piece, other))
        return other


def gather(piece, order, held=()):
    return Gather(piece, order, held).rest()


def along_line(value, by):
    size = lax.axis_size("fsdp")
    return lax.ppermute(value, "fsdp", [(i, (i + 2 * by) % size) for i in range(size)])


def join(pieces, bit):
    both = [pair(own, swap(own, bit), bit_here(bit), own.ndim - 2) for own in pieces]
    both = both[0] if len(both) == 1 else jnp.concatenate(both, axis=-1)
    return both.reshape(-1, both.shape[-1])


def term_sum(terms, kind):
    total = terms[0].astype(F32)
    for term in terms[1:]:
        total = total + term.astype(F32)
    return total.astype(kind)


class Fold:
    def __init__(self, terms, order, held=None):
        self.terms, self.order, self.send = list(terms), list(order), None
        self.left = list(all_bits() if held is None else held)

    def cut(self):
        if self.send is not None:
            return
        bit = self.order[0]
        dim = self.left.index(bit)
        here = bit_here(bit)

        def half(index):
            return [lax.dynamic_index_in_dim(t, index, dim, keepdims=False) for t in self.terms]

        self.send, self.terms = term_sum(half(1 - here), LOW), half(here)

    def pass_on(self):
        bit = self.order.pop(0)
        self.left.remove(bit)
        self.terms.append(swap(self.send, bit))
        self.send = None


def split_fold(keep, send, order, held=None):
    held = all_bits() if held is None else held
    dims = (2,) * (len(held) - 1) + keep.shape[-2:]
    fold = Fold([keep.reshape(dims)], order, held)
    fold.send = send.reshape(dims)
    return fold


def start_beside(folds, inputs):
    for fold in folds:
        fold.cut()
    sends, inputs = lax.optimization_barrier(([f.send for f in folds], inputs))
    for fold, send in zip(folds, sends):
        fold.send = send
        fold.pass_on()
    return inputs


def end_beside(folds, outputs):
    last, outputs = lax.optimization_barrier(([f.terms[-1] for f in folds], outputs))
    for fold, got in zip(folds, last):
        fold.terms[-1] = got
    return outputs


def one_round(folds):
    for fold in folds:
        fold.cut()
        fold.pass_on()
    end_beside(folds, ())


def joined(folds, line):
    terms = [term_sum(f.terms, F32) for f in folds]
    return Fold([jnp.concatenate(terms, axis=-1)], line[::-1], line)


def by_bits(grads):
    bits = len(all_bits())
    rows = grads.shape[0] >> bits
    return grads.reshape((2,) * bits + (rows, grads.shape[1]))


def pack_vectors(pieces, rows):
    wide = jnp.concatenate([p.reshape(-1, rows) for p in pieces], axis=0)
    wide = jnp.pad(wide, ((0, LANES - wide.shape[0]), (0, 0)))
    return wide.T


def unpack_tall(columns, devices, width):
    rows = columns.shape[0] // devices
    parts = columns.shape[1] // width
    return (
        columns.reshape(devices, rows, parts, width)
        .transpose(0, 2, 1, 3)
        .reshape(devices * parts * rows, width)
    )


def repack_tall(weight, devices, rows):
    parts = weight.shape[0] // (devices * rows)
    width = weight.shape[1]
    return (
        weight.reshape(devices, parts, rows, width)
        .transpose(0, 2, 1, 3)
        .reshape(devices * rows, parts * width)
    )


def split_columns(array, widths):
    out, at = [], 0
    for w in widths:
        out.append(array[:, at : at + w])
        at += w
    return out


def long_vector(rows_of, devices):
    parts, total = rows_of.shape
    return rows_of.reshape(parts, devices, total // devices).transpose(1, 0, 2).reshape(1, -1)


def long_rows(vector, devices, rows):
    parts = vector.shape[0] // (devices * rows)
    return vector.reshape(devices, parts, rows).transpose(1, 0, 2).reshape(parts, -1)


def per_device(
    enc_input,
    enc_segments,
    dec_segments,
    block_order,
    dec_cotangent,
    enc_qkv,
    enc_proj,
    enc_fc1,
    enc_fc2,
    enc_gains,
    enc_biases,
    enc_fc1_bias,
    embed,
    mask_token,
    dec_qkv,
    dec_proj,
    dec_fc1,
    dec_fc2,
    dec_gains,
    dec_biases,
    dec_fc1_bias,
    dec_fc2_bias,
):
    devices = lax.axis_size("dp") * lax.axis_size("fsdp")
    enc_rows, width = enc_input.shape
    dec_rows, dwidth = dec_cotangent.shape
    erows = enc_qkv.shape[0]
    drows = dec_qkv.shape[0]
    ff = enc_fc1.shape[1]
    dff = dec_fc1.shape[1]
    emb_row = jnp.pad(dec_biases[0], (0, erows - drows))
    enc_first = jnp.concatenate(
        [
            enc_qkv,
            enc_proj,
            embed,
            pack_vectors([enc_gains, enc_biases, enc_fc1_bias, emb_row], erows),
        ],
        axis=1,
    )
    dec_first = jnp.concatenate(
        [
            dec_qkv,
            dec_proj,
            pack_vectors(
                [dec_gains, dec_biases, dec_fc2_bias[None], mask_token[None], dec_fc1_bias], drows
            ),
        ],
        axis=1,
    )
    proj_at, emb_at = 3 * width, 4 * width
    vec_at = emb_at + dwidth
    dproj_at, dvec_at = 3 * dwidth, 4 * dwidth
    ecut = (vec_at + LANES) // 2 // LANES * LANES
    here = bit_here(bits_of("fsdp")[-1]).reshape(1)
    chips = lax.axis_size("fsdp") // 2
    chip = lax.axis_index("fsdp") // 2
    dp, fsdp = bits_of("dp"), bits_of("fsdp")
    line, core = fsdp[:-1], fsdp[-1]
    packed = erows % 8 == 0 and drows % 16 == 0
    enc_rest, dec_rest = [enc_fc1, enc_fc2], [dec_fc1, dec_fc2]
    if packed:
        enc_rest, dec_rest = ([w] for w in pack_shards(*enc_rest, *dec_rest))
    enc_rest = [lax.all_gather(w, AXES, axis=0, tiled=True) for w in enc_rest]
    lined = gather(enc_first, line)
    one = Gather(lined[..., :ecut], dp[::-1], line)
    two = Gather(lined[..., ecut:], dp, line)
    one.begin()
    two.begin()
    pos = positions(dec_rows, dwidth)
    pos = one.end_beside(pos)
    two.finish()
    while one.order:
        one.step()
        two.step()
    dec_gather = Gather(dec_first, line + dp)
    one.piece = dec_gather.tie(one.piece)
    dec_gather.begin()
    enc_all = join([one.piece, two.piece], core)
    enc_all = dec_gather.end_beside(enc_all)
    while len(dec_gather.order) > 3:
        dec_gather.step()
    evecs = enc_all[:, vec_at:].T[:16].astype(F32)
    up_bias = long_vector(evecs[10:14], devices)
    emb_bias = evecs[14].reshape(devices, erows)[:, :drows].reshape(1, -1)

    enc_all, evecs = dec_gather.tie((enc_all, evecs))
    dec_gather.begin()
    qkv = enc_qkv_call(enc_input, evecs, enc_all)
    enc_col = enc_segments.reshape(-1, 1)
    qkv = dec_gather.end_beside(qkv)
    dec_gather.begin()
    attended, inverse, weights = attend(qkv, enc_segments, enc_col, HDIM)
    attended = dec_gather.end_beside(attended)
    dec_gather.begin()
    mid, enc_out, final, act, slope, embedded, down_w = enc_mid(
        enc_input,
        attended,
        evecs,
        up_bias,
        emb_bias,
        enc_all,
        enc_rest,
        proj_at,
        emb_at,
    )
    embedded, dec_rest = dec_gather.end_beside((embedded, dec_rest))
    emb_got = [along_line(embedded, by) for by in range(1, chips)]
    dec_rest = [lax.all_gather(w, AXES, axis=0, tiled=True) for w in dec_rest]
    dec_got = swap(dec_gather.piece, core)
    dim = dec_got.ndim - 2
    dec_all = pair(dec_gather.piece, dec_got, bit_here(core), dim)
    dec_all = dec_all.reshape(-1, dec_got.shape[-1])
    dvecs = pair(dec_gather.piece[..., dvec_at:], dec_got[..., dvec_at:], bit_here(core), dim)
    dvecs = dvecs.reshape(-1, LANES).T[:16].astype(F32)
    dup_bias = long_vector(dvecs[10:14], devices)
    emb_got, dec_all, dvecs, dup_bias = lax.optimization_barrier(
        (emb_got, dec_all, dvecs, dup_bias)
    )
    emb_own = jnp.stack([embedded] + emb_got)
    emb_got = swap(emb_own, core)
    limit = 2 * chips * enc_rows // BLOCK
    dec_in, dqkv = dec_in_call(
        block_order, chip.reshape(1), here, emb_own, emb_got, pos, dvecs, dec_all
    )
    dec_col = dec_segments.reshape(-1, 1)
    dattended, dinverse, dweights = attend(dqkv, dec_segments, dec_col, DHDIM)
    dec_out, dgmid, dgatt, dw_rest, db1, dsum_mid = dec_mid(
        dec_in,
        dattended,
        dec_cotangent,
        dinverse,
        dvecs,
        dup_bias,
        dec_all,
        dec_rest,
        dproj_at,
    )
    if not packed:
        chunks = dff // dwidth
        tall = dw_rest[:, dff + dwidth :].reshape(dwidth, chunks, dwidth).transpose(1, 0, 2)
        tall = repack_tall(tall.reshape(dff, dwidth), devices, drows)
        dw_rest = jnp.concatenate([dw_rest[:, : dff + dwidth], tall], axis=1)
    dec_own = lax.psum_scatter(dw_rest, "dp", scatter_dimension=0, tiled=True)
    dec_more = jnp.concatenate(
        [
            jnp.zeros((1, dwidth), F32),
            dsum_mid[0:1],
            jnp.zeros((3, dwidth), F32),
            dsum_mid[2:3],
            dsum_mid[1:2],
            dsum_mid[3:4],
            jnp.zeros((1, dwidth), F32),
            long_rows(db1.reshape(-1), devices, drows),
            jnp.zeros((3, dwidth), F32),
        ],
        axis=0,
    )
    dgatt, dec_more = lax.optimization_barrier((dgatt, dec_more))
    ddq, ddk, ddv = attend_back(dqkv, dattended, dgatt, dweights, dec_segments, DHDIM)
    dsum, keep, send = dec_back(
        block_order,
        here,
        dec_in,
        ddq,
        ddk,
        ddv,
        dgmid,
        dvecs,
        dec_more,
        dec_all,
        limit,
        enc_rows // BLOCK,
    )
    emb_terms, dsum = lax.optimization_barrier((swap(send, core), dsum))
    emb_terms = [keep, emb_terms]

    def piece_of(place):
        return [lax.dynamic_index_in_dim(t, place % chips, 0, keepdims=False) for t in emb_terms]

    emb_back = [along_line(term_sum(piece_of(chip + by), LOW), by) for by in range(1, chips)]
    dec_grads = dec_grad(dec_in, ddq, ddk, ddv, dvecs, dsum)
    emb_back, dec_grads, dec_own = lax.optimization_barrier((emb_back, dec_grads, dec_own))
    dec_grads = lax.psum_scatter(dec_grads, "dp", scatter_dimension=0, tiled=True)
    elow = term_sum(piece_of(chip) + emb_back, LOW)
    *ew, eb1, esum_emb, esum_mid, gmid, gatt = enc_mid_back(
        here,
        elow,
        final,
        enc_out,
        mid,
        attended,
        act,
        slope,
        inverse,
        evecs,
        enc_all,
        enc_rest[0],
        down_w,
        proj_at,
        emb_at,
    )
    gatt, dec_own, dec_grads = lax.optimization_barrier((gatt, dec_own, dec_grads))
    dec_own = jnp.concatenate([dec_own, dec_grads], axis=1)
    dec_own = lax.psum_scatter(dec_own, "fsdp", scatter_dimension=0, tiled=True)
    spread = [core] + line[::-1] + dp
    if packed:
        early = split_fold(ew[0], ew[1], spread)
        edown = split_fold(ew[2], ew[3], [core] + dp[::-1])
        eup = split_fold(ew[4], ew[5], [core] + dp)
    else:
        early = Fold([by_bits(ew[0])], spread)
        edown = Fold([by_bits(repack_tall(ew[1], devices, erows))], [core] + dp[::-1])
        eup = Fold([by_bits(ew[2])], [core] + dp)
    side = [eup, edown, early]
    for fold in side:
        fold.cut()
        fold.pass_on()
    emb_sum = jnp.pad(esum_emb[0].reshape(devices, drows), ((0, 0), (0, erows - drows)))
    enc_more = jnp.concatenate(
        [
            jnp.zeros((1, width), F32),
            esum_mid[3:4],
            esum_mid[0:1],
            jnp.zeros((3, width), F32),
            esum_mid[5:6],
            esum_mid[4:5],
            esum_mid[2:3],
            esum_mid[1:2],
            long_rows(eb1.reshape(-1), devices, erows),
            emb_sum.reshape(1, -1),
            jnp.zeros((1, width), F32),
        ],
        axis=0,
    )
    gatt, enc_more = end_beside(side, (gatt, enc_more))
    gatt, early.terms[-1] = start_beside([eup, edown], (gatt, early.terms[-1]))
    gatt = start_beside([early], gatt)
    dq, dk, dv = attend_back(qkv, attended, gatt, weights, enc_segments, HDIM)
    enc_in_grad, *enc_grads = enc_qkv_back(
        here, enc_input, dq, dk, dv, gmid, evecs, enc_more, enc_all
    )
    if packed:
        halves = [split_fold(enc_grads[i], enc_grads[i + 2], [core]) for i in range(2)]
    else:
        halves = [Fold([by_bits(grads)], [core]) for grads in enc_grads]
        for half in halves:
            half.cut()
    sends, dec_own = end_beside(side, ([half.send for half in halves], dec_own))
    for half, half.send in zip(halves, sends):
        half.pass_on()
    while eup.order:
        one_round(side)
    end_beside(halves, ())
    one = Fold(halves[0].terms, dp, all_bits()[:-1])
    two = Fold(halves[1].terms, dp[::-1], all_bits()[:-1])
    for fold in (one, two):
        fold.cut()
    sends, last = lax.optimization_barrier(
        ([one.send, two.send], [eup.terms[-1], edown.terms[-1]])
    )
    one.send, two.send = sends
    eup.terms[-1], edown.terms[-1] = last
    rest = joined([eup, edown], line)
    one_round([one, two, rest, early])
    if rest.order:
        rest.cut()
        rest.pass_on()
    while one.order or early.order:
        one_round([f for f in (one, two, early) if f.order])
    first = joined([one, two], line)
    first.cut()
    first.pass_on()
    end_beside([first, rest], ())
    while first.order or rest.order:
        one_round([f for f in (first, rest) if f.order])
    ep, em = split_columns(term_sum(early.terms, F32), [width, dwidth])
    eu, ed = split_columns(term_sum(rest.terms, F32), [ff, ff])
    ed = unpack_tall(ed, 1, width)
    eq, ev = split_columns(term_sum(first.terms, F32), [3 * width, LANES])
    ru, rp, rd, rq, rv = split_columns(
        dec_own.astype(F32), [dff, dwidth, dff, 3 * dwidth, LANES]
    )
    rd = unpack_tall(rd, 1, dwidth)
    rv = rv.T
    ev = ev.T
    return (
        dec_out,
        enc_in_grad,
        eq,
        ep,
        eu,
        ed,
        ev[:3],
        ev[3:10],
        ev[10:14].reshape(-1),
        em,
        rv[8],
        rq,
        rp,
        ru,
        rd,
        rv[:2],
        jnp.concatenate([ev[14:15, :drows], rv[2:7]], axis=0),
        rv[9:13].reshape(-1),
        rv[7],
    )


def solution(mesh):
    in_specs = (
        P(("dp", "fsdp"), None),
        P(("dp", "fsdp"), None),
        P(("dp", "fsdp"), None),
        P("dp", "fsdp"),
        P(("dp", "fsdp"), None),
        P(("dp", "fsdp"), None),
        P(("dp", "fsdp"), None),
        P(("dp", "fsdp"), None),
        P(("dp", "fsdp"), None),
        P(None, ("dp", "fsdp")),
        P(None, ("dp", "fsdp")),
        P(("dp", "fsdp")),
        P(("dp", "fsdp"), None),
        P(("dp", "fsdp")),
        P(("dp", "fsdp"), None),
        P(("dp", "fsdp"), None),
        P(("dp", "fsdp"), None),
        P(("dp", "fsdp"), None),
        P(None, ("dp", "fsdp")),
        P(None, ("dp", "fsdp")),
        P(("dp", "fsdp")),
        P(("dp", "fsdp")),
    )
    out_specs = (
        P(("dp", "fsdp"), None),
        P(("dp", "fsdp"), None),
        P(("dp", "fsdp"), None),
        P(("dp", "fsdp"), None),
        P(("dp", "fsdp"), None),
        P(("dp", "fsdp"), None),
        P(None, ("dp", "fsdp")),
        P(None, ("dp", "fsdp")),
        P(("dp", "fsdp")),
        P(("dp", "fsdp"), None),
        P(("dp", "fsdp")),
        P(("dp", "fsdp"), None),
        P(("dp", "fsdp"), None),
        P(("dp", "fsdp"), None),
        P(("dp", "fsdp"), None),
        P(None, ("dp", "fsdp")),
        P(None, ("dp", "fsdp")),
        P(("dp", "fsdp")),
        P(("dp", "fsdp")),
    )
    return jax.shard_map(
        per_device, mesh=mesh, in_specs=in_specs, out_specs=out_specs, check_vma=False
    )
```

```python
import functools
import math

import jax
import jax.numpy as jnp
from jax import lax
from jax.experimental import pallas as pl
from jax.experimental.pallas import tpu as pltpu
from jax.sharding import PartitionSpec as P

HDIM = 64
DHDIM = 32
BLOCK = 128
LANES = 128
TILE = 256
SPAN = 128
GROUP = 256
EPSILON = 1e-06
NEGATIVE = -1e30
LOG2E = math.log2(math.e)
AXES = ("dp", "fsdp")
F32 = jnp.float32
LOW = jnp.bfloat16
PARAMS = pltpu.CompilerParams(vmem_limit_bytes=56 * 1024 * 1024)


def mm(left, right):
    return jnp.dot(left, right, preferred_element_type=F32)


def mm_tn(left, right):
    return lax.dot_general(left, right, (((0,), (0,)), ((), ())), preferred_element_type=F32)


def mm_nt(left, right):
    return lax.dot_general(left, right, (((1,), (1,)), ((), ())), preferred_element_type=F32)


def col_sum(values):
    return jnp.sum(values, axis=0, keepdims=True)


def norm_parts(values):
    centred = values - jnp.mean(values, axis=-1, keepdims=True)
    variance = jnp.mean(centred * centred, axis=-1, keepdims=True)
    scale = lax.rsqrt(variance + EPSILON)
    return centred * scale, scale


def norm_back(grad, unit, scale, gain):
    inner = grad * gain
    mean_inner = jnp.mean(inner, axis=-1, keepdims=True)
    mean_cross = jnp.mean(inner * unit, axis=-1, keepdims=True)
    return scale * (inner - mean_inner - unit * mean_cross)


def gelu_parts(hidden):
    cdf = 0.5 + 0.5 * lax.erf(hidden * (0.5**0.5))
    density = jnp.exp(hidden * hidden * -0.5) * (1.0 / math.sqrt(2.0 * math.pi))
    return hidden * cdf, cdf + hidden * density


CHEAP = pl.CostEstimate(flops=1 << 20, bytes_accessed=1 << 16, transcendentals=0)


def full(shape):
    return pl.BlockSpec(shape, lambda *_: (0,) * len(shape))


def at_col(rows, cols, index):
    return pl.BlockSpec((rows, cols), lambda *_: (0, index))


def shape(dims, kind):
    return jax.ShapeDtypeStruct(dims, kind)


def lane_mask(head, head_dim, kind):
    lane = lax.broadcasted_iota(jnp.int32, (1, GROUP), 1)
    inside = (lane >= head * head_dim) & (lane < (head + 1) * head_dim)
    return inside.astype(F32).astype(kind)


def stack_heads(stacked, index, rows, head_dim):
    count = rows.shape[0]
    for h in range(GROUP // head_dim):
        stacked[index, h * count : (h + 1) * count, :] = rows * lane_mask(h, head_dim, LOW)


def tile_range(seg_ref, start, size, other, count):
    first, last = seg_ref[0, start], seg_ref[0, start + size - 1]
    low, high = jnp.int32(0), jnp.int32(count)
    for tile in range(count):
        low += (seg_ref[0, tile * other + other - 1] < first).astype(jnp.int32)
        high -= (seg_ref[0, tile * other] > last).astype(jnp.int32)
    return low, high


def attend_kernel(
    head_dim,
    tiles,
    seg_ref,
    q_ref,
    k_ref,
    v_ref,
    row_ref,
    col_ref,
    out_ref,
    inv_ref,
    exp_ref,
    km,
    vt,
    held,
    acc,
    inverse,
    top,
    tot,
):
    heads = GROUP // head_dim
    here = pl.program_id(1)
    factor = head_dim ** (-0.5) * LOG2E

    @pl.when(here == 0)
    def _():
        for u in range(tiles):
            rows = slice(u * SPAN, (u + 1) * SPAN)
            vt[u] = v_ref[rows, :].astype(F32).T.astype(LOW)
            stack_heads(km, u, k_ref[rows, :], head_dim)

    acc[...] = jnp.zeros_like(acc)
    top[...] = jnp.full_like(top, NEGATIVE)
    tot[...] = jnp.zeros_like(tot)
    query = q_ref[...]
    row = row_ref[...]

    def score(u, carry):
        start = pl.multiple_of(u * SPAN, SPAN)
        same = col_ref[pl.ds(start, SPAN), :] == row
        every = mm_nt(km[u], query)
        for h in range(heads):
            scores = jnp.where(same, every[h * SPAN : (h + 1) * SPAN, :], NEGATIVE)
            held[u, h] = scores
            top[h : h + 1, :] = jnp.maximum(
                top[h : h + 1, :], jnp.max(scores, axis=0, keepdims=True)
            )
        return carry

    def mix(u, carry):
        for h in range(heads):
            weights = jnp.exp2((held[u, h] - top[h : h + 1, :]) * factor)
            tot[h : h + 1, :] += col_sum(weights)
            span = slice(h * head_dim, (h + 1) * head_dim)
            weights = weights.astype(LOW)
            exp_ref[0, 0, u, :, h * TILE : (h + 1) * TILE] = weights
            acc[span, :] += mm(vt[u, span, :], weights)
        return carry

    low, high = tile_range(seg_ref, here * TILE, TILE, SPAN, tiles)
    lax.fori_loop(low, high, score, 0)
    lax.fori_loop(low, high, mix, 0)
    for h in range(heads):
        span = slice(h * head_dim, (h + 1) * head_dim)
        inverse[span, :] = jnp.broadcast_to(1.0 / tot[h : h + 1, :], (head_dim, TILE))
    out_ref[...] = (acc[...] * inverse[...]).T.astype(LOW)
    inv_ref[...] = inverse[...].T


def attend(qkv, segments, seg_col, head_dim):
    rows, width = qkv.shape[0], qkv.shape[1] // 3
    groups, steps, tiles, heads = width // GROUP, rows // TILE, rows // SPAN, GROUP // head_dim
    return pl.pallas_call(
        functools.partial(attend_kernel, head_dim, tiles),
        grid_spec=pltpu.PrefetchScalarGridSpec(
            num_scalar_prefetch=1,
            grid=(groups, steps),
            in_specs=[
                pl.BlockSpec((TILE, GROUP), lambda g, t, s: (t, g)),
                pl.BlockSpec((rows, GROUP), lambda g, t, s: (0, groups + g)),
                pl.BlockSpec((rows, GROUP), lambda g, t, s: (0, 2 * groups + g)),
                pl.BlockSpec((1, TILE), lambda g, t, s: (0, t)),
                pl.BlockSpec((rows, 1), lambda g, t, s: (0, 0)),
            ],
            out_specs=[
                pl.BlockSpec((TILE, GROUP), lambda g, t, s: (t, g)),
                pl.BlockSpec((TILE, GROUP), lambda g, t, s: (t, g)),
                pl.BlockSpec((1, 1, tiles, SPAN, heads * TILE), lambda g, t, s: (g, t, 0, 0, 0)),
            ],
            scratch_shapes=[
                pltpu.VMEM((tiles, heads * SPAN, GROUP), LOW),
                pltpu.VMEM((tiles, GROUP, SPAN), LOW),
                pltpu.VMEM((tiles, heads, SPAN, TILE), F32),
                pltpu.VMEM((GROUP, TILE), F32),
                pltpu.VMEM((GROUP, TILE), F32),
                pltpu.VMEM((8, TILE), F32),
                pltpu.VMEM((8, TILE), F32),
            ],
        ),
        out_shape=[
            shape((rows, width), LOW),
            shape((rows, width), F32),
            shape((groups, steps, tiles, SPAN, heads * TILE), LOW),
        ],
        compiler_params=PARAMS,
        cost_estimate=CHEAP,
        name="attend",
    )(segments, qkv, qkv, qkv, segments, seg_col)


def attend_back_kernel(
    head_dim,
    tiles,
    seg_ref,
    q_ref,
    k_ref,
    v_ref,
    o_ref,
    g_ref,
    exp_ref,
    dq_ref,
    dk_ref,
    dv_ref,
    kt,
    vm,
    qm,
    gm,
    dqt,
    delta,
    dk_acc,
    dv_acc,
):
    heads = GROUP // head_dim
    here = pl.program_id(1)
    scale = head_dim ** (-0.5)

    @pl.when(here == 0)
    def _():
        dk_acc[...] = jnp.zeros_like(dk_acc)
        dv_acc[...] = jnp.zeros_like(dv_acc)
        for u in range(tiles):
            rows = slice(u * SPAN, (u + 1) * SPAN)
            kt[u] = k_ref[rows, :].astype(F32).T.astype(LOW)
            stack_heads(vm, u, v_ref[rows, :], head_dim)

    grads = g_ref[...]
    both = (grads.astype(F32) * o_ref[...].astype(F32)).T
    for h in range(heads):
        delta[h : h + 1, :] = col_sum(both[h * head_dim : (h + 1) * head_dim, :])
    stack_heads(qm, 0, q_ref[...], head_dim)
    stack_heads(gm, 0, grads, head_dim)
    dqt[...] = jnp.zeros_like(dqt)

    def step(u, carry):
        rows = pl.ds(pl.multiple_of(u * SPAN, SPAN), SPAN)
        every = mm_nt(vm[u], grads)
        dv_acc[rows, :] += mm(exp_ref[0, 0, u], gm[0])
        pieces = []
        for h in range(heads):
            grad_probs = every[h * SPAN : (h + 1) * SPAN, :] - delta[h : h + 1, :]
            weights = exp_ref[0, 0, u, :, h * TILE : (h + 1) * TILE]
            pieces.append((weights.astype(F32) * grad_probs).astype(LOW))
        for h in range(heads):
            span = slice(h * head_dim, (h + 1) * head_dim)
            dqt[span, :] += mm(kt[u, span, :], pieces[h])
        dk_acc[rows, :] += mm(jnp.concatenate(pieces, axis=1), qm[0])
        return carry

    low, high = tile_range(seg_ref, here * TILE, TILE, SPAN, tiles)
    lax.fori_loop(low, high, step, 0)
    dq_ref[...] = (dqt[...] * scale).T.astype(LOW)

    @pl.when(here == pl.num_programs(1) - 1)
    def _():
        dk_ref[...] = (dk_acc[...] * scale).astype(LOW)
        dv_ref[...] = dv_acc[...].astype(LOW)


def attend_back(qkv, attended, grad, weights, segments, head_dim):
    rows, width = attended.shape
    groups, steps, tiles, heads = width // GROUP, rows // TILE, rows // SPAN, GROUP // head_dim
    whole = pl.BlockSpec((rows, GROUP), lambda g, t, s: (0, g))
    piece = pl.BlockSpec((TILE, GROUP), lambda g, t, s: (t, g))
    return pl.pallas_call(
        functools.partial(attend_back_kernel, head_dim, tiles),
        grid_spec=pltpu.PrefetchScalarGridSpec(
            num_scalar_prefetch=1,
            grid=(groups, steps),
            in_specs=[
                piece,
                pl.BlockSpec((rows, GROUP), lambda g, t, s: (0, groups + g)),
                pl.BlockSpec((rows, GROUP), lambda g, t, s: (0, 2 * groups + g)),
                piece,
                piece,
                pl.BlockSpec((1, 1, tiles, SPAN, heads * TILE), lambda g, t, s: (g, t, 0, 0, 0)),
            ],
            out_specs=[piece, whole, whole],
            scratch_shapes=[
                pltpu.VMEM((tiles, GROUP, SPAN), LOW),
                pltpu.VMEM((tiles, heads * SPAN, GROUP), LOW),
                pltpu.VMEM((1, heads * TILE, GROUP), LOW),
                pltpu.VMEM((1, heads * TILE, GROUP), LOW),
                pltpu.VMEM((GROUP, TILE), F32),
                pltpu.VMEM((8, TILE), F32),
                pltpu.VMEM((rows, GROUP), F32),
                pltpu.VMEM((rows, GROUP), F32),
            ],
        ),
        out_shape=[shape((rows, width), LOW)] * 3,
        compiler_params=PARAMS,
        cost_estimate=CHEAP,
        name="attend_back",
    )(segments, qkv, qkv, qkv, attended, grad, weights)


def pack_kernel(up_ref, down_ref, dup_ref, ddown_ref, out_ref, dout_ref):
    for up, down, out in ((up_ref, down_ref, out_ref), (dup_ref, ddown_ref, dout_ref)):
        rows, cols = up.shape
        out[:, :cols] = up[...]
        wide = down[...].astype(F32)
        width = down.shape[1]
        for part in range(4):
            piece = wide[part * rows : (part + 1) * rows, :].astype(LOW)
            out[:, cols + part * width : cols + (part + 1) * width] = piece


def pack_shards(*shards):
    outs = [shape((w.shape[0], 2 * w.shape[1]), LOW) for w in shards[::2]]
    return pl.pallas_call(
        pack_kernel,
        in_specs=[full(s.shape) for s in shards],
        out_specs=[full(o.shape) for o in outs],
        out_shape=outs,
        grid=(1,),
        compiler_params=PARAMS,
        cost_estimate=CHEAP,
        name="pack",
    )(*shards)


def by_core(grads, group):
    pairs = grads.reshape(-1, 2, group, grads.shape[1])
    return pairs[:, 0], pairs[:, 1]


def natural_rows(block, group, kind):
    width = block.shape[1] // 4
    parts = [
        block[:, i * width : (i + 1) * width].astype(kind).reshape(-1, group, width)
        for i in range(4)
    ]
    return jnp.stack(parts, axis=1).reshape(-1, width).astype(LOW)


def enc_qkv_kernel(x_ref, vec_ref, w_ref, out_ref, normed):
    part = pl.program_id(0)

    @pl.when(part == 0)
    def _():
        unit, _ = norm_parts(x_ref[...].astype(F32))
        normed[...] = (unit * vec_ref[0:1, :] + vec_ref[3:4, :]).astype(LOW)

    bias = jnp.where(part == 0, vec_ref[4:5, :], jnp.where(part == 2, vec_ref[5:6, :], 0.0))
    out_ref[...] = (mm(normed[...], w_ref[...]) + bias).astype(LOW)


def enc_qkv_call(rows_in, vecs, weight):
    rows, width = rows_in.shape
    return pl.pallas_call(
        enc_qkv_kernel,
        grid=(3,),
        in_specs=[
            full((rows, width)),
            full(vecs.shape),
            pl.BlockSpec((width, width), lambda i: (0, i)),
        ],
        out_specs=pl.BlockSpec((rows, width), lambda i: (0, i)),
        out_shape=shape((rows, 3 * width), LOW),
        scratch_shapes=[pltpu.VMEM((rows, width), LOW)],
        compiler_params=PARAMS,
        cost_estimate=CHEAP,
        name="enc_qkv",
    )(rows_in, vecs, weight)


def enc_mid_kernel(
    chunks,
    packed,
    x_ref,
    att_ref,
    vec_ref,
    b1_ref,
    eb_ref,
    wo_ref,
    we_ref,
    *refs,
):
    up_ref, down_ref, *refs = refs
    mid_ref, out_ref, final_ref, act_ref, slope_ref, emb_ref, *refs = refs
    naturals, (normed, acc) = refs[:-2], refs[-2:]
    part = pl.program_id(0)

    @pl.when(part == 0)
    def _():
        middle = x_ref[...].astype(F32) + mm(att_ref[...], wo_ref[...]) + vec_ref[6:7, :]
        mid_ref[...] = middle
        unit, _ = norm_parts(middle)
        normed[...] = (unit * vec_ref[1:2, :] + vec_ref[7:8, :]).astype(LOW)
        acc[...] = middle + vec_ref[8:9, :]

    down = down_ref[...]
    if packed:
        down = natural_rows(down, packed, F32)
        naturals[0][...] = down
    hidden = mm(normed[...], up_ref[...]) + b1_ref[...]
    value, slope = gelu_parts(hidden)
    value = value.astype(LOW)
    act_ref[...] = value
    slope_ref[...] = slope
    acc[...] += mm(value, down)

    @pl.when(part == chunks - 1)
    def _():
        result = acc[...]
        out_ref[...] = result
        unit, _ = norm_parts(result)
        final = (unit * vec_ref[2:3, :] + vec_ref[9:10, :]).astype(LOW)
        final_ref[...] = final
        emb_ref[...] = (mm(final, we_ref[...]) + eb_ref[...]).astype(LOW)


def enc_mid(rows_in, attended, vecs, up_bias, emb_bias, wide, weights, proj_at, emb_at):
    rows, width = rows_in.shape
    hidden = up_bias.shape[1]
    emb_width = emb_bias.shape[1]
    chunks = hidden // width
    by_row = pl.BlockSpec((width, width), lambda i: (i, 0))
    specs = [pl.BlockSpec((width, width), lambda i: (0, i))]
    if len(weights) == 1:
        packed = width // (lax.axis_size("dp") * lax.axis_size("fsdp"))
        specs.append(pl.BlockSpec((width // 4, hidden), lambda i: (i, 1)))
        operands = [weights[0]] * 2
        natural_specs, natural_shapes = [by_row], [shape((hidden, width), LOW)]
    else:
        packed = 0
        specs.append(by_row)
        operands, natural_specs, natural_shapes = list(weights), [], []
    outs = pl.pallas_call(
        functools.partial(enc_mid_kernel, chunks, packed),
        grid=(chunks,),
        in_specs=[
            full((rows, width)),
            full((rows, width)),
            full(vecs.shape),
            pl.BlockSpec((1, width), lambda i: (0, i)),
            full((1, emb_width)),
            at_col(width, width, proj_at // width),
            at_col(width, emb_width, emb_at // emb_width),
        ]
        + specs,
        out_specs=[
            full((rows, width)),
            full((rows, width)),
            full((rows, width)),
            pl.BlockSpec((rows, width), lambda i: (0, i)),
            pl.BlockSpec((rows, width), lambda i: (0, i)),
            full((rows, emb_width)),
        ]
        + natural_specs,
        out_shape=[
            shape((rows, width), F32),
            shape((rows, width), F32),
            shape((rows, width), LOW),
            shape((rows, hidden), LOW),
            shape((rows, hidden), F32),
            shape((rows, emb_width), LOW),
        ]
        + natural_shapes,
        scratch_shapes=[pltpu.VMEM((rows, width), LOW), pltpu.VMEM((rows, width), F32)],
        compiler_params=PARAMS,
        cost_estimate=CHEAP,
        name="enc_mid",
    )(rows_in, attended, vecs, up_bias, emb_bias, wide, wide, *operands)
    return outs if packed else list(outs) + [weights[1]]


def enc_mid_back_kernel(
    chunks,
    packed,
    core_ref,
    elow_ref,
    final_ref,
    out_ref,
    mid_ref,
    att_ref,
    act_ref,
    slope_ref,
    vec_ref,
    wo_ref,
    w1_ref,
    w2_ref,
    we_ref,
    inv_ref,
    *refs,
):
    if packed:
        keep_ref, send_ref, keep2_ref, send2_ref, keep1_ref, send1_ref, *refs = refs
    else:
        keep_ref, dw2_ref, dw1_ref, *refs = refs
    (
        db1_ref,
    esum_ref,
    sum_ref,
    gmid_ref,
    gatt_ref,
    grad,
    grad_low,
    unit_two,
    scale_two,
    normed,
        dnorm,
    ) = refs
    first = core_ref[0] == 0

    def put(cols, grads):
        if packed:
            zero, one = by_core(grads, packed)
            keep_ref[:, :, cols] = jnp.where(first, zero, one).astype(LOW)
            send_ref[:, :, cols] = jnp.where(first, one, zero).astype(LOW)
        else:
            keep_ref[:, cols] = grads.astype(LOW)

    part = pl.program_id(0)

    @pl.when(part == 0)
    def _():
        elow = elow_ref[...]
        width = final_ref.shape[1]
        put(slice(width, width + elow.shape[1]), mm_tn(final_ref[...], elow))
        esum_ref[...] = jnp.zeros_like(esum_ref)
        esum_ref[0:1, :] = col_sum(elow.astype(F32))
        unit, scale = norm_parts(out_ref[...])
        dfinal = mm_nt(elow, we_ref[...])
        sum_ref[...] = jnp.zeros_like(sum_ref)
        sum_ref[0:1, :] = col_sum(dfinal * unit)
        sum_ref[1:2, :] = col_sum(dfinal)
        total = norm_back(dfinal, unit, scale, vec_ref[2:3, :])
        grad[...] = total
        low = total.astype(LOW)
        grad_low[...] = low
        sum_ref[2:3, :] = col_sum(low.astype(F32))
        unit, scale = norm_parts(mid_ref[...])
        unit_two[...] = unit
        scale_two[...] = jnp.broadcast_to(scale, scale_two.shape)
        normed[...] = (unit * vec_ref[1:2, :] + vec_ref[7:8, :]).T.astype(LOW)
        dnorm[...] = jnp.zeros_like(dnorm)

    low = grad_low[...]
    down = mm_tn(act_ref[...], low)
    if packed:
        width = low.shape[1]
        down = down.reshape(-1, 4, packed, width)
        for i in range(4):
            zero, one = by_core(down[:, i].reshape(-1, width), packed)
            cols = slice(i * width, (i + 1) * width)
            keep2_ref[:, :, cols] = jnp.where(first, zero, one).astype(LOW)
            send2_ref[:, :, cols] = jnp.where(first, one, zero).astype(LOW)
    else:
        dw2_ref[...] = down.astype(LOW)
    dhid = (slope_ref[...] * mm_nt(low, w2_ref[...])).astype(LOW)
    up = mm(normed[...], dhid)
    if packed:
        zero, one = by_core(up, packed)
        keep1_ref[...] = jnp.where(first, zero, one).astype(LOW)
        send1_ref[...] = jnp.where(first, one, zero).astype(LOW)
    else:
        dw1_ref[...] = up.astype(LOW)
    db1_ref[...] = col_sum(dhid.astype(F32))
    dnorm[...] += mm_nt(dhid, w1_ref[...])

    @pl.when(part == chunks - 1)
    def _():
        dn = dnorm[...]
        unit = unit_two[...]
        sum_ref[3:4, :] = col_sum(dn * unit)
        sum_ref[4:5, :] = col_sum(dn)
        gmid = grad[...] + norm_back(dn, unit, scale_two[:, 0:1], vec_ref[1:2, :])
        gmid_ref[...] = gmid
        mlow = gmid.astype(LOW)
        sum_ref[5:6, :] = col_sum(mlow.astype(F32))
        put(slice(0, mlow.shape[1]), mm_tn(att_ref[...], mlow))
        gatt_ref[...] = (mm_nt(mlow, wo_ref[...]) * inv_ref[...]).astype(LOW)


def enc_mid_back(
    core, elow, final, out, mid, attended, act, slope, inverse, vecs, wide, up_w, down_w, proj_at, emb_at
):
    rows, width = mid.shape
    hidden = down_w.shape[0]
    emb_width = elow.shape[1]
    chunks = hidden // width
    packed = width // (lax.axis_size("dp") * lax.axis_size("fsdp"))
    packed = packed if packed % 8 == 0 else 0
    by_col = pl.BlockSpec((rows, width), lambda i: (0, i))
    if packed:
        chips = width // packed // 2
        two = pl.BlockSpec((chips // chunks, packed, hidden), lambda i: (i, 0, 0))
        one = pl.BlockSpec((chips, packed, width), lambda i: (0, 0, i))
        side = (chips, packed, width + emb_width)
        specs = [full(side), full(side), two, two, one, one]
        shapes = [shape(side, LOW)] * 2 + [shape((chips, packed, hidden), LOW)] * 4
    else:
        specs = [
            full((width, width + emb_width)),
            pl.BlockSpec((width, width), lambda i: (i, 0)),
            pl.BlockSpec((width, width), lambda i: (0, i)),
        ]
        shapes = [
            shape((width, width + emb_width), LOW),
            shape((hidden, width), LOW),
            shape((width, hidden), LOW),
        ]
    return pl.pallas_call(
        functools.partial(enc_mid_back_kernel, chunks, packed),
        grid=(chunks,),
        in_specs=[
            pl.BlockSpec(memory_space=pltpu.SMEM),
            full((rows, emb_width)),
            full((rows, width)),
            full((rows, width)),
            full((rows, width)),
            full((rows, width)),
            by_col,
            by_col,
            full(vecs.shape),
            at_col(width, width, proj_at // width),
            pl.BlockSpec((width, width), lambda i: (0, i)),
            pl.BlockSpec((width, width), lambda i: (i, 0)),
            at_col(width, emb_width, emb_at // emb_width),
            full((rows, width)),
        ],
        out_specs=[
            *specs,
            pl.BlockSpec((1, width), lambda i: (0, i)),
            full((8, emb_width)),
            full((8, width)),
            full((rows, width)),
            full((rows, width)),
        ],
        out_shape=[
            *shapes,
            shape((1, hidden), F32),
            shape((8, emb_width), F32),
            shape((8, width), F32),
            shape((rows, width), F32),
            shape((rows, width), LOW),
        ],
        scratch_shapes=[
            pltpu.VMEM((rows, width), F32),
            pltpu.VMEM((rows, width), LOW),
            pltpu.VMEM((rows, width), F32),
            pltpu.VMEM((rows, LANES), F32),
            pltpu.VMEM((width, rows), LOW),
            pltpu.VMEM((rows, width), F32),
        ],
        compiler_params=PARAMS,
        cost_estimate=CHEAP,
        name="enc_mid_back",
    )(core, elow, final, out, mid, attended, act, slope, vecs, wide, up_w, down_w, wide, inverse)


def enc_qkv_back_kernel(
    packed,
    core_ref,
    x_ref,
    dq_ref,
    dk_ref,
    dv_ref,
    gmid_ref,
    vec_ref,
    more_ref,
    w_ref,
    din_ref,
    *refs,
):
    outs, sums = refs[:-1], refs[-1]
    first = core_ref[0] == 0
    width = x_ref.shape[1]

    cut = outs[0].shape[-1]

    def put(ref, cols, grads):
        if packed:
            zero, one = by_core(grads, packed)
            outs[ref][:, :, cols] = jnp.where(first, zero, one).astype(LOW)
            outs[ref + 2][:, :, cols] = jnp.where(first, one, zero).astype(LOW)
        else:
            outs[ref][:, cols] = grads.astype(LOW)

    unit, scale = norm_parts(x_ref[...].astype(F32))
    normed = (unit * vec_ref[0:1, :] + vec_ref[3:4, :]).astype(LOW)
    grads = jnp.concatenate([dq_ref[...], dk_ref[...], dv_ref[...]], axis=1)
    weight_grad = mm_tn(normed, grads)
    put(0, slice(0, cut), weight_grad[:, :cut])
    put(1, slice(0, 3 * width - cut), weight_grad[:, cut:])
    dn = mm_nt(grads, w_ref[...])
    sums[...] = jnp.zeros_like(sums)
    sums[0:16, :] = more_ref[...]
    sums[0:1, :] = col_sum(dn * unit)
    sums[3:4, :] = col_sum(dn)
    sums[4:5, :] = col_sum(dq_ref[...].astype(F32))
    sums[5:6, :] = col_sum(dv_ref[...].astype(F32))
    put(1, slice(3 * width - cut, 3 * width - cut + LANES), sums[...].T)
    din = gmid_ref[...] + norm_back(dn, unit, scale, vec_ref[0:1, :])
    din_ref[...] = din.astype(LOW)


def enc_qkv_back(core, rows_in, dq, dk, dv, gmid, vecs, more, weight):
    rows, width = rows_in.shape
    whole = full((rows, width))
    cut = (3 * width + LANES) // 2 // LANES * LANES
    halves = [cut, 3 * width + LANES - cut]
    packed = width // (lax.axis_size("dp") * lax.axis_size("fsdp"))
    packed = packed if packed % 8 == 0 else 0
    if packed:
        outs = [(width // packed // 2, packed, cols) for cols in halves * 2]
    else:
        outs = [(width, cols) for cols in halves]
    return pl.pallas_call(
        functools.partial(enc_qkv_back_kernel, packed),
        grid=(1,),
        in_specs=[pl.BlockSpec(memory_space=pltpu.SMEM)]
        + [whole] * 5
        + [full(vecs.shape), full((16, width)), at_col(width, 3 * width, 0)],
        out_specs=[whole] + [full(o) for o in outs],
        out_shape=[shape((rows, width), LOW)] + [shape(o, LOW) for o in outs],
        scratch_shapes=[pltpu.VMEM((LANES, width), F32)],
        compiler_params=PARAMS,
        cost_estimate=CHEAP,
        name="enc_qkv_back",
    )(core, rows_in, dq, dk, dv, gmid, vecs, more, weight)


def dec_in_kernel(
    limit,
    each,
    order_ref,
    line_ref,
    core_ref,
    own_one,
    own_two,
    got_one,
    got_two,
    pos_ref,
    vec_ref,
    w_ref,
    in_ref,
    qkv_ref,
):
    step = pl.program_id(0)
    width = in_ref.shape[1]
    for half, (own, got) in enumerate(((own_one, got_one), (own_two, got_two))):
        place = order_ref[0, 2 * step + half]
        rows = slice(half * BLOCK, (half + 1) * BLOCK)
        block = jnp.where(place // each % 2 == core_ref[0], own[0], got[0]).astype(F32)
        in_ref[rows, :] = jnp.where(place < limit, block, vec_ref[9:10, :]) + pos_ref[rows, :]
    unit, _ = norm_parts(in_ref[...])
    normed = (unit * vec_ref[0:1, :] + vec_ref[3:4, :]).astype(LOW)
    qkv = mm(normed, w_ref[...])
    qkv_ref[:, :width] = (qkv[:, :width] + vec_ref[4:5, :]).astype(LOW)
    qkv_ref[:, width : 2 * width] = qkv[:, width : 2 * width].astype(LOW)
    qkv_ref[:, 2 * width :] = (qkv[:, 2 * width :] + vec_ref[5:6, :]).astype(LOW)


def dec_in_call(order, line, core, own, got, pos, vecs, weight):
    rows, width = pos.shape
    each = own.shape[1] // BLOCK
    limit = 2 * own.shape[0] * each

    def chosen(half):
        def index(i, order_ref, line_ref):
            place = jnp.clip(order_ref[0, 2 * i + half], 0, limit - 1)
            chip = lax.rem(line_ref[0] - place // each // 2 + own.shape[0], own.shape[0])
            return (chip, place % each, 0)

        return pl.BlockSpec((1, BLOCK, width), index)

    return pl.pallas_call(
        functools.partial(dec_in_kernel, limit, each),
        grid_spec=pltpu.PrefetchScalarGridSpec(
            num_scalar_prefetch=2,
            grid=(rows // TILE,),
            in_specs=[
                pl.BlockSpec(memory_space=pltpu.SMEM),
                chosen(0),
                chosen(1),
                chosen(0),
                chosen(1),
                pl.BlockSpec((TILE, width), lambda i, o, z: (i, 0)),
                full(vecs.shape),
                at_col(width, 3 * width, 0),
            ],
            out_specs=[
                pl.BlockSpec((TILE, width), lambda i, o, z: (i, 0)),
                pl.BlockSpec((TILE, 3 * width), lambda i, o, z: (i, 0)),
            ],
        ),
        out_shape=[shape((rows, width), F32), shape((rows, 3 * width), LOW)],
        compiler_params=PARAMS,
        cost_estimate=CHEAP,
        name="dec_in",
    )(order, line, core, own, own, got, got, pos, vecs, weight)


def dec_mid_kernel(
    steps,
    chunks,
    packed,
    x_ref,
    att_ref,
    cot_ref,
    inv_ref,
    vec_ref,
    b1_ref,
    wo_ref,
    up_ref,
    down_ref,
    out_ref,
    gmid_ref,
    gatt_ref,
    dw_ref,
    db1_ref,
    sum_ref,
    aw1,
    aw2,
    acc,
    dnorm,
    turned,
):
    step = pl.program_id(0)
    width = x_ref.shape[1]
    hidden = chunks * width
    lead = width // 4

    @pl.when(step == 0)
    def _():
        aw1[...] = jnp.zeros_like(aw1)
        aw2[...] = jnp.zeros_like(aw2)
        db1_ref[...] = jnp.zeros_like(db1_ref)
        sum_ref[...] = jnp.zeros_like(sum_ref)

    att = att_ref[...]
    low = cot_ref[...]
    middle = x_ref[...] + mm(att, wo_ref[...]) + vec_ref[6:7, :]
    unit, scale = norm_parts(middle)
    normed = unit * vec_ref[1:2, :] + vec_ref[7:8, :]
    turned[...] = normed.T.astype(LOW)
    normed = normed.astype(LOW)
    acc[...] = middle + vec_ref[8:9, :]
    dnorm[...] = jnp.zeros_like(dnorm)

    def chunk(j, carry):
        cols = pl.ds(pl.multiple_of(j * width, width), width)
        some = pl.ds(pl.multiple_of(j * lead, lead), lead)
        up = up_ref[:, cols]
        down = natural_rows(down_ref[some, :], packed, LOW) if packed else down_ref[cols, :]
        value, slope = gelu_parts(mm(normed, up) + b1_ref[j])
        value = value.astype(LOW)
        acc[...] += mm(value, down)
        grad = mm_tn(value, low)
        if packed:
            grad = grad.reshape(-1, 4, packed, width)
            for part in range(4):
                piece = grad[:, part].reshape(lead, width)
                aw2[some, part * width : (part + 1) * width] += piece
        else:
            aw2[cols, :] += grad
        dhid = (slope * mm_nt(low, down)).astype(LOW)
        aw1[:, cols] += mm(turned[...], dhid)
        db1_ref[j] += col_sum(dhid.astype(F32))
        dnorm[...] += mm_nt(dhid, up)
        return carry

    lax.fori_loop(0, chunks, chunk, 0, unroll=2)
    out_ref[...] = acc[...].astype(LOW)
    dn = dnorm[...]
    sum_ref[0:1, :] += col_sum(dn * unit)
    sum_ref[1:2, :] += col_sum(dn)
    gmid = low.astype(F32) + norm_back(dn, unit, scale, vec_ref[1:2, :])
    gmid_ref[...] = gmid
    mlow = gmid.astype(LOW)
    sum_ref[2:3, :] += col_sum(mlow.astype(F32))
    sum_ref[3:4, :] += col_sum(low.astype(F32))
    aw1[:, hidden:] += mm_tn(att, mlow)
    gatt_ref[...] = (mm_nt(mlow, wo_ref[...]) * inv_ref[...]).astype(LOW)

    @pl.when(step == steps - 1)
    def _():
        dw_ref[:, : hidden + width] = aw1[...].astype(LOW)
        if packed:
            dw_ref[:, hidden + width :] = aw2[...].astype(LOW)
        else:
            for c in range(chunks):
                col = hidden + (1 + c) * width
                dw_ref[:, col : col + width] = aw2[c * width : (c + 1) * width, :].astype(LOW)


def dec_mid(dec_in, attended, cotangent, inverse, vecs, up_bias, wide, weights, proj_at):
    rows, width = dec_in.shape
    hidden = up_bias.shape[1]
    chunks = hidden // width
    tile = 2 * TILE
    steps = rows // tile
    by_row = pl.BlockSpec((tile, width), lambda i: (i, 0))
    if len(weights) == 1:
        packed = width // (lax.axis_size("dp") * lax.axis_size("fsdp"))
        down_shape = (width, hidden)
        specs, operands = [at_col(width, hidden, 0), at_col(width, hidden, 1)], [weights[0]] * 2
    else:
        packed, down_shape = 0, (hidden, width)
        specs, operands = [full((width, hidden)), full(down_shape)], list(weights)
    return pl.pallas_call(
        functools.partial(dec_mid_kernel, steps, chunks, packed),
        grid=(steps,),
        in_specs=[
            by_row,
            by_row,
            by_row,
            by_row,
            full(vecs.shape),
            full((chunks, 1, width)),
            at_col(width, width, proj_at // width),
        ]
        + specs,
        out_specs=[
            by_row,
            by_row,
            by_row,
            full((width, 2 * hidden + width)),
            full((chunks, 1, width)),
            full((8, width)),
        ],
        out_shape=[
            shape((rows, width), LOW),
            shape((rows, width), F32),
            shape((rows, width), LOW),
            shape((width, 2 * hidden + width), LOW),
            shape((chunks, 1, width), F32),
            shape((8, width), F32),
        ],
        scratch_shapes=[
            pltpu.VMEM((width, hidden + width), F32),
            pltpu.VMEM(down_shape, F32),
            pltpu.VMEM((tile, width), F32),
            pltpu.VMEM((tile, width), F32),
            pltpu.VMEM((width, tile), LOW),
        ],
        compiler_params=PARAMS,
        cost_estimate=CHEAP,
        name="dec_mid",
    )(
        dec_in,
        attended,
        cotangent,
        inverse,
        vecs,
        up_bias.reshape(chunks, 1, width),
        wide,
        *operands,
    )


def dec_back_kernel(
    limit,
    each,
    order_ref,
    core_ref,
    x_ref,
    dq_ref,
    dk_ref,
    dv_ref,
    gmid_ref,
    vec_ref,
    more_ref,
    w_ref,
    sum_ref,
    keep_ref,
    send_ref,
):
    step = pl.program_id(0)

    @pl.when(step == 0)
    def _():
        sum_ref[...] = more_ref[...]
        keep_ref[...] = jnp.zeros_like(keep_ref)
        send_ref[...] = jnp.zeros_like(send_ref)

    unit, scale = norm_parts(x_ref[...])
    grads = jnp.concatenate([dq_ref[...], dk_ref[...], dv_ref[...]], axis=1)
    dn = mm_nt(grads, w_ref[...])
    sum_ref[0:1, :] += col_sum(dn * unit)
    sum_ref[2:3, :] += col_sum(dn)
    sum_ref[3:4, :] += col_sum(dq_ref[...].astype(F32))
    sum_ref[4:5, :] += col_sum(dv_ref[...].astype(F32))
    din = gmid_ref[...] + norm_back(dn, unit, scale, vec_ref[0:1, :])
    per = x_ref.shape[0] // BLOCK
    for b in range(per):
        place = order_ref[0, per * step + b]
        rows = din[b * BLOCK : (b + 1) * BLOCK, :]

        owner = place // each
        spot = pl.ds(pl.multiple_of(place % each * BLOCK, BLOCK), BLOCK)

        @pl.when((place < limit) & (owner % 2 == core_ref[0]))
        def _():
            keep_ref[owner // 2, spot, :] = rows.astype(LOW)

        @pl.when((place < limit) & (owner % 2 != core_ref[0]))
        def _():
            send_ref[owner // 2, spot, :] = rows.astype(LOW)

        @pl.when(place >= limit)
        def _():
            sum_ref[8:9, :] += col_sum(rows)


def dec_back(order, core, dec_in, dq, dk, dv, gmid, vecs, more, weight, limit, each):
    rows, width = dec_in.shape
    tile = TILE
    by_row = pl.BlockSpec((tile, width), lambda i, o: (i, 0))
    side = (limit // each // 2, each * BLOCK, width)
    return pl.pallas_call(
        functools.partial(dec_back_kernel, limit, each),
        grid_spec=pltpu.PrefetchScalarGridSpec(
            num_scalar_prefetch=1,
            grid=(rows // tile,),
            in_specs=[pl.BlockSpec(memory_space=pltpu.SMEM)]
            + [by_row] * 5
            + [full(vecs.shape), full((16, width)), at_col(width, 3 * width, 0)],
            out_specs=[full((16, width)), full(side), full(side)],
        ),
        out_shape=[shape((16, width), F32), shape(side, LOW), shape(side, LOW)],
        compiler_params=PARAMS,
        cost_estimate=CHEAP,
        name="dec_back",
    )(order, core, dec_in, dq, dk, dv, gmid, vecs, more, weight)


def dec_grad_kernel(x_ref, dq_ref, dk_ref, dv_ref, vec_ref, sum_ref, dw_ref, acc, sums):
    step = pl.program_id(0)
    width = x_ref.shape[1]

    @pl.when(step == 0)
    def _():
        acc[...] = jnp.zeros_like(acc)

    unit, _ = norm_parts(x_ref[...])
    normed = (unit * vec_ref[0:1, :] + vec_ref[3:4, :]).astype(LOW)
    grads = jnp.concatenate([dq_ref[...], dk_ref[...], dv_ref[...]], axis=1)
    acc[...] += mm_tn(normed, grads)

    @pl.when(step == pl.num_programs(0) - 1)
    def _():
        dw_ref[:, : 3 * width] = acc[...].astype(LOW)
        sums[...] = jnp.zeros_like(sums)
        sums[0:16, :] = sum_ref[...]
        dw_ref[:, 3 * width :] = sums[...].T.astype(LOW)


def dec_grad(dec_in, dq, dk, dv, vecs, sums):
    rows, width = dec_in.shape
    tile = 2 * TILE
    by_row = pl.BlockSpec((tile, width), lambda i: (i, 0))
    packed = (width, 3 * width + LANES)
    return pl.pallas_call(
        dec_grad_kernel,
        grid=(rows // tile,),
        in_specs=[by_row] * 4 + [full(vecs.shape), full((16, width))],
        out_specs=full(packed),
        out_shape=shape(packed, LOW),
        scratch_shapes=[pltpu.VMEM((width, 3 * width), F32), pltpu.VMEM((LANES, width), F32)],
        compiler_params=PARAMS,
        cost_estimate=CHEAP,
        name="dec_grad",
    )(dec_in, dq, dk, dv, vecs, sums)


def positions(count, width):
    places = jnp.arange(count, dtype=jnp.float32)[:, None]
    columns = jnp.arange(width)
    rates = jnp.exp((2 * (columns // 2)).astype(jnp.float32) * (-math.log(10000.0) / width))
    angles = places * rates[None, :]
    return jnp.where((columns % 2 == 0)[None, :], jnp.sin(angles), jnp.cos(angles))


def bits_of(axis):
    size, out = lax.axis_size(axis), []
    while size > 1:
        size //= 2
        out.append((axis, size))
    return out


def all_bits():
    return bits_of("dp") + bits_of("fsdp")


def bit_here(bit):
    axis, stride = bit
    return lax.axis_index(axis) // stride % 2


def swap(value, bit):
    axis, stride = bit
    return lax.ppermute(value, axis, [(i, i ^ stride) for i in range(lax.axis_size(axis))])


def pair(own, got, here, dim):
    dims = tuple(2 if d == dim else 1 for d in range(own.ndim + 1))
    mine = lax.broadcasted_iota(jnp.int32, dims, dim) == here
    return jnp.where(mine, jnp.expand_dims(own, dim), jnp.expand_dims(got, dim))


class Gather:
    def __init__(self, piece, order, held=()):
        self.piece, self.order, self.held = piece, list(order), list(held)

    def begin(self):
        self.got = swap(self.piece, self.order[0])

    def finish(self):
        canon, bit = all_bits(), self.order.pop(0)
        dim = sum(canon.index(b) < canon.index(bit) for b in self.held)
        self.piece = pair(self.piece, self.got, bit_here(bit), dim)
        self.held.append(bit)

    def step(self):
        self.begin()
        self.finish()

    def end_beside(self, outputs):
        self.got, outputs = lax.optimization_barrier((self.got, outputs))
        self.finish()
        return outputs

    def rest(self):
        while self.order:
            self.step()
        return self.piece

    def tie(self, other):
        self.piece, other = lax.optimization_barrier((self.piece, other))
        return other


def gather(piece, order, held=()):
    return Gather(piece, order, held).rest()


def along_line(value, by):
    size = lax.axis_size("fsdp")
    return lax.ppermute(value, "fsdp", [(i, (i + 2 * by) % size) for i in range(size)])


def join(pieces, bit):
    both = [pair(own, swap(own, bit), bit_here(bit), own.ndim - 2) for own in pieces]
    both = both[0] if len(both) == 1 else jnp.concatenate(both, axis=-1)
    return both.reshape(-1, both.shape[-1])


def term_sum(terms, kind):
    total = terms[0].astype(F32)
    for term in terms[1:]:
        total = total + term.astype(F32)
    return total.astype(kind)


class Fold:
    def __init__(self, terms, order, held=None):
        self.terms, self.order, self.send = list(terms), list(order), None
        self.left = list(all_bits() if held is None else held)

    def cut(self):
        if self.send is not None:
            return
        bit = self.order[0]
        dim = self.left.index(bit)
        here = bit_here(bit)

        def half(index):
            return [lax.dynamic_index_in_dim(t, index, dim, keepdims=False) for t in self.terms]

        self.send, self.terms = term_sum(half(1 - here), LOW), half(here)

    def pass_on(self):
        bit = self.order.pop(0)
        self.left.remove(bit)
        self.terms.append(swap(self.send, bit))
        self.send = None


def split_fold(keep, send, order, held=None):
    held = all_bits() if held is None else held
    dims = (2,) * (len(held) - 1) + keep.shape[-2:]
    fold = Fold([keep.reshape(dims)], order, held)
    fold.send = send.reshape(dims)
    return fold


def start_beside(folds, inputs):
    for fold in folds:
        fold.cut()
    sends, inputs = lax.optimization_barrier(([f.send for f in folds], inputs))
    for fold, send in zip(folds, sends):
        fold.send = send
        fold.pass_on()
    return inputs


def end_beside(folds, outputs):
    last, outputs = lax.optimization_barrier(([f.terms[-1] for f in folds], outputs))
    for fold, got in zip(folds, last):
        fold.terms[-1] = got
    return outputs


def one_round(folds):
    for fold in folds:
        fold.cut()
        fold.pass_on()
    end_beside(folds, ())


def joined(folds, line):
    terms = [term_sum(f.terms, F32) for f in folds]
    return Fold([jnp.concatenate(terms, axis=-1)], line[::-1], line)


def by_bits(grads):
    bits = len(all_bits())
    rows = grads.shape[0] >> bits
    return grads.reshape((2,) * bits + (rows, grads.shape[1]))


def pack_vectors(pieces, rows):
    wide = jnp.concatenate([p.reshape(-1, rows) for p in pieces], axis=0)
    wide = jnp.pad(wide, ((0, LANES - wide.shape[0]), (0, 0)))
    return wide.T


def unpack_tall(columns, devices, width):
    rows = columns.shape[0] // devices
    parts = columns.shape[1] // width
    return (
        columns.reshape(devices, rows, parts, width)
        .transpose(0, 2, 1, 3)
        .reshape(devices * parts * rows, width)
    )


def repack_tall(weight, devices, rows):
    parts = weight.shape[0] // (devices * rows)
    width = weight.shape[1]
    return (
        weight.reshape(devices, parts, rows, width)
        .transpose(0, 2, 1, 3)
        .reshape(devices * rows, parts * width)
    )


def split_columns(array, widths):
    out, at = [], 0
    for w in widths:
        out.append(array[:, at : at + w])
        at += w
    return out


def long_vector(rows_of, devices):
    parts, total = rows_of.shape
    return rows_of.reshape(parts, devices, total // devices).transpose(1, 0, 2).reshape(1, -1)


def long_rows(vector, devices, rows):
    parts = vector.shape[0] // (devices * rows)
    return vector.reshape(devices, parts, rows).transpose(1, 0, 2).reshape(parts, -1)


def per_device(
    enc_input,
    enc_segments,
    dec_segments,
    block_order,
    dec_cotangent,
    enc_qkv,
    enc_proj,
    enc_fc1,
    enc_fc2,
    enc_gains,
    enc_biases,
    enc_fc1_bias,
    embed,
    mask_token,
    dec_qkv,
    dec_proj,
    dec_fc1,
    dec_fc2,
    dec_gains,
    dec_biases,
    dec_fc1_bias,
    dec_fc2_bias,
):
    devices = lax.axis_size("dp") * lax.axis_size("fsdp")
    enc_rows, width = enc_input.shape
    dec_rows, dwidth = dec_cotangent.shape
    erows = enc_qkv.shape[0]
    drows = dec_qkv.shape[0]
    ff = enc_fc1.shape[1]
    dff = dec_fc1.shape[1]
    emb_row = jnp.pad(dec_biases[0], (0, erows - drows))
    enc_first = jnp.concatenate(
        [
            enc_qkv,
            enc_proj,
            embed,
            pack_vectors([enc_gains, enc_biases, enc_fc1_bias, emb_row], erows),
        ],
        axis=1,
    )
    dec_first = jnp.concatenate(
        [
            dec_qkv,
            dec_proj,
            pack_vectors(
                [dec_gains, dec_biases, dec_fc2_bias[None], mask_token[None], dec_fc1_bias], drows
            ),
        ],
        axis=1,
    )
    proj_at, emb_at = 3 * width, 4 * width
    vec_at = emb_at + dwidth
    dproj_at, dvec_at = 3 * dwidth, 4 * dwidth
    ecut = (vec_at + LANES) // 2 // LANES * LANES
    here = bit_here(bits_of("fsdp")[-1]).reshape(1)
    chips = lax.axis_size("fsdp") // 2
    chip = lax.axis_index("fsdp") // 2
    dp, fsdp = bits_of("dp"), bits_of("fsdp")
    line, core = fsdp[:-1], fsdp[-1]
    packed = erows % 8 == 0 and drows % 16 == 0
    enc_rest, dec_rest = [enc_fc1, enc_fc2], [dec_fc1, dec_fc2]
    if packed:
        enc_rest, dec_rest = ([w] for w in pack_shards(*enc_rest, *dec_rest))
    enc_rest = [lax.all_gather(w, AXES, axis=0, tiled=True) for w in enc_rest]
    lined = gather(enc_first, line)
    one = Gather(lined[..., :ecut], dp[::-1], line)
    two = Gather(lined[..., ecut:], dp, line)
    one.begin()
    two.begin()
    pos = positions(dec_rows, dwidth)
    pos = one.end_beside(pos)
    two.finish()
    while one.order:
        one.step()
        two.step()
    enc_all = join([one.piece, two.piece], core)
    evecs = enc_all[:, vec_at:].T[:16].astype(F32)
    up_bias = long_vector(evecs[10:14], devices)
    emb_bias = evecs[14].reshape(devices, erows)[:, :drows].reshape(1, -1)

    dec_gather = Gather(dec_first, line + dp)
    enc_all, evecs = dec_gather.tie((enc_all, evecs))
    dec_gather.begin()
    qkv = enc_qkv_call(enc_input, evecs, enc_all)
    enc_col = enc_segments.reshape(-1, 1)
    qkv = dec_gather.end_beside(qkv)
    dec_gather.begin()
    attended, inverse, weights = attend(qkv, enc_segments, enc_col, HDIM)
    attended = dec_gather.end_beside(attended)
    while len(dec_gather.order) > 2:
        dec_gather.step()
    dec_gather.begin()
    mid, enc_out, final, act, slope, embedded, down_w = enc_mid(
        enc_input,
        attended,
        evecs,
        up_bias,
        emb_bias,
        enc_all,
        enc_rest,
        proj_at,
        emb_at,
    )
    embedded, dec_rest = dec_gather.end_beside((embedded, dec_rest))
    emb_got = [along_line(embedded, by) for by in range(1, chips)]
    dec_rest = [lax.all_gather(w, AXES, axis=0, tiled=True) for w in dec_rest]
    dec_gather.begin()
    emb_got = dec_gather.end_beside(emb_got)
    emb_own = jnp.stack([embedded] + emb_got)
    emb_got = swap(emb_own, core)
    dec_got = swap(dec_gather.piece, core)
    dim = dec_got.ndim - 2
    dec_all = pair(dec_gather.piece, dec_got, bit_here(core), dim)
    dec_all = dec_all.reshape(-1, dec_got.shape[-1])
    dvecs = pair(dec_gather.piece[..., dvec_at:], dec_got[..., dvec_at:], bit_here(core), dim)
    dvecs = dvecs.reshape(-1, LANES).T[:16].astype(F32)
    dup_bias = long_vector(dvecs[10:14], devices)
    limit = 2 * chips * enc_rows // BLOCK
    dec_in, dqkv = dec_in_call(
        block_order, chip.reshape(1), here, emb_own, emb_got, pos, dvecs, dec_all
    )
    dec_col = dec_segments.reshape(-1, 1)
    dattended, dinverse, dweights = attend(dqkv, dec_segments, dec_col, DHDIM)
    dec_out, dgmid, dgatt, dw_rest, db1, dsum_mid = dec_mid(
        dec_in,
        dattended,
        dec_cotangent,
        dinverse,
        dvecs,
        dup_bias,
        dec_all,
        dec_rest,
        dproj_at,
    )
    if not packed:
        chunks = dff // dwidth
        tall = dw_rest[:, dff + dwidth :].reshape(dwidth, chunks, dwidth).transpose(1, 0, 2)
        tall = repack_tall(tall.reshape(dff, dwidth), devices, drows)
        dw_rest = jnp.concatenate([dw_rest[:, : dff + dwidth], tall], axis=1)
    dec_own = lax.psum_scatter(dw_rest, "dp", scatter_dimension=0, tiled=True)
    dec_more = jnp.concatenate(
        [
            jnp.zeros((1, dwidth), F32),
            dsum_mid[0:1],
            jnp.zeros((3, dwidth), F32),
            dsum_mid[2:3],
            dsum_mid[1:2],
            dsum_mid[3:4],
            jnp.zeros((1, dwidth), F32),
            long_rows(db1.reshape(-1), devices, drows),
            jnp.zeros((3, dwidth), F32),
        ],
        axis=0,
    )
    dgatt, dec_more = lax.optimization_barrier((dgatt, dec_more))
    ddq, ddk, ddv = attend_back(dqkv, dattended, dgatt, dweights, dec_segments, DHDIM)
    dsum, keep, send = dec_back(
        block_order,
        here,
        dec_in,
        ddq,
        ddk,
        ddv,
        dgmid,
        dvecs,
        dec_more,
        dec_all,
        limit,
        enc_rows // BLOCK,
    )
    emb_terms, dsum = lax.optimization_barrier((swap(send, core), dsum))
    emb_terms = [keep, emb_terms]

    def piece_of(place):
        return [lax.dynamic_index_in_dim(t, place % chips, 0, keepdims=False) for t in emb_terms]

    emb_back = [along_line(term_sum(piece_of(chip + by), LOW), by) for by in range(1, chips)]
    dec_grads = dec_grad(dec_in, ddq, ddk, ddv, dvecs, dsum)
    emb_back[0], dec_grads, dec_own = lax.optimization_barrier(
        (emb_back[0], dec_grads, dec_own)
    )
    dec_grads = lax.psum_scatter(dec_grads, "dp", scatter_dimension=0, tiled=True)
    elow = term_sum(piece_of(chip) + emb_back, LOW)
    *ew, eb1, esum_emb, esum_mid, gmid, gatt = enc_mid_back(
        here,
        elow,
        final,
        enc_out,
        mid,
        attended,
        act,
        slope,
        inverse,
        evecs,
        enc_all,
        enc_rest[0],
        down_w,
        proj_at,
        emb_at,
    )
    gatt, dec_own, dec_grads = lax.optimization_barrier((gatt, dec_own, dec_grads))
    dec_own = jnp.concatenate([dec_own, dec_grads], axis=1)
    dec_own = lax.psum_scatter(dec_own, "fsdp", scatter_dimension=0, tiled=True)
    spread = [core] + line[::-1] + dp
    if packed:
        early = split_fold(ew[0], ew[1], spread)
        edown = split_fold(ew[2], ew[3], [core] + dp[::-1])
        eup = split_fold(ew[4], ew[5], [core] + dp)
    else:
        early = Fold([by_bits(ew[0])], spread)
        edown = Fold([by_bits(repack_tall(ew[1], devices, erows))], [core] + dp[::-1])
        eup = Fold([by_bits(ew[2])], [core] + dp)
    side = [eup, edown, early]
    for fold in side:
        fold.cut()
        fold.pass_on()
    emb_sum = jnp.pad(esum_emb[0].reshape(devices, drows), ((0, 0), (0, erows - drows)))
    enc_more = jnp.concatenate(
        [
            jnp.zeros((1, width), F32),
            esum_mid[3:4],
            esum_mid[0:1],
            jnp.zeros((3, width), F32),
            esum_mid[5:6],
            esum_mid[4:5],
            esum_mid[2:3],
            esum_mid[1:2],
            long_rows(eb1.reshape(-1), devices, erows),
            emb_sum.reshape(1, -1),
            jnp.zeros((1, width), F32),
        ],
        axis=0,
    )
    gatt, enc_more = end_beside(side, (gatt, enc_more))
    gatt, early.terms[-1] = start_beside([eup, edown], (gatt, early.terms[-1]))
    gatt = start_beside([early], gatt)
    dq, dk, dv = attend_back(qkv, attended, gatt, weights, enc_segments, HDIM)
    enc_in_grad, *enc_grads = enc_qkv_back(
        here, enc_input, dq, dk, dv, gmid, evecs, enc_more, enc_all
    )
    if packed:
        halves = [split_fold(enc_grads[i], enc_grads[i + 2], [core]) for i in range(2)]
    else:
        halves = [Fold([by_bits(grads)], [core]) for grads in enc_grads]
        for half in halves:
            half.cut()
    sends, dec_own = end_beside(side, ([half.send for half in halves], dec_own))
    for half, half.send in zip(halves, sends):
        half.pass_on()
    while eup.order:
        one_round(side)
    end_beside(halves, ())
    one = Fold(halves[0].terms, dp, all_bits()[:-1])
    two = Fold(halves[1].terms, dp[::-1], all_bits()[:-1])
    for fold in (one, two):
        fold.cut()
    sends, last = lax.optimization_barrier(
        ([one.send, two.send], [eup.terms[-1], edown.terms[-1]])
    )
    one.send, two.send = sends
    eup.terms[-1], edown.terms[-1] = last
    rest = joined([eup, edown], line)
    one_round([one, two, rest, early])
    if rest.order:
        rest.cut()
        rest.pass_on()
    while one.order or early.order:
        one_round([f for f in (one, two, early) if f.order])
    first = joined([one, two], line)
    first.cut()
    first.pass_on()
    end_beside([first, rest], ())
    while first.order or rest.order:
        one_round([f for f in (first, rest) if f.order])
    ep, em = split_columns(term_sum(early.terms, F32), [width, dwidth])
    eu, ed = split_columns(term_sum(rest.terms, F32), [ff, ff])
    ed = unpack_tall(ed, 1, width)
    eq, ev = split_columns(term_sum(first.terms, F32), [3 * width, LANES])
    ru, rp, rd, rq, rv = split_columns(
        dec_own.astype(F32), [dff, dwidth, dff, 3 * dwidth, LANES]
    )
    rd = unpack_tall(rd, 1, dwidth)
    rv = rv.T
    ev = ev.T
    return (
        dec_out,
        enc_in_grad,
        eq,
        ep,
        eu,
        ed,
        ev[:3],
        ev[3:10],
        ev[10:14].reshape(-1),
        em,
        rv[8],
        rq,
        rp,
        ru,
        rd,
        rv[:2],
        jnp.concatenate([ev[14:15, :drows], rv[2:7]], axis=0),
        rv[9:13].reshape(-1),
        rv[7],
    )


def solution(mesh):
    in_specs = (
        P(("dp", "fsdp"), None),
        P(("dp", "fsdp"), None),
        P(("dp", "fsdp"), None),
        P("dp", "fsdp"),
        P(("dp", "fsdp"), None),
        P(("dp", "fsdp"), None),
        P(("dp", "fsdp"), None),
        P(("dp", "fsdp"), None),
        P(("dp", "fsdp"), None),
        P(None, ("dp", "fsdp")),
        P(None, ("dp", "fsdp")),
        P(("dp", "fsdp")),
        P(("dp", "fsdp"), None),
        P(("dp", "fsdp")),
        P(("dp", "fsdp"), None),
        P(("dp", "fsdp"), None),
        P(("dp", "fsdp"), None),
        P(("dp", "fsdp"), None),
        P(None, ("dp", "fsdp")),
        P(None, ("dp", "fsdp")),
        P(("dp", "fsdp")),
        P(("dp", "fsdp")),
    )
    out_specs = (
        P(("dp", "fsdp"), None),
        P(("dp", "fsdp"), None),
        P(("dp", "fsdp"), None),
        P(("dp", "fsdp"), None),
        P(("dp", "fsdp"), None),
        P(("dp", "fsdp"), None),
        P(None, ("dp", "fsdp")),
        P(None, ("dp", "fsdp")),
        P(("dp", "fsdp")),
        P(("dp", "fsdp"), None),
        P(("dp", "fsdp")),
        P(("dp", "fsdp"), None),
        P(("dp", "fsdp"), None),
        P(("dp", "fsdp"), None),
        P(("dp", "fsdp"), None),
        P(None, ("dp", "fsdp")),
        P(None, ("dp", "fsdp")),
        P(("dp", "fsdp")),
        P(("dp", "fsdp")),
    )
    return jax.shard_map(
        per_device, mesh=mesh, in_specs=in_specs, out_specs=out_specs, check_vma=False
    )
```
